32 devices in a mesh: row: 4 (over z), col: 8 (over y, x, core).
Axes of the slice: x: 2, y: 2, z: 4, core: 2. Of those that a mesh axis runs over, the one named last changes fastest.
Arguments:
- tokens: bfloat16 [16384, 1024], P('row', 'col'), may hold values from -6 to 6
- cotangent: bfloat16 [16384, 1024], P('row', 'col'), may hold values from -6 to 6
- adapter_ids: int32 [16, 4], P('row'), may hold values from 0 to 7
- qkv_weight: bfloat16 [2, 1024, 3, 1024], P(None, 'row', None, 'col'), may hold values from -0.09375 to 0.09375
- qkv_bias: bfloat16 [2, 3, 1024], P(None, None, 'col'), may hold values from -1.796875 to 1.796875
- proj_weight: bfloat16 [2, 1024, 1024], P(None, 'col', 'row'), may hold values from -4 to 4
- proj_bias: bfloat16 [2, 1024], P(None, 'col'), may hold values from -1.796875 to 1.796875
- up_weight: bfloat16 [2, 1024, 4096], P(None, 'row', 'col'), may hold values from -0.09375 to 0.09375
- up_bias: bfloat16 [2, 4096], P(None, 'col'), may hold values from -1.796875 to 1.796875
- down_weight: bfloat16 [2, 4096, 1024], P(None, 'col', 'row'), may hold values from -0.09375 to 0.09375
- down_bias: bfloat16 [2, 1024], P(None, 'col'), may hold values from -1.796875 to 1.796875
- first_gain: bfloat16 [2, 1024], P(None, 'col'), may hold values from 0.5 to 1.5
- first_shift: bfloat16 [2, 1024], P(None, 'col'), may hold values from -1.796875 to 1.796875
- second_gain: bfloat16 [2, 1024], P(None, 'col'), may hold values from 0.5 to 1.5
- second_shift: bfloat16 [2, 1024], P(None, 'col'), may hold values from -1.796875 to 1.796875
- qkv_lower: bfloat16 [2, 8, 1024, 16], replicated, may hold values from -0.1875 to 0.1875
- qkv_raise: bfloat16 [2, 8, 16, 3, 1024], replicated, may hold values from -0.75 to 0.75
- proj_lower: bfloat16 [2, 8, 1024, 16], replicated, may hold values from -4 to 4
- proj_raise: bfloat16 [2, 8, 16, 1024], replicated, may hold values from -0.75 to 0.75
- up_lower: bfloat16 [2, 8, 1024, 16], replicated, may hold values from -0.1875 to 0.1875
- up_raise: bfloat16 [2, 8, 16, 4096], replicated, may hold values from -0.75 to 0.75
- down_lower: bfloat16 [2, 8, 4096, 16], replicated, may hold values from -0.09375 to 0.09375
- down_raise: bfloat16 [2, 8, 16, 1024], replicated, may hold values from -0.75 to 0.75
Outputs:
- result: float32 [16384, 1024], P('row', 'col')
- input_grad: float32 [16384, 1024], P('row', 'col')
- grad_qkv_lower: float32 [2, 8, 1024, 16], P(None, None, 'col')
- grad_qkv_raise: float32 [2, 8, 16, 3, 1024], P(None, None, None, None, 'col')
- grad_proj_lower: float32 [2, 8, 1024, 16], P(None, None, 'col')
- grad_proj_raise: float32 [2, 8, 16, 1024], P(None, None, None, 'col')
- grad_up_lower: float32 [2, 8, 1024, 16], P(None, None, 'col')
- grad_up_raise: float32 [2, 8, 16, 4096], P(None, None, None, 'col')
- grad_down_lower: float32 [2, 8, 4096, 16], P(None, None, 'col')
- grad_down_raise: float32 [2, 8, 16, 1024], P(None, None, None, 'col')
The draws below stay inside these ranges and needn't reach their ends.
Inputs may be any that keep to these rules, and one draw needn't show every extreme that they name: adapter_ids[s, k] names the adapter of sequence s at site k.
All inputs are finite; a program needn't handle non-finite values.
Results may differ from the reference program's by a relative error of at most 0.018.
Values may be sent and summed in bfloat16 or wider, within the bound.
A program may use at most 256 MiB of HBM per device.

```python
from functools import partial
import jax
import jax.numpy as jnp
from jax import lax

D = 1024
HEADS = 16
HD = 64
FF = 4096
RANK = 16
ADAPTERS = 8
LAYERS = 2
LEN = 1024
BLOCK = 256
SEQS = 16
TOKENS = 16384


def frozen_matrix(key, array_shape, column_shape, low_scale, high_scale):
    key_entries, key_offset, key_scale = jax.random.split(key, 3)
    row_shape = array_shape[:2] + (1,) * (len(array_shape) - 2)
    scales = jax.random.uniform(key_scale, row_shape, jnp.float32, low_scale, high_scale)
    entries = jax.random.normal(key_entries, array_shape, jnp.float32) * scales
    offsets = jnp.clip(jax.random.normal(key_offset, column_shape, jnp.float32), -2.0, 2.0) * 0.15
    values = jnp.clip(entries + offsets, -3.0, 3.0) * D ** (-0.5)
    return values.astype(jnp.bfloat16)


def draw_qkv_weight(key, part):
    key = jax.random.fold_in(key, 11)
    low_scale, high_scale = (1.0, 1.0)
    return frozen_matrix(key, (LAYERS, D, 3, D), (LAYERS, 1, 3, D), low_scale, high_scale)


def draw_up_weight(key, part):
    key = jax.random.fold_in(key, 23)
    low_scale, high_scale = (1.0, 1.0)
    return frozen_matrix(key, (LAYERS, D, FF), (LAYERS, 1, FF), low_scale, high_scale)


def touch_ends(result, rng, smallest, largest):
    shape = result.shape
    index_at = [jax.random.randint(jax.random.fold_in(rng, axis), (), 0, shape[axis]) for axis in range(len(shape))]
    result = result.at[tuple(index_at)].set(smallest)
    longest = shape.index(max(shape))
    index_at[longest] = (index_at[longest] + 1) % shape[longest]
    return result.at[tuple(index_at)].set(largest)


def block_scale(rng, shape, pieces, smallest, largest):
    def one(dim, shards_of):
        draws = jax.random.uniform(jax.random.fold_in(jax.random.fold_in(rng, 6), dim), (shards_of,), jnp.float32, smallest / len(pieces), largest / len(pieces))
        return jnp.repeat(jnp.exp(draws), shape[dim] // shards_of).reshape((-1,) + (1,) * (len(shape) - dim - 1))

    loudness = one(*pieces[0])
    for cut in pieces[1:]:
        loudness = loudness * one(*cut)
    return loudness


def gaussian(own_key, extent, deviation, limit, pieces=(), kind=jnp.bfloat16):
    drawn = deviation * jax.random.normal(own_key, extent, jnp.float32)
    if pieces:
        drawn = drawn * block_scale(own_key, extent, pieces, -0.22, 0.18)
    return jnp.clip(drawn, -limit, limit).astype(kind)


def setup_inputs(seed: int = 0) -> dict:
    key_of = jax.random.split(jax.random.key(seed), 24)
    tokens = gaussian(key_of[0], (TOKENS, D), 1.0, 6.0, ((0, 4), (1, 8)))
    cotangent = gaussian(key_of[1], (TOKENS, D), 1.0, 6.0, ((0, 4), (1, 8)))
    adapter_ids = touch_ends(jax.random.randint(key_of[2], (SEQS, 4), 0, ADAPTERS), jax.random.fold_in(key_of[2], 1), 0, ADAPTERS - 1).astype(jnp.int32)
    qkv_weight = draw_qkv_weight(jax.random.fold_in(key_of[23], 71), 0)
    qkv_bias = gaussian(key_of[4], (LAYERS, 3, D), 0.3, 1.796875, ((2, 8),))
    proj_weight = gaussian(key_of[5], (LAYERS, D, D), (max(1, D * 2 // LEN)) ** -0.5, 4.0, ((1, 8), (2, 4)))
    proj_bias = gaussian(key_of[6], (LAYERS, D), 0.3, 1.796875, ((1, 8),))
    up_weight = draw_up_weight(jax.random.fold_in(key_of[23], 71), 0)
    up_bias = gaussian(key_of[8], (LAYERS, FF), 0.3, 1.796875, ((1, 8),))
    down_weight = gaussian(key_of[9], (LAYERS, FF, D), FF ** -0.5, 0.09375, ((1, 8), (2, 4)))
    down_bias = gaussian(key_of[10], (LAYERS, D), 0.3, 1.796875, ((1, 8),))
    first_gain = jnp.clip(1.0 + 0.1 * jax.random.normal(key_of[11], (LAYERS, D), jnp.float32), 0.5, 1.5).astype(jnp.bfloat16)
    first_shift = gaussian(key_of[12], (LAYERS, D), 0.3, 1.796875, ((1, 8),))
    second_gain = jnp.clip(1.0 + 0.1 * jax.random.normal(key_of[13], (LAYERS, D), jnp.float32), 0.5, 1.5).astype(jnp.bfloat16)
    second_shift = gaussian(key_of[14], (LAYERS, D), 0.3, 1.796875, ((1, 8),))
    qkv_lower = gaussian(key_of[15], (LAYERS, ADAPTERS, D, RANK), D ** -0.5, 0.1875)
    qkv_raise = gaussian(key_of[16], (LAYERS, ADAPTERS, RANK, 3, D), (4 * RANK) ** -0.5, 0.75)
    proj_lower = gaussian(key_of[17], (LAYERS, ADAPTERS, D, RANK), (max(1, D * 2 // LEN)) ** -0.5, 4.0)
    proj_raise = gaussian(key_of[18], (LAYERS, ADAPTERS, RANK, D), (4 * RANK) ** -0.5, 0.75)
    up_lower = gaussian(key_of[19], (LAYERS, ADAPTERS, D, RANK), D ** -0.5, 0.1875)
    up_raise = gaussian(key_of[20], (LAYERS, ADAPTERS, RANK, FF), (4 * RANK) ** -0.5, 0.75)
    down_lower = gaussian(key_of[21], (LAYERS, ADAPTERS, FF, RANK), FF ** -0.5, 0.09375)
    down_raise = gaussian(key_of[22], (LAYERS, ADAPTERS, RANK, D), (4 * RANK) ** -0.5, 0.75)
    return {"tokens": tokens, "cotangent": cotangent, "adapter_ids": adapter_ids, "qkv_weight": qkv_weight, "qkv_bias": qkv_bias, "proj_weight": proj_weight, "proj_bias": proj_bias, "up_weight": up_weight, "up_bias": up_bias, "down_weight": down_weight, "down_bias": down_bias, "first_gain": first_gain, "first_shift": first_shift, "second_gain": second_gain, "second_shift": second_shift, "qkv_lower": qkv_lower, "qkv_raise": qkv_raise, "proj_lower": proj_lower, "proj_raise": proj_raise, "up_lower": up_lower, "up_raise": up_raise, "down_lower": down_lower, "down_raise": down_raise}


epsilon = 1e-05
highest = lax.Precision.HIGHEST

@jax.custom_vjp
def low(v):
    return lax.optimization_barrier(v.astype(jnp.bfloat16)).astype(jnp.float32)

@jax.custom_vjp
def low_back(v):
    return v

def low_keep(v):
    return (low(v), None)

def low_pass(kept, grad):
    return (grad,)

def back_keep(v):
    return (v, None)

def back_low(kept, grad):
    return (low(grad),)
low.defvjp(low_keep, low_pass)
low_back.defvjp(back_keep, back_low)

def matmul(left_side, right_side):
    return jnp.dot(left_side, right_side, precision=highest, preferred_element_type=jnp.float32)

def norm_rows(stream, gain_row, shift_row):
    center = stream - lax.optimization_barrier(jnp.mean(stream, axis=-1, keepdims=True))
    spread = lax.optimization_barrier(jnp.mean(center * center, axis=-1, keepdims=True))
    return center * lax.rsqrt(spread + epsilon) * gain_row + shift_row

def head_attention(bundle):
    query_rows, key_rows, value_rows = bundle
    length = query_rows.shape[0]
    places = jnp.arange(length, dtype=jnp.int32) // BLOCK
    allowed = places[None, :] <= places[:, None]
    scores = low_back(matmul(query_rows, key_rows.T) * HD ** (-0.5))
    softmax_full = jax.nn.softmax(jnp.where(allowed, scores, -1e+30), axis=-1)
    return matmul(low(softmax_full), value_rows)

def layer_forward(stream, frozen, picked):
    qkv_weight, qkv_bias, proj_weight, proj_bias, up_weight, up_bias, down_weight, down_bias, first_gain, first_shift, second_gain, second_shift = frozen
    qkv_lower, qkv_raise, proj_lower, proj_raise, up_lower, up_raise, down_lower, down_raise = picked
    length = stream.shape[0]
    normed = low(norm_rows(stream, first_gain, first_shift))
    reduced = low_back(low(matmul(normed, qkv_lower)))
    mixed_rows = matmul(normed, qkv_weight.reshape(D, 3 * D)) + qkv_bias.reshape(3 * D)
    mixed_rows = mixed_rows + matmul(reduced, qkv_raise.reshape(RANK, 3 * D))
    mixed_rows = low_back(low(mixed_rows)).reshape(length, 3, HEADS, HD)
    head_major = jnp.transpose(mixed_rows, (1, 2, 0, 3))
    attended = lax.map(jax.checkpoint(head_attention), (head_major[0], head_major[1], head_major[2]))
    attended = low_back(low(jnp.transpose(attended, (1, 0, 2)).reshape(length, D)))
    reduced_proj = low_back(low(matmul(attended, proj_lower)))
    middle = stream + low_back(matmul(attended, proj_weight) + proj_bias + matmul(reduced_proj, proj_raise))
    normed_two = low(norm_rows(middle, second_gain, second_shift))
    reduced_up = low_back(low(matmul(normed_two, up_lower)))
    hidden = low_back(matmul(normed_two, up_weight) + up_bias + matmul(reduced_up, up_raise))
    active = low(jax.nn.gelu(hidden, approximate=True))
    reduced_down = low_back(low(matmul(active, down_lower)))
    return middle + low_back(matmul(active, down_weight) + down_bias + matmul(reduced_down, down_raise))

def two_layers(stream, picked, frozen):
    for layer_number in range(LAYERS):
        stream = layer_forward(stream, [matrix[layer_number] for matrix in frozen], [matrix[layer_number] for matrix in picked])
    return stream

def reference(tokens, cotangent, adapter_ids, qkv_weight, qkv_bias, proj_weight, proj_bias, up_weight, up_bias, down_weight, down_bias, first_gain, first_shift, second_gain, second_shift, qkv_lower, qkv_raise, proj_lower, proj_raise, up_lower, up_raise, down_lower, down_raise):
    frozen = [matrix.astype(jnp.float32) for matrix in (qkv_weight, qkv_bias, proj_weight, proj_bias, up_weight, up_bias, down_weight, down_bias, first_gain, first_shift, second_gain, second_shift)]
    tables = [matrix.astype(jnp.float32) for matrix in (qkv_lower, qkv_raise, proj_lower, proj_raise, up_lower, up_raise, down_lower, down_raise)]
    site_of = (0, 0, 1, 1, 2, 2, 3, 3)
    inputs = tokens.astype(jnp.float32).reshape(SEQS, LEN, D)
    upstream = cotangent.astype(jnp.float32).reshape(SEQS, LEN, D)

    def one_sequence(running, bundle):
        stream, incoming, chosen = bundle
        picked = [matrix[:, chosen[target]] for matrix, target in zip(tables, site_of)]
        output, pullback = jax.vjp(partial(two_layers, frozen=frozen), stream, picked)
        grad_stream, grad_picked = pullback(incoming)
        running = [total_sum.at[:, chosen[target]].add(increment) for total_sum, increment, target in zip(running, grad_picked, site_of)]
        return (running, (output, grad_stream))
    starts = [jnp.zeros(matrix.shape, jnp.float32) for matrix in tables]
    totals, (outputs, input_grads) = lax.scan(one_sequence, starts, (inputs, upstream, adapter_ids))
    return (outputs.reshape(TOKENS, D), input_grads.reshape(TOKENS, D), totals[0], totals[1], totals[2], totals[3], totals[4], totals[5], totals[6], totals[7])
```

```python
import functools

import jax
import jax.numpy as jnp
from jax import lax
from jax.experimental import pallas as pl
from jax.experimental.pallas import tpu as pltpu
from jax.sharding import PartitionSpec as P

HD = 64
LEN = 1024
BLOCK = 256
BLOCKS = LEN // BLOCK
EPSILON = 1e-05
SCALE = HD**-0.5
MESH = pl.DeviceIdType.MESH
F32 = jnp.float32
BF16 = jnp.bfloat16


ORDERS = {
    "qkv": ((0, "z", 1), (1, "z", 0)),
    "proj": ((0, "z", 1), (1, "z", 0)),
    "up": (("z", 0, 1), ("z", 1, 0)),
    "down": (("z", 0, 1), ("z", 1, 0)),
}
KINDS = ("qkv", "proj", "up", "down")
WINDOW = 4


def gather_body(n_row, n_col, layers, *refs):
    shard = dict(zip(KINDS, refs[:4]))
    full = dict(zip(KINDS, refs[4:8]))
    local_sem, send_sem, recv_sem = refs[8:]
    r = lax.axis_index("row")
    c = lax.axis_index("col")
    link_bits = [b for b in (2**k for k in range(1, 8)) if b < n_col]
    depth = shard["up"].shape[1]

    def row_peer(s):
        return (lax.rem(r + s, n_row), c)

    def col_peer(bit):
        return (r, c ^ bit)

    peers = [row_peer(s) for s in range(1, n_row)]
    peers += [col_peer(b) for b in [1] + link_bits]
    barrier = pltpu.get_barrier_semaphore()
    for peer in peers:
        pl.semaphore_signal(barrier, inc=1, device_id=peer, device_id_type=MESH)
    pl.semaphore_wait(barrier, len(peers))

    def own(kind, l, h):
        ref = shard[kind]
        half = ref.shape[1] // 2
        return ref.at[l, pl.ds(h * half, half)]

    def block(kind, l, h, row, col):
        if kind in ("qkv", "up"):
            return full[kind].at[l, col, row, h]
        start = pl.multiple_of(row * depth, depth)
        return full[kind].at[l, col, h, :, pl.ds(start, depth)]

    def strip(kind, l, h, col):
        if kind in ("qkv", "up"):
            return full[kind].at[l, col, :, h]
        return full[kind].at[l, col, h]

    def amount(kind, l, h, strips, rows):
        if kind in ("qkv", "up"):
            return full[kind].at[l, pl.ds(0, strips), pl.ds(0, rows), h]
        return full[kind].at[l, pl.ds(0, strips), h, :, pl.ds(0, rows * depth)]

    chunks = []
    for l in range(layers):
        for kind in KINDS:
            for h in range(2):
                order = []
                for d in ORDERS[kind][h]:
                    if d == "z":
                        order.append("z")
                    elif d < len(link_bits):
                        order.append(link_bits[d])
                order += link_bits[2:]
                chunks.append((kind, l, h, tuple(order)))
    phases = len(link_bits) + 1

    def plan(order):
        masks, whole, steps = [0], False, []
        for d in order:
            steps.append((d, tuple(masks), whole))
            if d == "z":
                whole = True
            else:
                masks = masks + [m ^ d for m in masks]
        steps.append((None, tuple(masks), whole))
        return steps

    def remote(src, dst, k, p, peer):
        return pltpu.make_async_remote_copy(
            src_ref=src, dst_ref=dst, send_sem=send_sem.at[k, p], recv_sem=recv_sem.at[k, p],
            device_id=peer, device_id_type=MESH,
        )

    def local(k):
        kind, l, h, _ = chunks[k]
        return pltpu.make_async_copy(own(kind, l, h), block(kind, l, h, r, c), local_sem.at[k])

    def issue(k, p):
        kind, l, h, order = chunks[k]
        d, masks, whole = plan(order)[p]
        for m in masks:
            if d == "z":
                src = own(kind, l, h) if m == 0 else block(kind, l, h, r, c ^ m)
                for s in range(1, n_row):
                    remote(src, block(kind, l, h, r, c ^ m), k, p, row_peer(s)).start()
            elif whole:
                ref = strip(kind, l, h, c ^ m)
                remote(ref, ref, k, p, col_peer(d)).start()
            else:
                src = own(kind, l, h) if m == 0 else block(kind, l, h, r, c ^ m)
                remote(src, block(kind, l, h, r, c ^ m), k, p, col_peer(d)).start()

    def moved(k, p):
        kind, l, h, order = chunks[k]
        d, masks, whole = plan(order)[p]
        if d == "z":
            rows = n_row - 1
        else:
            rows = n_row if whole else 1
        ref = amount(kind, l, h, len(masks), rows)
        return remote(ref, ref, k, p, col_peer(1))

    def share(k, p):
        kind, l, h, order = chunks[k]
        steps = plan(order)
        (d, masks, _), (_, later, whole) = steps[p], steps[p + 1]
        if not whole:
            return
        fresh = masks if d == "z" else later[len(masks):]
        for m in fresh:
            ref = strip(kind, l, h, c ^ m)
            remote(ref, ref, k, phases, col_peer(1)).start()

    def shared(k):
        kind, l, h, _ = chunks[k]
        ref = amount(kind, l, h, n_col // 2, n_row)
        return remote(ref, ref, k, phases, col_peer(1))

    def finish(k, p):
        moved(k, p).wait_recv()
        if chunks[k][3][p] == "z":
            local(k).wait()
        if p + 1 < phases:
            issue(k, p + 1)
        share(k, p)

    count = len(chunks)
    for k in range(count):
        local(k).start()
    for t in range(count + WINDOW + phases):
        if t < count:
            issue(t, 0)
        for p in range(phases):
            k = t - WINDOW - p
            if 0 <= k < count:
                finish(k, p)
    for k in range(count):
        for p in range(phases):
            moved(k, p).wait_send()
        shared(k).wait_send()
        shared(k).wait_recv()


def gather_weights(n_row, n_col, qkv, proj, up, down):
    layers, depth = up.shape[0], up.shape[1]
    width, units = proj.shape[1], down.shape[1]
    dim = depth * n_row
    shapes = (
        (layers, n_col, n_row, 2, depth // 2, qkv.shape[2]),
        (layers, n_col, 2, width // 2, dim),
        (layers, n_col, n_row, 2, depth // 2, units),
        (layers, n_col, 2, units // 2, dim),
    )
    count = layers * 8
    phases = n_col.bit_length()
    outs = pl.pallas_call(
        functools.partial(gather_body, n_row, n_col, layers),
        out_shape=[jax.ShapeDtypeStruct(s, BF16) for s in shapes],
        in_specs=[pl.BlockSpec(memory_space=pltpu.HBM)] * 4,
        out_specs=[pl.BlockSpec(memory_space=pltpu.HBM)] * 4,
        scratch_shapes=[
            pltpu.SemaphoreType.DMA((count,)),
            pltpu.SemaphoreType.DMA((count, phases)),
            pltpu.SemaphoreType.DMA((count, phases)),
        ],
        compiler_params=pltpu.CompilerParams(collective_id=0, has_side_effects=True),
        name="gather_weights",
    )(qkv, proj, up, down)
    return (
        outs[0].reshape(layers, n_col, dim, qkv.shape[2]),
        outs[1].reshape(layers, dim, dim),
        outs[2].reshape(layers, n_col, dim, units),
        outs[3].reshape(layers, units * n_col, dim),
    )


def dot(a, b, dims=((1,), (0,))):
    return lax.dot_general(a, b, (dims, ((), ())), preferred_element_type=F32)


def norm_forward(stream, gain, shift):
    center = stream - jnp.mean(stream, axis=1, keepdims=True)
    inverse = lax.rsqrt(jnp.mean(center * center, axis=1, keepdims=True) + EPSILON)
    scaled = center * inverse
    return (scaled * gain + shift).astype(BF16), scaled, inverse


def norm_backward(grad, scaled, inverse, gain):
    w = grad * gain
    first = jnp.mean(w, axis=1, keepdims=True)
    second = jnp.mean(w * scaled, axis=1, keepdims=True)
    return inverse * (w - first - scaled * second)


def positions(group):
    if group == 2:
        return ((0, 3), (1, 2))
    per = BLOCKS // group
    return tuple(tuple(range(g * per, (g + 1) * per)) for g in range(group))


def shards(mesh_shape, *args):
    (
        tokens, cotangent, adapter_ids, qkv_weight, qkv_bias, proj_weight, proj_bias,
        up_weight, up_bias, down_weight, down_bias, first_gain, first_shift, second_gain,
        second_shift, qkv_lower, qkv_raise, proj_lower, proj_raise, up_lower, up_raise,
        down_lower, down_raise,
    ) = args
    n_row, n_col = mesh_shape
    layers, adapters, dim, rank = qkv_lower.shape
    rows, width = tokens.shape
    units = up_weight.shape[2]
    seqs = rows // LEN
    group = n_col // seqs
    held = positions(group)
    per = BLOCKS // group
    mine = per * BLOCK
    heads = width // HD
    c = lax.axis_index("col")
    g = lax.rem(c, group)
    seq = c // group

    qkv_full, proj_full, up_full, down_full = gather_weights(
        n_row, n_col, qkv_weight.reshape(layers, -1, 3 * width), proj_weight, up_weight, down_weight
    )

    def vectors(v):
        return lax.all_gather(v, "col", axis=v.ndim - 1, tiled=True).astype(F32)

    qkv_b = lax.all_gather(qkv_bias, "col", axis=0).astype(F32)
    proj_b, up_b, down_b, gain1, shift1, gain2, shift2 = [
        vectors(v)
        for v in (proj_bias, up_bias, down_bias, first_gain, first_shift, second_gain, second_shift)
    ]

    order = [s * BLOCKS + b for s in range(seqs) for q in range(group) for b in held[q]]
    back = [order.index(i) for i in range(len(order))]

    def to_own(x):
        x = x.reshape(seqs * BLOCKS, BLOCK, width)
        x = jnp.concatenate([x[i] for i in order], axis=0)
        return lax.all_to_all(x, "col", split_axis=0, concat_axis=1, tiled=True)

    def to_columns(x):
        x = lax.all_to_all(x.astype(BF16), "col", split_axis=1, concat_axis=0, tiled=True)
        x = x.reshape(seqs * BLOCKS, BLOCK, width)
        return jnp.concatenate([x[i] for i in back], axis=0).astype(F32)

    def peer_values(x, step):
        pairs = [(q, q - q % group + (q + step) % group) for q in range(n_col)]
        return lax.ppermute(x, "col", pairs)

    table = jnp.asarray(held, jnp.int32)
    own_place = table[g]
    key_place = jnp.concatenate([table[lax.rem(g - s + group, group)] for s in range(group)])
    allowed = key_place[None, :] <= own_place[:, None]
    mask = jnp.repeat(jnp.repeat(allowed, BLOCK, axis=0), BLOCK, axis=1)

    ids = lax.dynamic_index_in_dim(adapter_ids, seq, 0, keepdims=False)

    def picked(tab, l, site):
        return lax.dynamic_index_in_dim(tab[l], ids[site], 0, keepdims=False)

    def attend(q, k, v):
        s = jnp.einsum("hqd,hkd->hqk", q, k, preferred_element_type=F32) * SCALE
        s = jnp.where(mask, s, -1e30)
        top = jnp.max(s, axis=2, keepdims=True)
        e = jnp.exp(s - top)
        total = jnp.sum(e, axis=2, keepdims=True)
        out = jnp.einsum("hqk,hkd->hqd", (e / total).astype(BF16), v, preferred_element_type=F32)
        return out.astype(BF16), (top + jnp.log(total))

    def attend_back(q, k, v, lse, grad):
        s = jnp.einsum("hqd,hkd->hqk", q, k, preferred_element_type=F32) * SCALE
        p = jnp.exp(jnp.where(mask, s, -1e30) - lse)
        gp = jnp.einsum("hqd,hkd->hqk", grad, v, preferred_element_type=F32)
        gv = jnp.einsum("hqk,hqd->hkd", p.astype(BF16), grad, preferred_element_type=F32)
        gs = (p * (gp - jnp.sum(p * gp, axis=2, keepdims=True))).astype(BF16)
        gq = jnp.einsum("hqk,hkd->hqd", gs, k, preferred_element_type=F32) * SCALE
        gk = jnp.einsum("hqk,hqd->hkd", gs, q, preferred_element_type=F32) * SCALE
        return gq, gk, gv

    def by_head(x):
        t = x.shape[1]
        return x.reshape(n_col, t, heads, HD).transpose(0, 2, 1, 3).reshape(n_col * heads, t, HD)

    def by_strip(x):
        t = x.shape[1]
        return x.reshape(n_col, heads, t, HD).transpose(0, 2, 1, 3).reshape(n_col, t, width)

    stream = to_own(tokens).astype(F32)
    records = []
    for l in range(layers):
        rec = {}
        a_qkv, b_qkv = picked(qkv_lower, l, 0), picked(qkv_raise, l, 0)
        a_proj, b_proj = picked(proj_lower, l, 1), picked(proj_raise, l, 1)
        a_up, b_up = picked(up_lower, l, 2), picked(up_raise, l, 2)
        a_down, b_down = picked(down_lower, l, 3), picked(down_raise, l, 3)
        b_qkv = b_qkv.reshape(rank, 3, n_col, width).transpose(2, 0, 1, 3).reshape(n_col, rank, 3 * width)
        b_up = b_up.reshape(rank, n_col, units).transpose(1, 0, 2)
        rec["picks"] = (a_qkv, b_qkv, a_proj, b_proj, a_up, b_up, a_down, b_down)
        rec["normed"], rec["n1"], rec["r1"] = norm_forward(stream, gain1[l], shift1[l])
        rec["reduced"] = dot(rec["normed"], a_qkv).astype(BF16)
        mixed = (
            jnp.einsum("tk,ckn->ctn", rec["normed"], qkv_full[l], preferred_element_type=F32)
            + qkv_b[:, l].reshape(n_col, 1, 3 * width)
            + jnp.einsum("tk,ckn->ctn", rec["reduced"], b_qkv, preferred_element_type=F32)
        ).astype(BF16)
        q, kv = mixed[:, :, :width], mixed[:, :, width:]
        kvs = jnp.concatenate([kv] + [peer_values(kv, s) for s in range(1, group)], axis=1)
        rec["q"], rec["k"], rec["v"] = by_head(q), by_head(kvs[:, :, :width]), by_head(kvs[:, :, width:])
        attended, rec["lse"] = attend(rec["q"], rec["k"], rec["v"])
        attended = by_strip(attended).transpose(1, 0, 2).reshape(mine, dim)
        rec["attended"] = attended
        rec["reduced_proj"] = dot(attended, a_proj).astype(BF16)
        middle = stream + dot(attended, proj_full[l]) + proj_b[l] + dot(rec["reduced_proj"], b_proj)
        rec["normed2"], rec["n2"], rec["r2"] = norm_forward(middle, gain2[l], shift2[l])
        rec["reduced_up"] = dot(rec["normed2"], a_up).astype(BF16)
        rec["hidden"] = (
            jnp.einsum("tk,ckn->ctn", rec["normed2"], up_full[l], preferred_element_type=F32)
            + up_b[l].reshape(n_col, 1, units)
            + jnp.einsum("tk,ckn->ctn", rec["reduced_up"], b_up, preferred_element_type=F32)
        )
        rec["active"] = jax.nn.gelu(rec["hidden"], approximate=True).astype(BF16)
        a_down_c = a_down.reshape(n_col, units, rank)
        rec["reduced_down"] = jnp.einsum(
            "ctn,cnk->tk", rec["active"], a_down_c, preferred_element_type=F32
        ).astype(BF16)
        stream = (
            middle
            + jnp.einsum(
                "ctn,cnk->tk", rec["active"], down_full[l].reshape(n_col, units, dim),
                preferred_element_type=F32,
            )
            + down_b[l]
            + dot(rec["reduced_down"], b_down)
        )
        records.append(rec)
    result = to_columns(stream)

    grad = to_own(cotangent).astype(F32)
    grads = [None] * layers
    cross = ((0,), (0,))
    turned = ((1,), (1,))
    for l in reversed(range(layers)):
        rec = records[l]
        a_qkv, b_qkv, a_proj, b_proj, a_up, b_up, a_down, b_down = rec["picks"]
        low = grad.astype(BF16)
        g_red_down = dot(low, b_down, turned).astype(BF16)
        g_b_down = dot(rec["reduced_down"], low, cross)
        g_a_down = jnp.einsum("tk,ctn->ckn", g_red_down, rec["active"], preferred_element_type=F32)
        g_active = jnp.einsum(
            "tk,cnk->ctn", low, down_full[l].reshape(n_col, units, dim), preferred_element_type=F32
        ) + jnp.einsum(
            "tk,cnk->ctn", g_red_down, a_down.reshape(n_col, units, rank), preferred_element_type=F32
        )
        g_hidden = jax.vjp(lambda x: jax.nn.gelu(x, approximate=True), rec["hidden"])[1](g_active)[0]
        g_hidden = g_hidden.astype(BF16)
        g_red_up = jnp.einsum("ctn,ckn->tk", g_hidden, b_up, preferred_element_type=F32).astype(BF16)
        g_b_up = jnp.einsum("tk,ctn->ckn", rec["reduced_up"], g_hidden, preferred_element_type=F32)
        g_a_up = dot(g_red_up, rec["normed2"], cross)
        g_normed2 = jnp.einsum("ctn,ckn->tk", g_hidden, up_full[l], preferred_element_type=F32) + dot(
            g_red_up, a_up, turned
        )
        grad = grad + norm_backward(g_normed2, rec["n2"], rec["r2"], gain2[l])
        low = grad.astype(BF16)
        g_red_proj = dot(low, b_proj, turned).astype(BF16)
        g_b_proj = dot(rec["reduced_proj"], low, cross)
        g_a_proj = dot(g_red_proj, rec["attended"], cross)
        g_att = (dot(low, proj_full[l], turned) + dot(g_red_proj, a_proj, turned)).astype(BF16)
        g_att = by_head(g_att.reshape(mine, n_col, width).transpose(1, 0, 2))
        gq, gk, gv = attend_back(rec["q"], rec["k"], rec["v"], rec["lse"], g_att)
        gkv = jnp.concatenate([by_strip(gk), by_strip(gv)], axis=2)
        total = gkv[:, :mine]
        for s in range(1, group):
            part = gkv[:, s * mine : (s + 1) * mine].astype(BF16)
            total = total + peer_values(part, group - s).astype(F32)
        g_mixed = jnp.concatenate([by_strip(gq), total], axis=2).astype(BF16)
        g_red = jnp.einsum("ctn,ckn->tk", g_mixed, b_qkv, preferred_element_type=F32).astype(BF16)
        g_b_qkv = jnp.einsum("tk,ctn->ckn", rec["reduced"], g_mixed, preferred_element_type=F32)
        g_a_qkv = dot(g_red, rec["normed"], cross)
        g_normed = jnp.einsum("ctn,ckn->tk", g_mixed, qkv_full[l], preferred_element_type=F32) + dot(
            g_red, a_qkv, turned
        )
        grad = grad + norm_backward(g_normed, rec["n1"], rec["r1"], gain1[l])

        def strips(x):
            return x.reshape(rank, n_col, -1).transpose(1, 0, 2)

        grads[l] = jnp.concatenate(
            [
                strips(g_a_qkv), g_b_qkv, strips(g_a_proj), strips(g_b_proj),
                strips(g_a_up), g_b_up, g_a_down, strips(g_b_down),
            ],
            axis=2,
        )
    input_grad = to_columns(grad)

    sizes = (width, 3 * width, width, width, width, units, units, width)
    sites = (0, 0, 1, 1, 2, 2, 3, 3)
    parts = jnp.stack(grads, axis=1).astype(BF16)
    parts = lax.all_to_all(parts, "col", split_axis=0, concat_axis=0, tiled=True)
    parts = parts.reshape((seqs, group) + parts.shape[1:]).astype(F32).sum(axis=1)
    onehot = (adapter_ids.T[:, :, None] == jnp.arange(adapters)[None, None, :]).astype(F32)
    placed, at = [], 0
    for size, site in zip(sizes, sites):
        piece = parts[:, :, :, at : at + size]
        at += size
        placed.append(
            jnp.einsum("sa,slrn->larn", onehot[site], piece, precision=lax.Precision.HIGHEST)
        )
    summed = lax.psum([p.astype(BF16) for p in placed], "row")
    outs = []
    for number, p in enumerate(summed):
        p = p.astype(F32)
        if number == 1:
            outs.append(p.reshape(layers, adapters, rank, 3, width))
        elif number in (0, 2, 4, 6):
            outs.append(p.transpose(0, 1, 3, 2))
        else:
            outs.append(p)
    return (result, input_grad) + tuple(outs)


def solution(mesh):
    mesh_shape = (mesh.shape["row"], mesh.shape["col"])
    return jax.shard_map(
        functools.partial(shards, mesh_shape),
        mesh=mesh,
        in_specs=(
            P("row", "col"), P("row", "col"), P("row", None),
            P(None, "row", None, "col"), P(None, None, "col"),
            P(None, "col", "row"), P(None, "col"),
            P(None, "row", "col"), P(None, "col"),
            P(None, "col", "row"), P(None, "col"),
            P(None, "col"), P(None, "col"), P(None, "col"), P(None, "col"),
            P(), P(), P(), P(), P(), P(), P(), P(),
        ),
        out_specs=(
            P("row", "col"), P("row", "col"),
            P(None, None, "col", None), P(None, None, None, None, "col"),
            P(None, None, "col", None), P(None, None, None, "col"),
            P(None, None, "col", None), P(None, None, None, "col"),
            P(None, None, "col", None), P(None, None, None, "col"),
        ),
        check_vma=False,
    )
```

```python
import functools

import jax
import jax.numpy as jnp
from jax import lax
from jax.experimental import pallas as pl
from jax.experimental.pallas import tpu as pltpu
from jax.sharding import PartitionSpec as P

HD = 64
LEN = 1024
BLOCK = 256
BLOCKS = LEN // BLOCK
EPSILON = 1e-05
SCALE = HD**-0.5
ROOT = (2.0 / 3.141592653589793) ** 0.5
MESH = pl.DeviceIdType.MESH
F32 = jnp.float32
BF16 = jnp.bfloat16


ORDERS = {
    "qkv": ((0, "z", 1), (1, "z", 0)),
    "proj": ((0, "z", 1), (1, "z", 0)),
    "up": (("z", 0, 1), ("z", 1, 0)),
    "down": (("z", 0, 1), ("z", 1, 0)),
}
KINDS = ("qkv", "proj", "up", "down")
WINDOW = 4


def place_of(group, g, b):
    if group == 2:
        return g + b * (BLOCKS - 1 - 2 * g)
    return g * (BLOCKS // group) + b


def gather_body(n_row, n_col, layers, group, *refs):
    shard = dict(zip(KINDS, refs[:4]))
    tokens, cotangent, vector = refs[4:7]
    full = dict(zip(KINDS, refs[7:11]))
    own_tokens, own_cotangent, vectors = refs[11:14]
    local_sem, send_sem, recv_sem, near_sem, out_sem, in_sem = refs[14:]
    r = lax.axis_index("row")
    c = lax.axis_index("col")
    link_bits = [b for b in (2**k for k in range(1, 8)) if b < n_col]
    depth = shard["up"].shape[1]

    def row_peer(s):
        return (lax.rem(r + s, n_row), c)

    def col_peer(bit):
        return (r, c ^ bit)

    peers = [row_peer(s) for s in range(1, n_row)]
    peers += [(r, lax.rem(c + d, n_col)) for d in range(1, n_col)]
    barrier = pltpu.get_barrier_semaphore()
    for peer in peers:
        pl.semaphore_signal(barrier, inc=1, device_id=peer, device_id_type=MESH)
    pl.semaphore_wait(barrier, len(peers))

    per, width = BLOCKS // group, tokens.shape[1]

    def own_place(ref, b, col):
        if len(ref.shape) == 2:
            start = pl.multiple_of(col * width, width)
            return ref.at[pl.ds(b * BLOCK, BLOCK), pl.ds(start, width)]
        return ref.at[col, pl.ds(b * BLOCK, BLOCK)]

    def from_place(ref, b, col):
        start = (col // group) * LEN + place_of(group, lax.rem(col, group), b) * BLOCK
        return ref.at[pl.ds(pl.multiple_of(start, BLOCK), BLOCK)]

    exchanged = ((tokens, own_tokens), (cotangent, own_cotangent))

    def near(n, b):
        src, dst = exchanged[n]
        return pltpu.make_async_copy(from_place(src, b, c), own_place(dst, b, c), near_sem.at[n * per + b])

    def near_vector():
        return pltpu.make_async_copy(vector, vectors.at[c], near_sem.at[2 * per])

    def far(src, dst, n, peer):
        return pltpu.make_async_remote_copy(
            src_ref=src, dst_ref=dst, send_sem=out_sem.at[n], recv_sem=in_sem.at[n],
            device_id=peer, device_id_type=MESH,
        )

    def start_exchange(n):
        src, dst = exchanged[n]
        for b in range(per):
            near(n, b).start()
        for d in range(1, n_col):
            to = lax.rem(c + d, n_col)
            for b in range(per):
                far(from_place(src, b, to), own_place(dst, b, c), n, (r, to)).start()

    def wait_exchange(n):
        _, dst = exchanged[n]
        for b in range(per):
            near(n, b).wait()
        if len(dst.shape) == 2:
            ref = dst.at[:, pl.ds(0, (n_col - 1) * width)]
        else:
            ref = dst.at[pl.ds(0, n_col - 1)]
        far(ref, ref, n, col_peer(1)).wait()

    def own(kind, l, h):
        ref = shard[kind]
        half = ref.shape[1] // 2
        return ref.at[l, pl.ds(h * half, half)]

    def block(kind, l, h, row, col):
        if kind in ("qkv", "up"):
            return full[kind].at[l, col, row, h]
        start = pl.multiple_of(row * depth, depth)
        return full[kind].at[l, col, h, :, pl.ds(start, depth)]

    def strip(kind, l, h, col):
        if kind in ("qkv", "up"):
            return full[kind].at[l, col, :, h]
        return full[kind].at[l, col, h]

    def amount(kind, l, h, strips, rows):
        if kind in ("qkv", "up"):
            return full[kind].at[l, pl.ds(0, strips), pl.ds(0, rows), h]
        return full[kind].at[l, pl.ds(0, strips), h, :, pl.ds(0, rows * depth)]

    chunks = []
    for l in range(layers):
        for kind in KINDS:
            for h in range(2):
                order = []
                for d in ORDERS[kind][h]:
                    if d == "z":
                        order.append("z")
                    elif d < len(link_bits):
                        order.append(link_bits[d])
                order += link_bits[2:]
                chunks.append((kind, l, h, tuple(order)))
    phases = len(link_bits) + 1

    def plan(order):
        masks, whole, steps = [0], False, []
        for d in order:
            steps.append((d, tuple(masks), whole))
            if d == "z":
                whole = True
            else:
                masks = masks + [m ^ d for m in masks]
        steps.append((None, tuple(masks), whole))
        return steps

    def remote(src, dst, k, p, peer):
        return pltpu.make_async_remote_copy(
            src_ref=src, dst_ref=dst, send_sem=send_sem.at[k, p], recv_sem=recv_sem.at[k, p],
            device_id=peer, device_id_type=MESH,
        )

    def local(k):
        kind, l, h, _ = chunks[k]
        return pltpu.make_async_copy(own(kind, l, h), block(kind, l, h, r, c), local_sem.at[k])

    def issue(k, p):
        kind, l, h, order = chunks[k]
        d, masks, whole = plan(order)[p]
        for m in masks:
            if d == "z":
                src = own(kind, l, h) if m == 0 else block(kind, l, h, r, c ^ m)
                for s in range(1, n_row):
                    remote(src, block(kind, l, h, r, c ^ m), k, p, row_peer(s)).start()
            elif whole:
                ref = strip(kind, l, h, c ^ m)
                remote(ref, ref, k, p, col_peer(d)).start()
            else:
                src = own(kind, l, h) if m == 0 else block(kind, l, h, r, c ^ m)
                remote(src, block(kind, l, h, r, c ^ m), k, p, col_peer(d)).start()

    def moved(k, p):
        kind, l, h, order = chunks[k]
        d, masks, whole = plan(order)[p]
        if d == "z":
            rows = n_row - 1
        else:
            rows = n_row if whole else 1
        ref = amount(kind, l, h, len(masks), rows)
        return remote(ref, ref, k, p, col_peer(1))

    def share(k, p):
        kind, l, h, order = chunks[k]
        steps = plan(order)
        (d, masks, _), (_, later, whole) = steps[p], steps[p + 1]
        if not whole:
            return
        fresh = masks if d == "z" else later[len(masks):]
        for m in fresh:
            ref = strip(kind, l, h, c ^ m)
            remote(ref, ref, k, phases, col_peer(1)).start()

    def shared(k):
        kind, l, h, _ = chunks[k]
        ref = amount(kind, l, h, n_col // 2, n_row)
        return remote(ref, ref, k, phases, col_peer(1))

    def finish(k, p):
        moved(k, p).wait_recv()
        if chunks[k][3][p] == "z":
            local(k).wait()
        if p + 1 < phases:
            issue(k, p + 1)
        share(k, p)

    count = len(chunks)
    near_vector().start()
    for d in range(1, n_col):
        far(vector, vectors.at[c], 2, (r, lax.rem(c + d, n_col))).start()
    start_exchange(0)
    for k in range(count):
        local(k).start()
    for t in range(count + WINDOW + phases):
        if t < count:
            issue(t, 0)
        if t == count - 1:
            start_exchange(1)
        for p in range(phases):
            k = t - WINDOW - p
            if 0 <= k < count:
                finish(k, p)
    for k in range(count):
        for p in range(phases):
            moved(k, p).wait_send()
        shared(k).wait_send()
        shared(k).wait_recv()
    near_vector().wait()
    rest = vectors.at[pl.ds(0, n_col - 1)]
    far(rest, rest, 2, col_peer(1)).wait()
    wait_exchange(0)
    wait_exchange(1)


def gather_inputs(n_row, n_col, group, qkv, proj, up, down, tokens, cotangent, vector):
    layers, depth = up.shape[0], up.shape[1]
    width, units = proj.shape[1], down.shape[1]
    dim = depth * n_row
    mine = LEN // group
    own = (mine, dim) if width % 128 == 0 else (n_col, mine, width)
    shapes = (
        (layers, n_col, n_row, 2, depth // 2, qkv.shape[2]),
        (layers, n_col, 2, width // 2, dim),
        (layers, n_col, n_row, 2, depth // 2, units),
        (layers, n_col, 2, units // 2, dim),
        own,
        own,
        (n_col,) + vector.shape,
    )
    count = layers * 8
    phases = n_col.bit_length()
    outs = pl.pallas_call(
        functools.partial(gather_body, n_row, n_col, layers, group),
        out_shape=[jax.ShapeDtypeStruct(s, BF16) for s in shapes],
        in_specs=[pl.BlockSpec(memory_space=pltpu.HBM)] * 7,
        out_specs=[pl.BlockSpec(memory_space=pltpu.HBM)] * 7,
        scratch_shapes=[
            pltpu.SemaphoreType.DMA((count,)),
            pltpu.SemaphoreType.DMA((count, phases)),
            pltpu.SemaphoreType.DMA((count, phases)),
            pltpu.SemaphoreType.DMA((2 * (BLOCKS // group) + 1,)),
            pltpu.SemaphoreType.DMA((3,)),
            pltpu.SemaphoreType.DMA((3,)),
        ],
        compiler_params=pltpu.CompilerParams(collective_id=0, has_side_effects=True),
        name="gather_inputs",
    )(qkv, proj, up, down, tokens, cotangent, vector)

    merge = 128 // width
    strips = n_col // merge
    qkv_full = outs[0].reshape(layers, n_col, dim, qkv.shape[2])
    up_full = outs[2].reshape(layers, n_col, dim, units)
    own_rows = outs[4:6]
    if merge > 1:
        qkv_full = qkv_full.reshape(layers, strips, merge, dim, 3, width).transpose(0, 1, 3, 4, 2, 5)
        up_full = up_full.reshape(layers, strips, merge, dim, units).transpose(0, 1, 3, 2, 4)
        own_rows = [x.transpose(1, 0, 2).reshape(mine, dim) for x in own_rows]
    return (
        qkv_full.reshape(layers, strips, dim, 384),
        outs[1].reshape(layers, dim, dim),
        up_full.reshape(layers, strips, dim, units * merge),
        outs[3].reshape(layers, units * n_col, dim),
        own_rows[0],
        own_rows[1],
        outs[6],
    )


PARAMS = pltpu.CompilerParams(vmem_limit_bytes=60 * 2**20)
NARROW = 8
CROSS = ((0,), (0,))
TURNED = ((1,), (1,))


def dot(a, b, dims=((1,), (0,))):
    return lax.dot_general(a, b, (dims, ((), ())), preferred_element_type=F32)


def whole(shape):
    return pl.BlockSpec(shape, lambda i, ids: (0,) * len(shape))


def layer_of(shape, l):
    return pl.BlockSpec((None,) + shape, lambda i, ids: (l,) + (0,) * len(shape))


def chosen(shape, l, site):
    return pl.BlockSpec((None, None) + shape, lambda i, ids: (l, ids[site]) + (0,) * len(shape))


def call(body, ids, steps, operands, outs, scratch, name):
    return pl.pallas_call(
        body,
        grid_spec=pltpu.PrefetchScalarGridSpec(
            num_scalar_prefetch=1,
            grid=(steps,),
            in_specs=[spec for _, spec in operands],
            out_specs=[spec for _, spec in outs],
            scratch_shapes=scratch,
        ),
        out_shape=[shape for shape, _ in outs],
        compiler_params=PARAMS,
        name=name,
    )(ids, *[array for array, _ in operands])


def shape_of(shape, kind):
    return jax.ShapeDtypeStruct(shape, kind)


def stream_spec(tokens, dim, final):
    if final:
        shape = (NARROW, tokens, dim // NARROW)
        return shape_of(shape, BF16), whole(shape)
    return shape_of((tokens, dim), F32), whole((tokens, dim))


def put(ref, value):
    if len(ref.shape) == 2:
        ref[...] = value
    else:
        for i in range(ref.shape[0]):
            ref[i] = value[:, i * 128 : (i + 1) * 128].astype(BF16)


def norm_parts(x):
    center = x - jnp.mean(x, axis=1, keepdims=True)
    inverse = lax.rsqrt(jnp.mean(center * center, axis=1, keepdims=True) + EPSILON)
    return center * inverse, inverse


def norm_grad(grad, scaled, inverse, gain):
    w = grad * gain
    first = jnp.mean(w, axis=1, keepdims=True)
    second = jnp.mean(w * scaled, axis=1, keepdims=True)
    return inverse * (w - first - scaled * second)


def qkv_body(ids, x, gain, shift, w, bias, a, b, q, kv, red, normed):
    @pl.when(pl.program_id(0) == 0)
    def _():
        scaled, _ = norm_parts(x[...])
        normed[...] = (scaled * gain[...] + shift[...]).astype(BF16)
        red[...] = dot(normed[...], a[...]).astype(BF16)

    for j in range(w.shape[0]):
        mixed = (dot(normed[...], w[j]) + bias[j] + dot(red[...], b[j])).astype(BF16)
        q[j] = mixed[:, :128]
        kv[j] = mixed[:, 128:]


def qkv_kernel(l, ids, x, gain, shift, w, bias, a, b):
    tokens, dim = x.shape
    rank = a.shape[-1]
    two = 2

    def strips(shape):
        return pl.BlockSpec((two,) + shape, lambda i, ids: (i, 0, 0))

    return call(
        qkv_body, ids, NARROW // two,
        [
            (x, whole((tokens, dim))),
            (gain, layer_of((1, dim), l)),
            (shift, layer_of((1, dim), l)),
            (w, pl.BlockSpec((None, two, dim, 384), lambda i, ids: (l, i, 0, 0))),
            (bias, pl.BlockSpec((None, two, 1, 384), lambda i, ids: (l, i, 0, 0))),
            (a, chosen((dim, rank), l, 0)),
            (b, pl.BlockSpec((None, two, rank, 384), lambda i, ids: (l, i, 0, 0))),
        ],
        [
            (shape_of((NARROW, tokens, 128), BF16), strips((tokens, 128))),
            (shape_of((NARROW, tokens, 256), BF16), strips((tokens, 256))),
            (shape_of((tokens, rank), BF16), whole((tokens, rank))),
        ],
        [pltpu.VMEM((tokens, dim), BF16)],
        "qkv",
    )


def pair_state(held):
    group, per = len(held), len(held[0])
    state = {}
    for s in range(per):
        for j in range(group):
            for b in range(per):
                seen = {held[(g - j) % group][b] <= held[g][s] for g in range(group)}
                state[s, j, b] = 0 if len(seen) == 2 else (1 if True in seen else -1)
    return state


def head_mask(h):
    lane = lax.broadcasted_iota(jnp.int32, (1, 128), 1)
    return (lane // HD) == h


def attend_body(held, bias, q, *refs):
    group, per = len(held), len(held[0])
    kvs, (out, lse) = refs[:group], refs[group:]
    state = pair_state(held)
    turned = {}
    for s in range(per):
        rows = pl.ds(s * BLOCK, BLOCK)
        queries = q[rows, :] * SCALE
        pieces = []
        for h in range(2):
            query = jnp.where(head_mask(h), queries, 0).astype(BF16)
            scores, values = [], []
            for j in range(group):
                for b in range(per):
                    if state[s, j, b] < 0:
                        continue
                    keys = kvs[j][b * BLOCK : (b + 1) * BLOCK, :128]
                    score = dot(keys, query, TURNED)
                    if state[s, j, b] == 0:
                        score = score + bias[s * group * per + j * per + b].astype(F32)
                    scores.append(score)
                    if (j, b) not in turned:
                        turned[j, b] = kvs[j][b * BLOCK : (b + 1) * BLOCK, 128:].T
                    values.append(turned[j, b][h * HD : (h + 1) * HD])
            top = functools.reduce(jnp.maximum, [jnp.max(x, axis=0, keepdims=True) for x in scores])
            total, made = 0.0, 0.0
            for score, value in zip(scores, values):
                e = jnp.exp(score - top)
                total = total + jnp.sum(e, axis=0, keepdims=True)
                made = made + dot(value, e.astype(BF16))
            pieces.append(made / total)
            lse[h : h + 1, rows] = top + jnp.log(total)
        out[rows, :] = jnp.concatenate(pieces, axis=0).T.astype(BF16)


def attend_kernel(held, bias, q, kvs):
    _, tokens, _ = q.shape

    def strip(shape):
        return pl.BlockSpec((None,) + shape, lambda i, ids: (i, 0, 0))

    return call(
        functools.partial(attend_body, held), bias, NARROW,
        [(q, strip((tokens, 128)))] + [(kv, strip((tokens, 256))) for kv in kvs],
        [
            (shape_of((tokens, NARROW * 128), BF16), pl.BlockSpec((tokens, 128), lambda i, ids: (0, i))),
            (shape_of((NARROW, 8, tokens), F32), strip((8, tokens))),
        ],
        [],
        "attend",
    )


def attend_back_body(held, bias, q, lse, out, grad, *refs):
    group, per = len(held), len(held[0])
    kvs, gq, gkvs = refs[:group], refs[group], refs[group + 1 :]
    state = pair_state(held)
    turned, gk, gv = {}, {}, {}
    for s in range(per):
        rows = pl.ds(s * BLOCK, BLOCK)
        queries = q[rows, :] * SCALE
        up = grad[rows, :]
        product = (up.astype(F32) * out[rows, :].astype(F32)).T
        pieces = []
        for h in range(2):
            query = jnp.where(head_mask(h), queries, 0).astype(BF16)
            given = jnp.where(head_mask(h), up, 0).astype(BF16)
            inner = jnp.sum(product[h * HD : (h + 1) * HD], axis=0, keepdims=True)
            level = lse[h : h + 1, rows]
            made = 0.0
            for j in range(group):
                for b in range(per):
                    if state[s, j, b] < 0:
                        continue
                    keys = kvs[j][b * BLOCK : (b + 1) * BLOCK, :128]
                    values = kvs[j][b * BLOCK : (b + 1) * BLOCK, 128:]
                    score = dot(keys, query, TURNED)
                    if state[s, j, b] == 0:
                        score = score + bias[s * group * per + j * per + b].astype(F32)
                    probs = jnp.exp(score - level)
                    g_probs = dot(values, given, TURNED)
                    g_scores = (probs * (g_probs - inner)).astype(BF16)
                    if (j, b) not in turned:
                        turned[j, b] = keys.T
                        gk[j, b], gv[j, b] = 0.0, 0.0
                    gv[j, b] = gv[j, b] + dot(probs.astype(BF16), given)
                    gk[j, b] = gk[j, b] + dot(g_scores, query)
                    made = made + dot(turned[j, b][h * HD : (h + 1) * HD], g_scores)
            pieces.append(made)
        gq[rows, :] = (jnp.concatenate(pieces, axis=0) * SCALE).T.astype(BF16)
    for j in range(group):
        for b in range(per):
            rows = pl.ds(b * BLOCK, BLOCK)
            gkvs[j][rows, :128] = gk[j, b].astype(BF16)
            gkvs[j][rows, 128:] = gv[j, b].astype(BF16)


def attend_back_kernel(held, bias, q, lse, out, grad, kvs):
    _, tokens, _ = q.shape

    def strip(shape):
        return pl.BlockSpec((None,) + shape, lambda i, ids: (i, 0, 0))

    columns = pl.BlockSpec((tokens, 128), lambda i, ids: (0, i))
    return call(
        functools.partial(attend_back_body, held), bias, NARROW,
        [(q, strip((tokens, 128))), (lse, strip((8, tokens))), (out, columns), (grad, columns)]
        + [(kv, strip((tokens, 256))) for kv in kvs],
        [(shape_of((NARROW, tokens, 128), BF16), strip((tokens, 128)))]
        + [(shape_of((NARROW, tokens, 256), BF16), strip((tokens, 256))) for _ in kvs],
        [],
        "attend_back",
    )


def gelu_parts(x):
    square = x * x
    t = jnp.tanh(ROOT * (x + 0.044715 * (x * square)))
    half = 0.5 * (1.0 + t)
    slope = half + 0.5 * x * (1.0 - t * t) * (ROOT * (1.0 + 3 * 0.044715 * square))
    return x * half, slope


def mlp_body(
    ids, x, att, w_proj, b_proj, low_proj, up_proj, gain, shift, low_up, w_up, b_up, up_up,
    w_down, low_down, up_down, b_down,
    middle, result, hidden, red_proj, red_up, red_down, normed, total, small,
):
    i = pl.program_id(0)

    @pl.when(i == 0)
    def _():
        red_proj[...] = dot(att[...], low_proj[...]).astype(BF16)
        mid = x[...] + (dot(att[...], w_proj[...]) + b_proj[...] + dot(red_proj[...], up_proj[...]))
        middle[...] = mid
        scaled, _ = norm_parts(mid)
        normed[...] = (scaled * gain[...] + shift[...]).astype(BF16)
        red_up[...] = dot(normed[...], low_up[...]).astype(BF16)
        total[...] = jnp.zeros_like(total)
        small[...] = jnp.zeros_like(small)

    value = dot(normed[...], w_up[...]) + b_up[...] + dot(red_up[...], up_up[...])
    hidden[...] = value
    active = (0.5 * value * (1.0 + jnp.tanh(ROOT * (value + 0.044715 * (value * value * value))))).astype(BF16)
    total[...] += dot(active, w_down[...])
    small[...] += dot(active, low_down[...])

    @pl.when(i == pl.num_programs(0) - 1)
    def _():
        red_down[...] = small[...].astype(BF16)
        put(result, middle[...] + (total[...] + b_down[...] + dot(red_down[...], up_down[...])))


def mlp_kernel(l, final, ids, x, att, w_proj, b_proj, low_proj, up_proj, gain, shift, low_up, w_up, b_up, up_up, w_down, low_down, up_down, b_down):
    tokens, dim = x.shape
    rank = low_proj.shape[-1]
    units = w_up.shape[-1]
    return call(
        mlp_body, ids, NARROW,
        [
            (x, whole((tokens, dim))),
            (att, whole((tokens, dim))),
            (w_proj, layer_of((dim, dim), l)),
            (b_proj, layer_of((1, dim), l)),
            (low_proj, chosen((dim, rank), l, 1)),
            (up_proj, chosen((rank, dim), l, 1)),
            (gain, layer_of((1, dim), l)),
            (shift, layer_of((1, dim), l)),
            (low_up, chosen((dim, rank), l, 2)),
            (w_up, pl.BlockSpec((None, None, dim, units), lambda i, ids: (l, i, 0, 0))),
            (b_up, pl.BlockSpec((None, None, 1, units), lambda i, ids: (l, i, 0, 0))),
            (up_up, pl.BlockSpec((None, None, rank, units), lambda i, ids: (l, ids[2], 0, i))),
            (w_down, pl.BlockSpec((None, units, dim), lambda i, ids: (l, i, 0))),
            (low_down, pl.BlockSpec((None, None, units, rank), lambda i, ids: (l, ids[3], i, 0))),
            (up_down, chosen((rank, dim), l, 3)),
            (b_down, layer_of((1, dim), l)),
        ],
        [
            (shape_of((tokens, dim), F32), whole((tokens, dim))),
            stream_spec(tokens, dim, final),
            (shape_of((NARROW, tokens, units), F32), pl.BlockSpec((None, tokens, units), lambda i, ids: (i, 0, 0))),
            (shape_of((tokens, rank), BF16), whole((tokens, rank))),
            (shape_of((tokens, rank), BF16), whole((tokens, rank))),
            (shape_of((tokens, rank), BF16), whole((tokens, rank))),
        ],
        [pltpu.VMEM((tokens, dim), BF16), pltpu.VMEM((tokens, dim), F32), pltpu.VMEM((tokens, rank), F32)],
        "mlp",
    )


def mlp_back_body(
    ids, grad, hidden, mid, att, red_proj, red_up, red_down, w_proj, low_proj, up_proj, gain, shift,
    low_up, w_up, up_up, w_down, low_down, up_down,
    g_mid, g_att, g_low_proj, g_up_proj, g_low_up, g_up_up, g_low_down, g_up_down,
    low, g_red, total, small,
):
    i = pl.program_id(0)

    @pl.when(i == 0)
    def _():
        low[...] = grad[...].astype(BF16)
        g_red[...] = dot(low[...], up_down[...], TURNED).astype(BF16)
        g_up_down[...] = dot(red_down[...], low[...], CROSS).astype(BF16)
        total[...] = jnp.zeros_like(total)
        small[...] = jnp.zeros_like(small)

    active, slope = gelu_parts(hidden[...])
    active = active.astype(BF16)
    g_low_down[...] = dot(g_red[...], active, CROSS).astype(BF16)
    g_active = dot(low[...], w_down[...], TURNED) + dot(g_red[...], low_down[...], TURNED)
    g_hidden = (g_active * slope).astype(BF16)
    g_up_up[...] = dot(red_up[...], g_hidden, CROSS).astype(BF16)
    small[...] += dot(g_hidden, up_up[...], TURNED)
    total[...] += dot(g_hidden, w_up[...], TURNED)

    @pl.when(i == pl.num_programs(0) - 1)
    def _():
        g_red_up = small[...].astype(BF16)
        scaled, inverse = norm_parts(mid[...])
        normed = (scaled * gain[...] + shift[...]).astype(BF16)
        g_low_up[...] = dot(g_red_up, normed, CROSS).astype(BF16)
        g_normed = total[...] + dot(g_red_up, low_up[...], TURNED)
        g = grad[...] + norm_grad(g_normed, scaled, inverse, gain[...])
        g_mid[...] = g
        low[...] = g.astype(BF16)
        g_red_proj = dot(low[...], up_proj[...], TURNED).astype(BF16)
        g_up_proj[...] = dot(red_proj[...], low[...], CROSS).astype(BF16)
        g_low_proj[...] = dot(g_red_proj, att[...], CROSS).astype(BF16)
        g_att[...] = (dot(low[...], w_proj[...], TURNED) + dot(g_red_proj, low_proj[...], TURNED)).astype(BF16)


def mlp_back_kernel(l, ids, grad, hidden, mid, att, red_proj, red_up, red_down, w_proj, low_proj, up_proj, gain, shift, low_up, w_up, up_up, w_down, low_down, up_down):
    tokens, dim = grad.shape
    rank = low_proj.shape[-1]
    units = w_up.shape[-1]
    flat = (shape_of((rank, dim), BF16), whole((rank, dim)))
    cut = (shape_of((rank, NARROW * units), BF16), pl.BlockSpec((rank, units), lambda i, ids: (0, i)))
    return call(
        mlp_back_body, ids, NARROW,
        [
            (grad, whole((tokens, dim))),
            (hidden, pl.BlockSpec((None, tokens, units), lambda i, ids: (i, 0, 0))),
            (mid, whole((tokens, dim))),
            (att, whole((tokens, dim))),
            (red_proj, whole((tokens, rank))),
            (red_up, whole((tokens, rank))),
            (red_down, whole((tokens, rank))),
            (w_proj, layer_of((dim, dim), l)),
            (low_proj, chosen((dim, rank), l, 1)),
            (up_proj, chosen((rank, dim), l, 1)),
            (gain, layer_of((1, dim), l)),
            (shift, layer_of((1, dim), l)),
            (low_up, chosen((dim, rank), l, 2)),
            (w_up, pl.BlockSpec((None, None, dim, units), lambda i, ids: (l, i, 0, 0))),
            (up_up, pl.BlockSpec((None, None, rank, units), lambda i, ids: (l, ids[2], 0, i))),
            (w_down, pl.BlockSpec((None, units, dim), lambda i, ids: (l, i, 0))),
            (low_down, pl.BlockSpec((None, None, units, rank), lambda i, ids: (l, ids[3], i, 0))),
            (up_down, chosen((rank, dim), l, 3)),
        ],
        [
            (shape_of((tokens, dim), F32), whole((tokens, dim))),
            (shape_of((tokens, dim), BF16), whole((tokens, dim))),
            flat, flat, flat, cut, cut, flat,
        ],
        [
            pltpu.VMEM((tokens, dim), BF16), pltpu.VMEM((tokens, rank), BF16),
            pltpu.VMEM((tokens, dim), F32), pltpu.VMEM((tokens, rank), F32),
        ],
        "mlp_back",
    )


def qkv_back_body(group, ids, g_mid, x, gain, shift, red, w, a, b, gq, *refs):
    parts, (g_x, g_low, g_raise, total, small) = refs[:group], refs[group:]
    i = pl.program_id(0)

    @pl.when(i == 0)
    def _():
        total[...] = jnp.zeros_like(total)
        small[...] = jnp.zeros_like(small)

    for j in range(w.shape[0]):
        g_kv = sum(part[j].astype(F32) for part in parts).astype(BF16)
        g_mixed = jnp.concatenate([gq[j], g_kv], axis=1)
        g_raise[j] = dot(red[...], g_mixed, CROSS).astype(BF16)
        small[...] += dot(g_mixed, b[j], TURNED)
        total[...] += dot(g_mixed, w[j], TURNED)

    @pl.when(i == pl.num_programs(0) - 1)
    def _():
        g_red = small[...].astype(BF16)
        scaled, inverse = norm_parts(x[...])
        normed = (scaled * gain[...] + shift[...]).astype(BF16)
        g_low[...] = dot(g_red, normed, CROSS).astype(BF16)
        g_normed = total[...] + dot(g_red, a[...], TURNED)
        put(g_x, g_mid[...] + norm_grad(g_normed, scaled, inverse, gain[...]))


def qkv_back_kernel(l, final, ids, g_mid, x, gain, shift, red, w, a, b, gq, parts):
    tokens, dim = x.shape
    rank = a.shape[-1]
    two = 2

    def strips(shape):
        return pl.BlockSpec((two,) + shape, lambda i, ids: (i, 0, 0))

    return call(
        functools.partial(qkv_back_body, len(parts)), ids, NARROW // two,
        [
            (g_mid, whole((tokens, dim))),
            (x, whole((tokens, dim))),
            (gain, layer_of((1, dim), l)),
            (shift, layer_of((1, dim), l)),
            (red, whole((tokens, rank))),
            (w, pl.BlockSpec((None, two, dim, 384), lambda i, ids: (l, i, 0, 0))),
            (a, chosen((dim, rank), l, 0)),
            (b, pl.BlockSpec((None, two, rank, 384), lambda i, ids: (l, i, 0, 0))),
            (gq, strips((tokens, 128))),
        ]
        + [(part, strips((tokens, 256))) for part in parts],
        [
            stream_spec(tokens, dim, final),
            (shape_of((rank, dim), BF16), whole((rank, dim))),
            (shape_of((NARROW, rank, 384), BF16), strips((rank, 384))),
        ],
        [pltpu.VMEM((tokens, dim), F32), pltpu.VMEM((tokens, rank), F32)],
        "qkv_back",
    )


def to_rows_body(held, x, out):
    n = 0
    for s in range(x.shape[0] // (len(held) * len(held[0]))):
        for g in range(len(held)):
            for place in held[g]:
                start = (s * BLOCKS + place) * BLOCK
                out[start : start + BLOCK, :] = x[n].astype(F32)
                n += 1


def to_rows(held, x):
    blocks, _, width = x.shape
    return pl.pallas_call(
        functools.partial(to_rows_body, held),
        out_shape=shape_of((blocks * BLOCK, width), F32),
        compiler_params=PARAMS,
        name="to_rows",
    )(x)


def positions(group):
    per = BLOCKS // group
    return tuple(tuple(place_of(group, g, b) for b in range(per)) for g in range(group))


def shards(mesh_shape, *args):
    (
        tokens, cotangent, adapter_ids, qkv_weight, qkv_bias, proj_weight, proj_bias,
        up_weight, up_bias, down_weight, down_bias, first_gain, first_shift, second_gain,
        second_shift, qkv_lower, qkv_raise, proj_lower, proj_raise, up_lower, up_raise,
        down_lower, down_raise,
    ) = args
    n_row, n_col = mesh_shape
    layers, adapters, dim, rank = qkv_lower.shape
    rows, width = tokens.shape
    units = up_weight.shape[2]
    seqs = rows // LEN
    group = n_col // seqs
    held = positions(group)
    per = BLOCKS // group
    mine = per * BLOCK
    merge = 128 // width
    c = lax.axis_index("col")
    g = lax.rem(c, group)
    ids = lax.dynamic_index_in_dim(adapter_ids, c // group, 0, keepdims=False)

    vector = jnp.concatenate(
        [qkv_bias.reshape(layers, 3 * width), proj_bias, up_bias, down_bias]
        + [first_gain, first_shift, second_gain, second_shift],
        axis=1,
    ).reshape(-1)
    cells = vector.shape[0]
    lanes = -(-cells // 2048) * 128
    vector = jnp.pad(vector, (0, 16 * lanes - cells)).reshape(16, lanes)

    qkv_full, proj_full, up_full, down_full, x, grad, vectors = gather_inputs(
        n_row, n_col, group, qkv_weight.reshape(layers, -1, 3 * width), proj_weight, up_weight,
        down_weight, tokens, cotangent, vector
    )
    x, grad = x.astype(F32), grad.astype(F32)
    vectors = vectors.reshape(n_col, -1)[:, :cells].reshape(n_col, layers, -1).astype(F32)
    vectors = vectors.transpose(1, 0, 2)
    at = 0
    cut = []
    for size in (3 * width, width, units, width, width, width, width, width):
        cut.append(vectors[:, :, at : at + size])
        at += size
    qkv_b = cut[0].reshape(layers, NARROW, merge, 3, width).transpose(0, 1, 3, 2, 4)
    qkv_b = qkv_b.reshape(layers, NARROW, 1, 384)
    up_b = cut[2].reshape(layers, NARROW, 1, -1)
    proj_b, down_b, gain1, shift1, gain2, shift2 = [
        cut[i].reshape(layers, 1, dim) for i in (1, 3, 4, 5, 6, 7)
    ]
    raise_qkv = lax.dynamic_index_in_dim(qkv_raise, ids[0], 1, keepdims=False)
    raise_qkv = raise_qkv.reshape(layers, rank, 3, NARROW, 128).transpose(0, 3, 1, 2, 4)
    raise_qkv = raise_qkv.reshape(layers, NARROW, rank, 384)

    def peer_values(x, step):
        pairs = [(q, q - q % group + (q + step) % group) for q in range(n_col)]
        return lax.ppermute(x, "col", pairs)

    def to_columns(x):
        if merge > 1:
            x = x.reshape(NARROW, mine, merge, width).transpose(0, 2, 1, 3).reshape(n_col, mine, width)
        x = lax.all_to_all(x, "col", split_axis=0, concat_axis=0, tiled=True)
        return to_rows(held, x.reshape(n_col * per, BLOCK, width))

    table = jnp.asarray(held, jnp.int32)
    own_place = table[g]
    key_place = jnp.concatenate([table[lax.rem(g - s + group, group)] for s in range(group)])
    bias = jnp.where(key_place[None, :] <= own_place[:, None], 0, -(2**30)).astype(jnp.int32).reshape(-1)

    records = []
    for l in range(layers):
        rec = {"x": x}
        rec["q"], kv, rec["red"] = qkv_kernel(l, ids, x, gain1, shift1, qkv_full, qkv_b, qkv_lower, raise_qkv)
        rec["kvs"] = [kv] + [peer_values(kv, s) for s in range(1, group)]
        rec["att"], rec["lse"] = attend_kernel(held, bias, rec["q"], rec["kvs"])
        rec["mid"], x, rec["hidden"], rec["red_proj"], rec["red_up"], rec["red_down"] = mlp_kernel(
            l, l == layers - 1, ids, x, rec["att"], proj_full, proj_b, proj_lower, proj_raise,
            gain2, shift2, up_lower, up_full, up_b, up_raise, down_full, down_lower, down_raise, down_b
        )
        records.append(rec)
    result = to_columns(x)

    onehot = (adapter_ids.T[:, :, None] == jnp.arange(adapters)[None, None, :]).astype(BF16)

    def all_rows(x):
        pairs = [[(q, (q + s) % n_row) for q in range(n_row)] for s in range(1, n_row)]
        return [x] + [lax.ppermute(x, "row", pair) for pair in pairs]

    onehots = jnp.concatenate(all_rows(onehot), axis=1)

    def collect(named):
        parts = jnp.concatenate([part for _, part in named], axis=2)
        parts = lax.all_to_all(parts, "col", split_axis=0, concat_axis=0, tiled=True)
        parts = parts.reshape((seqs, group) + parts.shape[1:]).astype(F32).sum(axis=1).astype(BF16)
        parts = jnp.concatenate(all_rows(parts), axis=0)
        outs, at = [], 0
        for site, part in named:
            piece = parts[:, :, at : at + part.shape[2]]
            at += part.shape[2]
            outs.append(jnp.einsum("sa,srn->arn", onehots[site], piece, preferred_element_type=F32))
        return outs

    def strips(x):
        return x.reshape(rank, n_col, -1).transpose(1, 0, 2)

    grads = [None] * layers
    for l in reversed(range(layers)):
        rec = records[l]
        g_mid, g_att, g_low_proj, g_up_proj, g_low_up, g_up_up, g_low_down, g_up_down = mlp_back_kernel(
            l, ids, grad, rec["hidden"], rec["mid"], rec["att"], rec["red_proj"], rec["red_up"],
            rec["red_down"], proj_full, proj_lower, proj_raise, gain2, shift2, up_lower, up_full,
            up_raise, down_full, down_lower, down_raise
        )
        done = collect(
            [(1, strips(g_low_proj)), (1, strips(g_up_proj)), (2, strips(g_low_up))]
            + [(2, strips(g_up_up)), (3, strips(g_low_down)), (3, strips(g_up_down))]
        )
        gq, *gkvs = attend_back_kernel(held, bias, rec["q"], rec["lse"], rec["att"], g_att, rec["kvs"])
        parts = [gkvs[0]] + [peer_values(gkvs[s], group - s) for s in range(1, group)]
        grad, g_low, g_raise = qkv_back_kernel(
            l, l == 0, ids, g_mid, rec["x"], gain1, shift1, rec["red"], qkv_full, qkv_lower, raise_qkv, gq, parts
        )
        g_raise = g_raise.reshape(NARROW, rank, 3, merge, width).transpose(0, 3, 1, 2, 4)
        first = collect([(0, strips(g_low)), (0, g_raise.reshape(n_col, rank, 3 * width))])
        grads[l] = first + done
    input_grad = to_columns(grad)

    outs = []
    for number in range(8):
        p = jnp.stack([grads[l][number] for l in range(layers)])
        if number == 1:
            p = p.reshape(layers, adapters, rank, 3, width)
        elif number % 2 == 0:
            p = p.transpose(0, 1, 3, 2)
        outs.append(p)
    return (result, input_grad) + tuple(outs)


def solution(mesh):
    mesh_shape = (mesh.shape["row"], mesh.shape["col"])
    return jax.shard_map(
        functools.partial(shards, mesh_shape),
        mesh=mesh,
        in_specs=(
            P("row", "col"), P("row", "col"), P("row", None),
            P(None, "row", None, "col"), P(None, None, "col"),
            P(None, "col", "row"), P(None, "col"),
            P(None, "row", "col"), P(None, "col"),
            P(None, "col", "row"), P(None, "col"),
            P(None, "col"), P(None, "col"), P(None, "col"), P(None, "col"),
            P(), P(), P(), P(), P(), P(), P(), P(),
        ),
        out_specs=(
            P("row", "col"), P("row", "col"),
            P(None, None, "col", None), P(None, None, None, None, "col"),
            P(None, None, "col", None), P(None, None, None, "col"),
            P(None, None, "col", None), P(None, None, None, "col"),
            P(None, None, "col", None), P(None, None, None, "col"),
        ),
        check_vma=False,
    )
```

```python
import functools

import jax
import jax.numpy as jnp
from jax import lax
from jax.experimental import pallas as pl
from jax.experimental.pallas import tpu as pltpu
from jax.sharding import PartitionSpec as P

HD = 64
LEN = 1024
BLOCK = 256
BLOCKS = LEN // BLOCK
EPSILON = 1e-05
SCALE = HD**-0.5
ROOT = (2.0 / 3.141592653589793) ** 0.5
MESH = pl.DeviceIdType.MESH
F32 = jnp.float32
BF16 = jnp.bfloat16


ROW_FIRST = (("z", 0, 1), ("z", 1, 0))
ROW_SECOND = ((0, "z", 1), (1, "z", 0))
ORDERS = {"qkv": (ROW_SECOND,), "proj": (ROW_SECOND,), "up": (ROW_FIRST,) * 2, "down": (ROW_FIRST,) * 2}
KINDS = ("qkv", "proj", "up", "down")
DEPTH = 4
FUSED = True
LINK = 90e3


def transfer_plan(order):
    masks, rows, steps = [0], False, []
    for d in order:
        steps.append((d, tuple(masks), rows))
        if d == "z":
            rows = True
        else:
            masks = masks + [m ^ d for m in masks]
    steps.append((None, tuple(masks), rows))
    return steps


def transfer_schedule(pieces, n_row, tasks):
    cost, parts = {}, {}
    for k, (name, order, size) in enumerate(pieces):
        parts.setdefault(name, set()).add(k)
        for p, (d, masks, rows) in enumerate(transfer_plan(order)[:-1]):
            load = (n_row // 2) * (n_row - n_row // 2) if d == "z" else (n_row if rows else 1)
            cost[k, p] = (d, 2 * len(masks) * load * size / LINK)
    ready = {d: [] for d, _ in cost.values()}
    free = dict.fromkeys(ready, 0.0)
    flight = {d: [] for d in ready}
    for k in range(len(pieces)):
        ready[cost[k, 0][0]].append((k, 0))
    tasks, left = list(tasks), {}
    for task in tasks:
        left[task[4]] = left.get(task[4], 0) + 1
    landed, staged, now, ops = {}, {}, 0.0, []

    def stage(name):
        kind, l = name
        if name in landed and name not in staged and landed[name] <= now and not left.get((kind, l - 1)):
            staged[name] = now + 3.0
            ops.append(("stage", kind, l))

    while tasks or any(ready.values()) or any(flight.values()):
        for d in ready:
            while ready[d] and len(flight[d]) < DEPTH:
                k, p = ready[d].pop(0)
                free[d] = max(now, free[d]) + cost[k, p][1]
                flight[d].append((free[d], k, p))
                ops.append(("start", k, p))
        if tasks:
            for name in list(landed):
                stage(name)
        events = [f for line in flight.values() for f in line]
        event = min(events) if events else None
        due = None
        if tasks:
            need = tasks[0][4]
            due = now if need is None else staged.get(need)
            if due is None and need in landed and not left.get((need[0], need[1] - 1)):
                due = landed[need]
        if due is not None and (event is None or max(due, now) < event[0]):
            now = max(due, now)
            need = tasks[0][4]
            if need is not None and need not in staged:
                continue
            name, l, part, micros, _ = tasks.pop(0)
            left[need] -= 1
            now += micros
            ops.append(("task", name, (l, part)))
            continue
        now, k, p = max(now, event[0]), event[1], event[2]
        d = cost[k, p][0]
        flight[d].remove(event)
        ops.append(("wait", k, p))
        if (k, p + 1) in cost:
            later = ready[cost[k, p + 1][0]]
            later.append((k, p + 1))
            later.sort()
        else:
            name = pieces[k][0]
            parts[name].discard(k)
            if not parts[name]:
                landed[name] = now + 4.0
    return ops


def place_of(group, g, b):
    if group == 2:
        return g + b * (BLOCKS - 1 - 2 * g)
    return g * (BLOCKS // group) + b


def positions(group):
    per = BLOCKS // group
    return tuple(tuple(place_of(group, g, b) for b in range(per)) for g in range(group))


NARROW = 8
CROSS = ((0,), (0,))
TURNED = ((1,), (1,))


def dot(a, b, dims=((1,), (0,))):
    return lax.dot_general(a, b, (dims, ((), ())), preferred_element_type=F32)


def columns(i, size=128):
    if isinstance(i, int):
        return pl.ds(i * size, size)
    return pl.ds(pl.multiple_of(i * size, size), size)


def norm_parts(x):
    center = x - jnp.mean(x, axis=1, keepdims=True)
    inverse = lax.rsqrt(jnp.mean(center * center, axis=1, keepdims=True) + EPSILON)
    return center * inverse, inverse


def norm_grad(grad, scaled, inverse, gain):
    w = grad * gain
    first = jnp.mean(w, axis=1, keepdims=True)
    second = jnp.mean(w * scaled, axis=1, keepdims=True)
    return inverse * (w - first - scaled * second)


def norm_low(x, gain, shift):
    return (norm_parts(x)[0] * gain + shift).astype(BF16)


def pair_state(held):
    group, per = len(held), len(held[0])
    state = {}
    for s in range(per):
        for j in range(group):
            for b in range(per):
                seen = {held[(g - j) % group][b] <= held[g][s] for g in range(group)}
                state[s, j, b] = 0 if len(seen) == 2 else (1 if True in seen else -1)
    return state


def pair_bias(held, g):
    group = len(held)
    bias = {}
    for (s, j, b), state in pair_state(held).items():
        if state == 0:
            keys = place_of(group, lax.rem(g - j + group, group), b)
            bias[s, j, b] = jnp.where(keys <= place_of(group, g, s), 0.0, -1e9).astype(F32)
    return bias


def head_mask(h):
    lane = lax.broadcasted_iota(jnp.int32, (1, 128), 1)
    return (lane // HD) == h


def attend_strip(held, bias, i, q, kvs, out, lse):
    group, per = len(held), len(held[0])
    state = pair_state(held)
    turned = {}
    for s in range(per):
        rows = pl.ds(s * BLOCK, BLOCK)
        queries = q[i, rows, :] * SCALE
        pieces = []
        for h in range(2):
            query = jnp.where(head_mask(h), queries, 0).astype(BF16)
            scores, values = [], []
            for j in range(group):
                for b in range(per):
                    if state[s, j, b] < 0:
                        continue
                    keys = kvs[j][i, b * BLOCK : (b + 1) * BLOCK, :128]
                    score = dot(keys, query, TURNED)
                    if state[s, j, b] == 0:
                        score = score + bias[s, j, b]
                    scores.append(score)
                    if (j, b) not in turned:
                        turned[j, b] = kvs[j][i, b * BLOCK : (b + 1) * BLOCK, 128:].T
                    values.append(turned[j, b][h * HD : (h + 1) * HD])
            top = functools.reduce(jnp.maximum, [jnp.max(x, axis=0, keepdims=True) for x in scores])
            total, made = 0.0, 0.0
            for score, value in zip(scores, values):
                e = jnp.exp(score - top)
                total = total + jnp.sum(e, axis=0, keepdims=True)
                made = made + dot(value, e.astype(BF16))
            pieces.append(made / total)
            lse[i, h : h + 1, rows] = top + jnp.log(total)
        out[rows, columns(i)] = jnp.concatenate(pieces, axis=0).T.astype(BF16)


def attend_back_strip(held, bias, i, q, lse, out, grad, kvs, gq, gkvs):
    group, per = len(held), len(held[0])
    state = pair_state(held)
    turned, gk, gv = {}, {}, {}
    for s in range(per):
        rows = pl.ds(s * BLOCK, BLOCK)
        queries = q[i, rows, :] * SCALE
        up = grad[rows, columns(i)]
        product = (up.astype(F32) * out[rows, columns(i)].astype(F32)).T
        pieces = []
        for h in range(2):
            query = jnp.where(head_mask(h), queries, 0).astype(BF16)
            given = jnp.where(head_mask(h), up, 0).astype(BF16)
            inner = jnp.sum(product[h * HD : (h + 1) * HD], axis=0, keepdims=True)
            level = lse[i, h : h + 1, rows]
            made = 0.0
            for j in range(group):
                for b in range(per):
                    if state[s, j, b] < 0:
                        continue
                    keys = kvs[j][i, b * BLOCK : (b + 1) * BLOCK, :128]
                    values = kvs[j][i, b * BLOCK : (b + 1) * BLOCK, 128:]
                    score = dot(keys, query, TURNED)
                    if state[s, j, b] == 0:
                        score = score + bias[s, j, b]
                    probs = jnp.exp(score - level)
                    g_probs = dot(values, given, TURNED)
                    g_scores = (probs * (g_probs - inner)).astype(BF16)
                    if (j, b) not in turned:
                        turned[j, b] = keys.T
                        gk[j, b], gv[j, b] = 0.0, 0.0
                    gv[j, b] = gv[j, b] + dot(probs.astype(BF16), given)
                    gk[j, b] = gk[j, b] + dot(g_scores, query)
                    made = made + dot(turned[j, b][h * HD : (h + 1) * HD], g_scores)
            pieces.append(made)
        gq[i, rows, :] = (jnp.concatenate(pieces, axis=0) * SCALE).T.astype(BF16)
    for j in range(group):
        for b in range(per):
            rows = pl.ds(b * BLOCK, BLOCK)
            gkvs[j][i, rows, :128] = gk[j, b].astype(BF16)
            gkvs[j][i, rows, 128:] = gv[j, b].astype(BF16)


def by_rows(count, body, size=128):
    each(count // size, lambda n: body(pl.ds(pl.multiple_of(n * size, size), size)))


def keep(value, red, red_out):
    red[...] = value.astype(BF16)
    red_out[...] = value.T.astype(BF16)


def each(count, body):
    def step(i, carry):
        body(i)
        return carry

    lax.fori_loop(0, count, step, 0)


def qkv_stage(x, gain, shift, w, bias, low, up, q, kv, red, red_out, normed):
    def norm(rows):
        normed[rows, :] = norm_low(x[rows, :], gain, shift)

    by_rows(x.shape[0], norm)
    keep(dot(normed[...], low[...], TURNED), red, red_out)

    def pair(j):
        made = dot(normed[...], w[j])
        for n in range(2):
            i = 2 * j + n
            mixed = made[:, n * 384 : (n + 1) * 384] + (bias[i] + dot(red[...], up[i]))
            q[i] = mixed[:, :128].astype(BF16)
            kv[i] = mixed[:, 128:].astype(BF16)

    each(NARROW // 2, pair)


def proj_stage(x, att, w, bias, low, up, gain, shift, low_up, mid, normed, red, red_out, red_up, red_up_out):
    keep(dot(att[...], low[...], TURNED), red, red_out)

    def part(rows):
        value = x[rows, :] + (dot(att[rows, :], w[...]) + bias + dot(red[rows, :], up[...]))
        mid[rows, :] = value
        normed[rows, :] = norm_low(value, gain, shift)

    by_rows(x.shape[0], part, 256)
    keep(dot(normed[...], low_up[...], TURNED), red_up, red_up_out)


def up_strip(i, normed, w, bias, red_up, up, hidden, active):
    units = w.shape[2]
    cols = columns(i, units)
    value = dot(normed[...], w[i]) + (bias[i] + dot(red_up[...], up[:, cols]))
    hidden[:, cols] = value.astype(BF16)
    inner = ROOT * (value + 0.044715 * (value * value * value))
    active[:, cols] = (0.5 * value * (1.0 + jnp.tanh(inner))).astype(BF16)


def down_stage(mid, active, w, bias, low, up, red, red_out, put):
    keep(dot(active[...], low[...], TURNED), red, red_out)

    for n in range(mid.shape[1] // 256):
        cols = slice(n * 256, (n + 1) * 256)
        put(n, mid[:, cols] + (dot(active[...], w[:, cols]) + bias[:, cols] + dot(red[...], up[:, cols])))


def gelu_parts(x):
    square = x * x
    t = jnp.tanh(ROOT * (x + 0.044715 * (x * square)))
    half = 0.5 * (1.0 + t)
    slope = half + 0.5 * x * (1.0 - t * t) * (ROOT * (1.0 + 3 * 0.044715 * square))
    return x * half, slope


class Vectors:
    def __init__(self, ref, l):
        self.ref, self.l = ref, l

    def qkv(self, i):
        return self.ref[i, pl.ds(4 * self.l, 1), :384]

    def up(self, i):
        return self.ref[i, pl.ds(4 * self.l + 1, 1), :]

    def row(self, name):
        at = ("proj", "down", "gain1", "shift1", "gain2", "shift2").index(name)
        row, lane = 4 * self.l + 2 + at // 4, at % 4 * 128
        return jnp.concatenate([self.ref[i, row : row + 1, lane : lane + 128] for i in range(NARROW)], axis=1)


class Strips:
    def __init__(self, read):
        self.read = read

    def __getitem__(self, i):
        return self.read(i)


TABLES = ("low_qkv", "up_qkv", "low_proj", "up_proj", "low_up", "up_up", "low_down", "up_down")
SAVED = ("q", "kv", "peer", "att", "lse", "mid", "hidden", "x")


def task_list(layers):
    tasks = [("load", 0, 0, 3.0, None)]
    for l in range(layers):
        tasks.append(("qkv", l, 0, 7.0, ("qkv", l)))
        tasks += [("attend", l, n, 5.0, None) for n in range(4)]
        tasks.append(("proj", l, 0, 4.0, ("proj", l)))
        tasks += [("up", l, n, 5.0, ("up", l)) for n in range(2)]
        tasks.append(("down", l, 0, 6.0, ("down", l)))
    return tasks


class ForwardWork:
    def __init__(self, n_col, group, refs):
        self.__dict__.update(refs)
        self.group = group
        self.held = positions(group)
        self.r, self.c = lax.axis_index("row"), lax.axis_index("col")
        self.g = lax.rem(self.c, group)
        self.bias = pair_bias(self.held, self.g)
        self.layers = self.low_qkv.shape[0]

    def stage_copies(self, kind, l):
        full = self.full[kind]
        if kind == "qkv":
            pieces = []
            for i in range(NARROW):
                src = full.at[l, i]
                pieces.append((src, self.wq.at[i // 2, :, :, :, pl.ds(i % 2 * 384, 384)]))
            return pieces, self.wq
        if kind == "up":
            return [(full.at[l, i], self.wu.at[i]) for i in range(NARROW)], self.wu
        target = self.wp if kind == "proj" else self.wd
        return [(full.at[l, i], target.at[i]) for i in range(NARROW)], target

    def stage(self, kind, l):
        for src, dst in self.stage_copies(kind, l)[0]:
            pltpu.make_async_copy(src, dst, self.stage_sem.at[KINDS.index(kind)]).start()

    def staged(self, kind, l):
        target = self.stage_copies(kind, l)[1]
        pltpu.make_async_copy(target, target, self.stage_sem.at[KINDS.index(kind)]).wait()

    def save_copy(self, name, l):
        src = {
            "q": self.q, "kv": self.kv, "peer": self.peer.at[l], "att": self.att, "lse": self.lse,
            "mid": self.mid, "hidden": self.hidden, "x": self.x,
        }[name]
        return pltpu.make_async_copy(src, self.saved[name].at[l], self.save_sem.at[l, SAVED.index(name)])

    def save(self, *names, l):
        for name in names:
            self.save_copy(name, l).start()

    def settled(self, *names, l):
        if l >= 0:
            for name in names:
                self.save_copy(name, l).wait()

    def exchange(self, l, s):
        to = self.c - self.g + lax.rem(self.g + s, self.group)
        return pltpu.make_async_remote_copy(
            src_ref=self.kv, dst_ref=self.peer.at[l, s - 1],
            send_sem=self.kv_send.at[l, s - 1], recv_sem=self.kv_recv.at[l, s - 1],
            device_id=(self.r, to), device_id_type=MESH,
        )

    def run(self, name, l, part):
        vec = Vectors(self.vec, l)
        if name == "load":
            self.arrive_tokens()
            self.x[...] = self.tokens_v[...].astype(F32)
        elif name == "qkv":
            self.staged("qkv", l)
            self.settled("q", "kv", l=l - 1)
            if l > 0:
                for s in range(1, self.group):
                    self.exchange(l - 1, s).wait_send()
            w = self.wq.reshape(NARROW // 2, -1, 768)
            qkv_stage(
                self.x, vec.row("gain1"), vec.row("shift1"), w, Strips(vec.qkv), self.low_qkv.at[l],
                self.up_qkv.at[l], self.q, self.kv, self.red, self.reds.at[l, 0], self.normed,
            )
            for s in range(1, self.group):
                self.exchange(l, s).start()
            self.save("q", "kv", l=l)
        elif name == "attend":
            if part == 0:
                for s in range(1, self.group):
                    self.exchange(l, s).wait_recv()
                self.save("peer", l=l)
                self.settled("att", "lse", l=l - 1)
            kvs = [self.kv] + [self.peer.at[l, s - 1] for s in range(1, self.group)]
            size = NARROW // 4
            each(size, lambda n: attend_strip(self.held, self.bias, part * size + n, self.q, kvs, self.att, self.lse))
            if part == 3:
                self.save("att", "lse", l=l)
        elif name == "proj":
            self.staged("proj", l)
            self.settled("mid", l=l - 1)
            dim = self.att.shape[1]
            proj_stage(
                self.x, self.att, self.wp.reshape(dim, dim), vec.row("proj"), self.low_proj.at[l],
                self.up_proj.at[l], vec.row("gain2"), vec.row("shift2"), self.low_up.at[l],
                self.mid, self.normed, self.red, self.reds.at[l, 1], self.red_up, self.reds.at[l, 2],
            )
            self.save("mid", l=l)
        elif name == "up":
            if part == 0:
                self.staged("up", l)
                self.settled("hidden", l=l - 1)
            w = self.wu.reshape(NARROW, self.x.shape[1], -1)
            size = NARROW // 2
            each(size, lambda n: up_strip(
                part * size + n, self.normed, w, Strips(vec.up), self.red_up, self.up_up.at[l],
                self.hidden, self.active,
            ))
            if part == 1:
                self.save("hidden", l=l)
        elif name == "down":
            self.staged("down", l)
            self.settled("x", l=l - 1)
            dim = self.x.shape[1]

            def put(n, value):
                if l < self.layers - 1:
                    self.x[:, columns(n, 256)] = value
                else:
                    for m in range(2):
                        self.result[2 * n + m] = value[:, m * 128 : (m + 1) * 128].astype(BF16)

            down_stage(
                self.mid, self.active, self.wd.reshape(-1, dim), vec.row("down"), self.low_down.at[l],
                self.up_down.at[l], self.red, self.reds.at[l, 3], put,
            )
            if l < self.layers - 1:
                self.save("x", l=l)

    def close(self):
        last = self.layers - 1
        self.settled(*[name for name in SAVED if name not in ("x", "peer")], l=last)
        for l in range(self.layers):
            self.settled("peer", l=l)
        for s in range(1, self.group):
            self.exchange(last, s).wait_send()
        if last > 0:
            pass


def gather_body(n_row, n_col, layers, group, names, *refs):
    refs = dict(zip(names, refs))
    shard = {kind: refs["shard_" + kind] for kind in KINDS}
    full = {kind: refs["full_" + kind] for kind in KINDS}
    tokens, cotangent, vector = refs["tokens"], refs["cotangent"], refs["vector"]
    own_tokens, own_cotangent, vectors = refs["own_tokens"], refs["own_cotangent"], refs["vectors"]
    local_sem, send_sem, recv_sem = refs["local_sem"], refs["send_sem"], refs["recv_sem"]
    near_sem, out_sem, in_sem = refs["near_sem"], refs["out_sem"], refs["in_sem"]
    r = lax.axis_index("row")
    c = lax.axis_index("col")
    link_bits = [b for b in (2**k for k in range(1, 8)) if b < n_col]
    depth = shard["up"].shape[1]

    def row_peer(s):
        return (lax.rem(r + s, n_row), c)

    def col_peer(bit):
        return (r, c ^ bit)

    peers = [row_peer(s) for s in range(1, n_row)]
    peers += [(r, lax.rem(c + d, n_col)) for d in range(1, n_col)]
    barrier = pltpu.get_barrier_semaphore()
    for peer in peers:
        pl.semaphore_signal(barrier, inc=1, device_id=peer, device_id_type=MESH)
    pl.semaphore_wait(barrier, len(peers))

    per, width = BLOCKS // group, tokens.shape[1]

    def own_place(ref, b, col):
        if len(ref.shape) == 2:
            start = pl.multiple_of(col * width, width)
            return ref.at[pl.ds(b * BLOCK, BLOCK), pl.ds(start, width)]
        return ref.at[col, pl.ds(b * BLOCK, BLOCK)]

    def from_place(ref, b, col):
        start = (col // group) * LEN + place_of(group, lax.rem(col, group), b) * BLOCK
        return ref.at[pl.ds(pl.multiple_of(start, BLOCK), BLOCK)]

    exchanged = ((tokens, own_tokens), (cotangent, own_cotangent))

    def near(n, b):
        src, dst = exchanged[n]
        return pltpu.make_async_copy(from_place(src, b, c), own_place(dst, b, c), near_sem.at[n * per + b])

    def near_vector():
        return pltpu.make_async_copy(vector, vectors.at[c], near_sem.at[2 * per])

    def far(src, dst, n, peer):
        return pltpu.make_async_remote_copy(
            src_ref=src, dst_ref=dst, send_sem=out_sem.at[n], recv_sem=in_sem.at[n],
            device_id=peer, device_id_type=MESH,
        )

    def start_exchange(n):
        src, dst = exchanged[n]
        for b in range(per):
            near(n, b).start()
        for d in range(1, n_col):
            to = lax.rem(c + d, n_col)
            for b in range(per):
                far(from_place(src, b, to), own_place(dst, b, c), n, (r, to)).start()

    def wait_exchange(n):
        _, dst = exchanged[n]
        for b in range(per):
            near(n, b).wait()
        if len(dst.shape) == 2:
            ref = dst.at[:, pl.ds(0, (n_col - 1) * width)]
        else:
            ref = dst.at[pl.ds(0, n_col - 1)]
        far(ref, ref, n, col_peer(1)).wait()

    def own(kind, l, h):
        ref = shard[kind]
        size = ref.shape[1] // (2 * len(ORDERS[kind]))
        return ref.at[l, pl.ds(h * size, size)]

    def block(kind, l, h, row, col):
        if kind in ("qkv", "up"):
            return full[kind].at[l, col, row, h]
        start = pl.multiple_of(row * depth, depth)
        return full[kind].at[l, col, h, :, pl.ds(start, depth)]

    def strip(kind, l, h, col):
        if kind in ("qkv", "up"):
            return full[kind].at[l, col, :, h]
        return full[kind].at[l, col, h]

    def amount(kind, l, h, strips, rows):
        if kind in ("qkv", "up"):
            return full[kind].at[l, pl.ds(0, strips), pl.ds(0, rows), h]
        return full[kind].at[l, pl.ds(0, strips), h, :, pl.ds(0, rows * depth)]

    chunks = []
    for l in range(layers):
        for kind in KINDS:
            for h in range(2 * len(ORDERS[kind])):
                order = []
                for d in ORDERS[kind][h // 2][h % 2]:
                    if d == "z":
                        order.append("z")
                    elif d < len(link_bits):
                        order.append(link_bits[d])
                order += link_bits[2:]
                chunks.append((kind, l, h, tuple(order)))
    phases = len(link_bits) + 1

    def remote(src, dst, k, p, peer):
        return pltpu.make_async_remote_copy(
            src_ref=src, dst_ref=dst, send_sem=send_sem.at[k, p], recv_sem=recv_sem.at[k, p],
            device_id=peer, device_id_type=MESH,
        )

    def local(k):
        kind, l, h, _ = chunks[k]
        return pltpu.make_async_copy(own(kind, l, h), block(kind, l, h, r, c), local_sem.at[k])

    def issue(k, p):
        kind, l, h, order = chunks[k]
        d, masks, whole = transfer_plan(order)[p]
        for m in masks:
            if d == "z":
                src = own(kind, l, h) if m == 0 else block(kind, l, h, r, c ^ m)
                for s in range(1, n_row):
                    remote(src, block(kind, l, h, r, c ^ m), k, p, row_peer(s)).start()
            elif whole:
                ref = strip(kind, l, h, c ^ m)
                remote(ref, ref, k, p, col_peer(d)).start()
            else:
                src = own(kind, l, h) if m == 0 else block(kind, l, h, r, c ^ m)
                remote(src, block(kind, l, h, r, c ^ m), k, p, col_peer(d)).start()

    def moved(k, p):
        kind, l, h, order = chunks[k]
        d, masks, whole = transfer_plan(order)[p]
        if d == "z":
            rows = n_row - 1
        else:
            rows = n_row if whole else 1
        ref = amount(kind, l, h, len(masks), rows)
        return remote(ref, ref, k, p, col_peer(1))

    def share(k, p):
        kind, l, h, order = chunks[k]
        steps = transfer_plan(order)
        (d, masks, _), (_, later, whole) = steps[p], steps[p + 1]
        if not whole:
            return
        fresh = masks if d == "z" else later[len(masks):]
        for m in fresh:
            ref = strip(kind, l, h, c ^ m)
            remote(ref, ref, k, phases, col_peer(1)).start()

    def shared(k):
        kind, l, h, _ = chunks[k]
        ref = amount(kind, l, h, n_col // 2, n_row)
        return remote(ref, ref, k, phases, col_peer(1))

    def finish(k, p):
        moved(k, p).wait_recv()
        if chunks[k][3][p] == "z":
            local(k).wait()
        share(k, p)

    count = len(chunks)
    near_vector().start()
    for d in range(1, n_col):
        far(vector, vectors.at[c], 2, (r, lax.rem(c + d, n_col))).start()
    start_exchange(0)
    for k in range(count):
        local(k).start()
    def vectors_arrive():
        near_vector().wait()
        rest = vectors.at[pl.ds(0, n_col - 1)]
        far(rest, rest, 2, col_peer(1)).wait()

    work = None
    if "x" in refs:
        refs.update(full=full, saved={name: refs["saved_" + name] for name in SAVED})

        def arrive_tokens():
            vectors_arrive()
            wait_exchange(0)
            load_sem = refs["load_sem"]
            loads = [(own_tokens, refs["tokens_v"]), (vectors, refs["vec"])]
            copies = [pltpu.make_async_copy(s, d, load_sem.at[n]) for n, (s, d) in enumerate(loads)]
            for copy in copies:
                copy.start()
            for copy in copies:
                copy.wait()

        refs.update(arrive_tokens=arrive_tokens)
        work = ForwardWork(n_col, group, refs)

    pieces = []
    for kind, l, h, order in chunks:
        size = 2 * shard[kind].shape[1] * shard[kind].shape[2] // (2 * len(ORDERS[kind]))
        pieces.append(((kind, l), order, size))
    for op, k, p in transfer_schedule(pieces, n_row, task_list(layers) if work else []):
        if op == "start":
            issue(k, p)
        elif op == "wait":
            finish(k, p)
        elif op == "stage":
            for n, (kind, l, _, _) in enumerate(chunks):
                if (kind, l) == (k, p):
                    shared(n).wait_recv()
            work.stage(k, p)
        else:
            work.run(k, *p)
    start_exchange(1)
    for k in range(count):
        for p in range(phases):
            moved(k, p).wait_send()
        shared(k).wait_send()
        if not work:
            shared(k).wait_recv()
    if work:
        work.close()
    else:
        vectors_arrive()
        wait_exchange(0)
    wait_exchange(1)


def gather_inputs(n_row, n_col, group, qkv, proj, up, down, tokens, cotangent, vector, tables=None):
    layers, depth = up.shape[0], up.shape[1]
    width, units = proj.shape[1], down.shape[1]
    dim, hidden = depth * n_row, units * n_col
    mine = LEN // group
    cuts = [2 * len(ORDERS[kind]) for kind in KINDS]
    own = (mine, dim) if width % 128 == 0 else (n_col, mine, width)
    hbm = pl.BlockSpec(memory_space=pltpu.HBM)
    vmem = pl.BlockSpec(memory_space=pltpu.VMEM)
    dma = pltpu.SemaphoreType.DMA
    count = layers * sum(cuts)
    phases = n_col.bit_length()
    inputs = [("shard_" + kind, array, hbm) for kind, array in zip(KINDS, (qkv, proj, up, down))]
    inputs += [("tokens", tokens, hbm), ("cotangent", cotangent, hbm), ("vector", vector, hbm)]
    outputs = [
        ("full_qkv", (layers, n_col, n_row, cuts[0], depth // cuts[0], qkv.shape[2]), BF16, hbm),
        ("full_proj", (layers, n_col, cuts[1], width // cuts[1], dim), BF16, hbm),
        ("full_up", (layers, n_col, n_row, cuts[2], depth // cuts[2], units), BF16, hbm),
        ("full_down", (layers, n_col, cuts[3], units // cuts[3], dim), BF16, hbm),
        ("own_tokens", own, BF16, hbm),
        ("own_cotangent", own, BF16, hbm),
        ("vectors", (n_col,) + vector.shape, F32, hbm),
    ]
    scratch = [
        ("local_sem", dma((count,))),
        ("send_sem", dma((count, phases))),
        ("recv_sem", dma((count, phases))),
        ("near_sem", dma((2 * (BLOCKS // group) + 1,))),
        ("out_sem", dma((3,))),
        ("in_sem", dma((3,))),
    ]
    if tables is not None:
        rank = tables[0].shape[1]
        inputs += [(name, table, vmem) for name, table in zip(TABLES, tables)]
        strip = (NARROW, mine)
        kept = {
            "q": (strip + (128,), BF16), "kv": (strip + (256,), BF16), "att": ((mine, dim), BF16),
            "lse": ((NARROW, 8, mine), F32), "mid": ((mine, dim), F32), "hidden": ((mine, hidden), BF16),
            "x": ((mine, dim), F32), "peer": ((group - 1,) + strip + (256,), BF16),
        }
        outputs += [("saved_" + name, (layers,) + kept[name][0], kept[name][1], hbm) for name in SAVED]
        outputs += [
            ("reds", (layers, 4, rank, mine), BF16, vmem),
            ("result", (NARROW, mine, 128), BF16, vmem),
        ]
        scratch += [
            (name, pltpu.VMEM(((layers,) if name == "peer" else ()) + kept[name][0], kept[name][1]))
            for name in SAVED
        ]
        scratch += [
            ("wq", pltpu.VMEM((NARROW // 2, n_row, cuts[0], depth // cuts[0], 768), BF16)),
            ("wp", pltpu.VMEM((NARROW, cuts[1], width // cuts[1], dim), BF16)),
            ("wu", pltpu.VMEM((NARROW, n_row, cuts[2], depth // cuts[2], units), BF16)),
            ("wd", pltpu.VMEM((NARROW, cuts[3], units // cuts[3], dim), BF16)),
            ("tokens_v", pltpu.VMEM((mine, dim), BF16)),
            ("normed", pltpu.VMEM((mine, dim), BF16)),
            ("active", pltpu.VMEM((mine, hidden), BF16)),
            ("red", pltpu.VMEM((mine, rank), BF16)),
            ("red_up", pltpu.VMEM((mine, rank), BF16)),
            ("vec", pltpu.VMEM((n_col,) + vector.shape, F32)),
            ("stage_sem", dma((4,))),
            ("save_sem", dma((layers, len(SAVED)))),
            ("kv_send", dma((layers, group - 1))),
            ("kv_recv", dma((layers, group - 1))),
            ("load_sem", dma((2,))),
        ]
    names = [x[0] for x in inputs] + [x[0] for x in outputs] + [x[0] for x in scratch]
    outs = pl.pallas_call(
        functools.partial(gather_body, n_row, n_col, layers, group, tuple(names)),
        out_shape=[jax.ShapeDtypeStruct(shape, kind) for _, shape, kind, _ in outputs],
        in_specs=[spec for _, _, spec in inputs],
        out_specs=[spec for _, _, _, spec in outputs],
        scratch_shapes=[shape for _, shape in scratch],
        compiler_params=pltpu.CompilerParams(
            collective_id=0, has_side_effects=True, vmem_limit_bytes=60 * 2**20
        ),
        name="gather_inputs",
    )(*[array for _, array, _ in inputs])
    outs = dict(zip([x[0] for x in outputs], outs))

    merge = 128 // width
    strips = n_col // merge
    qkv_full = outs["full_qkv"].reshape(layers, n_col, dim, qkv.shape[2])
    up_full = outs["full_up"].reshape(layers, n_col, dim, units)
    rows, vec = [outs["own_tokens"], outs["own_cotangent"]], outs["vectors"]
    if merge > 1:
        qkv_full = qkv_full.reshape(layers, strips, merge, dim, 3, width).transpose(0, 1, 3, 4, 2, 5)
        up_full = up_full.reshape(layers, strips, merge, dim, units).transpose(0, 1, 3, 2, 4)
        rows = [x.transpose(1, 0, 2).reshape(mine, dim) for x in rows]
        vec = vec.reshape(strips, merge, layers, 4, 4 * 128)
        first = vec[:, :, :, 0, : 3 * width].reshape(strips, merge, layers, 3, width).transpose(0, 2, 3, 1, 4)
        first = jnp.pad(first.reshape(strips, layers, 384), ((0, 0), (0, 0), (0, 128)))
        second = vec[:, :, :, 1, :units].transpose(0, 2, 1, 3).reshape(strips, layers, 512)
        rest = vec[:, :, :, 2:, : 4 * width].reshape(strips, merge, layers, 2, 4, width)
        rest = rest.transpose(0, 2, 3, 4, 1, 5).reshape(strips, layers, 2, 512)
        vec = jnp.concatenate([first[:, :, None], second[:, :, None], rest], axis=2)
        vec = vec.reshape(strips, layers * 4, 512)
    outs.update(
        qkv=qkv_full.reshape(layers, strips, dim, 384),
        proj=outs["full_proj"].reshape(layers, dim, dim),
        up=up_full.reshape(layers, strips, dim, units * merge),
        down=outs["full_down"].reshape(layers, hidden, dim),
        tokens=rows[0], cotangent=rows[1], vec=vec,
    )
    return outs


PARAMS = pltpu.CompilerParams(vmem_limit_bytes=60 * 2**20)


def shape_of(shape, kind):
    return jax.ShapeDtypeStruct(shape, kind)


def kernel(body, name, inputs, outputs, scratch=()):
    spaces = (pl.BlockSpec(memory_space=pltpu.VMEM), pl.BlockSpec(memory_space=pltpu.HBM))
    return pl.pallas_call(
        body,
        out_shape=[shape_of(shape, kind) for shape, kind, _ in outputs],
        in_specs=[spaces[far] for _, far in inputs],
        out_specs=[spaces[far] for _, _, far in outputs],
        scratch_shapes=list(scratch),
        compiler_params=PARAMS,
        name=name,
    )(*[array for array, _ in inputs])


def own_group(group):
    return lax.rem(lax.axis_index("col"), group)


def qkv_body(l, x, vec, w, low, up, q, kv, red_out, red, normed, buf, sem):
    copies = []
    for i in range(NARROW):
        copies.append(pltpu.make_async_copy(w.at[l, i], buf.at[i // 2, :, columns(i % 2, 384)], sem.at[i]))
        copies[-1].start()
    for copy in copies:
        copy.wait()
    v = Vectors(vec, l)
    qkv_stage(x, v.row("gain1"), v.row("shift1"), buf, Strips(v.qkv), low.at[l], up.at[l], q, kv, red, red_out, normed)


def qkv_kernel(l, x, vec, w, low, up):
    tokens, dim = x.shape
    return kernel(
        functools.partial(qkv_body, l), "qkv",
        [(x, False), (vec, False), (w, True), (low, False), (up, False)],
        [((NARROW, tokens, 128), BF16, False), ((NARROW, tokens, 256), BF16, False), ((low.shape[1], tokens), BF16, False)],
        [pltpu.VMEM((tokens, low.shape[1]), BF16), pltpu.VMEM((tokens, dim), BF16), pltpu.VMEM((NARROW // 2, dim, 768), BF16), pltpu.SemaphoreType.DMA((NARROW,))],
    )


def attend_body(group, g_ref, q, *refs):
    held = positions(group)
    kvs, (out, lse) = refs[:group], refs[group:]
    bias = pair_bias(held, g_ref[0])
    each(NARROW, lambda i: attend_strip(held, bias, i, q, kvs, out, lse))


def attend_kernel(group, g, q, kvs):
    tokens = q.shape[1]
    return pl.pallas_call(
        functools.partial(attend_body, group),
        out_shape=[shape_of((tokens, NARROW * 128), BF16), shape_of((NARROW, 8, tokens), F32)],
        in_specs=[pl.BlockSpec(memory_space=pltpu.SMEM)] + [pl.BlockSpec(memory_space=pltpu.VMEM)] * (group + 1),
        out_specs=[pl.BlockSpec(memory_space=pltpu.VMEM)] * 2,
        compiler_params=PARAMS,
        name="attend",
    )(g, q, *kvs)


def mlp_body(l, x, att, vec, wp, wu, wd, *refs):
    low_proj, up_proj, low_up, up_up, low_down, up_down = [ref.at[l] for ref in refs[:6]]
    mid, result, hidden, reds, red, red_up, normed, active, bp, bu, bd, sem = refs[6:]
    copies = []
    for n, (src, dst) in enumerate(((wp.at[l], bp), (wu.at[l], bu), (wd.at[l], bd))):
        copies.append(pltpu.make_async_copy(src, dst, sem.at[n]))
        copies[-1].start()
    v = Vectors(vec, l)
    copies[0].wait()
    proj_stage(
        x, att, bp, v.row("proj"), low_proj, up_proj, v.row("gain2"), v.row("shift2"), low_up,
        mid, normed, red, reds.at[0], red_up, reds.at[1],
    )
    copies[1].wait()
    each(NARROW, lambda i: up_strip(i, normed, bu, Strips(v.up), red_up, up_up, hidden, active))
    copies[2].wait()

    def put(n, value):
        if len(result.shape) == 2:
            result[:, columns(n, 256)] = value
        else:
            for m in range(2):
                result[2 * n + m] = value[:, m * 128 : (m + 1) * 128].astype(BF16)

    down_stage(mid, active, bd, v.row("down"), low_down, up_down, red, reds.at[2], put)


def mlp_kernel(l, final, x, att, vec, wp, wu, wd, tables):
    tokens, dim = x.shape
    hidden = wd.shape[1]
    rank = tables[0].shape[1]
    result = ((NARROW, tokens, 128), BF16, False) if final else ((tokens, dim), F32, False)
    return kernel(
        functools.partial(mlp_body, l), "mlp",
        [(x, False), (att, False), (vec, False), (wp, True), (wu, True), (wd, True)] + [(t, False) for t in tables],
        [((tokens, dim), F32, False), result, ((tokens, hidden), BF16, False), ((3, rank, tokens), BF16, False)],
        [
            pltpu.VMEM((tokens, rank), BF16), pltpu.VMEM((tokens, rank), BF16),
            pltpu.VMEM((tokens, dim), BF16), pltpu.VMEM((tokens, hidden), BF16), pltpu.VMEM(wp.shape[1:], BF16),
            pltpu.VMEM(wu.shape[1:], BF16), pltpu.VMEM(wd.shape[1:], BF16), pltpu.SemaphoreType.DMA((3,)),
        ],
    )


def mlp_back_stage(vec, grad, hidden, g_hid, mid, att, low, total, wp, wu, wd, reds, t, grads, g_mid, waits):
    low[...] = grad[...].astype(BF16)
    g_red = dot(low[...], t["up_down"], TURNED).astype(BF16)
    rank = g_red.shape[1]
    waits("hidden")
    waits("down")
    waits("up")
    units = wu.shape[2]
    total[...] = jnp.zeros_like(total)

    def strip(i):
        cols = columns(i, units)
        active, slope = gelu_parts(hidden[:, cols].astype(F32))
        hidden[:, cols] = active.astype(BF16)
        g_active = dot(low[...], wd[cols, :], TURNED) + dot(g_red, t["low_down"][:, cols])
        g_hid[:, cols] = (g_active * slope).astype(BF16)
        total[...] += dot(g_hid[:, cols], wu[i], TURNED)

    each(NARROW, strip)

    def give(at, value):
        size = value.shape[1] // NARROW
        for i in range(NARROW):
            grads[i, :, at : at + size] = value[:, i * size : (i + 1) * size].astype(BF16)

    give(384 + 2 * units, dot(reds[3], low[...]))
    give(384 + units, dot(g_red, hidden[...], CROSS))
    give(384, dot(reds[2], g_hid[...]))
    g_hid[:, :rank] = dot(g_hid[...], t["up_up"][...], TURNED).astype(BF16)
    waits("mid")
    gain, shift = vec.row("gain2"), vec.row("shift2")
    dim = mid.shape[1]

    def norm(rows):
        scaled, inverse = norm_parts(mid[rows, :])
        hidden[rows, :dim] = (scaled * gain + shift).astype(BF16)
        g_normed = total[rows, :] + dot(g_hid[rows, :rank], t["low_up"])
        value = grad[rows, :] + norm_grad(g_normed, scaled, inverse, gain)
        g_mid[rows, :] = value
        low[rows, :] = value.astype(BF16)

    by_rows(mid.shape[0], norm)
    give(256, dot(g_hid[:, :rank], hidden[:, :dim], CROSS))
    give(128, dot(reds[1], low[...]))
    g_red_proj = dot(low[...], t["up_proj"], TURNED).astype(BF16)
    waits("att")
    waits("proj")
    give(0, dot(g_red_proj, att[...], CROSS))
    low[...] = (dot(low[...], wp[...], TURNED) + dot(g_red_proj, t["low_proj"])).astype(BF16)


def qkv_back_stage(vec, x, g_mid, gq, parts, total, g_red, normed, wq, red, low, up, grads, put, waits):
    total[...] = jnp.zeros_like(total)
    waits("gq")
    waits("qkv")

    def pair(j, small):
        pieces = []
        for i in (2 * j, 2 * j + 1):
            g_kv = sum(part[i].astype(F32) for part in parts).astype(BF16)
            g_mixed = jnp.concatenate([gq[i], g_kv], axis=1)
            grads[i, :, 128:512] = dot(red[...], g_mixed).astype(BF16)
            small = small + dot(g_mixed, up[i], TURNED)
            pieces.append(g_mixed)
        total[...] += dot(jnp.concatenate(pieces, axis=1), wq[j], TURNED)
        return small

    rank, tokens = red.shape
    small = lax.fori_loop(0, NARROW // 2, pair, jnp.zeros((tokens, rank), F32))
    g_low_rank = small.astype(BF16)
    g_red[...] = g_low_rank
    waits("x")
    waits("g_mid")
    gain, shift = vec.row("gain1"), vec.row("shift1")

    def norm(rows):
        scaled, inverse = norm_parts(x[rows, :].astype(F32))
        normed[rows, :] = (scaled * gain + shift).astype(BF16)
        g_normed = total[rows, :] + dot(g_red[rows, :], low[...])
        put(rows, g_mid[rows, :] + norm_grad(g_normed, scaled, inverse, gain))

    by_rows(tokens, norm)
    g_low = dot(g_low_rank, normed[...], CROSS).astype(BF16)
    for i in range(NARROW):
        grads[i, :, :128] = g_low[:, i * 128 : (i + 1) * 128]


def back_body(lq, lm, group, names, *refs):
    R = dict(zip(names, refs))
    held = positions(group)
    sem, started = R["sem"], {}

    def waits(name):
        for copy in started.pop(name, ()):
            copy.wait()

    count = [0]

    def begin(name, *copies):
        started[name] = []
        for src, dst in copies:
            copy = pltpu.make_async_copy(src, dst, sem.at[count[0]])
            count[0] += 1
            copy.start()
            started[name].append(copy)

    if lq is not None:
        begin("gq", (R["in_gq"], R["gq"]), *[(R["in_part%d" % j], R["part%d" % j]) for j in range(group)])
        begin("qkv", *[
            (R["w_qkv"].at[lq, i], R["wq"].at[i // 2, :, columns(i % 2, 384)]) for i in range(NARROW)
        ])
        begin("x", (R["in_x"], R["x"]))
        begin("g_mid", (R["in_g_mid"], R["total2"]))
    else:
        begin("cotangent", (R["cotangent"], R["low"]))
    if lm is not None:
        begin("hidden", (R["hiddens"].at[lm], R["hidden"]))
        begin("down", *[
            (R["w_down"].at[lm, pl.ds(n * 1024, 1024)], R["wd"].at[pl.ds(n * 1024, 1024)])
            for n in range(R["wd"].shape[0] // 1024)
        ])
        begin("up", *[(R["w_up"].at[lm, i], R["wu"].at[i]) for i in range(NARROW)])
        begin("proj", (R["w_proj"].at[lm], R["wp"]))
        begin("att", (R["atts"].at[lm], R["att"]))
        begin("kv", (R["kvs"].at[lm], R["kv"]), (R["peers"].at[lm], R["peer"]), (R["lses"].at[lm], R["lse"]))
    if lq is not None:
        vec = Vectors(R["vec"], lq)

        def put(rows, value):
            if lm is None:
                for i in range(NARROW):
                    R["out"][i, rows, :] = value[:, i * 128 : (i + 1) * 128].astype(BF16)
            else:
                R["grad"][rows, :] = value

        qkv_back_stage(
            vec, R["x"], R["total2"], R["gq"], [R["part%d" % j] for j in range(group)], R["total"],
            R["g_red"], R["low"], R["wq"],
            R["reds"].at[lq, 0], R["low_qkv"].at[lq], R["up_qkv"].at[lq], R["grads_qkv"], put, waits,
        )
    else:
        waits("cotangent")
        R["grad"][...] = R["low"][...].astype(F32)
    if lm is None:
        return
    begin("q", (R["qs"].at[lm], R["gq"]))
    begin("mid", (R["mids"].at[lm], R["x" if lq is not None and R["x"].dtype == F32 else "mid"]))
    mid = R["x" if lq is not None and R["x"].dtype == F32 else "mid"]
    t = {name: R[name].at[lm] for name in TABLES}
    vec = Vectors(R["vec"], lm)
    mlp_back_stage(
        vec, R["grad"], R["hidden"], R["g_hid"], mid, R["att"], R["low"], R["total"], R["wp"], R["wu"], R["wd"],
        R["reds"].at[lm], {k: (v if k in ("low_down", "up_up") else v[...]) for k, v in t.items() if "qkv" not in k},
        R["grads_mlp"], R["total2"], waits,
    )
    out_mid = pltpu.make_async_copy(R["total2"], R["out_g_mid"], sem.at[count[0]])
    out_mid.start()
    waits("q")
    waits("kv")
    bias = pair_bias(held, R["g"][0])
    kvs = [R["kv"]] + [R["peer"].at[j] for j in range(group - 1)]
    gkvs = [R["part%d" % j] for j in range(group)]
    each(NARROW, lambda i: attend_back_strip(
        held, bias, i, R["gq"], R["lse"], R["att"], R["low"], kvs, R["gq"], gkvs
    ))
    outs = [(R["gq"], R["out_gq"])] + [(R["part%d" % j], R["out_part%d" % j]) for j in range(group)]
    copies = [pltpu.make_async_copy(src, dst, sem.at[count[0] + 1 + n]) for n, (src, dst) in enumerate(outs)]
    for copy in copies:
        copy.start()
    for copy in copies:
        copy.wait()
    out_mid.wait()


def back_kernel(lq, lm, group, g, outs, tables, carried):
    layers, _, dim, _ = outs["qkv"].shape
    hidden = outs["down"].shape[1]
    tokens = outs["tokens"].shape[0]
    rank = tables[0].shape[1]
    strip = (NARROW, tokens)
    inputs = [("g", g, pl.BlockSpec(memory_space=pltpu.SMEM))]
    near, far = pl.BlockSpec(memory_space=pltpu.VMEM), pl.BlockSpec(memory_space=pltpu.HBM)
    inputs += [(name, table, near) for name, table in zip(TABLES, tables)]
    inputs += [("vec", outs["vec"], near), ("reds", outs["reds"], near)]
    outputs, scratch = [], []

    def vmem(name, shape, kind):
        scratch.append((name, pltpu.VMEM(shape, kind)))

    vmem("gq", strip + (128,), BF16)
    for j in range(group):
        vmem("part%d" % j, strip + (256,), BF16)
    vmem("total", (tokens, dim), F32)
    vmem("total2", (tokens, dim), F32)
    vmem("low", (tokens, dim), BF16)
    if lq is not None:
        g_mid, gq, parts = carried
        x = outs["tokens"] if lq == 0 else outs["saved_x"][lq - 1]
        inputs += [("in_gq", gq, far), ("in_g_mid", g_mid, far), ("in_x", x, far), ("w_qkv", outs["qkv"], far)]
        inputs += [("in_part%d" % j, part, far) for j, part in enumerate(parts)]
        vmem("wq", (NARROW // 2, dim, 768), BF16)
        vmem("g_red", (tokens, rank), BF16)
        vmem("x", (tokens, dim), x.dtype)
        outputs.append(("grads_qkv", (NARROW, rank, 512), BF16, near))
        if lm is None:
            outputs.append(("out", strip + (128,), BF16, near))
    if lm is not None:
        if lq is None:
            inputs.append(("cotangent", outs["cotangent"], far))
        for name in ("hidden", "mid", "att", "q", "kv", "peer", "lse"):
            inputs.append((name + "s", outs["saved_" + name], far))
        inputs += [("w_" + name, outs[name], far) for name in ("proj", "up", "down")]
        vmem("wp", (dim, dim), BF16)
        vmem("wu", (NARROW, dim, hidden // NARROW), BF16)
        vmem("wd", (hidden, dim), BF16)
        vmem("grad", (tokens, dim), F32)
        if lq is None or x.dtype != F32:
            vmem("mid", (tokens, dim), F32)
        vmem("att", (tokens, dim), BF16)
        vmem("hidden", (tokens, hidden), BF16)
        vmem("g_hid", (tokens, hidden), BF16)
        vmem("kv", strip + (256,), BF16)
        vmem("peer", (group - 1,) + strip + (256,), BF16)
        vmem("lse", (NARROW, 8, tokens), F32)
        outputs.append(("grads_mlp", (NARROW, rank, 512 + 2 * hidden // NARROW), BF16, near))
        outputs += [("out_g_mid", (tokens, dim), F32, far), ("out_gq", strip + (128,), BF16, far)]
        outputs += [("out_part%d" % j, strip + (256,), BF16, far) for j in range(group)]
    scratch.append(("sem", pltpu.SemaphoreType.DMA((64,))))
    names = [x[0] for x in inputs] + [x[0] for x in outputs] + [x[0] for x in scratch]
    made = pl.pallas_call(
        functools.partial(back_body, lq, lm, group, tuple(names)),
        out_shape=[shape_of(shape, kind) for _, shape, kind, _ in outputs],
        in_specs=[spec for _, _, spec in inputs],
        out_specs=[spec for _, _, _, spec in outputs],
        scratch_shapes=[shape for _, shape in scratch],
        compiler_params=PARAMS,
        name="back",
    )(*[array for _, array, _ in inputs])
    return dict(zip([x[0] for x in outputs], made))


def to_rows_body(held, x, out):
    n = 0
    for s in range(x.shape[0] // (len(held) * len(held[0]))):
        for g in range(len(held)):
            for place in held[g]:
                start = (s * BLOCKS + place) * BLOCK
                out[start : start + BLOCK, :] = x[n].astype(F32)
                n += 1


def to_rows(held, x):
    blocks, _, width = x.shape
    return pl.pallas_call(
        functools.partial(to_rows_body, held),
        out_shape=shape_of((blocks * BLOCK, width), F32),
        compiler_params=PARAMS,
        name="to_rows",
    )(x)


def pick_body(count, ids, *refs):
    for ref, out in zip(refs[:count], refs[count:]):
        out[...] = ref[...]


def pick_tables(ids, tables):
    def chosen(site, shape):
        return pl.BlockSpec((shape[0], None) + shape[2:], lambda i, ids: (0, ids[site], 0, 0))

    return pl.pallas_call(
        functools.partial(pick_body, len(tables)),
        grid_spec=pltpu.PrefetchScalarGridSpec(
            num_scalar_prefetch=1,
            grid=(1,),
            in_specs=[chosen(site, table.shape) for site, table in tables],
            out_specs=[
                pl.BlockSpec(table.shape[:1] + table.shape[2:], lambda i, ids: (0, 0, 0)) for _, table in tables
            ],
        ),
        out_shape=[shape_of(table.shape[:1] + table.shape[2:], BF16) for _, table in tables],
        compiler_params=PARAMS,
        name="pick",
    )(ids, *[table for _, table in tables])


def shards(mesh_shape, *args):
    (
        tokens, cotangent, adapter_ids, qkv_weight, qkv_bias, proj_weight, proj_bias,
        up_weight, up_bias, down_weight, down_bias, first_gain, first_shift, second_gain,
        second_shift, qkv_lower, qkv_raise, proj_lower, proj_raise, up_lower, up_raise,
        down_lower, down_raise,
    ) = args
    n_row, n_col = mesh_shape
    layers, adapters, dim, rank = qkv_lower.shape
    rows, width = tokens.shape
    units = up_weight.shape[2]
    seqs = rows // LEN
    group = n_col // seqs
    held = positions(group)
    per = BLOCKS // group
    mine = per * BLOCK
    merge = 128 // width
    c = lax.axis_index("col")
    g = lax.rem(c, group)
    ids = lax.dynamic_index_in_dim(adapter_ids, c // group, 0, keepdims=False)

    def line(pieces):
        row = jnp.concatenate([piece.reshape(layers, -1).astype(F32) for piece in pieces], axis=1)
        return jnp.pad(row, ((0, 0), (0, 512 - row.shape[1])))

    vector = jnp.stack(
        [
            line([qkv_bias]), line([up_bias]), line([proj_bias, down_bias, first_gain, first_shift]),
            line([second_gain, second_shift]),
        ],
        axis=1,
    ).reshape(layers * 4, 512)

    def turned(table):
        return jnp.swapaxes(table, 2, 3)

    tables = pick_tables(ids, [
        (0, turned(qkv_lower)), (1, turned(proj_lower)), (1, proj_raise), (2, turned(up_lower)), (2, up_raise),
        (3, turned(down_lower)), (3, down_raise),
    ])
    raise_qkv = lax.dynamic_index_in_dim(qkv_raise, ids[0], 1, keepdims=False)
    raise_qkv = raise_qkv.reshape(layers, rank, 3, NARROW, 128).transpose(0, 3, 1, 2, 4)
    tables = [tables[0], raise_qkv.reshape(layers, NARROW, rank, 384)] + list(tables[1:])
    fused = FUSED and width == 128
    outs = gather_inputs(
        n_row, n_col, group, qkv_weight.reshape(layers, -1, 3 * width), proj_weight, up_weight,
        down_weight, tokens, cotangent, vector, tables if fused else None
    )
    g_one = g.reshape(1)

    def peer_values(x, step):
        pairs = [(q, q - q % group + (q + step) % group) for q in range(n_col)]
        return lax.ppermute(x, "col", pairs)

    def to_columns(x):
        if merge > 1:
            x = x.reshape(NARROW, mine, merge, width).transpose(0, 2, 1, 3).reshape(n_col, mine, width)
        x = lax.all_to_all(x, "col", split_axis=0, concat_axis=0, tiled=True)
        return to_rows(held, x.reshape(n_col * per, BLOCK, width))

    if not fused:
        x = outs["tokens"].astype(F32)
        kept = {name: [] for name in SAVED + ("reds",)}
        for l in range(layers):
            q, kv, red = qkv_kernel(l, x, outs["vec"], outs["qkv"], tables[0], tables[1])
            kvs = [kv] + [peer_values(kv, s) for s in range(1, group)]
            att, lse = attend_kernel(group, g_one, q, kvs)
            mid, x, hidden, reds = mlp_kernel(
                l, l == layers - 1, x, att, outs["vec"], outs["proj"], outs["up"], outs["down"], tables[2:]
            )
            reds = jnp.concatenate([red[None], reds])
            peer = jnp.stack(kvs[1:]) if group > 1 else kv[None][:0]
            for name, value in zip(SAVED + ("reds",), (q, kv, peer, att, lse, mid, hidden, x, reds)):
                kept[name].append(value)
        for name in SAVED:
            outs["saved_" + name] = jnp.stack(kept[name][: layers - 1] if name == "x" else kept[name])
        outs["reds"] = jnp.stack(kept["reds"])
        outs["result"] = x
    result = to_columns(outs["result"])

    onehot = (adapter_ids.T[:, :, None] == jnp.arange(adapters)[None, None, :]).astype(BF16)

    def all_rows(x):
        pairs = [[(q, (q + s) % n_row) for q in range(n_row)] for s in range(1, n_row)]
        return [x] + [lax.ppermute(x, "row", pair) for pair in pairs]

    onehots = jnp.concatenate(all_rows(onehot), axis=1)

    def collect(parts, named):
        if merge > 1:
            pieces, at = [], 0
            for _, size in named:
                piece = parts[:, :, at : at + size]
                at += size
                if size == 384:
                    piece = piece.reshape(NARROW, rank, 3, merge, width).transpose(0, 3, 1, 2, 4)
                else:
                    piece = piece.reshape(NARROW, rank, merge, size // merge).transpose(0, 2, 1, 3)
                pieces.append(piece.reshape(n_col, rank, size // merge))
            parts = jnp.concatenate(pieces, axis=2)
        parts = lax.all_to_all(parts, "col", split_axis=0, concat_axis=0, tiled=True)
        parts = parts.reshape((seqs, group) + parts.shape[1:]).astype(F32).sum(axis=1).astype(BF16)
        parts = jnp.concatenate(all_rows(parts), axis=0)
        sums, at = [], 0
        for site, size in named:
            piece = parts[:, :, at : at + size // merge]
            at += size // merge
            sums.append(jnp.einsum("sa,srn->arn", onehots[site], piece, preferred_element_type=F32))
        return sums

    wide = outs["down"].shape[1] // NARROW
    grads, carried = [None] * layers, None
    for l in reversed(range(layers + 1)):
        lq, lm = (l if l < layers else None), (l - 1 if l > 0 else None)
        made = back_kernel(lq, lm, group, g_one, outs, tables, carried)
        if lm is not None:
            grads[lm] = collect(made["grads_mlp"], [(1, 128), (1, 128), (2, 128), (2, wide), (3, wide), (3, 128)])
            parts = [made["out_part%d" % s] for s in range(group)]
            parts = [parts[0]] + [peer_values(parts[s], group - s) for s in range(1, group)]
            carried = (made["out_g_mid"], made["out_gq"], parts)
        if lq is not None:
            grads[lq] = collect(made["grads_qkv"], [(0, 128), (0, 384)]) + grads[lq]
    grad = made["out"]
    input_grad = to_columns(grad)

    final = []
    for number in range(8):
        p = jnp.stack([grads[l][number] for l in range(layers)])
        if number == 1:
            p = p.reshape(layers, adapters, rank, 3, width)
        elif number % 2 == 0:
            p = p.transpose(0, 1, 3, 2)
        final.append(p)
    return (result, input_grad) + tuple(final)


def solution(mesh):
    mesh_shape = (mesh.shape["row"], mesh.shape["col"])
    return jax.shard_map(
        functools.partial(shards, mesh_shape),
        mesh=mesh,
        in_specs=(
            P("row", "col"), P("row", "col"), P("row", None),
            P(None, "row", None, "col"), P(None, None, "col"),
            P(None, "col", "row"), P(None, "col"),
            P(None, "row", "col"), P(None, "col"),
            P(None, "col", "row"), P(None, "col"),
            P(None, "col"), P(None, "col"), P(None, "col"), P(None, "col"),
            P(), P(), P(), P(), P(), P(), P(), P(),
        ),
        out_specs=(
            P("row", "col"), P("row", "col"),
            P(None, None, "col", None), P(None, None, None, None, "col"),
            P(None, None, "col", None), P(None, None, None, "col"),
            P(None, None, "col", None), P(None, None, None, "col"),
            P(None, None, "col", None), P(None, None, None, "col"),
        ),
        check_vma=False,
    )
```

```python
import functools

import jax
import jax.numpy as jnp
from jax import lax
from jax.experimental import pallas as pl
from jax.experimental.pallas import tpu as pltpu
from jax.sharding import PartitionSpec as P

HD = 64
LEN = 1024
BLOCK = 256
BLOCKS = LEN // BLOCK
EPSILON = 1e-05
SCALE = HD**-0.5
ROOT = (2.0 / 3.141592653589793) ** 0.5
MESH = pl.DeviceIdType.MESH
F32 = jnp.float32
BF16 = jnp.bfloat16


ROW_FIRST = (("z", 0, 1), ("z", 1, 0))
ROW_SECOND = ((0, "z", 1), (1, "z", 0))
ORDERS = {"qkv": (ROW_SECOND,), "proj": (ROW_SECOND,), "up": (ROW_FIRST,) * 2, "down": (ROW_FIRST,) * 2}
KINDS = ("qkv", "proj", "up", "down")
DEPTH = 4
FUSED = True
LINK = 90e3


def transfer_plan(order):
    masks, rows, steps = [0], False, []
    for d in order:
        steps.append((d, tuple(masks), rows))
        if d == "z":
            rows = True
        else:
            masks = masks + [m ^ d for m in masks]
    steps.append((None, tuple(masks), rows))
    return steps


def transfer_schedule(pieces, n_row, tasks):
    cost, parts = {}, {}
    for k, (name, order, size) in enumerate(pieces):
        parts.setdefault(name, set()).add(k)
        for p, (d, masks, rows) in enumerate(transfer_plan(order)[:-1]):
            load = (n_row // 2) * (n_row - n_row // 2) if d == "z" else (n_row if rows else 1)
            cost[k, p] = (d, 2 * len(masks) * load * size / LINK)
    ready = {d: [] for d, _ in cost.values()}
    free = dict.fromkeys(ready, 0.0)
    flight = {d: [] for d in ready}
    for k in range(len(pieces)):
        ready[cost[k, 0][0]].append((k, 0))
    tasks, left = list(tasks), {}
    for task in tasks:
        left[task[4]] = left.get(task[4], 0) + 1
    landed, staged, now, ops = {}, {}, 0.0, []

    def stage(name):
        kind, l = name
        if name in landed and name not in staged and landed[name] <= now and not left.get((kind, l - 1)):
            staged[name] = now + 3.0
            ops.append(("stage", kind, l))

    while tasks or any(ready.values()) or any(flight.values()):
        for d in ready:
            while ready[d] and len(flight[d]) < DEPTH:
                k, p = ready[d].pop(0)
                free[d] = max(now, free[d]) + cost[k, p][1]
                flight[d].append((free[d], k, p))
                ops.append(("start", k, p))
        if tasks:
            for name in list(landed):
                stage(name)
        events = [f for line in flight.values() for f in line]
        event = min(events) if events else None
        due = None
        if tasks:
            need = tasks[0][4]
            due = now if need is None else staged.get(need)
            if due is None and need in landed and not left.get((need[0], need[1] - 1)):
                due = landed[need]
        if due is not None and (event is None or max(due, now) < event[0]):
            now = max(due, now)
            need = tasks[0][4]
            if need is not None and need not in staged:
                continue
            name, l, part, micros, _ = tasks.pop(0)
            left[need] -= 1
            now += micros
            ops.append(("task", name, (l, part)))
            continue
        now, k, p = max(now, event[0]), event[1], event[2]
        d = cost[k, p][0]
        flight[d].remove(event)
        ops.append(("wait", k, p))
        if (k, p + 1) in cost:
            later = ready[cost[k, p + 1][0]]
            later.append((k, p + 1))
            later.sort()
        else:
            name = pieces[k][0]
            parts[name].discard(k)
            if not parts[name]:
                landed[name] = now + 4.0
    return ops


def place_of(group, g, b):
    if group == 2:
        return g + b * (BLOCKS - 1 - 2 * g)
    return g * (BLOCKS // group) + b


def positions(group):
    per = BLOCKS // group
    return tuple(tuple(place_of(group, g, b) for b in range(per)) for g in range(group))


NARROW = 8
CROSS = ((0,), (0,))
TURNED = ((1,), (1,))


def dot(a, b, dims=((1,), (0,))):
    return lax.dot_general(a, b, (dims, ((), ())), preferred_element_type=F32)


def columns(i, size=128):
    if isinstance(i, int):
        return pl.ds(i * size, size)
    return pl.ds(pl.multiple_of(i * size, size), size)


def norm_parts(x):
    center = x - jnp.mean(x, axis=1, keepdims=True)
    inverse = lax.rsqrt(jnp.mean(center * center, axis=1, keepdims=True) + EPSILON)
    return center * inverse, inverse


def norm_grad(grad, scaled, inverse, gain):
    w = grad * gain
    first = jnp.mean(w, axis=1, keepdims=True)
    second = jnp.mean(w * scaled, axis=1, keepdims=True)
    return inverse * (w - first - scaled * second)


def norm_low(x, gain, shift):
    return (norm_parts(x)[0] * gain + shift).astype(BF16)


def pair_state(held):
    group, per = len(held), len(held[0])
    state = {}
    for s in range(per):
        for j in range(group):
            for b in range(per):
                seen = {held[(g - j) % group][b] <= held[g][s] for g in range(group)}
                state[s, j, b] = 0 if len(seen) == 2 else (1 if True in seen else -1)
    return state


def pair_bias(held, g):
    group = len(held)
    bias = {}
    for (s, j, b), state in pair_state(held).items():
        if state == 0:
            keys = place_of(group, lax.rem(g - j + group, group), b)
            bias[s, j, b] = jnp.where(keys <= place_of(group, g, s), 0.0, -1e9).astype(F32)
    return bias


def head_mask(h):
    lane = lax.broadcasted_iota(jnp.int32, (1, 128), 1)
    return (lane // HD) == h


def attend_strip(held, bias, i, q, kvs, out, lse):
    group, per = len(held), len(held[0])
    state = pair_state(held)
    turned = {}
    for s in range(per):
        rows = pl.ds(s * BLOCK, BLOCK)
        queries = q[i, rows, :] * SCALE
        pieces = []
        for h in range(2):
            query = jnp.where(head_mask(h), queries, 0).astype(BF16)
            scores, values = [], []
            for j in range(group):
                for b in range(per):
                    if state[s, j, b] < 0:
                        continue
                    keys = kvs[j][i, b * BLOCK : (b + 1) * BLOCK, :128]
                    score = dot(keys, query, TURNED)
                    if state[s, j, b] == 0:
                        score = score + bias[s, j, b]
                    scores.append(score)
                    if (j, b) not in turned:
                        turned[j, b] = kvs[j][i, b * BLOCK : (b + 1) * BLOCK, 128:].T
                    values.append(turned[j, b][h * HD : (h + 1) * HD])
            top = functools.reduce(jnp.maximum, [jnp.max(x, axis=0, keepdims=True) for x in scores])
            total, made = 0.0, 0.0
            for score, value in zip(scores, values):
                e = jnp.exp(score - top)
                total = total + jnp.sum(e, axis=0, keepdims=True)
                made = made + dot(value, e.astype(BF16))
            pieces.append(made / total)
            lse[i, h : h + 1, rows] = top + jnp.log(total)
        out[rows, columns(i)] = jnp.concatenate(pieces, axis=0).T.astype(BF16)


def attend_back_strip(held, bias, i, q, lse, out, grad, kvs, gq, gkvs):
    group, per = len(held), len(held[0])
    state = pair_state(held)
    turned, gk, gv = {}, {}, {}
    for s in range(per):
        rows = pl.ds(s * BLOCK, BLOCK)
        queries = q[i, rows, :] * SCALE
        up = grad[rows, columns(i)]
        product = (up.astype(F32) * out[rows, columns(i)].astype(F32)).T
        pieces = []
        for h in range(2):
            query = jnp.where(head_mask(h), queries, 0).astype(BF16)
            given = jnp.where(head_mask(h), up, 0).astype(BF16)
            inner = jnp.sum(product[h * HD : (h + 1) * HD], axis=0, keepdims=True)
            level = lse[i, h : h + 1, rows]
            made = 0.0
            for j in range(group):
                for b in range(per):
                    if state[s, j, b] < 0:
                        continue
                    keys = kvs[j][i, b * BLOCK : (b + 1) * BLOCK, :128]
                    values = kvs[j][i, b * BLOCK : (b + 1) * BLOCK, 128:]
                    score = dot(keys, query, TURNED)
                    if state[s, j, b] == 0:
                        score = score + bias[s, j, b]
                    probs = jnp.exp(score - level)
                    g_probs = dot(values, given, TURNED)
                    g_scores = (probs * (g_probs - inner)).astype(BF16)
                    if (j, b) not in turned:
                        turned[j, b] = keys.T
                        gk[j, b], gv[j, b] = 0.0, 0.0
                    gv[j, b] = gv[j, b] + dot(probs.astype(BF16), given)
                    gk[j, b] = gk[j, b] + dot(g_scores, query)
                    made = made + dot(turned[j, b][h * HD : (h + 1) * HD], g_scores)
            pieces.append(made)
        gq[i, rows, :] = (jnp.concatenate(pieces, axis=0) * SCALE).T.astype(BF16)
    for j in range(group):
        for b in range(per):
            rows = pl.ds(b * BLOCK, BLOCK)
            gkvs[j][i, rows, :128] = gk[j, b].astype(BF16)
            gkvs[j][i, rows, 128:] = gv[j, b].astype(BF16)


def by_rows(count, body, size=128):
    each(count // size, lambda n: body(pl.ds(pl.multiple_of(n * size, size), size)))


def keep(value, red, red_out):
    red[...] = value.astype(BF16)
    red_out[...] = value.T.astype(BF16)


def each(count, body):
    def step(i, carry):
        body(i)
        return carry

    lax.fori_loop(0, count, step, 0)


def qkv_stage(x, gain, shift, w, bias, low, up, q, kv, red, red_out, normed):
    def norm(rows):
        normed[rows, :] = norm_low(x[rows, :], gain, shift)

    by_rows(x.shape[0], norm)
    keep(dot(normed[...], low[...], TURNED), red, red_out)

    def pair(j):
        made = dot(normed[...], w[j])
        for n in range(2):
            i = 2 * j + n
            mixed = made[:, n * 384 : (n + 1) * 384] + (bias[i] + dot(red[...], up[i]))
            q[i] = mixed[:, :128].astype(BF16)
            kv[i] = mixed[:, 128:].astype(BF16)

    each(NARROW // 2, pair)


def proj_stage(x, att, w, bias, low, up, gain, shift, low_up, mid, normed, red, red_out, red_up, red_up_out):
    keep(dot(att[...], low[...], TURNED), red, red_out)

    def part(rows):
        value = x[rows, :] + (dot(att[rows, :], w[...]) + bias + dot(red[rows, :], up[...]))
        mid[rows, :] = value
        normed[rows, :] = norm_low(value, gain, shift)

    by_rows(x.shape[0], part, 256)
    keep(dot(normed[...], low_up[...], TURNED), red_up, red_up_out)


def up_strip(i, normed, w, bias, red_up, up, hidden, active):
    units = w.shape[2]
    cols = columns(i, units)
    value = dot(normed[...], w[i]) + (bias[i] + dot(red_up[...], up[:, cols]))
    hidden[:, cols] = value.astype(BF16)
    inner = ROOT * (value + 0.044715 * (value * value * value))
    active[:, cols] = (0.5 * value * (1.0 + jnp.tanh(inner))).astype(BF16)


def down_stage(mid, active, w, bias, low, up, red, red_out, put):
    keep(dot(active[...], low[...], TURNED), red, red_out)

    for n in range(mid.shape[1] // 256):
        cols = slice(n * 256, (n + 1) * 256)
        put(n, mid[:, cols] + (dot(active[...], w[:, cols]) + bias[:, cols] + dot(red[...], up[:, cols])))


def gelu_parts(x):
    square = x * x
    t = jnp.tanh(ROOT * (x + 0.044715 * (x * square)))
    half = 0.5 * (1.0 + t)
    slope = half + 0.5 * x * (1.0 - t * t) * (ROOT * (1.0 + 3 * 0.044715 * square))
    return x * half, slope


class Vectors:
    def __init__(self, ref, l):
        self.ref, self.l = ref, l

    def qkv(self, i):
        return self.ref[i, pl.ds(4 * self.l, 1), :384]

    def up(self, i):
        return self.ref[i, pl.ds(4 * self.l + 1, 1), :]

    def row(self, name):
        at = ("proj", "down", "gain1", "shift1", "gain2", "shift2").index(name)
        row, lane = 4 * self.l + 2 + at // 4, at % 4 * 128
        return jnp.concatenate([self.ref[i, row : row + 1, lane : lane + 128] for i in range(NARROW)], axis=1)


class Strips:
    def __init__(self, read):
        self.read = read

    def __getitem__(self, i):
        return self.read(i)


TABLES = ("low_qkv", "up_qkv", "low_proj", "up_proj", "low_up", "up_up", "low_down", "up_down")
SAVED = ("q", "kv", "peer", "att", "lse", "mid", "hidden", "x")


def task_list(layers):
    tasks = [("load", 0, 0, 3.0, None)]
    for l in range(layers):
        tasks.append(("qkv", l, 0, 7.0, ("qkv", l)))
        tasks += [("attend", l, n, 5.0, None) for n in range(4)]
        tasks.append(("proj", l, 0, 4.0, ("proj", l)))
        tasks += [("up", l, n, 5.0, ("up", l)) for n in range(2)]
        tasks.append(("down", l, 0, 6.0, ("down", l)))
    return tasks


class ForwardWork:
    def __init__(self, n_col, group, refs):
        self.__dict__.update(refs)
        self.group = group
        self.held = positions(group)
        self.r, self.c = lax.axis_index("row"), lax.axis_index("col")
        self.g = lax.rem(self.c, group)
        self.bias = pair_bias(self.held, self.g)
        self.layers = self.low_qkv.shape[0]

    def stage_copies(self, kind, l):
        full = self.full[kind]
        if kind == "qkv":
            pieces = []
            for i in range(NARROW):
                src = full.at[l, i]
                pieces.append((src, self.wq.at[i // 2, :, :, :, pl.ds(i % 2 * 384, 384)]))
            return pieces, self.wq
        if kind == "up":
            return [(full.at[l, i], self.wu.at[i]) for i in range(NARROW)], self.wu
        target = self.wp if kind == "proj" else self.wd
        return [(full.at[l, i], target.at[i]) for i in range(NARROW)], target

    def stage(self, kind, l):
        for src, dst in self.stage_copies(kind, l)[0]:
            pltpu.make_async_copy(src, dst, self.stage_sem.at[KINDS.index(kind)]).start()

    def staged(self, kind, l):
        target = self.stage_copies(kind, l)[1]
        pltpu.make_async_copy(target, target, self.stage_sem.at[KINDS.index(kind)]).wait()

    def save_copy(self, name, l):
        src = {
            "q": self.q, "kv": self.kv, "peer": self.peer.at[l], "att": self.att, "lse": self.lse,
            "mid": self.mid, "hidden": self.hidden, "x": self.x,
        }[name]
        return pltpu.make_async_copy(src, self.saved[name].at[l], self.save_sem.at[l, SAVED.index(name)])

    def save(self, *names, l):
        for name in names:
            self.save_copy(name, l).start()

    def settled(self, *names, l):
        if l >= 0:
            for name in names:
                self.save_copy(name, l).wait()

    def exchange(self, l, s):
        to = self.c - self.g + lax.rem(self.g + s, self.group)
        return pltpu.make_async_remote_copy(
            src_ref=self.kv, dst_ref=self.peer.at[l, s - 1],
            send_sem=self.kv_send.at[l, s - 1], recv_sem=self.kv_recv.at[l, s - 1],
            device_id=(self.r, to), device_id_type=MESH,
        )

    def run(self, name, l, part):
        vec = Vectors(self.vec, l)
        if name == "load":
            self.arrive_tokens()
            self.x[...] = self.tokens_v[...].astype(F32)
        elif name == "qkv":
            self.staged("qkv", l)
            self.settled("q", "kv", l=l - 1)
            if l > 0:
                for s in range(1, self.group):
                    self.exchange(l - 1, s).wait_send()
            w = self.wq.reshape(NARROW // 2, -1, 768)
            qkv_stage(
                self.x, vec.row("gain1"), vec.row("shift1"), w, Strips(vec.qkv), self.low_qkv.at[l],
                self.up_qkv.at[l], self.q, self.kv, self.red, self.reds.at[l, 0], self.normed,
            )
            for s in range(1, self.group):
                self.exchange(l, s).start()
            self.save("q", "kv", l=l)
        elif name == "attend":
            if part == 0:
                for s in range(1, self.group):
                    self.exchange(l, s).wait_recv()
                self.save("peer", l=l)
                self.settled("att", "lse", l=l - 1)
            kvs = [self.kv] + [self.peer.at[l, s - 1] for s in range(1, self.group)]
            size = NARROW // 4
            each(size, lambda n: attend_strip(self.held, self.bias, part * size + n, self.q, kvs, self.att, self.lse))
            if part == 3:
                self.save("att", "lse", l=l)
        elif name == "proj":
            self.staged("proj", l)
            self.settled("mid", l=l - 1)
            dim = self.att.shape[1]
            proj_stage(
                self.x, self.att, self.wp.reshape(dim, dim), vec.row("proj"), self.low_proj.at[l],
                self.up_proj.at[l], vec.row("gain2"), vec.row("shift2"), self.low_up.at[l],
                self.mid, self.normed, self.red, self.reds.at[l, 1], self.red_up, self.reds.at[l, 2],
            )
            self.save("mid", l=l)
        elif name == "up":
            if part == 0:
                self.staged("up", l)
                self.settled("hidden", l=l - 1)
            w = self.wu.reshape(NARROW, self.x.shape[1], -1)
            size = NARROW // 2
            each(size, lambda n: up_strip(
                part * size + n, self.normed, w, Strips(vec.up), self.red_up, self.up_up.at[l],
                self.hidden, self.active,
            ))
            if part == 1:
                self.save("hidden", l=l)
        elif name == "down":
            self.staged("down", l)
            self.settled("x", l=l - 1)
            dim = self.x.shape[1]

            def put(n, value):
                if l < self.layers - 1:
                    self.x[:, columns(n, 256)] = value
                else:
                    for m in range(2):
                        self.result[2 * n + m] = value[:, m * 128 : (m + 1) * 128].astype(BF16)

            down_stage(
                self.mid, self.active, self.wd.reshape(-1, dim), vec.row("down"), self.low_down.at[l],
                self.up_down.at[l], self.red, self.reds.at[l, 3], put,
            )
            if l < self.layers - 1:
                self.save("x", l=l)

    def close(self):
        last = self.layers - 1
        self.settled(*[name for name in SAVED if name not in ("x", "peer")], l=last)
        for l in range(self.layers):
            self.settled("peer", l=l)
        for s in range(1, self.group):
            self.exchange(last, s).wait_send()
        if last > 0:
            pass


def gather_body(n_row, n_col, layers, group, names, *refs):
    refs = dict(zip(names, refs))
    shard = {kind: refs["shard_" + kind] for kind in KINDS}
    full = {kind: refs["full_" + kind] for kind in KINDS}
    tokens, cotangent, vector = refs["tokens"], refs["cotangent"], refs["vector"]
    own_tokens, own_cotangent, vectors = refs["own_tokens"], refs["own_cotangent"], refs["vectors"]
    local_sem, send_sem, recv_sem = refs["local_sem"], refs["send_sem"], refs["recv_sem"]
    near_sem, out_sem, in_sem = refs["near_sem"], refs["out_sem"], refs["in_sem"]
    r = lax.axis_index("row")
    c = lax.axis_index("col")
    link_bits = [b for b in (2**k for k in range(1, 8)) if b < n_col]
    depth = shard["up"].shape[1]

    def row_peer(s):
        return (lax.rem(r + s, n_row), c)

    def col_peer(bit):
        return (r, c ^ bit)

    peers = [row_peer(s) for s in range(1, n_row)]
    peers += [(r, lax.rem(c + d, n_col)) for d in range(1, n_col)]
    barrier = pltpu.get_barrier_semaphore()
    for peer in peers:
        pl.semaphore_signal(barrier, inc=1, device_id=peer, device_id_type=MESH)
    pl.semaphore_wait(barrier, len(peers))

    per, width = BLOCKS // group, tokens.shape[1]

    def own_place(ref, b, col):
        if len(ref.shape) == 2:
            start = pl.multiple_of(col * width, width)
            return ref.at[pl.ds(b * BLOCK, BLOCK), pl.ds(start, width)]
        return ref.at[col, pl.ds(b * BLOCK, BLOCK)]

    def from_place(ref, b, col):
        start = (col // group) * LEN + place_of(group, lax.rem(col, group), b) * BLOCK
        return ref.at[pl.ds(pl.multiple_of(start, BLOCK), BLOCK)]

    exchanged = ((tokens, own_tokens), (cotangent, own_cotangent))

    def near(n, b):
        src, dst = exchanged[n]
        return pltpu.make_async_copy(from_place(src, b, c), own_place(dst, b, c), near_sem.at[n * per + b])

    def near_vector():
        return pltpu.make_async_copy(vector, vectors.at[c], near_sem.at[2 * per])

    def far(src, dst, n, peer):
        return pltpu.make_async_remote_copy(
            src_ref=src, dst_ref=dst, send_sem=out_sem.at[n], recv_sem=in_sem.at[n],
            device_id=peer, device_id_type=MESH,
        )

    def start_exchange(n):
        src, dst = exchanged[n]
        for b in range(per):
            near(n, b).start()
        for d in range(1, n_col):
            to = lax.rem(c + d, n_col)
            for b in range(per):
                far(from_place(src, b, to), own_place(dst, b, c), n, (r, to)).start()

    def wait_exchange(n):
        _, dst = exchanged[n]
        for b in range(per):
            near(n, b).wait()
        if len(dst.shape) == 2:
            ref = dst.at[:, pl.ds(0, (n_col - 1) * width)]
        else:
            ref = dst.at[pl.ds(0, n_col - 1)]
        far(ref, ref, n, col_peer(1)).wait()

    def own(kind, l, h):
        ref = shard[kind]
        size = ref.shape[1] // (2 * len(ORDERS[kind]))
        return ref.at[l, pl.ds(h * size, size)]

    def block(kind, l, h, row, col):
        if kind in ("qkv", "up"):
            return full[kind].at[l, col, row, h]
        start = pl.multiple_of(row * depth, depth)
        return full[kind].at[l, col, h, :, pl.ds(start, depth)]

    def strip(kind, l, h, col):
        if kind in ("qkv", "up"):
            return full[kind].at[l, col, :, h]
        return full[kind].at[l, col, h]

    def amount(kind, l, h, strips, rows):
        if kind in ("qkv", "up"):
            return full[kind].at[l, pl.ds(0, strips), pl.ds(0, rows), h]
        return full[kind].at[l, pl.ds(0, strips), h, :, pl.ds(0, rows * depth)]

    chunks = []
    for l in range(layers):
        for kind in KINDS:
            for h in range(2 * len(ORDERS[kind])):
                order = []
                for d in ORDERS[kind][h // 2][h % 2]:
                    if d == "z":
                        order.append("z")
                    elif d < len(link_bits):
                        order.append(link_bits[d])
                order += link_bits[2:]
                chunks.append((kind, l, h, tuple(order)))
    phases = len(link_bits) + 1

    def remote(src, dst, k, p, peer):
        return pltpu.make_async_remote_copy(
            src_ref=src, dst_ref=dst, send_sem=send_sem.at[k, p], recv_sem=recv_sem.at[k, p],
            device_id=peer, device_id_type=MESH,
        )

    def local(k):
        kind, l, h, _ = chunks[k]
        return pltpu.make_async_copy(own(kind, l, h), block(kind, l, h, r, c), local_sem.at[k])

    def issue(k, p):
        kind, l, h, order = chunks[k]
        d, masks, whole = transfer_plan(order)[p]
        for m in masks:
            if d == "z":
                src = own(kind, l, h) if m == 0 else block(kind, l, h, r, c ^ m)
                for s in range(1, n_row):
                    remote(src, block(kind, l, h, r, c ^ m), k, p, row_peer(s)).start()
            elif whole:
                ref = strip(kind, l, h, c ^ m)
                remote(ref, ref, k, p, col_peer(d)).start()
            else:
                src = own(kind, l, h) if m == 0 else block(kind, l, h, r, c ^ m)
                remote(src, block(kind, l, h, r, c ^ m), k, p, col_peer(d)).start()

    def moved(k, p):
        kind, l, h, order = chunks[k]
        d, masks, whole = transfer_plan(order)[p]
        if d == "z":
            rows = n_row - 1
        else:
            rows = n_row if whole else 1
        ref = amount(kind, l, h, len(masks), rows)
        return remote(ref, ref, k, p, col_peer(1))

    def share(k, p):
        kind, l, h, order = chunks[k]
        steps = transfer_plan(order)
        (d, masks, _), (_, later, whole) = steps[p], steps[p + 1]
        if not whole:
            return
        fresh = masks if d == "z" else later[len(masks):]
        for m in fresh:
            ref = strip(kind, l, h, c ^ m)
            remote(ref, ref, k, phases, col_peer(1)).start()

    def shared(k):
        kind, l, h, _ = chunks[k]
        ref = amount(kind, l, h, n_col // 2, n_row)
        return remote(ref, ref, k, phases, col_peer(1))

    def finish(k, p):
        moved(k, p).wait_recv()
        if chunks[k][3][p] == "z":
            local(k).wait()
        share(k, p)

    count = len(chunks)
    near_vector().start()
    for d in range(1, n_col):
        far(vector, vectors.at[c], 2, (r, lax.rem(c + d, n_col))).start()
    start_exchange(0)
    for k in range(count):
        local(k).start()
    def vectors_arrive():
        near_vector().wait()
        rest = vectors.at[pl.ds(0, n_col - 1)]
        far(rest, rest, 2, col_peer(1)).wait()

    work = None
    if "x" in refs:
        refs.update(full=full, saved={name: refs["saved_" + name] for name in SAVED})

        def arrive_tokens():
            vectors_arrive()
            wait_exchange(0)
            load_sem = refs["load_sem"]
            loads = [(own_tokens, refs["tokens_v"]), (vectors, refs["vec"])]
            copies = [pltpu.make_async_copy(s, d, load_sem.at[n]) for n, (s, d) in enumerate(loads)]
            for copy in copies:
                copy.start()
            for copy in copies:
                copy.wait()

        refs.update(arrive_tokens=arrive_tokens)
        work = ForwardWork(n_col, group, refs)

    pieces = []
    for kind, l, h, order in chunks:
        size = 2 * shard[kind].shape[1] * shard[kind].shape[2] // (2 * len(ORDERS[kind]))
        pieces.append(((kind, l), order, size))
    for op, k, p in transfer_schedule(pieces, n_row, task_list(layers) if work else []):
        if op == "start":
            issue(k, p)
        elif op == "wait":
            finish(k, p)
        elif op == "stage":
            for n, (kind, l, _, _) in enumerate(chunks):
                if (kind, l) == (k, p):
                    shared(n).wait_recv()
            work.stage(k, p)
        else:
            work.run(k, *p)
    start_exchange(1)
    for k in range(count):
        for p in range(phases):
            moved(k, p).wait_send()
        shared(k).wait_send()
        if not work:
            shared(k).wait_recv()
    if work:
        work.close()
    else:
        vectors_arrive()
        wait_exchange(0)
    wait_exchange(1)


def gather_inputs(n_row, n_col, group, qkv, proj, up, down, tokens, cotangent, vector, tables=None):
    layers, depth = up.shape[0], up.shape[1]
    width, units = proj.shape[1], down.shape[1]
    dim, hidden = depth * n_row, units * n_col
    mine = LEN // group
    cuts = [2 * len(ORDERS[kind]) for kind in KINDS]
    own = (mine, dim) if width % 128 == 0 else (n_col, mine, width)
    hbm = pl.BlockSpec(memory_space=pltpu.HBM)
    vmem = pl.BlockSpec(memory_space=pltpu.VMEM)
    dma = pltpu.SemaphoreType.DMA
    count = layers * sum(cuts)
    phases = n_col.bit_length()
    inputs = [("shard_" + kind, array, hbm) for kind, array in zip(KINDS, (qkv, proj, up, down))]
    inputs += [("tokens", tokens, hbm), ("cotangent", cotangent, hbm), ("vector", vector, hbm)]
    outputs = [
        ("full_qkv", (layers, n_col, n_row, cuts[0], depth // cuts[0], qkv.shape[2]), BF16, hbm),
        ("full_proj", (layers, n_col, cuts[1], width // cuts[1], dim), BF16, hbm),
        ("full_up", (layers, n_col, n_row, cuts[2], depth // cuts[2], units), BF16, hbm),
        ("full_down", (layers, n_col, cuts[3], units // cuts[3], dim), BF16, hbm),
        ("own_tokens", own, BF16, hbm),
        ("own_cotangent", own, BF16, hbm),
        ("vectors", (n_col,) + vector.shape, F32, hbm),
    ]
    scratch = [
        ("local_sem", dma((count,))),
        ("send_sem", dma((count, phases))),
        ("recv_sem", dma((count, phases))),
        ("near_sem", dma((2 * (BLOCKS // group) + 1,))),
        ("out_sem", dma((3,))),
        ("in_sem", dma((3,))),
    ]
    if tables is not None:
        rank = tables[0].shape[1]
        inputs += [(name, table, vmem) for name, table in zip(TABLES, tables)]
        strip = (NARROW, mine)
        kept = {
            "q": (strip + (128,), BF16), "kv": (strip + (256,), BF16), "att": ((mine, dim), BF16),
            "lse": ((NARROW, 8, mine), F32), "mid": ((mine, dim), F32), "hidden": ((mine, hidden), BF16),
            "x": ((mine, dim), F32), "peer": ((group - 1,) + strip + (256,), BF16),
        }
        outputs += [("saved_" + name, (layers,) + kept[name][0], kept[name][1], hbm) for name in SAVED]
        outputs += [
            ("reds", (layers, 4, rank, mine), BF16, vmem),
            ("result", (NARROW, mine, 128), BF16, vmem),
        ]
        scratch += [
            (name, pltpu.VMEM(((layers,) if name == "peer" else ()) + kept[name][0], kept[name][1]))
            for name in SAVED
        ]
        scratch += [
            ("wq", pltpu.VMEM((NARROW // 2, n_row, cuts[0], depth // cuts[0], 768), BF16)),
            ("wp", pltpu.VMEM((NARROW, cuts[1], width // cuts[1], dim), BF16)),
            ("wu", pltpu.VMEM((NARROW, n_row, cuts[2], depth // cuts[2], units), BF16)),
            ("wd", pltpu.VMEM((NARROW, cuts[3], units // cuts[3], dim), BF16)),
            ("tokens_v", pltpu.VMEM((mine, dim), BF16)),
            ("normed", pltpu.VMEM((mine, dim), BF16)),
            ("active", pltpu.VMEM((mine, hidden), BF16)),
            ("red", pltpu.VMEM((mine, rank), BF16)),
            ("red_up", pltpu.VMEM((mine, rank), BF16)),
            ("vec", pltpu.VMEM((n_col,) + vector.shape, F32)),
            ("stage_sem", dma((4,))),
            ("save_sem", dma((layers, len(SAVED)))),
            ("kv_send", dma((layers, group - 1))),
            ("kv_recv", dma((layers, group - 1))),
            ("load_sem", dma((2,))),
        ]
    names = [x[0] for x in inputs] + [x[0] for x in outputs] + [x[0] for x in scratch]
    outs = pl.pallas_call(
        functools.partial(gather_body, n_row, n_col, layers, group, tuple(names)),
        out_shape=[jax.ShapeDtypeStruct(shape, kind) for _, shape, kind, _ in outputs],
        in_specs=[spec for _, _, spec in inputs],
        out_specs=[spec for _, _, _, spec in outputs],
        scratch_shapes=[shape for _, shape in scratch],
        compiler_params=pltpu.CompilerParams(
            collective_id=0, has_side_effects=True, vmem_limit_bytes=60 * 2**20
        ),
        name="gather_inputs",
    )(*[array for _, array, _ in inputs])
    outs = dict(zip([x[0] for x in outputs], outs))

    merge = 128 // width
    strips = n_col // merge
    qkv_full = outs["full_qkv"].reshape(layers, n_col, dim, qkv.shape[2])
    up_full = outs["full_up"].reshape(layers, n_col, dim, units)
    rows, vec = [outs["own_tokens"], outs["own_cotangent"]], outs["vectors"]
    if merge > 1:
        qkv_full = qkv_full.reshape(layers, strips, merge, dim, 3, width).transpose(0, 1, 3, 4, 2, 5)
        up_full = up_full.reshape(layers, strips, merge, dim, units).transpose(0, 1, 3, 2, 4)
        rows = [x.transpose(1, 0, 2).reshape(mine, dim) for x in rows]
        vec = vec.reshape(strips, merge, layers, 4, 4 * 128)
        first = vec[:, :, :, 0, : 3 * width].reshape(strips, merge, layers, 3, width).transpose(0, 2, 3, 1, 4)
        first = jnp.pad(first.reshape(strips, layers, 384), ((0, 0), (0, 0), (0, 128)))
        second = vec[:, :, :, 1, :units].transpose(0, 2, 1, 3).reshape(strips, layers, 512)
        rest = vec[:, :, :, 2:, : 4 * width].reshape(strips, merge, layers, 2, 4, width)
        rest = rest.transpose(0, 2, 3, 4, 1, 5).reshape(strips, layers, 2, 512)
        vec = jnp.concatenate([first[:, :, None], second[:, :, None], rest], axis=2)
        vec = vec.reshape(strips, layers * 4, 512)
    outs.update(
        qkv=qkv_full.reshape(layers, strips, dim, 384),
        proj=outs["full_proj"].reshape(layers, dim, dim),
        up=up_full.reshape(layers, strips, dim, units * merge),
        down=outs["full_down"].reshape(layers, hidden, dim),
        tokens=rows[0], cotangent=rows[1], vec=vec,
    )
    return outs


PARAMS = pltpu.CompilerParams(vmem_limit_bytes=60 * 2**20)


def shape_of(shape, kind):
    return jax.ShapeDtypeStruct(shape, kind)


def kernel(body, name, inputs, outputs, scratch=()):
    spaces = (pl.BlockSpec(memory_space=pltpu.VMEM), pl.BlockSpec(memory_space=pltpu.HBM))
    return pl.pallas_call(
        body,
        out_shape=[shape_of(shape, kind) for shape, kind, _ in outputs],
        in_specs=[spaces[far] for _, far in inputs],
        out_specs=[spaces[far] for _, _, far in outputs],
        scratch_shapes=list(scratch),
        compiler_params=PARAMS,
        name=name,
    )(*[array for array, _ in inputs])


def own_group(group):
    return lax.rem(lax.axis_index("col"), group)


def qkv_body(l, x, vec, w, low, up, q, kv, red_out, red, normed, buf, sem):
    copies = []
    for i in range(NARROW):
        copies.append(pltpu.make_async_copy(w.at[l, i], buf.at[i // 2, :, columns(i % 2, 384)], sem.at[i]))
        copies[-1].start()
    for copy in copies:
        copy.wait()
    v = Vectors(vec, l)
    qkv_stage(x, v.row("gain1"), v.row("shift1"), buf, Strips(v.qkv), low.at[l], up.at[l], q, kv, red, red_out, normed)


def qkv_kernel(l, x, vec, w, low, up):
    tokens, dim = x.shape
    return kernel(
        functools.partial(qkv_body, l), "qkv",
        [(x, False), (vec, False), (w, True), (low, False), (up, False)],
        [((NARROW, tokens, 128), BF16, False), ((NARROW, tokens, 256), BF16, False), ((low.shape[1], tokens), BF16, False)],
        [pltpu.VMEM((tokens, low.shape[1]), BF16), pltpu.VMEM((tokens, dim), BF16), pltpu.VMEM((NARROW // 2, dim, 768), BF16), pltpu.SemaphoreType.DMA((NARROW,))],
    )


def attend_body(group, g_ref, q, *refs):
    held = positions(group)
    kvs, (out, lse) = refs[:group], refs[group:]
    bias = pair_bias(held, g_ref[0])
    each(NARROW, lambda i: attend_strip(held, bias, i, q, kvs, out, lse))


def attend_kernel(group, g, q, kvs):
    tokens = q.shape[1]
    return pl.pallas_call(
        functools.partial(attend_body, group),
        out_shape=[shape_of((tokens, NARROW * 128), BF16), shape_of((NARROW, 8, tokens), F32)],
        in_specs=[pl.BlockSpec(memory_space=pltpu.SMEM)] + [pl.BlockSpec(memory_space=pltpu.VMEM)] * (group + 1),
        out_specs=[pl.BlockSpec(memory_space=pltpu.VMEM)] * 2,
        compiler_params=PARAMS,
        name="attend",
    )(g, q, *kvs)


def mlp_body(l, x, att, vec, wp, wu, wd, *refs):
    low_proj, up_proj, low_up, up_up, low_down, up_down = [ref.at[l] for ref in refs[:6]]
    mid, result, hidden, reds, red, red_up, normed, active, bp, bu, bd, sem = refs[6:]
    copies = []
    for n, (src, dst) in enumerate(((wp.at[l], bp), (wu.at[l], bu), (wd.at[l], bd))):
        copies.append(pltpu.make_async_copy(src, dst, sem.at[n]))
        copies[-1].start()
    v = Vectors(vec, l)
    copies[0].wait()
    proj_stage(
        x, att, bp, v.row("proj"), low_proj, up_proj, v.row("gain2"), v.row("shift2"), low_up,
        mid, normed, red, reds.at[0], red_up, reds.at[1],
    )
    copies[1].wait()
    each(NARROW, lambda i: up_strip(i, normed, bu, Strips(v.up), red_up, up_up, hidden, active))
    copies[2].wait()

    def put(n, value):
        if len(result.shape) == 2:
            result[:, columns(n, 256)] = value
        else:
            for m in range(2):
                result[2 * n + m] = value[:, m * 128 : (m + 1) * 128].astype(BF16)

    down_stage(mid, active, bd, v.row("down"), low_down, up_down, red, reds.at[2], put)


def mlp_kernel(l, final, x, att, vec, wp, wu, wd, tables):
    tokens, dim = x.shape
    hidden = wd.shape[1]
    rank = tables[0].shape[1]
    result = ((NARROW, tokens, 128), BF16, False) if final else ((tokens, dim), F32, False)
    return kernel(
        functools.partial(mlp_body, l), "mlp",
        [(x, False), (att, False), (vec, False), (wp, True), (wu, True), (wd, True)] + [(t, False) for t in tables],
        [((tokens, dim), F32, False), result, ((tokens, hidden), BF16, False), ((3, rank, tokens), BF16, False)],
        [
            pltpu.VMEM((tokens, rank), BF16), pltpu.VMEM((tokens, rank), BF16),
            pltpu.VMEM((tokens, dim), BF16), pltpu.VMEM((tokens, hidden), BF16), pltpu.VMEM(wp.shape[1:], BF16),
            pltpu.VMEM(wu.shape[1:], BF16), pltpu.VMEM(wd.shape[1:], BF16), pltpu.SemaphoreType.DMA((3,)),
        ],
    )


def mlp_back_stage(vec, grad, hidden, g_hid, mid, att, low, total, wp, wu, wd, reds, t, grads, g_mid, waits):
    low[...] = grad[...].astype(BF16)
    g_red = dot(low[...], t["up_down"], TURNED).astype(BF16)
    rank = g_red.shape[1]
    waits("hidden")
    waits("down")
    waits("up")
    units = wu.shape[2]
    total[...] = jnp.zeros_like(total)

    def strip(i):
        cols = columns(i, units)
        active, slope = gelu_parts(hidden[:, cols].astype(F32))
        hidden[:, cols] = active.astype(BF16)
        g_active = dot(low[...], wd[cols, :], TURNED) + dot(g_red, t["low_down"][:, cols])
        g_hid[:, cols] = (g_active * slope).astype(BF16)
        total[...] += dot(g_hid[:, cols], wu[i], TURNED)

    each(NARROW, strip)

    def give(at, value):
        size = value.shape[1] // NARROW
        for i in range(NARROW):
            grads[i, :, at : at + size] = value[:, i * size : (i + 1) * size].astype(BF16)

    give(384 + 2 * units, dot(reds[3], low[...]))
    give(384 + units, dot(g_red, hidden[...], CROSS))
    give(384, dot(reds[2], g_hid[...]))
    g_hid[:, :rank] = dot(g_hid[...], t["up_up"][...], TURNED).astype(BF16)
    waits("mid")
    gain, shift = vec.row("gain2"), vec.row("shift2")
    dim = mid.shape[1]

    def norm(rows):
        scaled, inverse = norm_parts(mid[rows, :])
        hidden[rows, :dim] = (scaled * gain + shift).astype(BF16)
        g_normed = total[rows, :] + dot(g_hid[rows, :rank], t["low_up"])
        value = grad[rows, :] + norm_grad(g_normed, scaled, inverse, gain)
        g_mid[rows, :] = value
        low[rows, :] = value.astype(BF16)

    by_rows(mid.shape[0], norm)
    give(256, dot(g_hid[:, :rank], hidden[:, :dim], CROSS))
    give(128, dot(reds[1], low[...]))
    g_red_proj = dot(low[...], t["up_proj"], TURNED).astype(BF16)
    waits("att")
    waits("proj")
    give(0, dot(g_red_proj, att[...], CROSS))
    low[...] = (dot(low[...], wp[...], TURNED) + dot(g_red_proj, t["low_proj"])).astype(BF16)


def qkv_back_stage(vec, x, g_mid, gq, parts, total, g_red, normed, wq, red, low, up, grads, put, waits):
    total[...] = jnp.zeros_like(total)
    waits("gq")
    waits("qkv")

    def pair(j, small):
        pieces = []
        for i in (2 * j, 2 * j + 1):
            g_kv = sum(part[i].astype(F32) for part in parts).astype(BF16)
            g_mixed = jnp.concatenate([gq[i], g_kv], axis=1)
            grads[i, :, 128:512] = dot(red[...], g_mixed).astype(BF16)
            small = small + dot(g_mixed, up[i], TURNED)
            pieces.append(g_mixed)
        total[...] += dot(jnp.concatenate(pieces, axis=1), wq[j], TURNED)
        return small

    rank, tokens = red.shape
    small = lax.fori_loop(0, NARROW // 2, pair, jnp.zeros((tokens, rank), F32))
    g_low_rank = small.astype(BF16)
    g_red[...] = g_low_rank
    waits("x")
    waits("g_mid")
    gain, shift = vec.row("gain1"), vec.row("shift1")

    def norm(rows):
        scaled, inverse = norm_parts(x[rows, :].astype(F32))
        normed[rows, :] = (scaled * gain + shift).astype(BF16)
        g_normed = total[rows, :] + dot(g_red[rows, :], low[...])
        put(rows, g_mid[rows, :] + norm_grad(g_normed, scaled, inverse, gain))

    by_rows(tokens, norm)
    g_low = dot(g_low_rank, normed[...], CROSS).astype(BF16)
    for i in range(NARROW):
        grads[i, :, :128] = g_low[:, i * 128 : (i + 1) * 128]


def back_body(lq, lm, group, names, *refs):
    R = dict(zip(names, refs))
    held = positions(group)
    sem, started = R["sem"], {}

    def waits(name):
        for copy in started.pop(name, ()):
            copy.wait()

    count = [0]

    def begin(name, *copies):
        started[name] = []
        for src, dst in copies:
            copy = pltpu.make_async_copy(src, dst, sem.at[count[0]])
            count[0] += 1
            copy.start()
            started[name].append(copy)

    if lq is not None:
        begin("gq", (R["in_gq"], R["gq"]), *[(R["in_part%d" % j], R["part%d" % j]) for j in range(group)])
        begin("qkv", *[
            (R["w_qkv"].at[lq, i], R["wq"].at[i // 2, :, columns(i % 2, 384)]) for i in range(NARROW)
        ])
        begin("x", (R["in_x"], R["x"]))
        begin("g_mid", (R["in_g_mid"], R["total2"]))
    else:
        begin("cotangent", (R["cotangent"], R["low"]))
    if lm is not None:
        begin("hidden", (R["hiddens"].at[lm], R["hidden"]))
        begin("down", *[
            (R["w_down"].at[lm, pl.ds(n * 1024, 1024)], R["wd"].at[pl.ds(n * 1024, 1024)])
            for n in range(R["wd"].shape[0] // 1024)
        ])
        begin("up", *[(R["w_up"].at[lm, i], R["wu"].at[i]) for i in range(NARROW)])
        begin("proj", (R["w_proj"].at[lm], R["wp"]))
        begin("att", (R["atts"].at[lm], R["att"]))
        begin("kv", (R["kvs"].at[lm], R["kv"]), (R["peers"].at[lm], R["peer"]), (R["lses"].at[lm], R["lse"]))
    if lq is not None:
        vec = Vectors(R["vec"], lq)

        def put(rows, value):
            if lm is None:
                for i in range(NARROW):
                    R["out"][i, rows, :] = value[:, i * 128 : (i + 1) * 128].astype(BF16)
            else:
                R["grad"][rows, :] = value

        qkv_back_stage(
            vec, R["x"], R["total2"], R["gq"], [R["part%d" % j] for j in range(group)], R["total"],
            R["g_red"], R["low"], R["wq"],
            R["reds"].at[lq, 0], R["low_qkv"].at[lq], R["up_qkv"].at[lq], R["grads_qkv"], put, waits,
        )
    else:
        waits("cotangent")
        R["grad"][...] = R["low"][...].astype(F32)
    if lm is None:
        return
    begin("q", (R["qs"].at[lm], R["gq"]))
    begin("mid", (R["mids"].at[lm], R["x" if lq is not None and R["x"].dtype == F32 else "mid"]))
    mid = R["x" if lq is not None and R["x"].dtype == F32 else "mid"]
    t = {name: R[name].at[lm] for name in TABLES}
    vec = Vectors(R["vec"], lm)
    mlp_back_stage(
        vec, R["grad"], R["hidden"], R["g_hid"], mid, R["att"], R["low"], R["total"], R["wp"], R["wu"], R["wd"],
        R["reds"].at[lm], {k: (v if k in ("low_down", "up_up") else v[...]) for k, v in t.items() if "qkv" not in k},
        R["grads_mlp"], R["total2"], waits,
    )
    out_mid = pltpu.make_async_copy(R["total2"], R["out_g_mid"], sem.at[count[0]])
    out_mid.start()
    waits("q")
    waits("kv")
    bias = pair_bias(held, R["g"][0])
    kvs = [R["kv"]] + [R["peer"].at[j] for j in range(group - 1)]
    gkvs = [R["part%d" % j] for j in range(group)]
    each(NARROW, lambda i: attend_back_strip(
        held, bias, i, R["gq"], R["lse"], R["att"], R["low"], kvs, R["gq"], gkvs
    ))
    outs = [(R["gq"], R["out_gq"])] + [(R["part%d" % j], R["out_part%d" % j]) for j in range(group)]
    copies = [pltpu.make_async_copy(src, dst, sem.at[count[0] + 1 + n]) for n, (src, dst) in enumerate(outs)]
    for copy in copies:
        copy.start()
    for copy in copies:
        copy.wait()
    out_mid.wait()


def back_kernel(lq, lm, group, g, outs, tables, carried):
    layers, _, dim, _ = outs["qkv"].shape
    hidden = outs["down"].shape[1]
    tokens = outs["tokens"].shape[0]
    rank = tables[0].shape[1]
    strip = (NARROW, tokens)
    inputs = [("g", g, pl.BlockSpec(memory_space=pltpu.SMEM))]
    near, far = pl.BlockSpec(memory_space=pltpu.VMEM), pl.BlockSpec(memory_space=pltpu.HBM)
    inputs += [(name, table, near) for name, table in zip(TABLES, tables)]
    inputs += [("vec", outs["vec"], near), ("reds", outs["reds"], near)]
    outputs, scratch = [], []

    def vmem(name, shape, kind):
        scratch.append((name, pltpu.VMEM(shape, kind)))

    vmem("gq", strip + (128,), BF16)
    for j in range(group):
        vmem("part%d" % j, strip + (256,), BF16)
    vmem("total", (tokens, dim), F32)
    vmem("total2", (tokens, dim), F32)
    vmem("low", (tokens, dim), BF16)
    if lq is not None:
        g_mid, gq, parts = carried
        x = outs["tokens"] if lq == 0 else outs["saved_x"][lq - 1]
        inputs += [("in_gq", gq, far), ("in_g_mid", g_mid, far), ("in_x", x, far), ("w_qkv", outs["qkv"], far)]
        inputs += [("in_part%d" % j, part, far) for j, part in enumerate(parts)]
        vmem("wq", (NARROW // 2, dim, 768), BF16)
        vmem("g_red", (tokens, rank), BF16)
        vmem("x", (tokens, dim), x.dtype)
        outputs.append(("grads_qkv", (NARROW, rank, 512), BF16, near))
        if lm is None:
            outputs.append(("out", strip + (128,), BF16, near))
    if lm is not None:
        if lq is None:
            inputs.append(("cotangent", outs["cotangent"], far))
        for name in ("hidden", "mid", "att", "q", "kv", "peer", "lse"):
            inputs.append((name + "s", outs["saved_" + name], far))
        inputs += [("w_" + name, outs[name], far) for name in ("proj", "up", "down")]
        vmem("wp", (dim, dim), BF16)
        vmem("wu", (NARROW, dim, hidden // NARROW), BF16)
        vmem("wd", (hidden, dim), BF16)
        vmem("grad", (tokens, dim), F32)
        if lq is None or x.dtype != F32:
            vmem("mid", (tokens, dim), F32)
        vmem("att", (tokens, dim), BF16)
        vmem("hidden", (tokens, hidden), BF16)
        vmem("g_hid", (tokens, hidden), BF16)
        vmem("kv", strip + (256,), BF16)
        vmem("peer", (group - 1,) + strip + (256,), BF16)
        vmem("lse", (NARROW, 8, tokens), F32)
        outputs.append(("grads_mlp", (NARROW, rank, 512 + 2 * hidden // NARROW), BF16, near))
        outputs += [("out_g_mid", (tokens, dim), F32, far), ("out_gq", strip + (128,), BF16, far)]
        outputs += [("out_part%d" % j, strip + (256,), BF16, far) for j in range(group)]
    scratch.append(("sem", pltpu.SemaphoreType.DMA((64,))))
    names = [x[0] for x in inputs] + [x[0] for x in outputs] + [x[0] for x in scratch]
    made = pl.pallas_call(
        functools.partial(back_body, lq, lm, group, tuple(names)),
        out_shape=[shape_of(shape, kind) for _, shape, kind, _ in outputs],
        in_specs=[spec for _, _, spec in inputs],
        out_specs=[spec for _, _, _, spec in outputs],
        scratch_shapes=[shape for _, shape in scratch],
        compiler_params=PARAMS,
        name="back",
    )(*[array for _, array, _ in inputs])
    return dict(zip([x[0] for x in outputs], made))


SITES = {"mlp": (1, 1, 2, 2, 3, 3), "qkv": (0, 0)}


def backward_body(layers, group, n_row, n_col, names, *refs):
    R = dict(zip(names, refs))
    held = positions(group)
    per = BLOCKS // group
    r, c = lax.axis_index("row"), lax.axis_index("col")
    g = lax.rem(c, group)
    seqs = n_col // group
    tokens = per * BLOCK
    bias = pair_bias(held, g)

    def row_peer(s):
        return (lax.rem(r + s, n_row), c)

    def col_peer(d):
        return lax.rem(c + d, n_col)

    peers = [row_peer(s) for s in range(1, n_row)] + [(r, col_peer(d)) for d in range(1, n_col)]
    barrier = pltpu.get_barrier_semaphore()
    for peer in peers:
        pl.semaphore_signal(barrier, inc=1, device_id=peer, device_id_type=MESH)
    pl.semaphore_wait(barrier, len(peers))

    sem, started, count = R["sem"], {}, [0]

    def begin(name, *copies):
        started[name] = []
        for src, dst in copies:
            copy = pltpu.make_async_copy(src, dst, sem.at[count[0]])
            count[0] += 1
            copy.start()
            started[name].append(copy)

    def waits(name):
        for copy in started.pop(name, ()):
            copy.wait()

    far = [0]

    def remote(src, dst, n, peer):
        return pltpu.make_async_remote_copy(
            src_ref=src, dst_ref=dst, send_sem=R["out_sem"].at[n], recv_sem=R["in_sem"].at[n],
            device_id=peer, device_id_type=MESH,
        )

    def new_far():
        far[0] += 1
        return far[0] - 1

    def columns_start(n, src):
        to, at = R["columns"].at[n], new_far()
        start = (c // group) * LEN
        places = [pl.ds(pl.multiple_of(start + place_of(group, g, b) * BLOCK, BLOCK), BLOCK) for b in range(per)]
        begin("columns%d" % n, *[(src.at[c, pl.ds(b * BLOCK, BLOCK)], to.at[places[b]]) for b in range(per)])
        for d in range(1, n_col):
            for b in range(per):
                remote(src.at[col_peer(d), pl.ds(b * BLOCK, BLOCK)], to.at[places[b]], at, (r, col_peer(d))).start()
        return at

    def columns_end(n, at):
        waits("columns%d" % n)
        ref = R["columns"].at[n, pl.ds(0, (n_col - 1) * tokens)]
        remote(ref, ref, at, (r, col_peer(1))).wait()

    ends = {}

    def spread(kind, l):
        src, land, at = R["grads_" + kind], R["land_" + kind].at[l], new_far()
        begin("own_%s%d" % (kind, l), (src.at[c], land.at[c]))
        for d in range(1, n_col):
            remote(src.at[col_peer(d)], land.at[c], at, (r, col_peer(d))).start()
        ends["spread", kind, l] = at

    def spread_sent(kind, l):
        if l < layers:
            ref = R["land_" + kind].at[l, pl.ds(0, n_col - 1)]
            remote(ref, ref, ends["spread", kind, l], (r, col_peer(1))).wait_send()

    def add(kind, l):
        land, stage, total = R["land_" + kind].at[l], R["stage_" + kind], R["sum_" + kind]
        ref = land.at[pl.ds(0, n_col - 1)]
        remote(ref, ref, ends["spread", kind, l], (r, col_peer(1))).wait_recv()
        waits("own_%s%d" % (kind, l))
        begin("stage", (land, stage))
        add_sent(kind, l + 1)
        waits("stage")
        for q in range(seqs):
            value = sum(stage[q * group + n].astype(F32) for n in range(group))
            total[q] = value.astype(BF16)
        parts, at = R["parts_" + kind], new_far()
        begin("part_%s%d" % (kind, l), (total, parts.at[l, r]))
        for q in range(1, n_row):
            remote(total, parts.at[l, r], at, row_peer(q)).start()
        ends["add", kind, l] = at

    def added(kind, l):
        ref = R["parts_" + kind].at[l, pl.ds(0, n_row - 1)]
        return remote(ref, ref, ends["add", kind, l], row_peer(1))

    def add_sent(kind, l):
        if l < layers:
            waits("part_%s%d" % (kind, l))
            added(kind, l).wait_send()

    def part_copy(l, j, strips, at):
        to = c - g + lax.rem(g - j + group, group)
        return remote(R["part%d" % j].at[strips], R["in_part"].at[l, j - 1, strips], at, (r, to))

    def back_strip(l, i, at):
        kvs = [R["kv"]] + [R["peer"].at[j] for j in range(group - 1)]
        gkvs = [R["part%d" % j] for j in range(group)]
        attend_back_strip(held, bias, i, R["gq"], R["lse"], R["att"], R["low"], kvs, R["gq"], gkvs)
        for j in range(1, group):
            part_copy(l, j, pl.ds(i, 1), at[j]).start()

    def load_qkv(l):
        begin("qkv", *[
            (R["w_qkv"].at[l, i], R["wq"].at[i // 2, :, columns(i % 2, 384)]) for i in range(NARROW)
        ])

    def load_mlp(l):
        begin("hidden", (R["hiddens"].at[l], R["hidden"]))
        begin("down", *[
            (R["w_down"].at[l, pl.ds(n * 1024, 1024)], R["wd"].at[pl.ds(n * 1024, 1024)])
            for n in range(R["wd"].shape[0] // 1024)
        ])
        begin("up", *[(R["w_up"].at[l, i], R["wu"].at[i]) for i in range(NARROW)])
        begin("proj", (R["w_proj"].at[l], R["wp"]))

    def load_attention(l):
        begin("mid", (R["mids"].at[l], R["mid"]))
        begin("att", (R["atts"].at[l], R["att"]))
        begin("q", (R["qs"].at[l], R["gq"]))
        begin("kv", (R["kvs"].at[l], R["kv"]), (R["peers"].at[l], R["peer"]), (R["lses"].at[l], R["lse"]))

    last = layers - 1
    begin("cotangent", (R["cotangent"], R["low"]))
    load_mlp(last)
    load_attention(last)
    load_qkv(last)
    at_result = columns_start(0, R["result"])
    at_ids = new_far()
    begin("ids", (R["ids"], R["all_ids"].at[r]))
    for q in range(1, n_row):
        remote(R["ids"], R["all_ids"].at[r], at_ids, row_peer(q)).start()
    waits("cotangent")

    def widen(rows):
        R["grad"][rows, :] = R["low"][rows, :].astype(F32)

    by_rows(tokens, widen)
    for l in reversed(range(layers)):
        t = {name: R[name].at[l] for name in TABLES if "qkv" not in name}
        vec = Vectors(R["vec"], l)
        spread_sent("mlp", l + 1)
        mlp_back_stage(
            vec, R["grad"], R["hidden"], R["g_hid"], R["mid"], R["att"], R["low"], R["total"], R["wp"], R["wu"],
            R["wd"], R["reds"].at[l], {k: (v if k in ("low_down", "up_up") else v[...]) for k, v in t.items()},
            R["grads_mlp"], R["total2"], waits,
        )
        spread("mlp", l)
        if l < last:
            add("qkv", l + 1)
        if l > 0:
            load_mlp(l - 1)
        begin("x", (R["tokens"] if l == 0 else R["xs"].at[l - 1], R["x0"] if l == 0 else R["mid"]))
        waits("q")
        waits("kv")
        at = [new_far() for _ in range(group)]
        each(NARROW, lambda i: back_strip(l, i, at))
        add("mlp", l)
        every = pl.ds(0, NARROW)
        begin("parts", *[])
        for j in range(1, group):
            part_copy(l, j, every, at[j]).wait()
        begin("parts", *[(R["in_part"].at[l, j], R["peer"].at[j]) for j in range(group - 1)])
        waits("parts")
        parts = [R["part0"]] + [R["peer"].at[j] for j in range(group - 1)]
        spread_sent("qkv", l + 1)

        def put(rows, value):
            if l > 0:
                R["grad"][rows, :] = value
            else:
                for i in range(NARROW):
                    R["part0"][i, rows, :128] = value[:, i * 128 : (i + 1) * 128].astype(BF16)

        qkv_back_stage(
            vec, R["x0"] if l == 0 else R["mid"], R["total2"], R["gq"], parts, R["total"], R["g_red"], R["low"],
            R["wq"], R["reds"].at[l, 0], R["low_qkv"].at[l], R["up_qkv"].at[l], R["grads_qkv"], put, waits,
        )
        spread("qkv", l)
        if l > 0:
            load_qkv(l - 1)
            load_attention(l - 1)
    at_grad = columns_start(1, R["part0"].at[:, :, pl.ds(0, 128)])
    add("qkv", 0)
    columns_end(0, at_result)
    columns_end(1, at_grad)
    waits("ids")
    rest = R["all_ids"].at[pl.ds(0, n_row - 1)]
    remote(rest, rest, at_ids, row_peer(1)).wait()
    for kind in ("mlp", "qkv"):
        spread_sent(kind, 0)
        add_sent(kind, 0)
        for l in range(layers):
            added(kind, l).wait_recv()


def backward(n_row, n_col, group, outs, tables, ids):
    layers, _, dim, _ = outs["qkv"].shape
    hidden = outs["down"].shape[1]
    mine = outs["tokens"].shape[0]
    rank = tables[0].shape[1]
    seqs = n_col // group
    strip = (NARROW, mine)
    near, far = pl.BlockSpec(memory_space=pltpu.VMEM), pl.BlockSpec(memory_space=pltpu.HBM)
    inputs = [(name, table, near) for name, table in zip(TABLES, tables)]
    inputs += [("vec", outs["vec"], near), ("reds", outs["reds"], near), ("ids", ids, far)]
    for name in ("hidden", "mid", "att", "q", "kv", "peer", "lse", "x"):
        inputs.append((name + "s", outs["saved_" + name], far))
    inputs += [("w_" + name, outs[name], far) for name in KINDS]
    inputs += [(name, outs[name], far) for name in ("tokens", "cotangent", "result")]
    sizes = {"mlp": 512 + 2 * hidden // NARROW, "qkv": 512}
    outputs = [
        ("columns", (2, n_col * mine, 128), BF16, far),
        ("all_ids", (n_row,) + ids.shape, F32, far),
        ("in_part", (layers, group - 1) + strip + (256,), BF16, far),
    ]
    scratch = [
        ("gq", strip + (128,), BF16), ("kv", strip + (256,), BF16), ("peer", (group - 1,) + strip + (256,), BF16),
        ("lse", (NARROW, 8, mine), F32), ("total", (mine, dim), F32), ("total2", (mine, dim), F32),
        ("grad", (mine, dim), F32), ("mid", (mine, dim), F32), ("low", (mine, dim), BF16), ("att", (mine, dim), BF16),
        ("x0", (mine, dim), BF16), ("hidden", (mine, hidden), BF16), ("g_hid", (mine, hidden), BF16),
        ("g_red", (mine, rank), BF16), ("wq", (NARROW // 2, dim, 768), BF16), ("wp", (dim, dim), BF16),
        ("wu", (NARROW, dim, hidden // NARROW), BF16), ("wd", (hidden, dim), BF16),
    ]
    scratch += [("part%d" % j, strip + (256,), BF16) for j in range(group)]
    for kind, size in sizes.items():
        outputs.append(("land_" + kind, (layers, n_col, rank, size), BF16, far))
        outputs.append(("parts_" + kind, (layers, n_row, seqs, rank, size), BF16, far))
        scratch.append(("grads_" + kind, (NARROW, rank, size), BF16))
        scratch.append(("stage_" + kind, (n_col, rank, size), BF16))
        scratch.append(("sum_" + kind, (seqs, rank, size), BF16))
    scratch = [(name, pltpu.VMEM(shape, kind)) for name, shape, kind in scratch]
    scratch += [
        ("sem", pltpu.SemaphoreType.DMA((48 * layers + 16,))),
        ("out_sem", pltpu.SemaphoreType.DMA((8 * layers + 8,))),
        ("in_sem", pltpu.SemaphoreType.DMA((8 * layers + 8,))),
    ]
    names = [x[0] for x in inputs] + [x[0] for x in outputs] + [x[0] for x in scratch]
    made = pl.pallas_call(
        functools.partial(backward_body, layers, group, n_row, n_col, tuple(names)),
        out_shape=[shape_of(shape, kind) for _, shape, kind, _ in outputs],
        in_specs=[spec for _, _, spec in inputs],
        out_specs=[spec for _, _, _, spec in outputs],
        scratch_shapes=[shape for _, shape in scratch],
        compiler_params=pltpu.CompilerParams(
            collective_id=1, has_side_effects=True, vmem_limit_bytes=62 * 2**20
        ),
        name="backward",
    )(*[array for _, array, _ in inputs])
    return dict(zip([x[0] for x in outputs], made))


def place_body(sizes, weights, *refs):
    parts, outs = refs[: len(sizes)], refs[len(sizes) :]
    adapters = outs[0].shape[1]
    sequences = parts[0].shape[1]
    l = pl.program_id(0)
    n = 0
    for part, (kind, pieces) in zip(parts, sizes):
        at = 0
        for site, size in zip(SITES[kind], pieces):
            for a in range(adapters):
                value = 0.0
                for q in range(sequences):
                    value = value + part[0, q, :, at : at + size].astype(F32) * weights[a, site * sequences + q]
                outs[n][0, a] = value
            at += size
            n += 1


def place(parts, sizes, weights):
    layers, sequences, rank, _ = parts[0].shape
    adapters = weights.shape[0]
    widths = [size for _, pieces in sizes for size in pieces]
    return pl.pallas_call(
        functools.partial(place_body, sizes),
        grid=(layers,),
        out_shape=[shape_of((layers, adapters, rank, size), F32) for size in widths],
        in_specs=[pl.BlockSpec(memory_space=pltpu.SMEM)]
        + [pl.BlockSpec((1,) + part.shape[1:], lambda l: (l, 0, 0, 0)) for part in parts],
        out_specs=[pl.BlockSpec((1, adapters, rank, size), lambda l: (l, 0, 0, 0)) for size in widths],
        compiler_params=PARAMS,
        name="place",
    )(weights, *parts)


def to_rows_body(held, x, out):
    n = 0
    for s in range(x.shape[0] // (len(held) * len(held[0]))):
        for g in range(len(held)):
            for place in held[g]:
                start = (s * BLOCKS + place) * BLOCK
                out[start : start + BLOCK, :] = x[n].astype(F32)
                n += 1


def to_rows(held, x):
    blocks, _, width = x.shape
    return pl.pallas_call(
        functools.partial(to_rows_body, held),
        out_shape=shape_of((blocks * BLOCK, width), F32),
        compiler_params=PARAMS,
        name="to_rows",
    )(x)


def pick_body(count, ids, *refs):
    for ref, out in zip(refs[:count], refs[count:]):
        out[...] = ref[...]


def pick_tables(ids, tables):
    def chosen(site, shape):
        return pl.BlockSpec((shape[0], None) + shape[2:], lambda i, ids: (0, ids[site], 0, 0))

    return pl.pallas_call(
        functools.partial(pick_body, len(tables)),
        grid_spec=pltpu.PrefetchScalarGridSpec(
            num_scalar_prefetch=1,
            grid=(1,),
            in_specs=[chosen(site, table.shape) for site, table in tables],
            out_specs=[
                pl.BlockSpec(table.shape[:1] + table.shape[2:], lambda i, ids: (0, 0, 0)) for _, table in tables
            ],
        ),
        out_shape=[shape_of(table.shape[:1] + table.shape[2:], BF16) for _, table in tables],
        compiler_params=PARAMS,
        name="pick",
    )(ids, *[table for _, table in tables])


def shards(mesh_shape, *args):
    (
        tokens, cotangent, adapter_ids, qkv_weight, qkv_bias, proj_weight, proj_bias,
        up_weight, up_bias, down_weight, down_bias, first_gain, first_shift, second_gain,
        second_shift, qkv_lower, qkv_raise, proj_lower, proj_raise, up_lower, up_raise,
        down_lower, down_raise,
    ) = args
    n_row, n_col = mesh_shape
    layers, adapters, dim, rank = qkv_lower.shape
    rows, width = tokens.shape
    units = up_weight.shape[2]
    seqs = rows // LEN
    group = n_col // seqs
    held = positions(group)
    per = BLOCKS // group
    mine = per * BLOCK
    merge = 128 // width
    c = lax.axis_index("col")
    g = lax.rem(c, group)
    ids = lax.dynamic_index_in_dim(adapter_ids, c // group, 0, keepdims=False)

    def line(pieces):
        row = jnp.concatenate([piece.reshape(layers, -1).astype(F32) for piece in pieces], axis=1)
        return jnp.pad(row, ((0, 0), (0, 512 - row.shape[1])))

    vector = jnp.stack(
        [
            line([qkv_bias]), line([up_bias]), line([proj_bias, down_bias, first_gain, first_shift]),
            line([second_gain, second_shift]),
        ],
        axis=1,
    ).reshape(layers * 4, 512)

    def turned(table):
        return jnp.swapaxes(table, 2, 3)

    tables = pick_tables(ids, [
        (0, turned(qkv_lower)), (1, turned(proj_lower)), (1, proj_raise), (2, turned(up_lower)), (2, up_raise),
        (3, turned(down_lower)), (3, down_raise),
    ])
    raise_qkv = lax.dynamic_index_in_dim(qkv_raise, ids[0], 1, keepdims=False)
    raise_qkv = raise_qkv.reshape(layers, rank, 3, NARROW, 128).transpose(0, 3, 1, 2, 4)
    tables = [tables[0], raise_qkv.reshape(layers, NARROW, rank, 384)] + list(tables[1:])
    fused = FUSED and width == 128
    outs = gather_inputs(
        n_row, n_col, group, qkv_weight.reshape(layers, -1, 3 * width), proj_weight, up_weight,
        down_weight, tokens, cotangent, vector, tables if fused else None
    )
    g_one = g.reshape(1)

    def peer_values(x, step):
        pairs = [(q, q - q % group + (q + step) % group) for q in range(n_col)]
        return lax.ppermute(x, "col", pairs)

    def to_columns(x):
        if merge > 1:
            x = x.reshape(NARROW, mine, merge, width).transpose(0, 2, 1, 3).reshape(n_col, mine, width)
        x = lax.all_to_all(x, "col", split_axis=0, concat_axis=0, tiled=True)
        return to_rows(held, x.reshape(n_col * per, BLOCK, width))

    if not fused:
        x = outs["tokens"].astype(F32)
        kept = {name: [] for name in SAVED + ("reds",)}
        for l in range(layers):
            q, kv, red = qkv_kernel(l, x, outs["vec"], outs["qkv"], tables[0], tables[1])
            kvs = [kv] + [peer_values(kv, s) for s in range(1, group)]
            att, lse = attend_kernel(group, g_one, q, kvs)
            mid, x, hidden, reds = mlp_kernel(
                l, l == layers - 1, x, att, outs["vec"], outs["proj"], outs["up"], outs["down"], tables[2:]
            )
            reds = jnp.concatenate([red[None], reds])
            peer = jnp.stack(kvs[1:]) if group > 1 else kv[None][:0]
            for name, value in zip(SAVED + ("reds",), (q, kv, peer, att, lse, mid, hidden, x, reds)):
                kept[name].append(value)
        for name in SAVED:
            outs["saved_" + name] = jnp.stack(kept[name][: layers - 1] if name == "x" else kept[name])
        outs["reds"] = jnp.stack(kept["reds"])
        outs["result"] = x
    if fused:
        ids_rows = jnp.pad(adapter_ids.astype(F32), ((0, 8 - seqs), (0, 128 - adapter_ids.shape[1])))
        made = backward(n_row, n_col, group, outs, tables, ids_rows)
        every = made["all_ids"][:, :seqs, : adapter_ids.shape[1]].reshape(n_row * seqs, -1).T.reshape(-1)
        weights = (every[None, :] == jnp.arange(adapters, dtype=F32)[:, None]).astype(F32)
        wide = units
        sizes = (("qkv", (128, 384)), ("mlp", (128, 128, 128, wide, wide, 128)))
        parts = [made["parts_" + kind].reshape(layers, n_row * seqs, rank, -1) for kind, _ in sizes]
        sums = place(parts, sizes, weights)
        final = [made["columns"][0].astype(F32), made["columns"][1].astype(F32)]
        for number, p in enumerate(sums):
            if number == 1:
                p = p.reshape(layers, adapters, rank, 3, width)
            elif number % 2 == 0:
                p = p.transpose(0, 1, 3, 2)
            final.append(p)
        return tuple(final)

    result = to_columns(outs["result"])

    onehot = (adapter_ids.T[:, :, None] == jnp.arange(adapters)[None, None, :]).astype(BF16)

    def all_rows(x):
        pairs = [[(q, (q + s) % n_row) for q in range(n_row)] for s in range(1, n_row)]
        return [x] + [lax.ppermute(x, "row", pair) for pair in pairs]

    onehots = jnp.concatenate(all_rows(onehot), axis=1)

    def collect(parts, named):
        if merge > 1:
            pieces, at = [], 0
            for _, size in named:
                piece = parts[:, :, at : at + size]
                at += size
                if size == 384:
                    piece = piece.reshape(NARROW, rank, 3, merge, width).transpose(0, 3, 1, 2, 4)
                else:
                    piece = piece.reshape(NARROW, rank, merge, size // merge).transpose(0, 2, 1, 3)
                pieces.append(piece.reshape(n_col, rank, size // merge))
            parts = jnp.concatenate(pieces, axis=2)
        parts = lax.all_to_all(parts, "col", split_axis=0, concat_axis=0, tiled=True)
        parts = parts.reshape((seqs, group) + parts.shape[1:]).astype(F32).sum(axis=1).astype(BF16)
        parts = jnp.concatenate(all_rows(parts), axis=0)
        sums, at = [], 0
        for site, size in named:
            piece = parts[:, :, at : at + size // merge]
            at += size // merge
            sums.append(jnp.einsum("sa,srn->arn", onehots[site], piece, preferred_element_type=F32))
        return sums

    wide = outs["down"].shape[1] // NARROW
    grads, carried = [None] * layers, None
    for l in reversed(range(layers + 1)):
        lq, lm = (l if l < layers else None), (l - 1 if l > 0 else None)
        made = back_kernel(lq, lm, group, g_one, outs, tables, carried)
        if lm is not None:
            grads[lm] = collect(made["grads_mlp"], [(1, 128), (1, 128), (2, 128), (2, wide), (3, wide), (3, 128)])
            parts = [made["out_part%d" % s] for s in range(group)]
            parts = [parts[0]] + [peer_values(parts[s], group - s) for s in range(1, group)]
            carried = (made["out_g_mid"], made["out_gq"], parts)
        if lq is not None:
            grads[lq] = collect(made["grads_qkv"], [(0, 128), (0, 384)]) + grads[lq]
    grad = made["out"]
    input_grad = to_columns(grad)

    final = []
    for number in range(8):
        p = jnp.stack([grads[l][number] for l in range(layers)])
        if number == 1:
            p = p.reshape(layers, adapters, rank, 3, width)
        elif number % 2 == 0:
            p = p.transpose(0, 1, 3, 2)
        final.append(p)
    return (result, input_grad) + tuple(final)


def solution(mesh):
    mesh_shape = (mesh.shape["row"], mesh.shape["col"])
    return jax.shard_map(
        functools.partial(shards, mesh_shape),
        mesh=mesh,
        in_specs=(
            P("row", "col"), P("row", "col"), P("row", None),
            P(None, "row", None, "col"), P(None, None, "col"),
            P(None, "col", "row"), P(None, "col"),
            P(None, "row", "col"), P(None, "col"),
            P(None, "col", "row"), P(None, "col"),
            P(None, "col"), P(None, "col"), P(None, "col"), P(None, "col"),
            P(), P(), P(), P(), P(), P(), P(), P(),
        ),
        out_specs=(
            P("row", "col"), P("row", "col"),
            P(None, None, "col", None), P(None, None, None, None, "col"),
            P(None, None, "col", None), P(None, None, None, "col"),
            P(None, None, "col", None), P(None, None, None, "col"),
            P(None, None, "col", None), P(None, None, None, "col"),
        ),
        check_vma=False,
    )
```

```python
import functools

import jax
import jax.numpy as jnp
from jax import lax
from jax.experimental import pallas as pl
from jax.experimental.pallas import tpu as pltpu
from jax.sharding import PartitionSpec as P

HD = 64
LEN = 1024
BLOCK = 256
BLOCKS = LEN // BLOCK
EPSILON = 1e-05
SCALE = HD**-0.5
ROOT = (2.0 / 3.141592653589793) ** 0.5
MESH = pl.DeviceIdType.MESH
F32 = jnp.float32
BF16 = jnp.bfloat16


ROW_FIRST = (("z", 0, 1), ("z", 1, 0))
ROW_SECOND = ((0, "z", 1), (1, "z", 0))
ORDERS = (
    {"qkv": (ROW_FIRST,), "proj": (ROW_SECOND,), "up": (ROW_FIRST,) * 2, "down": (ROW_SECOND, ROW_FIRST)},
    {"qkv": (ROW_SECOND,), "proj": (ROW_FIRST,), "up": (ROW_SECOND,) * 2, "down": (ROW_SECOND,) * 2},
)
CUTS = {kind: 2 * len(pairs) for kind, pairs in ORDERS[0].items()}
KINDS = ("qkv", "proj", "up", "down")
DEPTH = 4
FUSED = True
LINK = 90e3
DELAY, ROW_DELAY = 2.0, 4.0
FIRST = 12.0


def transfer_plan(order, n_row):
    masks, rows, steps = [0], False, []
    for d in order:
        if d == "z":
            steps += [(("z", hop), tuple(masks), rows) for hop in range(1, n_row)]
            rows = True
        else:
            steps.append((d, tuple(masks), rows))
            masks = masks + [m ^ d for m in masks]
    steps.append((None, tuple(masks), rows))
    return steps


def transfer_schedule(pieces, n_row, tasks):
    cost, parts = {}, {}
    for k, (name, order, size) in enumerate(pieces):
        parts.setdefault(name, set()).add(k)
        for p, (d, masks, rows) in enumerate(transfer_plan(order, n_row)[:-1]):
            axis = "z" if isinstance(d, tuple) else d
            cost[k, p] = (axis, 2 * len(masks) * (n_row if rows else 1) * size / LINK)
    ready = {d: [] for d, _ in cost.values()}
    free = {d: 0.0 if d == "z" else FIRST for d in ready}
    flight = {d: [] for d in ready}
    for k in range(len(pieces)):
        ready[cost[k, 0][0]].append((k, 0))
    tasks, left = list(tasks), {}
    for task in tasks:
        left[task[4]] = left.get(task[4], 0) + 1
    landed, staged, now, ops = {}, {}, 0.0, []

    def stage(name):
        kind, l = name
        if name in landed and name not in staged and landed[name] <= now and not left.get((kind, l - 1)):
            staged[name] = now + 3.0
            ops.append(("stage", kind, l))

    while tasks or any(ready.values()) or any(flight.values()):
        for d in ready:
            while ready[d] and len(flight[d]) < DEPTH:
                k, p = ready[d].pop(0)
                free[d] = max(now, free[d]) + cost[k, p][1]
                flight[d].append((free[d] + (ROW_DELAY if d == "z" else DELAY), k, p))
                ops.append(("start", k, p))
        if tasks:
            for name in list(landed):
                stage(name)
        events = [f for line in flight.values() for f in line]
        event = min(events) if events else None
        due = None
        if tasks:
            need = tasks[0][4]
            due = now if need is None else staged.get(need)
            if due is None and need in landed and not left.get((need[0], need[1] - 1)):
                due = landed[need]
        if due is not None and (event is None or max(due, now) < event[0]):
            now = max(due, now)
            need = tasks[0][4]
            if need is not None and need not in staged:
                continue
            name, l, part, micros, _ = tasks.pop(0)
            left[need] -= 1
            now += micros
            ops.append(("task", name, (l, part)))
            continue
        now, k, p = max(now, event[0]), event[1], event[2]
        d = cost[k, p][0]
        flight[d].remove(event)
        ops.append(("wait", k, p))
        if (k, p + 1) in cost:
            later = ready[cost[k, p + 1][0]]
            later.append((k, p + 1))
            later.sort()
        else:
            name = pieces[k][0]
            parts[name].discard(k)
            if not parts[name]:
                landed[name] = now + 4.0
    return ops


def place_of(group, g, b):
    if group == 2:
        return g + b * (BLOCKS - 1 - 2 * g)
    return g * (BLOCKS // group) + b


def positions(group):
    per = BLOCKS // group
    return tuple(tuple(place_of(group, g, b) for b in range(per)) for g in range(group))


NARROW = 8
CROSS = ((0,), (0,))
TURNED = ((1,), (1,))


def dot(a, b, dims=((1,), (0,))):
    return lax.dot_general(a, b, (dims, ((), ())), preferred_element_type=F32)


def columns(i, size=128):
    if isinstance(i, int):
        return pl.ds(i * size, size)
    return pl.ds(pl.multiple_of(i * size, size), size)


def norm_parts(x):
    center = x - jnp.mean(x, axis=1, keepdims=True)
    inverse = lax.rsqrt(jnp.mean(center * center, axis=1, keepdims=True) + EPSILON)
    return center * inverse, inverse


def norm_grad(grad, scaled, inverse, gain):
    w = grad * gain
    first = jnp.mean(w, axis=1, keepdims=True)
    second = jnp.mean(w * scaled, axis=1, keepdims=True)
    return inverse * (w - first - scaled * second)


def norm_low(x, gain, shift):
    return (norm_parts(x)[0] * gain + shift).astype(BF16)


def pair_state(held):
    group, per = len(held), len(held[0])
    state = {}
    for s in range(per):
        for j in range(group):
            for b in range(per):
                seen = {held[(g - j) % group][b] <= held[g][s] for g in range(group)}
                state[s, j, b] = 0 if len(seen) == 2 else (1 if True in seen else -1)
    return state


def pair_bias(held, g):
    group = len(held)
    bias = {}
    for (s, j, b), state in pair_state(held).items():
        if state == 0:
            keys = place_of(group, lax.rem(g - j + group, group), b)
            bias[s, j, b] = jnp.where(keys <= place_of(group, g, s), 0.0, -1e9).astype(F32)
    return bias


def head_mask(h):
    lane = lax.broadcasted_iota(jnp.int32, (1, 128), 1)
    return (lane // HD) == h


def attend_strip(held, bias, i, q, kvs, out, lse):
    group, per = len(held), len(held[0])
    state = pair_state(held)
    turned = {}
    for s in range(per):
        rows = pl.ds(s * BLOCK, BLOCK)
        queries = q[i, rows, :] * SCALE
        pieces = []
        for h in range(2):
            query = jnp.where(head_mask(h), queries, 0).astype(BF16)
            scores, values = [], []
            for j in range(group):
                for b in range(per):
                    if state[s, j, b] < 0:
                        continue
                    keys = kvs[j][i, b * BLOCK : (b + 1) * BLOCK, :128]
                    score = dot(keys, query, TURNED)
                    if state[s, j, b] == 0:
                        score = score + bias[s, j, b]
                    scores.append(score)
                    if (j, b) not in turned:
                        turned[j, b] = kvs[j][i, b * BLOCK : (b + 1) * BLOCK, 128:].T
                    values.append(turned[j, b][h * HD : (h + 1) * HD])
            top = functools.reduce(jnp.maximum, [jnp.max(x, axis=0, keepdims=True) for x in scores])
            total, made = 0.0, 0.0
            for score, value in zip(scores, values):
                e = jnp.exp(score - top)
                total = total + jnp.sum(e, axis=0, keepdims=True)
                made = made + dot(value, e.astype(BF16))
            pieces.append(made / total)
            lse[i, h : h + 1, rows] = top + jnp.log(total)
        out[rows, columns(i)] = jnp.concatenate(pieces, axis=0).T.astype(BF16)


def attend_back_strip(held, bias, i, q, lse, out, grad, kvs, gq, gkvs):
    group, per = len(held), len(held[0])
    state = pair_state(held)
    turned, gk, gv = {}, {}, {}
    for s in range(per):
        rows = pl.ds(s * BLOCK, BLOCK)
        queries = q[i, rows, :] * SCALE
        up = grad[rows, columns(i)]
        product = (up.astype(F32) * out[rows, columns(i)].astype(F32)).T
        pieces = []
        for h in range(2):
            query = jnp.where(head_mask(h), queries, 0).astype(BF16)
            given = jnp.where(head_mask(h), up, 0).astype(BF16)
            inner = jnp.sum(product[h * HD : (h + 1) * HD], axis=0, keepdims=True)
            level = lse[i, h : h + 1, rows]
            made = 0.0
            for j in range(group):
                for b in range(per):
                    if state[s, j, b] < 0:
                        continue
                    keys = kvs[j][i, b * BLOCK : (b + 1) * BLOCK, :128]
                    values = kvs[j][i, b * BLOCK : (b + 1) * BLOCK, 128:]
                    score = dot(keys, query, TURNED)
                    if state[s, j, b] == 0:
                        score = score + bias[s, j, b]
                    probs = jnp.exp(score - level)
                    g_probs = dot(values, given, TURNED)
                    g_scores = (probs * (g_probs - inner)).astype(BF16)
                    if (j, b) not in turned:
                        turned[j, b] = keys.T
                        gk[j, b], gv[j, b] = 0.0, 0.0
                    gv[j, b] = gv[j, b] + dot(probs.astype(BF16), given)
                    gk[j, b] = gk[j, b] + dot(g_scores, query)
                    made = made + dot(turned[j, b][h * HD : (h + 1) * HD], g_scores)
            pieces.append(made)
        gq[i, rows, :] = (jnp.concatenate(pieces, axis=0) * SCALE).T.astype(BF16)
    for j in range(group):
        for b in range(per):
            rows = pl.ds(b * BLOCK, BLOCK)
            gkvs[j][i, rows, :128] = gk[j, b].astype(BF16)
            gkvs[j][i, rows, 128:] = gv[j, b].astype(BF16)


def by_rows(count, body, size=128):
    each(count // size, lambda n: body(pl.ds(pl.multiple_of(n * size, size), size)))


def keep(value, red, red_out):
    red[...] = value.astype(BF16)
    red_out[...] = value.T.astype(BF16)


def each(count, body):
    def step(i, carry):
        body(i)
        return carry

    lax.fori_loop(0, count, step, 0)


def qkv_stage(x, gain, shift, w, bias, low, up, q, kv, red, red_out, normed):
    def norm(rows):
        normed[rows, :] = norm_low(x[rows, :], gain, shift)

    by_rows(x.shape[0], norm)
    keep(dot(normed[...], low[...], TURNED), red, red_out)

    def pair(j):
        made = dot(normed[...], w[j])
        for n in range(2):
            i = 2 * j + n
            mixed = made[:, n * 384 : (n + 1) * 384] + (bias[i] + dot(red[...], up[i]))
            q[i] = mixed[:, :128].astype(BF16)
            kv[i] = mixed[:, 128:].astype(BF16)

    each(NARROW // 2, pair)


def proj_stage(x, att, w, bias, low, up, gain, shift, low_up, mid, normed, red, red_out, red_up, red_up_out):
    keep(dot(att[...], low[...], TURNED), red, red_out)

    def part(rows):
        value = x[rows, :] + (dot(att[rows, :], w[...]) + bias + dot(red[rows, :], up[...]))
        mid[rows, :] = value
        normed[rows, :] = norm_low(value, gain, shift)

    by_rows(x.shape[0], part, 256)
    keep(dot(normed[...], low_up[...], TURNED), red_up, red_up_out)


def up_strip(i, normed, w, bias, red_up, up, hidden, active):
    units = w.shape[2]
    cols = columns(i, units)
    value = dot(normed[...], w[i]) + (bias[i] + dot(red_up[...], up[:, cols]))
    hidden[:, cols] = value.astype(BF16)
    inner = ROOT * (value + 0.044715 * (value * value * value))
    active[:, cols] = (0.5 * value * (1.0 + jnp.tanh(inner))).astype(BF16)


def down_stage(mid, active, w, bias, up, red, put):
    for n in range(mid.shape[1] // 256):
        cols = slice(n * 256, (n + 1) * 256)
        put(n, mid[:, cols] + (dot(active[...], w[:, cols]) + bias[:, cols] + dot(red[...], up[:, cols])))


def gelu_parts(x):
    square = x * x
    t = jnp.tanh(ROOT * (x + 0.044715 * (x * square)))
    half = 0.5 * (1.0 + t)
    slope = half + 0.5 * x * (1.0 - t * t) * (ROOT * (1.0 + 3 * 0.044715 * square))
    return x * half, slope


class Vectors:
    def __init__(self, ref, l):
        self.ref, self.l = ref, l

    def qkv(self, i):
        return self.ref[i, pl.ds(4 * self.l, 1), :384]

    def up(self, i):
        return self.ref[i, pl.ds(4 * self.l + 1, 1), :]

    def row(self, name):
        at = ("proj", "down", "gain1", "shift1", "gain2", "shift2").index(name)
        row, lane = 4 * self.l + 2 + at // 4, at % 4 * 128
        return jnp.concatenate([self.ref[i, row : row + 1, lane : lane + 128] for i in range(NARROW)], axis=1)


class Strips:
    def __init__(self, read):
        self.read = read

    def __getitem__(self, i):
        return self.read(i)


TABLES = ("low_qkv", "up_qkv", "low_proj", "up_proj", "low_up", "up_up", "low_down", "up_down")
SAVED = ("q", "kv", "peer", "att", "lse", "mid", "hidden", "x")


def task_list(layers):
    tasks = [("load", 0, 0, 3.0, None)]
    for l in range(layers):
        tasks.append(("qkv", l, 0, 7.0, ("qkv", l)))
        tasks += [("attend", l, n, 5.0, None) for n in range(4)]
        tasks.append(("proj", l, 0, 4.0, ("proj", l)))
        tasks += [("up", l, n, 5.0, ("up", l)) for n in range(2)]
        tasks.append(("down", l, 0, 6.0, ("down", l)))
    return tasks


class ForwardWork:
    def __init__(self, n_col, group, refs):
        self.__dict__.update(refs)
        self.group = group
        self.held = positions(group)
        self.r, self.c = lax.axis_index("row"), lax.axis_index("col")
        self.g = lax.rem(self.c, group)
        self.bias = pair_bias(self.held, self.g)
        self.layers = self.low_qkv.shape[0]

    def stage_copies(self, kind, l):
        full = self.full[kind]
        if kind == "qkv":
            pieces = []
            for i in range(NARROW):
                src = full.at[l, i]
                pieces.append((src, self.wq.at[i // 2, :, :, :, pl.ds(i % 2 * 384, 384)]))
            return pieces, self.wq
        if kind == "up":
            return [(full.at[l, i], self.wu.at[i]) for i in range(NARROW)], self.wu
        target = self.wp if kind == "proj" else self.wd
        return [(full.at[l, i], target.at[i]) for i in range(NARROW)], target

    def stage(self, kind, l):
        for src, dst in self.stage_copies(kind, l)[0]:
            pltpu.make_async_copy(src, dst, self.stage_sem.at[KINDS.index(kind)]).start()

    def staged(self, kind, l):
        target = self.stage_copies(kind, l)[1]
        pltpu.make_async_copy(target, target, self.stage_sem.at[KINDS.index(kind)]).wait()

    def save_copy(self, name, l):
        src = {
            "q": self.q, "kv": self.kv, "peer": self.peer.at[l], "att": self.att, "lse": self.lse,
            "mid": self.mid, "hidden": self.hidden, "x": self.x,
        }[name]
        return pltpu.make_async_copy(src, self.saved[name].at[l], self.save_sem.at[l, SAVED.index(name)])

    def save(self, *names, l):
        for name in names:
            self.save_copy(name, l).start()

    def settled(self, *names, l):
        if l >= 0:
            for name in names:
                self.save_copy(name, l).wait()

    def exchange(self, l, s):
        to = self.c - self.g + lax.rem(self.g + s, self.group)
        return pltpu.make_async_remote_copy(
            src_ref=self.kv, dst_ref=self.peer.at[l, s - 1],
            send_sem=self.kv_send.at[l, s - 1], recv_sem=self.kv_recv.at[l, s - 1],
            device_id=(self.r, to), device_id_type=MESH,
        )

    def run(self, name, l, part):
        vec = Vectors(self.vec, l)
        if name == "load":
            self.arrive_tokens()
            self.x[...] = self.tokens_v[...].astype(F32)
        elif name == "qkv":
            self.staged("qkv", l)
            self.settled("q", "kv", l=l - 1)
            if l > 0:
                for s in range(1, self.group):
                    self.exchange(l - 1, s).wait_send()
            w = self.wq.reshape(NARROW // 2, -1, 768)
            qkv_stage(
                self.x, vec.row("gain1"), vec.row("shift1"), w, Strips(vec.qkv), self.low_qkv.at[l],
                self.up_qkv.at[l], self.q, self.kv, self.red, self.reds.at[l, 0], self.normed,
            )
            for s in range(1, self.group):
                self.exchange(l, s).start()
            self.save("q", "kv", l=l)
        elif name == "attend":
            if part == 0:
                for s in range(1, self.group):
                    self.exchange(l, s).wait_recv()
                self.save("peer", l=l)
                self.settled("att", "lse", l=l - 1)
            kvs = [self.kv] + [self.peer.at[l, s - 1] for s in range(1, self.group)]
            size = NARROW // 4
            each(size, lambda n: attend_strip(self.held, self.bias, part * size + n, self.q, kvs, self.att, self.lse))
            if part == 3:
                self.save("att", "lse", l=l)
        elif name == "proj":
            self.staged("proj", l)
            self.settled("mid", l=l - 1)
            dim = self.att.shape[1]
            proj_stage(
                self.x, self.att, self.wp.reshape(dim, dim), vec.row("proj"), self.low_proj.at[l],
                self.up_proj.at[l], vec.row("gain2"), vec.row("shift2"), self.low_up.at[l],
                self.mid, self.normed, self.red, self.reds.at[l, 1], self.red_up, self.reds.at[l, 2],
            )
            self.save("mid", l=l)
        elif name == "up":
            if part == 0:
                self.staged("up", l)
                self.settled("hidden", l=l - 1)
            w = self.wu.reshape(NARROW, self.x.shape[1], -1)
            size = NARROW // 2
            each(size, lambda n: up_strip(
                part * size + n, self.normed, w, Strips(vec.up), self.red_up, self.up_up.at[l],
                self.hidden, self.active,
            ))
            if part == 1:
                self.save("hidden", l=l)
                keep(dot(self.active[...], self.low_down[l], TURNED), self.red, self.reds.at[l, 3])
        elif name == "down":
            self.staged("down", l)
            self.settled("x", l=l - 1)
            dim = self.x.shape[1]

            def put(n, value):
                if l < self.layers - 1:
                    self.x[:, columns(n, 256)] = value
                else:
                    for m in range(2):
                        self.result[2 * n + m] = value[:, m * 128 : (m + 1) * 128].astype(BF16)

            down_stage(
                self.mid, self.active, self.wd.reshape(-1, dim), vec.row("down"), self.up_down.at[l], self.red, put,
            )
            if l < self.layers - 1:
                self.save("x", l=l)

    def close(self):
        last = self.layers - 1
        self.settled(*[name for name in SAVED if name not in ("x", "peer")], l=last)
        for l in range(self.layers):
            self.settled("peer", l=l)
        for s in range(1, self.group):
            self.exchange(last, s).wait_send()
        if last > 0:
            pass


def gather_body(n_row, n_col, layers, group, names, *refs):
    refs = dict(zip(names, refs))
    shard = {kind: refs["shard_" + kind] for kind in KINDS}
    full = {kind: refs["full_" + kind] for kind in KINDS}
    tokens, cotangent, vector = refs["tokens"], refs["cotangent"], refs["vector"]
    own_tokens, own_cotangent, vectors = refs["own_tokens"], refs["own_cotangent"], refs["vectors"]
    local_sem, send_sem, recv_sem = refs["local_sem"], refs["send_sem"], refs["recv_sem"]
    near_sem, out_sem, in_sem = refs["near_sem"], refs["out_sem"], refs["in_sem"]
    r = lax.axis_index("row")
    c = lax.axis_index("col")
    link_bits = [b for b in (2**k for k in range(1, 8)) if b < n_col]
    depth = shard["up"].shape[1]

    def row_peer(s):
        return (lax.rem(r + s, n_row), c)

    def col_peer(bit):
        return (r, c ^ bit)

    peers = [row_peer(s) for s in range(1, n_row)]
    peers += [(r, lax.rem(c + d, n_col)) for d in range(1, n_col)]
    barrier = pltpu.get_barrier_semaphore()
    for peer in peers:
        pl.semaphore_signal(barrier, inc=1, device_id=peer, device_id_type=MESH)
    pl.semaphore_wait(barrier, len(peers))

    per, width = BLOCKS // group, tokens.shape[1]

    def own_place(ref, b, col):
        if len(ref.shape) == 2:
            start = pl.multiple_of(col * width, width)
            return ref.at[pl.ds(b * BLOCK, BLOCK), pl.ds(start, width)]
        return ref.at[col, pl.ds(b * BLOCK, BLOCK)]

    def from_place(ref, b, col):
        start = (col // group) * LEN + place_of(group, lax.rem(col, group), b) * BLOCK
        return ref.at[pl.ds(pl.multiple_of(start, BLOCK), BLOCK)]

    exchanged = ((tokens, own_tokens), (cotangent, own_cotangent))

    def near(n, b):
        src, dst = exchanged[n]
        return pltpu.make_async_copy(from_place(src, b, c), own_place(dst, b, c), near_sem.at[n * per + b])

    def near_vector():
        return pltpu.make_async_copy(vector, vectors.at[c], near_sem.at[2 * per])

    def far(src, dst, n, peer):
        return pltpu.make_async_remote_copy(
            src_ref=src, dst_ref=dst, send_sem=out_sem.at[n], recv_sem=in_sem.at[n],
            device_id=peer, device_id_type=MESH,
        )

    def start_exchange(n):
        src, dst = exchanged[n]
        for b in range(per):
            near(n, b).start()
        for d in range(1, n_col):
            to = lax.rem(c + d, n_col)
            for b in range(per):
                far(from_place(src, b, to), own_place(dst, b, c), n, (r, to)).start()

    def wait_exchange(n):
        _, dst = exchanged[n]
        for b in range(per):
            near(n, b).wait()
        if len(dst.shape) == 2:
            ref = dst.at[:, pl.ds(0, (n_col - 1) * width)]
        else:
            ref = dst.at[pl.ds(0, n_col - 1)]
        far(ref, ref, n, col_peer(1)).wait()

    def own(kind, l, h):
        ref = shard[kind]
        size = ref.shape[1] // CUTS[kind]
        return ref.at[l, pl.ds(h * size, size)]

    def block(kind, l, h, row, col):
        if kind in ("qkv", "up"):
            return full[kind].at[l, col, row, h]
        start = pl.multiple_of(row * depth, depth)
        return full[kind].at[l, col, h, :, pl.ds(start, depth)]

    def strip(kind, l, h, col):
        if kind in ("qkv", "up"):
            return full[kind].at[l, col, :, h]
        return full[kind].at[l, col, h]

    def amount(kind, l, h, strips, rows):
        if kind in ("qkv", "up"):
            return full[kind].at[l, pl.ds(0, strips), pl.ds(0, rows), h]
        return full[kind].at[l, pl.ds(0, strips), h, :, pl.ds(0, rows * depth)]

    chunks = []
    for l in range(layers):
        for kind in KINDS:
            for h in range(CUTS[kind]):
                order = []
                for d in ORDERS[l % len(ORDERS)][kind][h // 2][h % 2]:
                    if d == "z":
                        order.append("z")
                    elif d < len(link_bits):
                        order.append(link_bits[d])
                order += link_bits[2:]
                chunks.append((kind, l, h, tuple(order)))
    phases = len(link_bits) + n_row - 1

    def remote(src, dst, k, p, peer, way=0):
        at = (k * (phases + 1) + p) * 2 + way
        return pltpu.make_async_remote_copy(
            src_ref=src, dst_ref=dst, send_sem=send_sem.at[at], recv_sem=recv_sem.at[at],
            device_id=peer, device_id_type=MESH,
        )

    def plan(k):
        return transfer_plan(chunks[k][3], n_row)

    def ways(hop):
        return (
            (r - hop + 1, (r - hop + 1 >= 0) & (r + 1 < n_row), r - hop >= 0, 1),
            (r + hop - 1, (r + hop - 1 < n_row) & (r >= 1), r + hop < n_row, n_row - 1),
        )

    def local(k):
        kind, l, h, _ = chunks[k]
        return pltpu.make_async_copy(own(kind, l, h), block(kind, l, h, r, c), local_sem.at[k])

    def issue(k, p):
        kind, l, h, order = chunks[k]
        d, masks, rows = plan(k)[p]

        def held(m, row, first):
            return own(kind, l, h) if m == 0 and first else block(kind, l, h, row, c ^ m)

        if isinstance(d, tuple):
            for way, (row, goes, _, step) in enumerate(ways(d[1])):

                @pl.when(goes)
                def _():
                    for m in masks:
                        dst = block(kind, l, h, row, c ^ m)
                        remote(held(m, row, d[1] == 1), dst, k, p, row_peer(step), way).start()

            return
        for m in masks:
            if rows:
                ref = strip(kind, l, h, c ^ m)
                remote(ref, ref, k, p, col_peer(d)).start()
            else:
                remote(held(m, r, True), block(kind, l, h, r, c ^ m), k, p, col_peer(d)).start()

    def moved(k, p, send):
        kind, l, h, order = chunks[k]
        d, masks, rows = plan(k)[p]
        ref = amount(kind, l, h, len(masks), n_row if rows else 1)
        if not isinstance(d, tuple):
            copy = remote(ref, ref, k, p, col_peer(1))
            copy.wait_send() if send else copy.wait_recv()
            return
        for way, (_, goes, comes, step) in enumerate(ways(d[1])):

            @pl.when(goes if send else comes)
            def _():
                copy = remote(ref, ref, k, p, row_peer(step), way)
                copy.wait_send() if send else copy.wait_recv()

    def share(k, p):
        kind, l, h, order = chunks[k]
        (d, masks, _), (_, later, rows) = plan(k)[p : p + 2]
        if not rows:
            return
        fresh = masks if isinstance(d, tuple) else later[len(masks):]
        for m in fresh:
            ref = strip(kind, l, h, c ^ m)
            remote(ref, ref, k, phases, col_peer(1)).start()

    def shared(k):
        kind, l, h, _ = chunks[k]
        ref = amount(kind, l, h, n_col // 2, n_row)
        return remote(ref, ref, k, phases, col_peer(1))

    def finish(k, p):
        moved(k, p, False)
        if plan(k)[p][0] == ("z", n_row - 1):
            local(k).wait()
        share(k, p)

    count = len(chunks)
    near_vector().start()
    for d in range(1, n_col):
        far(vector, vectors.at[c], 2, (r, lax.rem(c + d, n_col))).start()
    start_exchange(0)
    for k in range(count):
        local(k).start()
    def vectors_arrive():
        near_vector().wait()
        rest = vectors.at[pl.ds(0, n_col - 1)]
        far(rest, rest, 2, col_peer(1)).wait()

    work = None
    if "x" in refs:
        refs.update(full=full, saved={name: refs["saved_" + name] for name in SAVED})

        def arrive_tokens():
            vectors_arrive()
            wait_exchange(0)
            load_sem = refs["load_sem"]
            loads = [(own_tokens, refs["tokens_v"]), (vectors, refs["vec"])]
            copies = [pltpu.make_async_copy(s, d, load_sem.at[n]) for n, (s, d) in enumerate(loads)]
            for copy in copies:
                copy.start()
            for copy in copies:
                copy.wait()

        refs.update(arrive_tokens=arrive_tokens)
        work = ForwardWork(n_col, group, refs)

    pieces = []
    for kind, l, h, order in chunks:
        size = 2 * shard[kind].shape[1] * shard[kind].shape[2] // CUTS[kind]
        pieces.append(((kind, l), order, size))
    ops = transfer_schedule(pieces, n_row, task_list(layers) if work else [])
    quiet = max(n for n, (op, _, _) in enumerate(ops) if op == "wait")
    for n, (op, k, p) in enumerate(ops):
        if n == quiet + 1:
            start_exchange(1)
        if op == "start":
            issue(k, p)
        elif op == "wait":
            finish(k, p)
        elif op == "stage":
            for at, (kind, l, _, _) in enumerate(chunks):
                if (kind, l) == (k, p):
                    shared(at).wait_recv()
            work.stage(k, p)
        else:
            work.run(k, *p)
    for k in range(count):
        for p in range(phases):
            moved(k, p, True)
        shared(k).wait_send()
        if not work:
            shared(k).wait_recv()
    if work:
        work.close()
    else:
        vectors_arrive()
        wait_exchange(0)
    wait_exchange(1)


def gather_inputs(n_row, n_col, group, qkv, proj, up, down, tokens, cotangent, vector, tables=None):
    layers, depth = up.shape[0], up.shape[1]
    width, units = proj.shape[1], down.shape[1]
    dim, hidden = depth * n_row, units * n_col
    mine = LEN // group
    cuts = [CUTS[kind] for kind in KINDS]
    own = (mine, dim) if width % 128 == 0 else (n_col, mine, width)
    hbm = pl.BlockSpec(memory_space=pltpu.HBM)
    vmem = pl.BlockSpec(memory_space=pltpu.VMEM)
    dma = pltpu.SemaphoreType.DMA
    count = layers * sum(cuts)
    phases = n_col.bit_length() + n_row - 2
    inputs = [("shard_" + kind, array, hbm) for kind, array in zip(KINDS, (qkv, proj, up, down))]
    inputs += [("tokens", tokens, hbm), ("cotangent", cotangent, hbm), ("vector", vector, hbm)]
    outputs = [
        ("full_qkv", (layers, n_col, n_row, cuts[0], depth // cuts[0], qkv.shape[2]), BF16, hbm),
        ("full_proj", (layers, n_col, cuts[1], width // cuts[1], dim), BF16, hbm),
        ("full_up", (layers, n_col, n_row, cuts[2], depth // cuts[2], units), BF16, hbm),
        ("full_down", (layers, n_col, cuts[3], units // cuts[3], dim), BF16, hbm),
        ("own_tokens", own, BF16, hbm),
        ("own_cotangent", own, BF16, hbm),
        ("vectors", (n_col,) + vector.shape, F32, hbm),
    ]
    scratch = [
        ("local_sem", dma((count,))),
        ("send_sem", dma((count * phases * 2,))),
        ("recv_sem", dma((count * phases * 2,))),
        ("near_sem", dma((2 * (BLOCKS // group) + 1,))),
        ("out_sem", dma((3,))),
        ("in_sem", dma((3,))),
    ]
    if tables is not None:
        rank = tables[0].shape[1]
        inputs += [(name, table, vmem) for name, table in zip(TABLES, tables)]
        strip = (NARROW, mine)
        kept = {
            "q": (strip + (128,), BF16), "kv": (strip + (256,), BF16), "att": ((mine, dim), BF16),
            "lse": ((NARROW, 8, mine), F32), "mid": ((mine, dim), F32), "hidden": ((mine, hidden), BF16),
            "x": ((mine, dim), F32), "peer": ((group - 1,) + strip + (256,), BF16),
        }
        outputs += [("saved_" + name, (layers,) + kept[name][0], kept[name][1], hbm) for name in SAVED]
        outputs += [
            ("reds", (layers, 4, rank, mine), BF16, vmem),
            ("result", (NARROW, mine, 128), BF16, vmem),
        ]
        scratch += [
            (name, pltpu.VMEM(((layers,) if name == "peer" else ()) + kept[name][0], kept[name][1]))
            for name in SAVED
        ]
        scratch += [
            ("wq", pltpu.VMEM((NARROW // 2, n_row, cuts[0], depth // cuts[0], 768), BF16)),
            ("wp", pltpu.VMEM((NARROW, cuts[1], width // cuts[1], dim), BF16)),
            ("wu", pltpu.VMEM((NARROW, n_row, cuts[2], depth // cuts[2], units), BF16)),
            ("wd", pltpu.VMEM((NARROW, cuts[3], units // cuts[3], dim), BF16)),
            ("tokens_v", pltpu.VMEM((mine, dim), BF16)),
            ("normed", pltpu.VMEM((mine, dim), BF16)),
            ("active", pltpu.VMEM((mine, hidden), BF16)),
            ("red", pltpu.VMEM((mine, rank), BF16)),
            ("red_up", pltpu.VMEM((mine, rank), BF16)),
            ("vec", pltpu.VMEM((n_col,) + vector.shape, F32)),
            ("stage_sem", dma((4,))),
            ("save_sem", dma((layers, len(SAVED)))),
            ("kv_send", dma((layers, group - 1))),
            ("kv_recv", dma((layers, group - 1))),
            ("load_sem", dma((2,))),
        ]
    names = [x[0] for x in inputs] + [x[0] for x in outputs] + [x[0] for x in scratch]
    outs = pl.pallas_call(
        functools.partial(gather_body, n_row, n_col, layers, group, tuple(names)),
        out_shape=[jax.ShapeDtypeStruct(shape, kind) for _, shape, kind, _ in outputs],
        in_specs=[spec for _, _, spec in inputs],
        out_specs=[spec for _, _, _, spec in outputs],
        scratch_shapes=[shape for _, shape in scratch],
        compiler_params=pltpu.CompilerParams(
            collective_id=0, has_side_effects=True, vmem_limit_bytes=60 * 2**20
        ),
        name="gather_inputs",
    )(*[array for _, array, _ in inputs])
    outs = dict(zip([x[0] for x in outputs], outs))

    merge = 128 // width
    strips = n_col // merge
    qkv_full = outs["full_qkv"].reshape(layers, n_col, dim, qkv.shape[2])
    up_full = outs["full_up"].reshape(layers, n_col, dim, units)
    rows, vec = [outs["own_tokens"], outs["own_cotangent"]], outs["vectors"]
    if merge > 1:
        qkv_full = qkv_full.reshape(layers, strips, merge, dim, 3, width).transpose(0, 1, 3, 4, 2, 5)
        up_full = up_full.reshape(layers, strips, merge, dim, units).transpose(0, 1, 3, 2, 4)
        rows = [x.transpose(1, 0, 2).reshape(mine, dim) for x in rows]
        vec = vec.reshape(strips, merge, layers, 4, 4 * 128)
        first = vec[:, :, :, 0, : 3 * width].reshape(strips, merge, layers, 3, width).transpose(0, 2, 3, 1, 4)
        first = jnp.pad(first.reshape(strips, layers, 384), ((0, 0), (0, 0), (0, 128)))
        second = vec[:, :, :, 1, :units].transpose(0, 2, 1, 3).reshape(strips, layers, 512)
        rest = vec[:, :, :, 2:, : 4 * width].reshape(strips, merge, layers, 2, 4, width)
        rest = rest.transpose(0, 2, 3, 4, 1, 5).reshape(strips, layers, 2, 512)
        vec = jnp.concatenate([first[:, :, None], second[:, :, None], rest], axis=2)
        vec = vec.reshape(strips, layers * 4, 512)
    outs.update(
        qkv=qkv_full.reshape(layers, strips, dim, 384),
        proj=outs["full_proj"].reshape(layers, dim, dim),
        up=up_full.reshape(layers, strips, dim, units * merge),
        down=outs["full_down"].reshape(layers, hidden, dim),
        tokens=rows[0], cotangent=rows[1], vec=vec,
    )
    return outs


PARAMS = pltpu.CompilerParams(vmem_limit_bytes=60 * 2**20)


def shape_of(shape, kind):
    return jax.ShapeDtypeStruct(shape, kind)


def kernel(body, name, inputs, outputs, scratch=()):
    spaces = (pl.BlockSpec(memory_space=pltpu.VMEM), pl.BlockSpec(memory_space=pltpu.HBM))
    return pl.pallas_call(
        body,
        out_shape=[shape_of(shape, kind) for shape, kind, _ in outputs],
        in_specs=[spaces[far] for _, far in inputs],
        out_specs=[spaces[far] for _, _, far in outputs],
        scratch_shapes=list(scratch),
        compiler_params=PARAMS,
        name=name,
    )(*[array for array, _ in inputs])


def own_group(group):
    return lax.rem(lax.axis_index("col"), group)


def qkv_body(l, x, vec, w, low, up, q, kv, red_out, red, normed, buf, sem):
    copies = []
    for i in range(NARROW):
        copies.append(pltpu.make_async_copy(w.at[l, i], buf.at[i // 2, :, columns(i % 2, 384)], sem.at[i]))
        copies[-1].start()
    for copy in copies:
        copy.wait()
    v = Vectors(vec, l)
    qkv_stage(x, v.row("gain1"), v.row("shift1"), buf, Strips(v.qkv), low.at[l], up.at[l], q, kv, red, red_out, normed)


def qkv_kernel(l, x, vec, w, low, up):
    tokens, dim = x.shape
    return kernel(
        functools.partial(qkv_body, l), "qkv",
        [(x, False), (vec, False), (w, True), (low, False), (up, False)],
        [((NARROW, tokens, 128), BF16, False), ((NARROW, tokens, 256), BF16, False), ((low.shape[1], tokens), BF16, False)],
        [pltpu.VMEM((tokens, low.shape[1]), BF16), pltpu.VMEM((tokens, dim), BF16), pltpu.VMEM((NARROW // 2, dim, 768), BF16), pltpu.SemaphoreType.DMA((NARROW,))],
    )


def attend_body(group, g_ref, q, *refs):
    held = positions(group)
    kvs, (out, lse) = refs[:group], refs[group:]
    bias = pair_bias(held, g_ref[0])
    each(NARROW, lambda i: attend_strip(held, bias, i, q, kvs, out, lse))


def attend_kernel(group, g, q, kvs):
    tokens = q.shape[1]
    return pl.pallas_call(
        functools.partial(attend_body, group),
        out_shape=[shape_of((tokens, NARROW * 128), BF16), shape_of((NARROW, 8, tokens), F32)],
        in_specs=[pl.BlockSpec(memory_space=pltpu.SMEM)] + [pl.BlockSpec(memory_space=pltpu.VMEM)] * (group + 1),
        out_specs=[pl.BlockSpec(memory_space=pltpu.VMEM)] * 2,
        compiler_params=PARAMS,
        name="attend",
    )(g, q, *kvs)


def mlp_body(l, x, att, vec, wp, wu, wd, *refs):
    low_proj, up_proj, low_up, up_up, low_down, up_down = [ref.at[l] for ref in refs[:6]]
    mid, result, hidden, reds, red, red_up, normed, active, bp, bu, bd, sem = refs[6:]
    copies = []
    for n, (src, dst) in enumerate(((wp.at[l], bp), (wu.at[l], bu), (wd.at[l], bd))):
        copies.append(pltpu.make_async_copy(src, dst, sem.at[n]))
        copies[-1].start()
    v = Vectors(vec, l)
    copies[0].wait()
    proj_stage(
        x, att, bp, v.row("proj"), low_proj, up_proj, v.row("gain2"), v.row("shift2"), low_up,
        mid, normed, red, reds.at[0], red_up, reds.at[1],
    )
    copies[1].wait()
    each(NARROW, lambda i: up_strip(i, normed, bu, Strips(v.up), red_up, up_up, hidden, active))
    copies[2].wait()

    def put(n, value):
        if len(result.shape) == 2:
            result[:, columns(n, 256)] = value
        else:
            for m in range(2):
                result[2 * n + m] = value[:, m * 128 : (m + 1) * 128].astype(BF16)

    keep(dot(active[...], low_down[...], TURNED), red, reds.at[2])
    down_stage(mid, active, bd, v.row("down"), up_down, red, put)


def mlp_kernel(l, final, x, att, vec, wp, wu, wd, tables):
    tokens, dim = x.shape
    hidden = wd.shape[1]
    rank = tables[0].shape[1]
    result = ((NARROW, tokens, 128), BF16, False) if final else ((tokens, dim), F32, False)
    return kernel(
        functools.partial(mlp_body, l), "mlp",
        [(x, False), (att, False), (vec, False), (wp, True), (wu, True), (wd, True)] + [(t, False) for t in tables],
        [((tokens, dim), F32, False), result, ((tokens, hidden), BF16, False), ((3, rank, tokens), BF16, False)],
        [
            pltpu.VMEM((tokens, rank), BF16), pltpu.VMEM((tokens, rank), BF16),
            pltpu.VMEM((tokens, dim), BF16), pltpu.VMEM((tokens, hidden), BF16), pltpu.VMEM(wp.shape[1:], BF16),
            pltpu.VMEM(wu.shape[1:], BF16), pltpu.VMEM(wd.shape[1:], BF16), pltpu.SemaphoreType.DMA((3,)),
        ],
    )


def mlp_back_stage(vec, grad, hidden, g_hid, mid, att, low, total, wp, wu, wd, reds, t, grads, g_mid, waits):
    low[...] = grad[...].astype(BF16)
    g_red = dot(low[...], t["up_down"], TURNED).astype(BF16)
    rank = g_red.shape[1]
    waits("hidden")
    waits("down")
    waits("up")
    units = wu.shape[2]
    total[...] = jnp.zeros_like(total)

    def strip(i):
        cols = columns(i, units)
        active, slope = gelu_parts(hidden[:, cols].astype(F32))
        hidden[:, cols] = active.astype(BF16)
        g_active = dot(low[...], wd[cols, :], TURNED) + dot(g_red, t["low_down"][:, cols])
        g_hid[:, cols] = (g_active * slope).astype(BF16)
        total[...] += dot(g_hid[:, cols], wu[i], TURNED)

    each(NARROW, strip)

    def give(at, value):
        size = value.shape[1] // NARROW
        for i in range(NARROW):
            grads[i, :, at : at + size] = value[:, i * size : (i + 1) * size].astype(BF16)

    give(384 + 2 * units, dot(reds[3], low[...]))
    give(384 + units, dot(g_red, hidden[...], CROSS))
    give(384, dot(reds[2], g_hid[...]))
    g_hid[:, :rank] = dot(g_hid[...], t["up_up"][...], TURNED).astype(BF16)
    waits("mid")
    gain, shift = vec.row("gain2"), vec.row("shift2")
    dim = mid.shape[1]

    def norm(rows):
        scaled, inverse = norm_parts(mid[rows, :])
        hidden[rows, :dim] = (scaled * gain + shift).astype(BF16)
        g_normed = total[rows, :] + dot(g_hid[rows, :rank], t["low_up"])
        value = grad[rows, :] + norm_grad(g_normed, scaled, inverse, gain)
        g_mid[rows, :] = value
        low[rows, :] = value.astype(BF16)

    by_rows(mid.shape[0], norm)
    give(256, dot(g_hid[:, :rank], hidden[:, :dim], CROSS))
    give(128, dot(reds[1], low[...]))
    g_red_proj = dot(low[...], t["up_proj"], TURNED).astype(BF16)
    waits("att")
    waits("proj")
    give(0, dot(g_red_proj, att[...], CROSS))
    low[...] = (dot(low[...], wp[...], TURNED) + dot(g_red_proj, t["low_proj"])).astype(BF16)


def qkv_back_stage(vec, x, g_mid, gq, parts, total, g_red, normed, wq, red, low, up, grads, put, waits):
    total[...] = jnp.zeros_like(total)
    waits("gq")
    waits("qkv")

    def pair(j, small):
        pieces = []
        for i in (2 * j, 2 * j + 1):
            g_kv = sum(part[i].astype(F32) for part in parts).astype(BF16)
            g_mixed = jnp.concatenate([gq[i], g_kv], axis=1)
            grads[i, :, 128:512] = dot(red[...], g_mixed).astype(BF16)
            small = small + dot(g_mixed, up[i], TURNED)
            pieces.append(g_mixed)
        total[...] += dot(jnp.concatenate(pieces, axis=1), wq[j], TURNED)
        return small

    rank, tokens = red.shape
    small = lax.fori_loop(0, NARROW // 2, pair, jnp.zeros((tokens, rank), F32))
    g_low_rank = small.astype(BF16)
    g_red[...] = g_low_rank
    waits("x")
    waits("g_mid")
    gain, shift = vec.row("gain1"), vec.row("shift1")

    def norm(rows):
        scaled, inverse = norm_parts(x[rows, :].astype(F32))
        normed[rows, :] = (scaled * gain + shift).astype(BF16)
        g_normed = total[rows, :] + dot(g_red[rows, :], low[...])
        put(rows, g_mid[rows, :] + norm_grad(g_normed, scaled, inverse, gain))

    by_rows(tokens, norm)
    g_low = dot(g_low_rank, normed[...], CROSS).astype(BF16)
    for i in range(NARROW):
        grads[i, :, :128] = g_low[:, i * 128 : (i + 1) * 128]


def back_body(lq, lm, group, names, *refs):
    R = dict(zip(names, refs))
    held = positions(group)
    sem, started = R["sem"], {}

    def waits(name):
        for copy in started.pop(name, ()):
            copy.wait()

    count = [0]

    def begin(name, *copies):
        started[name] = []
        for src, dst in copies:
            copy = pltpu.make_async_copy(src, dst, sem.at[count[0]])
            count[0] += 1
            copy.start()
            started[name].append(copy)

    if lq is not None:
        begin("gq", (R["in_gq"], R["gq"]), *[(R["in_part%d" % j], R["part%d" % j]) for j in range(group)])
        begin("qkv", *[
            (R["w_qkv"].at[lq, i], R["wq"].at[i // 2, :, columns(i % 2, 384)]) for i in range(NARROW)
        ])
        begin("x", (R["in_x"], R["x"]))
        begin("g_mid", (R["in_g_mid"], R["total2"]))
    else:
        begin("cotangent", (R["cotangent"], R["low"]))
    if lm is not None:
        begin("hidden", (R["hiddens"].at[lm], R["hidden"]))
        begin("down", *[
            (R["w_down"].at[lm, pl.ds(n * 1024, 1024)], R["wd"].at[pl.ds(n * 1024, 1024)])
            for n in range(R["wd"].shape[0] // 1024)
        ])
        begin("up", *[(R["w_up"].at[lm, i], R["wu"].at[i]) for i in range(NARROW)])
        begin("proj", (R["w_proj"].at[lm], R["wp"]))
        begin("att", (R["atts"].at[lm], R["att"]))
        begin("kv", (R["kvs"].at[lm], R["kv"]), (R["peers"].at[lm], R["peer"]), (R["lses"].at[lm], R["lse"]))
    if lq is not None:
        vec = Vectors(R["vec"], lq)

        def put(rows, value):
            if lm is None:
                for i in range(NARROW):
                    R["out"][i, rows, :] = value[:, i * 128 : (i + 1) * 128].astype(BF16)
            else:
                R["grad"][rows, :] = value

        qkv_back_stage(
            vec, R["x"], R["total2"], R["gq"], [R["part%d" % j] for j in range(group)], R["total"],
            R["g_red"], R["low"], R["wq"],
            R["reds"].at[lq, 0], R["low_qkv"].at[lq], R["up_qkv"].at[lq], R["grads_qkv"], put, waits,
        )
    else:
        waits("cotangent")
        R["grad"][...] = R["low"][...].astype(F32)
    if lm is None:
        return
    begin("q", (R["qs"].at[lm], R["gq"]))
    begin("mid", (R["mids"].at[lm], R["x" if lq is not None and R["x"].dtype == F32 else "mid"]))
    mid = R["x" if lq is not None and R["x"].dtype == F32 else "mid"]
    t = {name: R[name].at[lm] for name in TABLES}
    vec = Vectors(R["vec"], lm)
    mlp_back_stage(
        vec, R["grad"], R["hidden"], R["g_hid"], mid, R["att"], R["low"], R["total"], R["wp"], R["wu"], R["wd"],
        R["reds"].at[lm], {k: (v if k in ("low_down", "up_up") else v[...]) for k, v in t.items() if "qkv" not in k},
        R["grads_mlp"], R["total2"], waits,
    )
    out_mid = pltpu.make_async_copy(R["total2"], R["out_g_mid"], sem.at[count[0]])
    out_mid.start()
    waits("q")
    waits("kv")
    bias = pair_bias(held, R["g"][0])
    kvs = [R["kv"]] + [R["peer"].at[j] for j in range(group - 1)]
    gkvs = [R["part%d" % j] for j in range(group)]
    each(NARROW, lambda i: attend_back_strip(
        held, bias, i, R["gq"], R["lse"], R["att"], R["low"], kvs, R["gq"], gkvs
    ))
    outs = [(R["gq"], R["out_gq"])] + [(R["part%d" % j], R["out_part%d" % j]) for j in range(group)]
    copies = [pltpu.make_async_copy(src, dst, sem.at[count[0] + 1 + n]) for n, (src, dst) in enumerate(outs)]
    for copy in copies:
        copy.start()
    for copy in copies:
        copy.wait()
    out_mid.wait()


def back_kernel(lq, lm, group, g, outs, tables, carried):
    layers, _, dim, _ = outs["qkv"].shape
    hidden = outs["down"].shape[1]
    tokens = outs["tokens"].shape[0]
    rank = tables[0].shape[1]
    strip = (NARROW, tokens)
    inputs = [("g", g, pl.BlockSpec(memory_space=pltpu.SMEM))]
    near, far = pl.BlockSpec(memory_space=pltpu.VMEM), pl.BlockSpec(memory_space=pltpu.HBM)
    inputs += [(name, table, near) for name, table in zip(TABLES, tables)]
    inputs += [("vec", outs["vec"], near), ("reds", outs["reds"], near)]
    outputs, scratch = [], []

    def vmem(name, shape, kind):
        scratch.append((name, pltpu.VMEM(shape, kind)))

    vmem("gq", strip + (128,), BF16)
    for j in range(group):
        vmem("part%d" % j, strip + (256,), BF16)
    vmem("total", (tokens, dim), F32)
    vmem("total2", (tokens, dim), F32)
    vmem("low", (tokens, dim), BF16)
    if lq is not None:
        g_mid, gq, parts = carried
        x = outs["tokens"] if lq == 0 else outs["saved_x"][lq - 1]
        inputs += [("in_gq", gq, far), ("in_g_mid", g_mid, far), ("in_x", x, far), ("w_qkv", outs["qkv"], far)]
        inputs += [("in_part%d" % j, part, far) for j, part in enumerate(parts)]
        vmem("wq", (NARROW // 2, dim, 768), BF16)
        vmem("g_red", (tokens, rank), BF16)
        vmem("x", (tokens, dim), x.dtype)
        outputs.append(("grads_qkv", (NARROW, rank, 512), BF16, near))
        if lm is None:
            outputs.append(("out", strip + (128,), BF16, near))
    if lm is not None:
        if lq is None:
            inputs.append(("cotangent", outs["cotangent"], far))
        for name in ("hidden", "mid", "att", "q", "kv", "peer", "lse"):
            inputs.append((name + "s", outs["saved_" + name], far))
        inputs += [("w_" + name, outs[name], far) for name in ("proj", "up", "down")]
        vmem("wp", (dim, dim), BF16)
        vmem("wu", (NARROW, dim, hidden // NARROW), BF16)
        vmem("wd", (hidden, dim), BF16)
        vmem("grad", (tokens, dim), F32)
        if lq is None or x.dtype != F32:
            vmem("mid", (tokens, dim), F32)
        vmem("att", (tokens, dim), BF16)
        vmem("hidden", (tokens, hidden), BF16)
        vmem("g_hid", (tokens, hidden), BF16)
        vmem("kv", strip + (256,), BF16)
        vmem("peer", (group - 1,) + strip + (256,), BF16)
        vmem("lse", (NARROW, 8, tokens), F32)
        outputs.append(("grads_mlp", (NARROW, rank, 512 + 2 * hidden // NARROW), BF16, near))
        outputs += [("out_g_mid", (tokens, dim), F32, far), ("out_gq", strip + (128,), BF16, far)]
        outputs += [("out_part%d" % j, strip + (256,), BF16, far) for j in range(group)]
    scratch.append(("sem", pltpu.SemaphoreType.DMA((64,))))
    names = [x[0] for x in inputs] + [x[0] for x in outputs] + [x[0] for x in scratch]
    made = pl.pallas_call(
        functools.partial(back_body, lq, lm, group, tuple(names)),
        out_shape=[shape_of(shape, kind) for _, shape, kind, _ in outputs],
        in_specs=[spec for _, _, spec in inputs],
        out_specs=[spec for _, _, _, spec in outputs],
        scratch_shapes=[shape for _, shape in scratch],
        compiler_params=PARAMS,
        name="back",
    )(*[array for _, array, _ in inputs])
    return dict(zip([x[0] for x in outputs], made))


SITES = {"mlp": (1, 1, 2, 2, 3, 3), "qkv": (0, 0)}


def backward_body(layers, group, n_row, n_col, names, *refs):
    R = dict(zip(names, refs))
    held = positions(group)
    per = BLOCKS // group
    r, c = lax.axis_index("row"), lax.axis_index("col")
    g = lax.rem(c, group)
    seqs = n_col // group
    tokens = per * BLOCK
    bias = pair_bias(held, g)

    def row_peer(s):
        return (lax.rem(r + s, n_row), c)

    def col_peer(d):
        return lax.rem(c + d, n_col)

    peers = [row_peer(s) for s in range(1, n_row)] + [(r, col_peer(d)) for d in range(1, n_col)]
    barrier = pltpu.get_barrier_semaphore()
    for peer in peers:
        pl.semaphore_signal(barrier, inc=1, device_id=peer, device_id_type=MESH)
    pl.semaphore_wait(barrier, len(peers))

    sem, started, count = R["sem"], {}, [0]

    def begin(name, *copies):
        started[name] = []
        for src, dst in copies:
            copy = pltpu.make_async_copy(src, dst, sem.at[count[0]])
            count[0] += 1
            copy.start()
            started[name].append(copy)

    def waits(name):
        for copy in started.pop(name, ()):
            copy.wait()

    far = [0]

    def remote(src, dst, n, peer):
        return pltpu.make_async_remote_copy(
            src_ref=src, dst_ref=dst, send_sem=R["out_sem"].at[n], recv_sem=R["in_sem"].at[n],
            device_id=peer, device_id_type=MESH,
        )

    def new_far():
        far[0] += 1
        return far[0] - 1

    def columns_start(n, src):
        to, at = R["columns"].at[n], new_far()
        start = (c // group) * LEN
        places = [pl.ds(pl.multiple_of(start + place_of(group, g, b) * BLOCK, BLOCK), BLOCK) for b in range(per)]
        begin("columns%d" % n, *[(src.at[c, pl.ds(b * BLOCK, BLOCK)], to.at[places[b]]) for b in range(per)])
        for d in range(1, n_col):
            for b in range(per):
                remote(src.at[col_peer(d), pl.ds(b * BLOCK, BLOCK)], to.at[places[b]], at, (r, col_peer(d))).start()
        return at

    def columns_end(n, at):
        waits("columns%d" % n)
        ref = R["columns"].at[n, pl.ds(0, (n_col - 1) * tokens)]
        remote(ref, ref, at, (r, col_peer(1))).wait()

    ends = {}

    def spread(kind, l):
        src, land, at = R["grads_" + kind], R["land_" + kind].at[l], new_far()
        begin("own_%s%d" % (kind, l), (src.at[c], land.at[c]))
        for d in range(1, n_col):
            remote(src.at[col_peer(d)], land.at[c], at, (r, col_peer(d))).start()
        ends["spread", kind, l] = at

    def spread_sent(kind, l):
        if l < layers:
            ref = R["land_" + kind].at[l, pl.ds(0, n_col - 1)]
            remote(ref, ref, ends["spread", kind, l], (r, col_peer(1))).wait_send()

    def add(kind, l):
        land, stage, total = R["land_" + kind].at[l], R["stage_" + kind], R["sum_" + kind]
        ref = land.at[pl.ds(0, n_col - 1)]
        remote(ref, ref, ends["spread", kind, l], (r, col_peer(1))).wait_recv()
        waits("own_%s%d" % (kind, l))
        begin("stage", (land, stage))
        add_sent(kind, l + 1)
        waits("stage")
        for q in range(seqs):
            value = sum(stage[q * group + n].astype(F32) for n in range(group))
            total[q] = value.astype(BF16)
        parts, at = R["parts_" + kind], new_far()
        begin("part_%s%d" % (kind, l), (total, parts.at[l, r]))
        for q in range(1, n_row):
            remote(total, parts.at[l, r], at, row_peer(q)).start()
        ends["add", kind, l] = at

    def added(kind, l):
        ref = R["parts_" + kind].at[l, pl.ds(0, n_row - 1)]
        return remote(ref, ref, ends["add", kind, l], row_peer(1))

    def add_sent(kind, l):
        if l < layers:
            waits("part_%s%d" % (kind, l))
            added(kind, l).wait_send()

    def part_copy(l, j, strips, at):
        to = c - g + lax.rem(g - j + group, group)
        return remote(R["part%d" % j].at[strips], R["in_part"].at[l, j - 1, strips], at, (r, to))

    def back_strip(l, i, at):
        kvs = [R["kv"]] + [R["peer"].at[j] for j in range(group - 1)]
        gkvs = [R["part%d" % j] for j in range(group)]
        attend_back_strip(held, bias, i, R["gq"], R["lse"], R["att"], R["low"], kvs, R["gq"], gkvs)
        for j in range(1, group):
            part_copy(l, j, pl.ds(i, 1), at[j]).start()

    def load_qkv(l):
        begin("qkv", *[
            (R["w_qkv"].at[l, i], R["wq"].at[i // 2, :, columns(i % 2, 384)]) for i in range(NARROW)
        ])

    def load_mlp(l):
        begin("hidden", (R["hiddens"].at[l], R["hidden"]))
        begin("down", *[
            (R["w_down"].at[l, pl.ds(n * 1024, 1024)], R["wd"].at[pl.ds(n * 1024, 1024)])
            for n in range(R["wd"].shape[0] // 1024)
        ])
        begin("up", *[(R["w_up"].at[l, i], R["wu"].at[i]) for i in range(NARROW)])
        begin("proj", (R["w_proj"].at[l], R["wp"]))

    def load_attention(l):
        begin("mid", (R["mids"].at[l], R["mid"]))
        begin("att", (R["atts"].at[l], R["att"]))
        begin("q", (R["qs"].at[l], R["gq"]))
        begin("kv", (R["kvs"].at[l], R["kv"]), (R["peers"].at[l], R["peer"]), (R["lses"].at[l], R["lse"]))

    last = layers - 1
    begin("cotangent", (R["cotangent"], R["low"]))
    load_mlp(last)
    load_attention(last)
    load_qkv(last)
    at_result = columns_start(0, R["result"])
    at_ids = new_far()
    begin("ids", (R["ids"], R["all_ids"].at[r]))
    for q in range(1, n_row):
        remote(R["ids"], R["all_ids"].at[r], at_ids, row_peer(q)).start()
    waits("cotangent")

    def widen(rows):
        R["grad"][rows, :] = R["low"][rows, :].astype(F32)

    by_rows(tokens, widen)
    for l in reversed(range(layers)):
        t = {name: R[name].at[l] for name in TABLES if "qkv" not in name}
        vec = Vectors(R["vec"], l)
        spread_sent("mlp", l + 1)
        mlp_back_stage(
            vec, R["grad"], R["hidden"], R["g_hid"], R["mid"], R["att"], R["low"], R["total"], R["wp"], R["wu"],
            R["wd"], R["reds"].at[l], {k: (v if k in ("low_down", "up_up") else v[...]) for k, v in t.items()},
            R["grads_mlp"], R["total2"], waits,
        )
        spread("mlp", l)
        if l < last:
            add("qkv", l + 1)
        if l > 0:
            load_mlp(l - 1)
        begin("x", (R["tokens"] if l == 0 else R["xs"].at[l - 1], R["x0"] if l == 0 else R["mid"]))
        waits("q")
        waits("kv")
        at = [new_far() for _ in range(group)]
        each(NARROW, lambda i: back_strip(l, i, at))
        add("mlp", l)
        every = pl.ds(0, NARROW)
        begin("parts", *[])
        for j in range(1, group):
            part_copy(l, j, every, at[j]).wait()
        begin("parts", *[(R["in_part"].at[l, j], R["peer"].at[j]) for j in range(group - 1)])
        waits("parts")
        parts = [R["part0"]] + [R["peer"].at[j] for j in range(group - 1)]
        spread_sent("qkv", l + 1)

        def put(rows, value):
            if l > 0:
                R["grad"][rows, :] = value
            else:
                for i in range(NARROW):
                    R["part0"][i, rows, :128] = value[:, i * 128 : (i + 1) * 128].astype(BF16)

        qkv_back_stage(
            vec, R["x0"] if l == 0 else R["mid"], R["total2"], R["gq"], parts, R["total"], R["g_red"], R["low"],
            R["wq"], R["reds"].at[l, 0], R["low_qkv"].at[l], R["up_qkv"].at[l], R["grads_qkv"], put, waits,
        )
        spread("qkv", l)
        if l > 0:
            load_qkv(l - 1)
            load_attention(l - 1)
    at_grad = columns_start(1, R["part0"].at[:, :, pl.ds(0, 128)])
    add("qkv", 0)
    columns_end(0, at_result)
    columns_end(1, at_grad)
    waits("ids")
    rest = R["all_ids"].at[pl.ds(0, n_row - 1)]
    remote(rest, rest, at_ids, row_peer(1)).wait()
    for kind in ("mlp", "qkv"):
        spread_sent(kind, 0)
        add_sent(kind, 0)
        for l in range(layers):
            added(kind, l).wait_recv()


def backward(n_row, n_col, group, outs, tables, ids):
    layers, _, dim, _ = outs["qkv"].shape
    hidden = outs["down"].shape[1]
    mine = outs["tokens"].shape[0]
    rank = tables[0].shape[1]
    seqs = n_col // group
    strip = (NARROW, mine)
    near, far = pl.BlockSpec(memory_space=pltpu.VMEM), pl.BlockSpec(memory_space=pltpu.HBM)
    inputs = [(name, table, near) for name, table in zip(TABLES, tables)]
    inputs += [("vec", outs["vec"], near), ("reds", outs["reds"], near), ("ids", ids, far)]
    for name in ("hidden", "mid", "att", "q", "kv", "peer", "lse", "x"):
        inputs.append((name + "s", outs["saved_" + name], far))
    inputs += [("w_" + name, outs[name], far) for name in KINDS]
    inputs += [(name, outs[name], far) for name in ("tokens", "cotangent", "result")]
    sizes = {"mlp": 512 + 2 * hidden // NARROW, "qkv": 512}
    outputs = [
        ("columns", (2, n_col * mine, 128), BF16, far),
        ("all_ids", (n_row,) + ids.shape, F32, far),
        ("in_part", (layers, group - 1) + strip + (256,), BF16, far),
    ]
    scratch = [
        ("gq", strip + (128,), BF16), ("kv", strip + (256,), BF16), ("peer", (group - 1,) + strip + (256,), BF16),
        ("lse", (NARROW, 8, mine), F32), ("total", (mine, dim), F32), ("total2", (mine, dim), F32),
        ("grad", (mine, dim), F32), ("mid", (mine, dim), F32), ("low", (mine, dim), BF16), ("att", (mine, dim), BF16),
        ("x0", (mine, dim), BF16), ("hidden", (mine, hidden), BF16), ("g_hid", (mine, hidden), BF16),
        ("g_red", (mine, rank), BF16), ("wq", (NARROW // 2, dim, 768), BF16), ("wp", (dim, dim), BF16),
        ("wu", (NARROW, dim, hidden // NARROW), BF16), ("wd", (hidden, dim), BF16),
    ]
    scratch += [("part%d" % j, strip + (256,), BF16) for j in range(group)]
    for kind, size in sizes.items():
        outputs.append(("land_" + kind, (layers, n_col, rank, size), BF16, far))
        outputs.append(("parts_" + kind, (layers, n_row, seqs, rank, size), BF16, far))
        scratch.append(("grads_" + kind, (NARROW, rank, size), BF16))
        scratch.append(("stage_" + kind, (n_col, rank, size), BF16))
        scratch.append(("sum_" + kind, (seqs, rank, size), BF16))
    scratch = [(name, pltpu.VMEM(shape, kind)) for name, shape, kind in scratch]
    scratch += [
        ("sem", pltpu.SemaphoreType.DMA((48 * layers + 16,))),
        ("out_sem", pltpu.SemaphoreType.DMA((8 * layers + 8,))),
        ("in_sem", pltpu.SemaphoreType.DMA((8 * layers + 8,))),
    ]
    names = [x[0] for x in inputs] + [x[0] for x in outputs] + [x[0] for x in scratch]
    made = pl.pallas_call(
        functools.partial(backward_body, layers, group, n_row, n_col, tuple(names)),
        out_shape=[shape_of(shape, kind) for _, shape, kind, _ in outputs],
        in_specs=[spec for _, _, spec in inputs],
        out_specs=[spec for _, _, _, spec in outputs],
        scratch_shapes=[shape for _, shape in scratch],
        compiler_params=pltpu.CompilerParams(
            collective_id=1, has_side_effects=True, vmem_limit_bytes=62 * 2**20
        ),
        name="backward",
    )(*[array for _, array, _ in inputs])
    return dict(zip([x[0] for x in outputs], made))


def place_body(sizes, weights, *refs):
    parts, outs = refs[: len(sizes)], refs[len(sizes) :]
    adapters = outs[0].shape[1]
    sequences = parts[0].shape[1]
    l = pl.program_id(0)
    n = 0
    for part, (kind, pieces) in zip(parts, sizes):
        at = 0
        for site, size in zip(SITES[kind], pieces):
            for a in range(adapters):
                value = 0.0
                for q in range(sequences):
                    value = value + part[0, q, :, at : at + size].astype(F32) * weights[a, site * sequences + q]
                outs[n][0, a] = value
            at += size
            n += 1


def place(parts, sizes, weights):
    layers, sequences, rank, _ = parts[0].shape
    adapters = weights.shape[0]
    widths = [size for _, pieces in sizes for size in pieces]
    return pl.pallas_call(
        functools.partial(place_body, sizes),
        grid=(layers,),
        out_shape=[shape_of((layers, adapters, rank, size), F32) for size in widths],
        in_specs=[pl.BlockSpec(memory_space=pltpu.SMEM)]
        + [pl.BlockSpec((1,) + part.shape[1:], lambda l: (l, 0, 0, 0)) for part in parts],
        out_specs=[pl.BlockSpec((1, adapters, rank, size), lambda l: (l, 0, 0, 0)) for size in widths],
        compiler_params=PARAMS,
        name="place",
    )(weights, *parts)


def to_rows_body(held, x, out):
    n = 0
    for s in range(x.shape[0] // (len(held) * len(held[0]))):
        for g in range(len(held)):
            for place in held[g]:
                start = (s * BLOCKS + place) * BLOCK
                out[start : start + BLOCK, :] = x[n].astype(F32)
                n += 1


def to_rows(held, x):
    blocks, _, width = x.shape
    return pl.pallas_call(
        functools.partial(to_rows_body, held),
        out_shape=shape_of((blocks * BLOCK, width), F32),
        compiler_params=PARAMS,
        name="to_rows",
    )(x)


def pick_body(count, ids, *refs):
    for ref, out in zip(refs[:count], refs[count:]):
        out[...] = ref[...]


def pick_tables(ids, tables):
    def chosen(site, shape):
        return pl.BlockSpec((shape[0], None) + shape[2:], lambda i, ids: (0, ids[site], 0, 0))

    return pl.pallas_call(
        functools.partial(pick_body, len(tables)),
        grid_spec=pltpu.PrefetchScalarGridSpec(
            num_scalar_prefetch=1,
            grid=(1,),
            in_specs=[chosen(site, table.shape) for site, table in tables],
            out_specs=[
                pl.BlockSpec(table.shape[:1] + table.shape[2:], lambda i, ids: (0, 0, 0)) for _, table in tables
            ],
        ),
        out_shape=[shape_of(table.shape[:1] + table.shape[2:], BF16) for _, table in tables],
        compiler_params=PARAMS,
        name="pick",
    )(ids, *[table for _, table in tables])


def shards(mesh_shape, *args):
    (
        tokens, cotangent, adapter_ids, qkv_weight, qkv_bias, proj_weight, proj_bias,
        up_weight, up_bias, down_weight, down_bias, first_gain, first_shift, second_gain,
        second_shift, qkv_lower, qkv_raise, proj_lower, proj_raise, up_lower, up_raise,
        down_lower, down_raise,
    ) = args
    n_row, n_col = mesh_shape
    layers, adapters, dim, rank = qkv_lower.shape
    rows, width = tokens.shape
    units = up_weight.shape[2]
    seqs = rows // LEN
    group = n_col // seqs
    held = positions(group)
    per = BLOCKS // group
    mine = per * BLOCK
    merge = 128 // width
    c = lax.axis_index("col")
    g = lax.rem(c, group)
    ids = lax.dynamic_index_in_dim(adapter_ids, c // group, 0, keepdims=False)

    def line(pieces):
        row = jnp.concatenate([piece.reshape(layers, -1).astype(F32) for piece in pieces], axis=1)
        return jnp.pad(row, ((0, 0), (0, 512 - row.shape[1])))

    vector = jnp.stack(
        [
            line([qkv_bias]), line([up_bias]), line([proj_bias, down_bias, first_gain, first_shift]),
            line([second_gain, second_shift]),
        ],
        axis=1,
    ).reshape(layers * 4, 512)

    def turned(table):
        return jnp.swapaxes(table, 2, 3)

    tables = pick_tables(ids, [
        (0, turned(qkv_lower)), (1, turned(proj_lower)), (1, proj_raise), (2, turned(up_lower)), (2, up_raise),
        (3, turned(down_lower)), (3, down_raise),
    ])
    raise_qkv = lax.dynamic_index_in_dim(qkv_raise, ids[0], 1, keepdims=False)
    raise_qkv = raise_qkv.reshape(layers, rank, 3, NARROW, 128).transpose(0, 3, 1, 2, 4)
    tables = [tables[0], raise_qkv.reshape(layers, NARROW, rank, 384)] + list(tables[1:])
    fused = FUSED and width == 128
    outs = gather_inputs(
        n_row, n_col, group, qkv_weight.reshape(layers, -1, 3 * width), proj_weight, up_weight,
        down_weight, tokens, cotangent, vector, tables if fused else None
    )
    g_one = g.reshape(1)

    def peer_values(x, step):
        pairs = [(q, q - q % group + (q + step) % group) for q in range(n_col)]
        return lax.ppermute(x, "col", pairs)

    def to_columns(x):
        if merge > 1:
            x = x.reshape(NARROW, mine, merge, width).transpose(0, 2, 1, 3).reshape(n_col, mine, width)
        x = lax.all_to_all(x, "col", split_axis=0, concat_axis=0, tiled=True)
        return to_rows(held, x.reshape(n_col * per, BLOCK, width))

    if not fused:
        x = outs["tokens"].astype(F32)
        kept = {name: [] for name in SAVED + ("reds",)}
        for l in range(layers):
            q, kv, red = qkv_kernel(l, x, outs["vec"], outs["qkv"], tables[0], tables[1])
            kvs = [kv] + [peer_values(kv, s) for s in range(1, group)]
            att, lse = attend_kernel(group, g_one, q, kvs)
            mid, x, hidden, reds = mlp_kernel(
                l, l == layers - 1, x, att, outs["vec"], outs["proj"], outs["up"], outs["down"], tables[2:]
            )
            reds = jnp.concatenate([red[None], reds])
            peer = jnp.stack(kvs[1:]) if group > 1 else kv[None][:0]
            for name, value in zip(SAVED + ("reds",), (q, kv, peer, att, lse, mid, hidden, x, reds)):
                kept[name].append(value)
        for name in SAVED:
            outs["saved_" + name] = jnp.stack(kept[name][: layers - 1] if name == "x" else kept[name])
        outs["reds"] = jnp.stack(kept["reds"])
        outs["result"] = x
    if fused:
        ids_rows = jnp.pad(adapter_ids.astype(F32), ((0, 8 - seqs), (0, 128 - adapter_ids.shape[1])))
        made = backward(n_row, n_col, group, outs, tables, ids_rows)
        every = made["all_ids"][:, :seqs, : adapter_ids.shape[1]].reshape(n_row * seqs, -1).T.reshape(-1)
        weights = (every[None, :] == jnp.arange(adapters, dtype=F32)[:, None]).astype(F32)
        wide = units
        sizes = (("qkv", (128, 384)), ("mlp", (128, 128, 128, wide, wide, 128)))
        parts = [made["parts_" + kind].reshape(layers, n_row * seqs, rank, -1) for kind, _ in sizes]
        sums = place(parts, sizes, weights)
        final = [made["columns"][0].astype(F32), made["columns"][1].astype(F32)]
        for number, p in enumerate(sums):
            if number == 1:
                p = p.reshape(layers, adapters, rank, 3, width)
            elif number % 2 == 0:
                p = p.transpose(0, 1, 3, 2)
            final.append(p)
        return tuple(final)

    result = to_columns(outs["result"])

    onehot = (adapter_ids.T[:, :, None] == jnp.arange(adapters)[None, None, :]).astype(BF16)

    def all_rows(x):
        pairs = [[(q, (q + s) % n_row) for q in range(n_row)] for s in range(1, n_row)]
        return [x] + [lax.ppermute(x, "row", pair) for pair in pairs]

    onehots = jnp.concatenate(all_rows(onehot), axis=1)

    def collect(parts, named):
        if merge > 1:
            pieces, at = [], 0
            for _, size in named:
                piece = parts[:, :, at : at + size]
                at += size
                if size == 384:
                    piece = piece.reshape(NARROW, rank, 3, merge, width).transpose(0, 3, 1, 2, 4)
                else:
                    piece = piece.reshape(NARROW, rank, merge, size // merge).transpose(0, 2, 1, 3)
                pieces.append(piece.reshape(n_col, rank, size // merge))
            parts = jnp.concatenate(pieces, axis=2)
        parts = lax.all_to_all(parts, "col", split_axis=0, concat_axis=0, tiled=True)
        parts = parts.reshape((seqs, group) + parts.shape[1:]).astype(F32).sum(axis=1).astype(BF16)
        parts = jnp.concatenate(all_rows(parts), axis=0)
        sums, at = [], 0
        for site, size in named:
            piece = parts[:, :, at : at + size // merge]
            at += size // merge
            sums.append(jnp.einsum("sa,srn->arn", onehots[site], piece, preferred_element_type=F32))
        return sums

    wide = outs["down"].shape[1] // NARROW
    grads, carried = [None] * layers, None
    for l in reversed(range(layers + 1)):
        lq, lm = (l if l < layers else None), (l - 1 if l > 0 else None)
        made = back_kernel(lq, lm, group, g_one, outs, tables, carried)
        if lm is not None:
            grads[lm] = collect(made["grads_mlp"], [(1, 128), (1, 128), (2, 128), (2, wide), (3, wide), (3, 128)])
            parts = [made["out_part%d" % s] for s in range(group)]
            parts = [parts[0]] + [peer_values(parts[s], group - s) for s in range(1, group)]
            carried = (made["out_g_mid"], made["out_gq"], parts)
        if lq is not None:
            grads[lq] = collect(made["grads_qkv"], [(0, 128), (0, 384)]) + grads[lq]
    grad = made["out"]
    input_grad = to_columns(grad)

    final = []
    for number in range(8):
        p = jnp.stack([grads[l][number] for l in range(layers)])
        if number == 1:
            p = p.reshape(layers, adapters, rank, 3, width)
        elif number % 2 == 0:
            p = p.transpose(0, 1, 3, 2)
        final.append(p)
    return (result, input_grad) + tuple(final)


def solution(mesh):
    mesh_shape = (mesh.shape["row"], mesh.shape["col"])
    return jax.shard_map(
        functools.partial(shards, mesh_shape),
        mesh=mesh,
        in_specs=(
            P("row", "col"), P("row", "col"), P("row", None),
            P(None, "row", None, "col"), P(None, None, "col"),
            P(None, "col", "row"), P(None, "col"),
            P(None, "row", "col"), P(None, "col"),
            P(None, "col", "row"), P(None, "col"),
            P(None, "col"), P(None, "col"), P(None, "col"), P(None, "col"),
            P(), P(), P(), P(), P(), P(), P(), P(),
        ),
        out_specs=(
            P("row", "col"), P("row", "col"),
            P(None, None, "col", None), P(None, None, None, None, "col"),
            P(None, None, "col", None), P(None, None, None, "col"),
            P(None, None, "col", None), P(None, None, None, "col"),
            P(None, None, "col", None), P(None, None, None, "col"),
        ),
        check_vma=False,
    )
```

```python
import functools

import jax
import jax.numpy as jnp
from jax import lax
from jax.experimental import pallas as pl
from jax.experimental.pallas import tpu as pltpu
from jax.sharding import PartitionSpec as P

HD = 64
LEN = 1024
BLOCK = 256
BLOCKS = LEN // BLOCK
EPSILON = 1e-05
SCALE = HD**-0.5
ROOT = (2.0 / 3.141592653589793) ** 0.5
MESH = pl.DeviceIdType.MESH
F32 = jnp.float32
BF16 = jnp.bfloat16


ROW_FIRST = (("z", 0, 1), ("z", 1, 0))
ROW_SECOND = ((0, "z", 1), (1, "z", 0))
ORDERS = (
    {"qkv": (ROW_FIRST,), "proj": (ROW_SECOND,), "up": (ROW_FIRST,) * 2, "down": (ROW_SECOND, ROW_FIRST)},
    {"qkv": (ROW_SECOND,), "proj": (ROW_FIRST,), "up": (ROW_SECOND,) * 2, "down": (ROW_SECOND,) * 2},
)
CUTS = {kind: 2 * len(pairs) for kind, pairs in ORDERS[0].items()}
KINDS = ("qkv", "proj", "up", "down")
DEPTH = 4
FUSED = True
LINK = 90e3
DELAY, ROW_DELAY = 2.0, 4.0
FIRST = 12.0


def transfer_plan(order, n_row):
    masks, rows, steps = [0], False, []
    for d in order:
        if d == "z":
            steps += [(("z", hop), tuple(masks), rows) for hop in range(1, n_row)]
            rows = True
        else:
            steps.append((d, tuple(masks), rows))
            masks = masks + [m ^ d for m in masks]
    steps.append((None, tuple(masks), rows))
    return steps


def transfer_schedule(pieces, n_row, tasks):
    cost, parts = {}, {}
    for k, (name, order, size) in enumerate(pieces):
        parts.setdefault(name, set()).add(k)
        for p, (d, masks, rows) in enumerate(transfer_plan(order, n_row)[:-1]):
            axis = "z" if isinstance(d, tuple) else d
            cost[k, p] = (axis, 2 * len(masks) * (n_row if rows else 1) * size / LINK)
    ready = {d: [] for d, _ in cost.values()}
    free = {d: 0.0 if d == "z" else FIRST for d in ready}
    flight = {d: [] for d in ready}
    for k in range(len(pieces)):
        ready[cost[k, 0][0]].append((k, 0))
    tasks, left = list(tasks), {}
    for task in tasks:
        left[task[4]] = left.get(task[4], 0) + 1
    landed, staged, now, ops = {}, {}, 0.0, []

    def stage(name):
        kind, l = name
        if name in landed and name not in staged and landed[name] <= now and not left.get((kind, l - 1)):
            staged[name] = now + 3.0
            ops.append(("stage", kind, l))

    while tasks or any(ready.values()) or any(flight.values()):
        for d in ready:
            while ready[d] and len(flight[d]) < DEPTH:
                k, p = ready[d].pop(0)
                free[d] = max(now, free[d]) + cost[k, p][1]
                flight[d].append((free[d] + (ROW_DELAY if d == "z" else DELAY), k, p))
                ops.append(("start", k, p))
        if tasks:
            for name in list(landed):
                stage(name)
        events = [f for line in flight.values() for f in line]
        event = min(events) if events else None
        due = None
        if tasks:
            need = tasks[0][4]
            due = now if need is None else staged.get(need)
            if due is None and need in landed and not left.get((need[0], need[1] - 1)):
                due = landed[need]
        if due is not None and (event is None or max(due, now) < event[0]):
            now = max(due, now)
            need = tasks[0][4]
            if need is not None and need not in staged:
                continue
            name, l, part, micros, _ = tasks.pop(0)
            left[need] -= 1
            now += micros
            ops.append(("task", name, (l, part)))
            continue
        now, k, p = max(now, event[0]), event[1], event[2]
        d = cost[k, p][0]
        flight[d].remove(event)
        ops.append(("wait", k, p))
        if (k, p + 1) in cost:
            later = ready[cost[k, p + 1][0]]
            later.append((k, p + 1))
            later.sort()
        else:
            name = pieces[k][0]
            parts[name].discard(k)
            if not parts[name]:
                landed[name] = now + 4.0
    return ops


def place_of(group, g, b):
    if group == 2:
        return g + b * (BLOCKS - 1 - 2 * g)
    return g * (BLOCKS // group) + b


def positions(group):
    per = BLOCKS // group
    return tuple(tuple(place_of(group, g, b) for b in range(per)) for g in range(group))


NARROW = 8
CROSS = ((0,), (0,))
TURNED = ((1,), (1,))


def dot(a, b, dims=((1,), (0,))):
    return lax.dot_general(a, b, (dims, ((), ())), preferred_element_type=F32)


def columns(i, size=128):
    if isinstance(i, int):
        return pl.ds(i * size, size)
    return pl.ds(pl.multiple_of(i * size, size), size)


def norm_parts(x):
    center = x - jnp.mean(x, axis=1, keepdims=True)
    inverse = lax.rsqrt(jnp.mean(center * center, axis=1, keepdims=True) + EPSILON)
    return center * inverse, inverse


def norm_grad(grad, scaled, inverse, gain):
    w = grad * gain
    first = jnp.mean(w, axis=1, keepdims=True)
    second = jnp.mean(w * scaled, axis=1, keepdims=True)
    return inverse * (w - first - scaled * second)


def norm_low(x, gain, shift):
    return (norm_parts(x)[0] * gain + shift).astype(BF16)


def pair_state(held):
    group, per = len(held), len(held[0])
    state = {}
    for s in range(per):
        for j in range(group):
            for b in range(per):
                seen = {held[(g - j) % group][b] <= held[g][s] for g in range(group)}
                state[s, j, b] = 0 if len(seen) == 2 else (1 if True in seen else -1)
    return state


def pair_bias(held, g):
    group = len(held)
    bias = {}
    for (s, j, b), state in pair_state(held).items():
        if state == 0:
            keys = place_of(group, lax.rem(g - j + group, group), b)
            bias[s, j, b] = jnp.where(keys <= place_of(group, g, s), 0.0, -1e9).astype(F32)
    return bias


def head_mask(h):
    lane = lax.broadcasted_iota(jnp.int32, (1, 128), 1)
    return (lane // HD) == h


def turning_pair(held, g):
    if len(held) != 2:
        return None, [0.0] * len(held[0])
    at = 1 - g
    return at, [jnp.where(at == n, 1.0, 0.0).astype(F32) for n in range(len(held[0]))]


def both_heads(x):
    return jnp.concatenate([jnp.where(head_mask(h), x, 0).astype(BF16) for h in range(2)], axis=0)


def slots_of(held, j, b, fixed):
    state = pair_state(held)
    return [s for s in range(len(held[0])) if state[s, j, b] > 0 or (state[s, j, b] == 0 and not fixed)]


def attend_strip(held, bias, g, i, q, kvs, out, lse):
    group, per = len(held), len(held[0])
    at, here = turning_pair(held, g)
    wide = 2 * BLOCK
    blocks = [(j, b, slots_of(held, j, b, at is not None)) for j in range(group) for b in range(per)]
    queries = [both_heads(q[i, s * BLOCK : (s + 1) * BLOCK, :] * SCALE) for s in range(per)]
    scores = {s: [] for s in range(per)}
    for j, b, slots in blocks:
        if slots:
            keys = kvs[j][i, b * BLOCK : (b + 1) * BLOCK, :128]
            score = dot(keys, jnp.concatenate([queries[s] for s in slots], axis=0), TURNED)
            for n, s in enumerate(slots):
                part = score[:, n * wide : (n + 1) * wide]
                scores[s].append(((j, b), part + bias[s, j, b] if (s, j, b) in bias and at is None else part))
    turned = {(j, b): kvs[j][i, b * BLOCK : (b + 1) * BLOCK, 128:].T for j, b, slots in blocks if slots}

    def weigh(e, values):
        e = e.astype(BF16)
        return jnp.concatenate(
            [dot(values[h * HD : (h + 1) * HD], e[:, h * BLOCK : (h + 1) * BLOCK]) for h in range(2)], axis=1
        )

    extra = None
    if at is not None:
        moving = pl.ds(pl.multiple_of(at * BLOCK, BLOCK), BLOCK)
        score = dot(kvs[1][i, moving, :128], both_heads(q[i, moving, :] * SCALE), TURNED)
        top = jnp.max(score, axis=0, keepdims=True)
        e = jnp.exp(score - top)
        extra = (top, jnp.sum(e, axis=0, keepdims=True), weigh(e, kvs[1][i, moving, 128:].T))
    for s in range(per):
        tops = [jnp.max(x, axis=0, keepdims=True) for _, x in scores[s]]
        if extra:
            tops.append(extra[0] + (here[s] - 1.0) * 1e9)
        top = functools.reduce(jnp.maximum, tops)
        total, made = 0.0, 0.0
        for place, score in scores[s]:
            e = jnp.exp(score - top)
            total = total + jnp.sum(e, axis=0, keepdims=True)
            made = made + weigh(e, turned[place])
        if extra:
            weight = jnp.exp(tops[-1] - top) * here[s]
            total = total + weight * extra[1]
            made = made + weight * extra[2]
        made = made / total
        level = top + jnp.log(total)
        rows = pl.ds(s * BLOCK, BLOCK)
        for h in range(2):
            lse[i, h : h + 1, rows] = level[:, h * BLOCK : (h + 1) * BLOCK]
        both = jnp.concatenate([made[:, :BLOCK], made[:, BLOCK:]], axis=0)
        out[rows, columns(i)] = both.T.astype(BF16)


def attend_back_strip(held, bias, g, i, q, lse, out, grad, kvs, gq, gkvs):
    group, per = len(held), len(held[0])
    at, here = turning_pair(held, g)

    def slot(rows):
        up = grad[rows, columns(i)]
        product = (up.astype(F32) * out[rows, columns(i)].astype(F32)).T
        inner = [jnp.sum(product[h * HD : (h + 1) * HD], axis=0, keepdims=True) for h in range(2)]
        level = [lse[i, h : h + 1, rows] for h in range(2)]
        return [
            both_heads(q[i, rows, :] * SCALE), both_heads(up),
            jnp.concatenate(inner, axis=1), jnp.concatenate(level, axis=1),
        ]

    def block(parts, keys, values):
        query, given = [jnp.concatenate([part[n] for part in parts], axis=0) for n in (0, 1)]
        inner, level = [jnp.concatenate([part[n] for part in parts], axis=1) for n in (2, 3)]
        probs = jnp.exp(dot(keys, query, TURNED) - level)
        g_scores = (probs * (dot(values, given, TURNED) - inner)).astype(BF16)
        turned = keys.T
        made = []
        for n in range(len(parts)):
            pieces = []
            for h in range(2):
                first = (2 * n + h) * BLOCK
                pieces.append(dot(turned[h * HD : (h + 1) * HD], g_scores[:, first : first + BLOCK]))
            made.append(jnp.concatenate(pieces, axis=0))
        return made, dot(g_scores, query), dot(probs.astype(BF16), given)

    slots = [slot(pl.ds(s * BLOCK, BLOCK)) for s in range(per)]
    total = [0.0] * per
    moved = None
    if at is not None:
        moving = pl.ds(pl.multiple_of(at * BLOCK, BLOCK), BLOCK)
        moved = block([slot(moving)], kvs[1][i, moving, :128], kvs[1][i, moving, 128:])
        total = [here[s] * moved[0][0] for s in range(per)]
    for j in range(group):
        for b in range(per):
            rows = pl.ds(b * BLOCK, BLOCK)
            k, v = 0.0, 0.0
            wanted = slots_of(held, j, b, at is not None)
            if wanted:
                parts = []
                for s in wanted:
                    part = list(slots[s])
                    if at is None and (s, j, b) in bias:
                        part[3] = part[3] - bias[s, j, b]
                    parts.append(part)
                made, k, v = block(parts, kvs[j][i, rows, :128], kvs[j][i, rows, 128:])
                for n, s in enumerate(wanted):
                    total[s] = total[s] + made[n]
            if at is not None and j == 1:
                k, v = k + here[b] * moved[1], v + here[b] * moved[2]
            gkvs[j][i, rows, :128] = k.astype(BF16)
            gkvs[j][i, rows, 128:] = v.astype(BF16)
    for s in range(per):
        gq[i, pl.ds(s * BLOCK, BLOCK), :] = (total[s] * SCALE).T.astype(BF16)


def by_rows(count, body, size=128):
    each(count // size, lambda n: body(pl.ds(pl.multiple_of(n * size, size), size)))


def keep(value, red, red_out):
    red[...] = value.astype(BF16)
    red_out[...] = value.T.astype(BF16)


def each(count, body):
    def step(i, carry):
        body(i)
        return carry

    lax.fori_loop(0, count, step, 0)


def qkv_stage(x, gain, shift, w, bias, low, up, q, kv, red, red_out, normed):
    def norm(rows):
        normed[rows, :] = norm_low(x[rows, :], gain, shift)

    by_rows(x.shape[0], norm)
    keep(dot(normed[...], low[...], TURNED), red, red_out)

    def pair(j):
        made = dot(normed[...], w[j])
        for n in range(2):
            i = 2 * j + n
            mixed = made[:, n * 384 : (n + 1) * 384] + (bias[i] + dot(red[...], up[i]))
            q[i] = mixed[:, :128].astype(BF16)
            kv[i] = mixed[:, 128:].astype(BF16)

    each(NARROW // 2, pair)


def proj_stage(x, att, w, bias, low, up, gain, shift, low_up, mid, normed, red, red_out, red_up, red_up_out):
    keep(dot(att[...], low[...], TURNED), red, red_out)

    def part(rows):
        value = x[rows, :] + (dot(att[rows, :], w[...]) + bias + dot(red[rows, :], up[...]))
        mid[rows, :] = value
        normed[rows, :] = norm_low(value, gain, shift)

    by_rows(x.shape[0], part, 256)
    keep(dot(normed[...], low_up[...], TURNED), red_up, red_up_out)


def up_strip(i, normed, w, bias, red_up, up, active, slope):
    units = w.shape[2]
    cols = columns(i, units)
    value = dot(normed[...], w[i]) + (bias[i] + dot(red_up[...], up[:, cols]))
    made, made_slope = gelu_parts(value)
    active[:, cols] = made.astype(BF16)
    slope[:, cols] = made_slope.astype(BF16)


def down_stage(mid, active, w, bias, up, red, put):
    for n in range(mid.shape[1] // 256):
        cols = slice(n * 256, (n + 1) * 256)
        put(n, mid[:, cols] + (dot(active[...], w[:, cols]) + bias[:, cols] + dot(red[...], up[:, cols])))


def gelu_parts(x):
    square = x * x
    t = jnp.tanh(ROOT * (x + 0.044715 * (x * square)))
    half = 0.5 * (1.0 + t)
    slope = half + 0.5 * x * (1.0 - t * t) * (ROOT * (1.0 + 3 * 0.044715 * square))
    return x * half, slope


class Vectors:
    def __init__(self, ref, l):
        self.ref, self.l = ref, l

    def qkv(self, i):
        return self.ref[i, pl.ds(4 * self.l, 1), :384]

    def up(self, i):
        return self.ref[i, pl.ds(4 * self.l + 1, 1), :]

    def row(self, name):
        at = ("proj", "down", "gain1", "shift1", "gain2", "shift2").index(name)
        row, lane = 4 * self.l + 2 + at // 4, at % 4 * 128
        return jnp.concatenate([self.ref[i, row : row + 1, lane : lane + 128] for i in range(NARROW)], axis=1)


class Strips:
    def __init__(self, read):
        self.read = read

    def __getitem__(self, i):
        return self.read(i)


TABLES = ("low_qkv", "up_qkv", "low_proj", "up_proj", "low_up", "up_up", "low_down", "up_down")
SAVED = ("q", "kv", "peer", "att", "lse", "mid", "active", "slope", "x")


def task_list(layers):
    tasks = [("load", 0, 0, 3.0, None)]
    for l in range(layers):
        tasks.append(("qkv", l, 0, 7.0, ("qkv", l)))
        tasks += [("attend", l, n, 3.0, None) for n in range(4)]
        tasks.append(("proj", l, 0, 4.0, ("proj", l)))
        tasks += [("up", l, n, 6.0, ("up", l)) for n in range(2)]
        tasks.append(("down", l, 0, 6.0, ("down", l)))
    return tasks


class ForwardWork:
    def __init__(self, n_col, group, refs):
        self.__dict__.update(refs)
        self.group = group
        self.held = positions(group)
        self.r, self.c = lax.axis_index("row"), lax.axis_index("col")
        self.g = lax.rem(self.c, group)
        self.bias = pair_bias(self.held, self.g)
        self.layers = self.low_qkv.shape[0]

    def stage_copies(self, kind, l):
        full = self.full[kind]
        if kind == "qkv":
            pieces = []
            for i in range(NARROW):
                src = full.at[l, i]
                pieces.append((src, self.wq.at[i // 2, :, :, :, pl.ds(i % 2 * 384, 384)]))
            return pieces, self.wq
        if kind == "up":
            return [(full.at[l, i], self.wu.at[i]) for i in range(NARROW)], self.wu
        target = self.wp if kind == "proj" else self.wd
        return [(full.at[l, i], target.at[i]) for i in range(NARROW)], target

    def stage(self, kind, l):
        for src, dst in self.stage_copies(kind, l)[0]:
            pltpu.make_async_copy(src, dst, self.stage_sem.at[KINDS.index(kind)]).start()

    def staged(self, kind, l):
        target = self.stage_copies(kind, l)[1]
        pltpu.make_async_copy(target, target, self.stage_sem.at[KINDS.index(kind)]).wait()

    def save_copy(self, name, l):
        src = {
            "q": self.q, "kv": self.kv, "peer": self.peer.at[l], "att": self.att, "lse": self.lse,
            "mid": self.mid, "active": self.active, "slope": self.slope, "x": self.x,
        }[name]
        return pltpu.make_async_copy(src, self.saved[name].at[l], self.save_sem.at[l, SAVED.index(name)])

    def save(self, *names, l):
        for name in names:
            self.save_copy(name, l).start()

    def settled(self, *names, l):
        if l >= 0:
            for name in names:
                self.save_copy(name, l).wait()

    def exchange(self, l, s):
        to = self.c - self.g + lax.rem(self.g + s, self.group)
        return pltpu.make_async_remote_copy(
            src_ref=self.kv, dst_ref=self.peer.at[l, s - 1],
            send_sem=self.kv_send.at[l, s - 1], recv_sem=self.kv_recv.at[l, s - 1],
            device_id=(self.r, to), device_id_type=MESH,
        )

    def run(self, name, l, part):
        vec = Vectors(self.vec, l)
        if name == "load":
            self.arrive_tokens()
            self.x[...] = self.tokens_v[...].astype(F32)
        elif name == "qkv":
            self.staged("qkv", l)
            self.settled("q", "kv", l=l - 1)
            if l > 0:
                for s in range(1, self.group):
                    self.exchange(l - 1, s).wait_send()
            w = self.wq.reshape(NARROW // 2, -1, 768)
            qkv_stage(
                self.x, vec.row("gain1"), vec.row("shift1"), w, Strips(vec.qkv), self.low_qkv.at[l],
                self.up_qkv.at[l], self.q, self.kv, self.red, self.reds.at[l, 0], self.normed,
            )
            for s in range(1, self.group):
                self.exchange(l, s).start()
            self.save("q", "kv", l=l)
        elif name == "attend":
            if part == 0:
                for s in range(1, self.group):
                    self.exchange(l, s).wait_recv()
                self.save("peer", l=l)
                self.settled("att", "lse", l=l - 1)
            kvs = [self.kv] + [self.peer.at[l, s - 1] for s in range(1, self.group)]
            size = NARROW // 4
            each(size, lambda n: attend_strip(self.held, self.bias, self.g, part * size + n, self.q, kvs, self.att, self.lse))
            if part == 3:
                self.save("att", "lse", l=l)
        elif name == "proj":
            self.staged("proj", l)
            self.settled("mid", l=l - 1)
            dim = self.att.shape[1]
            proj_stage(
                self.x, self.att, self.wp.reshape(dim, dim), vec.row("proj"), self.low_proj.at[l],
                self.up_proj.at[l], vec.row("gain2"), vec.row("shift2"), self.low_up.at[l],
                self.mid, self.normed, self.red, self.reds.at[l, 1], self.red_up, self.reds.at[l, 2],
            )
            self.save("mid", l=l)
        elif name == "up":
            if part == 0:
                self.staged("up", l)
                self.settled("active", "slope", l=l - 1)
            w = self.wu.reshape(NARROW, self.x.shape[1], -1)
            size = NARROW // 2
            each(size, lambda n: up_strip(
                part * size + n, self.normed, w, Strips(vec.up), self.red_up, self.up_up.at[l],
                self.active, self.slope,
            ))
            if part == 1:
                self.save("active", "slope", l=l)
                keep(dot(self.active[...], self.low_down[l], TURNED), self.red, self.reds.at[l, 3])
        elif name == "down":
            self.staged("down", l)
            self.settled("x", l=l - 1)
            dim = self.x.shape[1]

            def put(n, value):
                if l < self.layers - 1:
                    self.x[:, columns(n, 256)] = value
                else:
                    for m in range(2):
                        self.result[2 * n + m] = value[:, m * 128 : (m + 1) * 128].astype(BF16)

            down_stage(
                self.mid, self.active, self.wd.reshape(-1, dim), vec.row("down"), self.up_down.at[l], self.red, put,
            )
            if l < self.layers - 1:
                self.save("x", l=l)

    def close(self):
        last = self.layers - 1
        self.settled(*[name for name in SAVED if name not in ("x", "peer")], l=last)
        for l in range(self.layers):
            self.settled("peer", l=l)
        for s in range(1, self.group):
            self.exchange(last, s).wait_send()
        if last > 0:
            pass


def gather_body(n_row, n_col, layers, group, names, *refs):
    refs = dict(zip(names, refs))
    shard = {kind: refs["shard_" + kind] for kind in KINDS}
    full = {kind: refs["full_" + kind] for kind in KINDS}
    tokens, cotangent, vector = refs["tokens"], refs["cotangent"], refs["vector"]
    own_tokens, own_cotangent, vectors = refs["own_tokens"], refs["own_cotangent"], refs["vectors"]
    local_sem, send_sem, recv_sem = refs["local_sem"], refs["send_sem"], refs["recv_sem"]
    near_sem, out_sem, in_sem = refs["near_sem"], refs["out_sem"], refs["in_sem"]
    r = lax.axis_index("row")
    c = lax.axis_index("col")
    link_bits = [b for b in (2**k for k in range(1, 8)) if b < n_col]
    depth = shard["up"].shape[1]

    def row_peer(s):
        return (lax.rem(r + s, n_row), c)

    def col_peer(bit):
        return (r, c ^ bit)

    peers = [row_peer(s) for s in range(1, n_row)]
    peers += [(r, lax.rem(c + d, n_col)) for d in range(1, n_col)]
    barrier = pltpu.get_barrier_semaphore()
    for peer in peers:
        pl.semaphore_signal(barrier, inc=1, device_id=peer, device_id_type=MESH)
    pl.semaphore_wait(barrier, len(peers))

    per, width = BLOCKS // group, tokens.shape[1]

    def own_place(ref, b, col):
        if len(ref.shape) == 2:
            start = pl.multiple_of(col * width, width)
            return ref.at[pl.ds(b * BLOCK, BLOCK), pl.ds(start, width)]
        return ref.at[col, pl.ds(b * BLOCK, BLOCK)]

    def from_place(ref, b, col):
        start = (col // group) * LEN + place_of(group, lax.rem(col, group), b) * BLOCK
        return ref.at[pl.ds(pl.multiple_of(start, BLOCK), BLOCK)]

    exchanged = ((tokens, own_tokens), (cotangent, own_cotangent))

    def near(n, b):
        src, dst = exchanged[n]
        return pltpu.make_async_copy(from_place(src, b, c), own_place(dst, b, c), near_sem.at[n * per + b])

    def near_vector():
        return pltpu.make_async_copy(vector, vectors.at[c], near_sem.at[2 * per])

    def far(src, dst, n, peer):
        return pltpu.make_async_remote_copy(
            src_ref=src, dst_ref=dst, send_sem=out_sem.at[n], recv_sem=in_sem.at[n],
            device_id=peer, device_id_type=MESH,
        )

    def start_exchange(n):
        src, dst = exchanged[n]
        for b in range(per):
            near(n, b).start()
        for d in range(1, n_col):
            to = lax.rem(c + d, n_col)
            for b in range(per):
                far(from_place(src, b, to), own_place(dst, b, c), n, (r, to)).start()

    def wait_exchange(n):
        _, dst = exchanged[n]
        for b in range(per):
            near(n, b).wait()
        if len(dst.shape) == 2:
            ref = dst.at[:, pl.ds(0, (n_col - 1) * width)]
        else:
            ref = dst.at[pl.ds(0, n_col - 1)]
        far(ref, ref, n, col_peer(1)).wait()

    def own(kind, l, h):
        ref = shard[kind]
        size = ref.shape[1] // CUTS[kind]
        return ref.at[l, pl.ds(h * size, size)]

    def block(kind, l, h, row, col):
        if kind in ("qkv", "up"):
            return full[kind].at[l, col, row, h]
        start = pl.multiple_of(row * depth, depth)
        return full[kind].at[l, col, h, :, pl.ds(start, depth)]

    def strip(kind, l, h, col):
        if kind in ("qkv", "up"):
            return full[kind].at[l, col, :, h]
        return full[kind].at[l, col, h]

    def amount(kind, l, h, strips, rows):
        if kind in ("qkv", "up"):
            return full[kind].at[l, pl.ds(0, strips), pl.ds(0, rows), h]
        return full[kind].at[l, pl.ds(0, strips), h, :, pl.ds(0, rows * depth)]

    chunks = []
    for l in range(layers):
        for kind in KINDS:
            for h in range(CUTS[kind]):
                order = []
                for d in ORDERS[l % len(ORDERS)][kind][h // 2][h % 2]:
                    if d == "z":
                        order.append("z")
                    elif d < len(link_bits):
                        order.append(link_bits[d])
                order += link_bits[2:]
                chunks.append((kind, l, h, tuple(order)))
    phases = len(link_bits) + n_row - 1

    def remote(src, dst, k, p, peer, way=0):
        at = (k * (phases + 1) + p) * 2 + way
        return pltpu.make_async_remote_copy(
            src_ref=src, dst_ref=dst, send_sem=send_sem.at[at], recv_sem=recv_sem.at[at],
            device_id=peer, device_id_type=MESH,
        )

    def plan(k):
        return transfer_plan(chunks[k][3], n_row)

    def ways(hop):
        return (
            (r - hop + 1, (r - hop + 1 >= 0) & (r + 1 < n_row), r - hop >= 0, 1),
            (r + hop - 1, (r + hop - 1 < n_row) & (r >= 1), r + hop < n_row, n_row - 1),
        )

    def local(k):
        kind, l, h, _ = chunks[k]
        return pltpu.make_async_copy(own(kind, l, h), block(kind, l, h, r, c), local_sem.at[k])

    def issue(k, p):
        kind, l, h, order = chunks[k]
        d, masks, rows = plan(k)[p]

        def held(m, row, first):
            return own(kind, l, h) if m == 0 and first else block(kind, l, h, row, c ^ m)

        if isinstance(d, tuple):
            for way, (row, goes, _, step) in enumerate(ways(d[1])):

                @pl.when(goes)
                def _():
                    for m in masks:
                        dst = block(kind, l, h, row, c ^ m)
                        remote(held(m, row, d[1] == 1), dst, k, p, row_peer(step), way).start()

            return
        for m in masks:
            if rows:
                ref = strip(kind, l, h, c ^ m)
                remote(ref, ref, k, p, col_peer(d)).start()
            else:
                remote(held(m, r, True), block(kind, l, h, r, c ^ m), k, p, col_peer(d)).start()

    def moved(k, p, send):
        kind, l, h, order = chunks[k]
        d, masks, rows = plan(k)[p]
        ref = amount(kind, l, h, len(masks), n_row if rows else 1)
        if not isinstance(d, tuple):
            copy = remote(ref, ref, k, p, col_peer(1))
            copy.wait_send() if send else copy.wait_recv()
            return
        for way, (_, goes, comes, step) in enumerate(ways(d[1])):

            @pl.when(goes if send else comes)
            def _():
                copy = remote(ref, ref, k, p, row_peer(step), way)
                copy.wait_send() if send else copy.wait_recv()

    def share(k, p):
        kind, l, h, order = chunks[k]
        (d, masks, _), (_, later, rows) = plan(k)[p : p + 2]
        if not rows:
            return
        fresh = masks if isinstance(d, tuple) else later[len(masks):]
        for m in fresh:
            ref = strip(kind, l, h, c ^ m)
            remote(ref, ref, k, phases, col_peer(1)).start()

    def shared(k):
        kind, l, h, _ = chunks[k]
        ref = amount(kind, l, h, n_col // 2, n_row)
        return remote(ref, ref, k, phases, col_peer(1))

    def finish(k, p):
        moved(k, p, False)
        if plan(k)[p][0] == ("z", n_row - 1):
            local(k).wait()
        share(k, p)

    count = len(chunks)
    near_vector().start()
    for d in range(1, n_col):
        far(vector, vectors.at[c], 2, (r, lax.rem(c + d, n_col))).start()
    start_exchange(0)
    for k in range(count):
        local(k).start()
    def vectors_arrive():
        near_vector().wait()
        rest = vectors.at[pl.ds(0, n_col - 1)]
        far(rest, rest, 2, col_peer(1)).wait()

    work = None
    if "x" in refs:
        refs.update(full=full, saved={name: refs["saved_" + name] for name in SAVED})

        def arrive_tokens():
            vectors_arrive()
            wait_exchange(0)
            load_sem = refs["load_sem"]
            loads = [(own_tokens, refs["tokens_v"]), (vectors, refs["vec"])]
            copies = [pltpu.make_async_copy(s, d, load_sem.at[n]) for n, (s, d) in enumerate(loads)]
            for copy in copies:
                copy.start()
            for copy in copies:
                copy.wait()

        refs.update(arrive_tokens=arrive_tokens)
        work = ForwardWork(n_col, group, refs)

    pieces = []
    for kind, l, h, order in chunks:
        size = 2 * shard[kind].shape[1] * shard[kind].shape[2] // CUTS[kind]
        pieces.append(((kind, l), order, size))
    ops = transfer_schedule(pieces, n_row, task_list(layers) if work else [])
    quiet = max(n for n, (op, _, _) in enumerate(ops) if op == "wait")
    for n, (op, k, p) in enumerate(ops):
        if n == quiet + 1:
            start_exchange(1)
        if op == "start":
            issue(k, p)
        elif op == "wait":
            finish(k, p)
        elif op == "stage":
            for at, (kind, l, _, _) in enumerate(chunks):
                if (kind, l) == (k, p):
                    shared(at).wait_recv()
            work.stage(k, p)
        else:
            work.run(k, *p)
    for k in range(count):
        for p in range(phases):
            moved(k, p, True)
        shared(k).wait_send()
        if not work:
            shared(k).wait_recv()
    if work:
        work.close()
    else:
        vectors_arrive()
        wait_exchange(0)
    wait_exchange(1)


def gather_inputs(n_row, n_col, group, qkv, proj, up, down, tokens, cotangent, vector, tables=None):
    layers, depth = up.shape[0], up.shape[1]
    width, units = proj.shape[1], down.shape[1]
    dim, hidden = depth * n_row, units * n_col
    mine = LEN // group
    cuts = [CUTS[kind] for kind in KINDS]
    own = (mine, dim) if width % 128 == 0 else (n_col, mine, width)
    hbm = pl.BlockSpec(memory_space=pltpu.HBM)
    vmem = pl.BlockSpec(memory_space=pltpu.VMEM)
    dma = pltpu.SemaphoreType.DMA
    count = layers * sum(cuts)
    phases = n_col.bit_length() + n_row - 2
    inputs = [("shard_" + kind, array, hbm) for kind, array in zip(KINDS, (qkv, proj, up, down))]
    inputs += [("tokens", tokens, hbm), ("cotangent", cotangent, hbm), ("vector", vector, hbm)]
    outputs = [
        ("full_qkv", (layers, n_col, n_row, cuts[0], depth // cuts[0], qkv.shape[2]), BF16, hbm),
        ("full_proj", (layers, n_col, cuts[1], width // cuts[1], dim), BF16, hbm),
        ("full_up", (layers, n_col, n_row, cuts[2], depth // cuts[2], units), BF16, hbm),
        ("full_down", (layers, n_col, cuts[3], units // cuts[3], dim), BF16, hbm),
        ("own_tokens", own, BF16, hbm),
        ("own_cotangent", own, BF16, hbm),
        ("vectors", (n_col,) + vector.shape, F32, hbm),
    ]
    scratch = [
        ("local_sem", dma((count,))),
        ("send_sem", dma((count * phases * 2,))),
        ("recv_sem", dma((count * phases * 2,))),
        ("near_sem", dma((2 * (BLOCKS // group) + 1,))),
        ("out_sem", dma((3,))),
        ("in_sem", dma((3,))),
    ]
    if tables is not None:
        rank = tables[0].shape[1]
        inputs += [(name, table, vmem) for name, table in zip(TABLES, tables)]
        strip = (NARROW, mine)
        kept = {
            "q": (strip + (128,), BF16), "kv": (strip + (256,), BF16), "att": ((mine, dim), BF16),
            "lse": ((NARROW, 8, mine), F32), "mid": ((mine, dim), F32), "active": ((mine, hidden), BF16),
            "slope": ((mine, hidden), BF16),
            "x": ((mine, dim), F32), "peer": ((group - 1,) + strip + (256,), BF16),
        }
        outputs += [("saved_" + name, (layers,) + kept[name][0], kept[name][1], hbm) for name in SAVED]
        outputs += [
            ("reds", (layers, 4, rank, mine), BF16, vmem),
            ("result", (NARROW, mine, 128), BF16, vmem),
        ]
        scratch += [
            (name, pltpu.VMEM(((layers,) if name == "peer" else ()) + kept[name][0], kept[name][1]))
            for name in SAVED
        ]
        scratch += [
            ("wq", pltpu.VMEM((NARROW // 2, n_row, cuts[0], depth // cuts[0], 768), BF16)),
            ("wp", pltpu.VMEM((NARROW, cuts[1], width // cuts[1], dim), BF16)),
            ("wu", pltpu.VMEM((NARROW, n_row, cuts[2], depth // cuts[2], units), BF16)),
            ("wd", pltpu.VMEM((NARROW, cuts[3], units // cuts[3], dim), BF16)),
            ("tokens_v", pltpu.VMEM((mine, dim), BF16)),
            ("normed", pltpu.VMEM((mine, dim), BF16)),
            ("red", pltpu.VMEM((mine, rank), BF16)),
            ("red_up", pltpu.VMEM((mine, rank), BF16)),
            ("vec", pltpu.VMEM((n_col,) + vector.shape, F32)),
            ("stage_sem", dma((4,))),
            ("save_sem", dma((layers, len(SAVED)))),
            ("kv_send", dma((layers, group - 1))),
            ("kv_recv", dma((layers, group - 1))),
            ("load_sem", dma((2,))),
        ]
    names = [x[0] for x in inputs] + [x[0] for x in outputs] + [x[0] for x in scratch]
    outs = pl.pallas_call(
        functools.partial(gather_body, n_row, n_col, layers, group, tuple(names)),
        out_shape=[jax.ShapeDtypeStruct(shape, kind) for _, shape, kind, _ in outputs],
        in_specs=[spec for _, _, spec in inputs],
        out_specs=[spec for _, _, _, spec in outputs],
        scratch_shapes=[shape for _, shape in scratch],
        compiler_params=pltpu.CompilerParams(
            collective_id=0, has_side_effects=True, vmem_limit_bytes=60 * 2**20
        ),
        name="gather_inputs",
    )(*[array for _, array, _ in inputs])
    outs = dict(zip([x[0] for x in outputs], outs))

    merge = 128 // width
    strips = n_col // merge
    qkv_full = outs["full_qkv"].reshape(layers, n_col, dim, qkv.shape[2])
    up_full = outs["full_up"].reshape(layers, n_col, dim, units)
    rows, vec = [outs["own_tokens"], outs["own_cotangent"]], outs["vectors"]
    if merge > 1:
        qkv_full = qkv_full.reshape(layers, strips, merge, dim, 3, width).transpose(0, 1, 3, 4, 2, 5)
        up_full = up_full.reshape(layers, strips, merge, dim, units).transpose(0, 1, 3, 2, 4)
        rows = [x.transpose(1, 0, 2).reshape(mine, dim) for x in rows]
        vec = vec.reshape(strips, merge, layers, 4, 4 * 128)
        first = vec[:, :, :, 0, : 3 * width].reshape(strips, merge, layers, 3, width).transpose(0, 2, 3, 1, 4)
        first = jnp.pad(first.reshape(strips, layers, 384), ((0, 0), (0, 0), (0, 128)))
        second = vec[:, :, :, 1, :units].transpose(0, 2, 1, 3).reshape(strips, layers, 512)
        rest = vec[:, :, :, 2:, : 4 * width].reshape(strips, merge, layers, 2, 4, width)
        rest = rest.transpose(0, 2, 3, 4, 1, 5).reshape(strips, layers, 2, 512)
        vec = jnp.concatenate([first[:, :, None], second[:, :, None], rest], axis=2)
        vec = vec.reshape(strips, layers * 4, 512)
    outs.update(
        qkv=qkv_full.reshape(layers, strips, dim, 384),
        proj=outs["full_proj"].reshape(layers, dim, dim),
        up=up_full.reshape(layers, strips, dim, units * merge),
        down=outs["full_down"].reshape(layers, hidden, dim),
        tokens=rows[0], cotangent=rows[1], vec=vec,
    )
    return outs


PARAMS = pltpu.CompilerParams(vmem_limit_bytes=60 * 2**20)


def shape_of(shape, kind):
    return jax.ShapeDtypeStruct(shape, kind)


def kernel(body, name, inputs, outputs, scratch=()):
    spaces = (pl.BlockSpec(memory_space=pltpu.VMEM), pl.BlockSpec(memory_space=pltpu.HBM))
    return pl.pallas_call(
        body,
        out_shape=[shape_of(shape, kind) for shape, kind, _ in outputs],
        in_specs=[spaces[far] for _, far in inputs],
        out_specs=[spaces[far] for _, _, far in outputs],
        scratch_shapes=list(scratch),
        compiler_params=PARAMS,
        name=name,
    )(*[array for array, _ in inputs])


def own_group(group):
    return lax.rem(lax.axis_index("col"), group)


def qkv_body(l, x, vec, w, low, up, q, kv, red_out, red, normed, buf, sem):
    copies = []
    for i in range(NARROW):
        copies.append(pltpu.make_async_copy(w.at[l, i], buf.at[i // 2, :, columns(i % 2, 384)], sem.at[i]))
        copies[-1].start()
    for copy in copies:
        copy.wait()
    v = Vectors(vec, l)
    qkv_stage(x, v.row("gain1"), v.row("shift1"), buf, Strips(v.qkv), low.at[l], up.at[l], q, kv, red, red_out, normed)


def qkv_kernel(l, x, vec, w, low, up):
    tokens, dim = x.shape
    return kernel(
        functools.partial(qkv_body, l), "qkv",
        [(x, False), (vec, False), (w, True), (low, False), (up, False)],
        [((NARROW, tokens, 128), BF16, False), ((NARROW, tokens, 256), BF16, False), ((low.shape[1], tokens), BF16, False)],
        [pltpu.VMEM((tokens, low.shape[1]), BF16), pltpu.VMEM((tokens, dim), BF16), pltpu.VMEM((NARROW // 2, dim, 768), BF16), pltpu.SemaphoreType.DMA((NARROW,))],
    )


def attend_body(group, g_ref, q, *refs):
    held = positions(group)
    kvs, (out, lse) = refs[:group], refs[group:]
    bias = pair_bias(held, g_ref[0])
    each(NARROW, lambda i: attend_strip(held, bias, g_ref[0], i, q, kvs, out, lse))


def attend_kernel(group, g, q, kvs):
    tokens = q.shape[1]
    return pl.pallas_call(
        functools.partial(attend_body, group),
        out_shape=[shape_of((tokens, NARROW * 128), BF16), shape_of((NARROW, 8, tokens), F32)],
        in_specs=[pl.BlockSpec(memory_space=pltpu.SMEM)] + [pl.BlockSpec(memory_space=pltpu.VMEM)] * (group + 1),
        out_specs=[pl.BlockSpec(memory_space=pltpu.VMEM)] * 2,
        compiler_params=PARAMS,
        name="attend",
    )(g, q, *kvs)


def mlp_body(l, x, att, vec, wp, wu, wd, *refs):
    low_proj, up_proj, low_up, up_up, low_down, up_down = [ref.at[l] for ref in refs[:6]]
    mid, result, active, slope, reds, red, red_up, normed, bp, bu, bd, sem = refs[6:]
    copies = []
    for n, (src, dst) in enumerate(((wp.at[l], bp), (wu.at[l], bu), (wd.at[l], bd))):
        copies.append(pltpu.make_async_copy(src, dst, sem.at[n]))
        copies[-1].start()
    v = Vectors(vec, l)
    copies[0].wait()
    proj_stage(
        x, att, bp, v.row("proj"), low_proj, up_proj, v.row("gain2"), v.row("shift2"), low_up,
        mid, normed, red, reds.at[0], red_up, reds.at[1],
    )
    copies[1].wait()
    each(NARROW, lambda i: up_strip(i, normed, bu, Strips(v.up), red_up, up_up, active, slope))
    copies[2].wait()

    def put(n, value):
        if len(result.shape) == 2:
            result[:, columns(n, 256)] = value
        else:
            for m in range(2):
                result[2 * n + m] = value[:, m * 128 : (m + 1) * 128].astype(BF16)

    keep(dot(active[...], low_down[...], TURNED), red, reds.at[2])
    down_stage(mid, active, bd, v.row("down"), up_down, red, put)


def mlp_kernel(l, final, x, att, vec, wp, wu, wd, tables):
    tokens, dim = x.shape
    hidden = wd.shape[1]
    rank = tables[0].shape[1]
    result = ((NARROW, tokens, 128), BF16, False) if final else ((tokens, dim), F32, False)
    return kernel(
        functools.partial(mlp_body, l), "mlp",
        [(x, False), (att, False), (vec, False), (wp, True), (wu, True), (wd, True)] + [(t, False) for t in tables],
        [((tokens, dim), F32, False), result] + [((tokens, hidden), BF16, False)] * 2 + [((3, rank, tokens), BF16, False)],
        [
            pltpu.VMEM((tokens, rank), BF16), pltpu.VMEM((tokens, rank), BF16),
            pltpu.VMEM((tokens, dim), BF16), pltpu.VMEM(wp.shape[1:], BF16),
            pltpu.VMEM(wu.shape[1:], BF16), pltpu.VMEM(wd.shape[1:], BF16), pltpu.SemaphoreType.DMA((3,)),
        ],
    )


def mlp_back_stage(vec, grad, active, g_hid, mid, att, low, total, wp, wu, wd, reds, t, grads, g_mid, waits, strip_waits):
    low[...] = grad[...].astype(BF16)
    g_red = dot(low[...], t["up_down"], TURNED).astype(BF16)
    rank = g_red.shape[1]
    units = wu.shape[2]
    total[...] = jnp.zeros_like(total)

    def strip(i):
        cols = columns(i, units)
        strip_waits(i)
        g_active = dot(low[...], wd[cols, :], TURNED) + dot(g_red, t["low_down"][:, cols])
        g_hid[:, cols] = (g_active * g_hid[:, cols].astype(F32)).astype(BF16)
        total[...] += dot(g_hid[:, cols], wu[i], TURNED)

    each(NARROW, strip)

    def give(at, value):
        size = value.shape[1] // NARROW
        for i in range(NARROW):
            grads[i, :, at : at + size] = value[:, i * size : (i + 1) * size].astype(BF16)

    give(384 + 2 * units, dot(reds[3], low[...]))
    give(384 + units, dot(g_red, active[...], CROSS))
    give(384, dot(reds[2], g_hid[...]))
    g_hid[:, :rank] = dot(g_hid[...], t["up_up"][...], TURNED).astype(BF16)
    waits("mid")
    gain, shift = vec.row("gain2"), vec.row("shift2")
    dim = mid.shape[1]

    def norm(rows):
        scaled, inverse = norm_parts(mid[rows, :])
        active[rows, :dim] = (scaled * gain + shift).astype(BF16)
        g_normed = total[rows, :] + dot(g_hid[rows, :rank], t["low_up"])
        value = grad[rows, :] + norm_grad(g_normed, scaled, inverse, gain)
        g_mid[rows, :] = value
        low[rows, :] = value.astype(BF16)

    by_rows(mid.shape[0], norm)
    give(256, dot(g_hid[:, :rank], active[:, :dim], CROSS))
    give(128, dot(reds[1], low[...]))
    g_red_proj = dot(low[...], t["up_proj"], TURNED).astype(BF16)
    waits("att")
    waits("proj")
    give(0, dot(g_red_proj, att[...], CROSS))
    low[...] = (dot(low[...], wp[...], TURNED) + dot(g_red_proj, t["low_proj"])).astype(BF16)


def qkv_back_stage(vec, x, g_mid, gq, parts, total, g_red, normed, wq, red, low, up, grads, put, waits):
    waits("gq")
    waits("qkv")
    rank, tokens = red.shape
    small = jnp.zeros((tokens, rank), F32)
    for j in range(NARROW // 2):
        pieces = []
        for i in (2 * j, 2 * j + 1):
            waits(("part", i))
            g_kv = sum(part[i].astype(F32) for part in parts).astype(BF16)
            g_mixed = jnp.concatenate([gq[i], g_kv], axis=1)
            grads[i, :, 128:512] = dot(red[...], g_mixed).astype(BF16)
            small = small + dot(g_mixed, up[i], TURNED)
            pieces.append(g_mixed)
        made = dot(jnp.concatenate(pieces, axis=1), wq[j], TURNED)
        total[...] = made if j == 0 else total[...] + made
    g_low_rank = small.astype(BF16)
    g_red[...] = g_low_rank
    waits("x")
    waits("g_mid")
    gain, shift = vec.row("gain1"), vec.row("shift1")

    def norm(rows):
        scaled, inverse = norm_parts(x[rows, :].astype(F32))
        normed[rows, :] = (scaled * gain + shift).astype(BF16)
        g_normed = total[rows, :] + dot(g_red[rows, :], low[...])
        put(rows, g_mid[rows, :] + norm_grad(g_normed, scaled, inverse, gain))

    by_rows(tokens, norm)
    g_low = dot(g_low_rank, normed[...], CROSS).astype(BF16)
    for i in range(NARROW):
        grads[i, :, :128] = g_low[:, i * 128 : (i + 1) * 128]


def back_body(lq, lm, group, names, *refs):
    R = dict(zip(names, refs))
    held = positions(group)
    sem, started = R["sem"], {}

    def waits(name):
        for copy in started.pop(name, ()):
            copy.wait()

    count = [0]

    def begin(name, *copies):
        started[name] = []
        for src, dst in copies:
            copy = pltpu.make_async_copy(src, dst, sem.at[count[0]])
            count[0] += 1
            copy.start()
            started[name].append(copy)

    def strip_copies(l, i, base):
        cols = columns(i, R["wu"].shape[2])
        pairs = (
            (R["slopes"].at[l, :, cols], R["g_hid"].at[:, cols]), (R["actives"].at[l, :, cols], R["active"].at[:, cols]),
            (R["w_down"].at[l, cols], R["wd"].at[cols]), (R["w_up"].at[l, i], R["wu"].at[i]),
        )
        return [pltpu.make_async_copy(src, dst, sem.at[base + 4 * i + n]) for n, (src, dst) in enumerate(pairs)]

    strip_base = {}

    def load_strips(l):
        strip_base[l] = count[0]
        count[0] += 4 * NARROW
        for i in range(NARROW):
            for copy in strip_copies(l, i, strip_base[l]):
                copy.start()

    def strip_waits(l):
        def wait(i):
            for copy in strip_copies(l, i, strip_base[l]):
                copy.wait()

        return wait

    if lq is not None:
        begin("gq", (R["in_gq"], R["gq"]), *[(R["in_part%d" % j], R["part%d" % j]) for j in range(group)])
        begin("qkv", *[
            (R["w_qkv"].at[lq, i], R["wq"].at[i // 2, :, columns(i % 2, 384)]) for i in range(NARROW)
        ])
        begin("x", (R["in_x"], R["x"]))
        begin("g_mid", (R["in_g_mid"], R["total2"]))
    else:
        begin("cotangent", (R["cotangent"], R["low"]))
    if lm is not None:
        load_strips(lm)
        begin("proj", (R["w_proj"].at[lm], R["wp"]))
        begin("att", (R["atts"].at[lm], R["att"]))
        begin("kv", (R["kvs"].at[lm], R["kv"]), (R["peers"].at[lm], R["peer"]), (R["lses"].at[lm], R["lse"]))
    if lq is not None:
        vec = Vectors(R["vec"], lq)

        def put(rows, value):
            if lm is None:
                for i in range(NARROW):
                    R["out"][i, rows, :] = value[:, i * 128 : (i + 1) * 128].astype(BF16)
            else:
                R["grad"][rows, :] = value

        qkv_back_stage(
            vec, R["x"], R["total2"], R["gq"], [R["part%d" % j] for j in range(group)], R["total"],
            R["g_red"], R["low"], R["wq"],
            R["reds"].at[lq, 0], R["low_qkv"].at[lq], R["up_qkv"].at[lq], R["grads_qkv"], put, waits,
        )
    else:
        waits("cotangent")
        R["grad"][...] = R["low"][...].astype(F32)
    if lm is None:
        return
    begin("q", (R["qs"].at[lm], R["gq"]))
    begin("mid", (R["mids"].at[lm], R["x" if lq is not None and R["x"].dtype == F32 else "mid"]))
    mid = R["x" if lq is not None and R["x"].dtype == F32 else "mid"]
    t = {name: R[name].at[lm] for name in TABLES}
    vec = Vectors(R["vec"], lm)
    mlp_back_stage(
        vec, R["grad"], R["active"], R["g_hid"], mid, R["att"], R["low"], R["total"], R["wp"], R["wu"], R["wd"],
        R["reds"].at[lm], {k: (v if k in ("low_down", "up_up") else v[...]) for k, v in t.items() if "qkv" not in k},
        R["grads_mlp"], R["total2"], waits, strip_waits(lm),
    )
    out_mid = pltpu.make_async_copy(R["total2"], R["out_g_mid"], sem.at[count[0]])
    out_mid.start()
    waits("q")
    waits("kv")
    bias = pair_bias(held, R["g"][0])
    kvs = [R["kv"]] + [R["peer"].at[j] for j in range(group - 1)]
    gkvs = [R["part%d" % j] for j in range(group)]
    each(NARROW, lambda i: attend_back_strip(
        held, bias, R["g"][0], i, R["gq"], R["lse"], R["att"], R["low"], kvs, R["gq"], gkvs
    ))
    outs = [(R["gq"], R["out_gq"])] + [(R["part%d" % j], R["out_part%d" % j]) for j in range(group)]
    copies = [pltpu.make_async_copy(src, dst, sem.at[count[0] + 1 + n]) for n, (src, dst) in enumerate(outs)]
    for copy in copies:
        copy.start()
    for copy in copies:
        copy.wait()
    out_mid.wait()


def back_kernel(lq, lm, group, g, outs, tables, carried):
    layers, _, dim, _ = outs["qkv"].shape
    hidden = outs["down"].shape[1]
    tokens = outs["tokens"].shape[0]
    rank = tables[0].shape[1]
    strip = (NARROW, tokens)
    inputs = [("g", g, pl.BlockSpec(memory_space=pltpu.SMEM))]
    near, far = pl.BlockSpec(memory_space=pltpu.VMEM), pl.BlockSpec(memory_space=pltpu.HBM)
    inputs += [(name, table, near) for name, table in zip(TABLES, tables)]
    inputs += [("vec", outs["vec"], near), ("reds", outs["reds"], near)]
    outputs, scratch = [], []

    def vmem(name, shape, kind):
        scratch.append((name, pltpu.VMEM(shape, kind)))

    vmem("gq", strip + (128,), BF16)
    for j in range(group):
        vmem("part%d" % j, strip + (256,), BF16)
    vmem("total", (tokens, dim), F32)
    vmem("total2", (tokens, dim), F32)
    vmem("low", (tokens, dim), BF16)
    if lq is not None:
        g_mid, gq, parts = carried
        x = outs["tokens"] if lq == 0 else outs["saved_x"][lq - 1]
        inputs += [("in_gq", gq, far), ("in_g_mid", g_mid, far), ("in_x", x, far), ("w_qkv", outs["qkv"], far)]
        inputs += [("in_part%d" % j, part, far) for j, part in enumerate(parts)]
        vmem("wq", (NARROW // 2, dim, 768), BF16)
        vmem("g_red", (tokens, rank), BF16)
        vmem("x", (tokens, dim), x.dtype)
        outputs.append(("grads_qkv", (NARROW, rank, 512), BF16, near))
        if lm is None:
            outputs.append(("out", strip + (128,), BF16, near))
    if lm is not None:
        if lq is None:
            inputs.append(("cotangent", outs["cotangent"], far))
        for name in ("active", "slope", "mid", "att", "q", "kv", "peer", "lse"):
            inputs.append((name + "s", outs["saved_" + name], far))
        inputs += [("w_" + name, outs[name], far) for name in ("proj", "up", "down")]
        vmem("wp", (dim, dim), BF16)
        vmem("wu", (NARROW, dim, hidden // NARROW), BF16)
        vmem("wd", (hidden, dim), BF16)
        vmem("grad", (tokens, dim), F32)
        if lq is None or x.dtype != F32:
            vmem("mid", (tokens, dim), F32)
        vmem("att", (tokens, dim), BF16)
        vmem("active", (tokens, hidden), BF16)
        vmem("g_hid", (tokens, hidden), BF16)
        vmem("kv", strip + (256,), BF16)
        vmem("peer", (group - 1,) + strip + (256,), BF16)
        vmem("lse", (NARROW, 8, tokens), F32)
        outputs.append(("grads_mlp", (NARROW, rank, 512 + 2 * hidden // NARROW), BF16, near))
        outputs += [("out_g_mid", (tokens, dim), F32, far), ("out_gq", strip + (128,), BF16, far)]
        outputs += [("out_part%d" % j, strip + (256,), BF16, far) for j in range(group)]
    scratch.append(("sem", pltpu.SemaphoreType.DMA((96,))))
    names = [x[0] for x in inputs] + [x[0] for x in outputs] + [x[0] for x in scratch]
    made = pl.pallas_call(
        functools.partial(back_body, lq, lm, group, tuple(names)),
        out_shape=[shape_of(shape, kind) for _, shape, kind, _ in outputs],
        in_specs=[spec for _, _, spec in inputs],
        out_specs=[spec for _, _, _, spec in outputs],
        scratch_shapes=[shape for _, shape in scratch],
        compiler_params=PARAMS,
        name="back",
    )(*[array for _, array, _ in inputs])
    return dict(zip([x[0] for x in outputs], made))


SITES = {"mlp": (1, 1, 2, 2, 3, 3), "qkv": (0, 0)}


def backward_body(layers, group, n_row, n_col, names, *refs):
    R = dict(zip(names, refs))
    held = positions(group)
    per = BLOCKS // group
    r, c = lax.axis_index("row"), lax.axis_index("col")
    g = lax.rem(c, group)
    seqs = n_col // group
    tokens = per * BLOCK
    bias = pair_bias(held, g)

    def row_peer(s):
        return (lax.rem(r + s, n_row), c)

    def col_peer(d):
        return lax.rem(c + d, n_col)

    peers = [row_peer(s) for s in range(1, n_row)] + [(r, col_peer(d)) for d in range(1, n_col)]
    barrier = pltpu.get_barrier_semaphore()
    for peer in peers:
        pl.semaphore_signal(barrier, inc=1, device_id=peer, device_id_type=MESH)
    pl.semaphore_wait(barrier, len(peers))

    sem, started, count = R["sem"], {}, [0]

    def begin(name, *copies):
        started[name] = []
        for src, dst in copies:
            copy = pltpu.make_async_copy(src, dst, sem.at[count[0]])
            count[0] += 1
            copy.start()
            started[name].append(copy)

    def waits(name):
        for copy in started.pop(name, ()):
            copy.wait()

    def strip_copies(l, i, base):
        cols = columns(i, R["wu"].shape[2])
        pairs = (
            (R["slopes"].at[l, :, cols], R["g_hid"].at[:, cols]), (R["actives"].at[l, :, cols], R["active"].at[:, cols]),
            (R["w_down"].at[l, cols], R["wd"].at[cols]), (R["w_up"].at[l, i], R["wu"].at[i]),
        )
        return [pltpu.make_async_copy(src, dst, sem.at[base + 4 * i + n]) for n, (src, dst) in enumerate(pairs)]

    strip_base = {}

    def load_strips(l):
        strip_base[l] = count[0]
        count[0] += 4 * NARROW
        for i in range(NARROW):
            for copy in strip_copies(l, i, strip_base[l]):
                copy.start()

    def strip_waits(l):
        def wait(i):
            for copy in strip_copies(l, i, strip_base[l]):
                copy.wait()

        return wait

    far = [0]

    def remote(src, dst, n, peer):
        return pltpu.make_async_remote_copy(
            src_ref=src, dst_ref=dst, send_sem=R["out_sem"].at[n], recv_sem=R["in_sem"].at[n],
            device_id=peer, device_id_type=MESH,
        )

    def new_far():
        far[0] += 1
        return far[0] - 1

    def columns_start(n, src):
        to, at = R["columns"].at[n], new_far()
        start = (c // group) * LEN
        places = [pl.ds(pl.multiple_of(start + place_of(group, g, b) * BLOCK, BLOCK), BLOCK) for b in range(per)]
        begin("columns%d" % n, *[(src.at[c, pl.ds(b * BLOCK, BLOCK)], to.at[places[b]]) for b in range(per)])
        for d in range(1, n_col):
            for b in range(per):
                remote(src.at[col_peer(d), pl.ds(b * BLOCK, BLOCK)], to.at[places[b]], at, (r, col_peer(d))).start()
        return at

    def columns_end(n, at):
        waits("columns%d" % n)
        ref = R["columns"].at[n, pl.ds(0, (n_col - 1) * tokens)]
        remote(ref, ref, at, (r, col_peer(1))).wait()

    ends = {}

    def spread(kind, l):
        src, land, at = R["grads_" + kind], R["land_" + kind].at[l], new_far()
        begin("own_%s%d" % (kind, l), (src.at[c], land.at[c]))
        for d in range(1, n_col):
            remote(src.at[col_peer(d)], land.at[c], at, (r, col_peer(d))).start()
        ends["spread", kind, l] = at

    def spread_sent(kind, l):
        if l < layers:
            ref = R["land_" + kind].at[l, pl.ds(0, n_col - 1)]
            remote(ref, ref, ends["spread", kind, l], (r, col_peer(1))).wait_send()

    def add_load(kind, l):
        land = R["land_" + kind].at[l]
        ref = land.at[pl.ds(0, n_col - 1)]
        remote(ref, ref, ends["spread", kind, l], (r, col_peer(1))).wait_recv()
        waits("own_%s%d" % (kind, l))
        begin("stage_" + kind, (land, R["stage_" + kind]))

    def add(kind, l):
        stage, total = R["stage_" + kind], R["sum_" + kind]
        add_sent(kind, l + 1)
        waits("stage_" + kind)
        for q in range(seqs):
            value = sum(stage[q * group + n].astype(F32) for n in range(group))
            total[q] = value.astype(BF16)
        parts, at = R["parts_" + kind], new_far()
        begin("part_%s%d" % (kind, l), (total, parts.at[l, r]))
        for q in range(1, n_row):
            remote(total, parts.at[l, r], at, row_peer(q)).start()
        ends["add", kind, l] = at

    def added(kind, l):
        ref = R["parts_" + kind].at[l, pl.ds(0, n_row - 1)]
        return remote(ref, ref, ends["add", kind, l], row_peer(1))

    def add_sent(kind, l):
        if l < layers:
            waits("part_%s%d" % (kind, l))
            added(kind, l).wait_send()

    def part_copy(l, j, i, at):
        to = c - g + lax.rem(g - j + group, group)
        strip = pl.ds(i, 1)
        return remote(R["part%d" % j].at[strip], R["in_part"].at[l, j - 1, strip], at[j] + i, (r, to))

    def back_strip(l, i, at):
        kvs = [R["kv"]] + [R["peer"].at[j] for j in range(group - 1)]
        gkvs = [R["part%d" % j] for j in range(group)]
        attend_back_strip(held, bias, g, i, R["gq"], R["lse"], R["att"], R["low"], kvs, R["gq"], gkvs)
        for j in range(1, group):
            part_copy(l, j, i, at).start()

    def load_qkv(l):
        begin("qkv", *[
            (R["w_qkv"].at[l, i], R["wq"].at[i // 2, :, columns(i % 2, 384)]) for i in range(NARROW)
        ])

    def load_mlp(l):
        load_strips(l)
        begin("proj", (R["w_proj"].at[l], R["wp"]))

    def load_attention(l):
        begin("mid", (R["mids"].at[l], R["mid"]))
        begin("att", (R["atts"].at[l], R["att"]))
        begin("q", (R["qs"].at[l], R["gq"]))
        begin("kv", (R["kvs"].at[l], R["kv"]), (R["peers"].at[l], R["peer"]), (R["lses"].at[l], R["lse"]))

    last = layers - 1
    begin("cotangent", (R["cotangent"], R["low"]))
    begin("tables", *[(R["in_" + name], R[name]) for name in TABLES + ("vec", "reds")])
    load_mlp(last)
    load_attention(last)
    load_qkv(last)
    at_result = columns_start(0, R["result"])
    at_ids = new_far()
    begin("ids", (R["ids"], R["all_ids"].at[r]))
    for q in range(1, n_row):
        remote(R["ids"], R["all_ids"].at[r], at_ids, row_peer(q)).start()
    waits("cotangent")

    def widen(rows):
        R["grad"][rows, :] = R["low"][rows, :].astype(F32)

    by_rows(tokens, widen)
    waits("tables")
    for l in reversed(range(layers)):
        t = {name: R[name].at[l] for name in TABLES if "qkv" not in name}
        vec = Vectors(R["vec"], l)
        spread_sent("mlp", l + 1)
        mlp_back_stage(
            vec, R["grad"], R["active"], R["g_hid"], R["mid"], R["att"], R["low"], R["total"], R["wp"], R["wu"],
            R["wd"], R["reds"].at[l], {k: (v if k in ("low_down", "up_up") else v[...]) for k, v in t.items()},
            R["grads_mlp"], R["total2"], waits, strip_waits(l),
        )
        spread("mlp", l)
        if l > 0:
            load_mlp(l - 1)
        begin("x", (R["tokens"] if l == 0 else R["xs"].at[l - 1], R["x0"] if l == 0 else R["mid"]))
        waits("q")
        waits("kv")
        at = [far[0] + j * NARROW for j in range(group)]
        far[0] += group * NARROW
        quarter = NARROW // 4

        def strips_from(first, count):
            each(count, lambda i: back_strip(l, first + i, at))

        strips_from(0, quarter)
        add_load("mlp", l)
        if l < last:
            add_load("qkv", l + 1)
        strips_from(quarter, quarter)
        add("mlp", l)
        if l < last:
            add("qkv", l + 1)
        strips_from(2 * quarter, 2 * quarter)
        for i in range(NARROW):
            for j in range(1, group):
                part_copy(l, j, i, at).wait_recv()
            begin(("part", i), *[(R["in_part"].at[l, j, i], R["peer"].at[j, i]) for j in range(group - 1)])
        parts = [R["part0"]] + [R["peer"].at[j] for j in range(group - 1)]
        spread_sent("qkv", l + 1)

        def put(rows, value):
            if l > 0:
                R["grad"][rows, :] = value
            else:
                for i in range(NARROW):
                    R["part0"][i, rows, :128] = value[:, i * 128 : (i + 1) * 128].astype(BF16)

        qkv_back_stage(
            vec, R["x0"] if l == 0 else R["mid"], R["total2"], R["gq"], parts, R["total"], R["g_red"], R["low"],
            R["wq"], R["reds"].at[l, 0], R["low_qkv"].at[l], R["up_qkv"].at[l], R["grads_qkv"], put, waits,
        )
        spread("qkv", l)
        for i in range(NARROW):
            for j in range(1, group):
                part_copy(l, j, i, at).wait_send()
        if l > 0:
            load_qkv(l - 1)
            load_attention(l - 1)
    at_grad = columns_start(1, R["part0"].at[:, :, pl.ds(0, 128)])
    add_load("qkv", 0)
    add("qkv", 0)
    columns_end(0, at_result)
    columns_end(1, at_grad)
    waits("ids")
    rest = R["all_ids"].at[pl.ds(0, n_row - 1)]
    remote(rest, rest, at_ids, row_peer(1)).wait()
    for kind in ("mlp", "qkv"):
        spread_sent(kind, 0)
        add_sent(kind, 0)
        for l in range(layers):
            added(kind, l).wait_recv()


def backward(n_row, n_col, group, outs, tables, ids):
    layers, _, dim, _ = outs["qkv"].shape
    hidden = outs["down"].shape[1]
    mine = outs["tokens"].shape[0]
    rank = tables[0].shape[1]
    seqs = n_col // group
    strip = (NARROW, mine)
    near, far = pl.BlockSpec(memory_space=pltpu.VMEM), pl.BlockSpec(memory_space=pltpu.HBM)
    small = list(zip(TABLES, tables)) + [("vec", outs["vec"]), ("reds", outs["reds"])]
    inputs = [("in_" + name, table, far) for name, table in small] + [("ids", ids, far)]
    for name in ("active", "slope", "mid", "att", "q", "kv", "peer", "lse", "x"):
        inputs.append((name + "s", outs["saved_" + name], far))
    inputs += [("w_" + name, outs[name], far) for name in KINDS]
    inputs += [(name, outs[name], far) for name in ("tokens", "cotangent", "result")]
    sizes = {"mlp": 512 + 2 * hidden // NARROW, "qkv": 512}
    outputs = [
        ("columns", (2, n_col * mine, 128), BF16, far),
        ("all_ids", (n_row,) + ids.shape, F32, far),
        ("in_part", (layers, group - 1) + strip + (256,), BF16, far),
    ]
    scratch = [
        ("gq", strip + (128,), BF16), ("kv", strip + (256,), BF16), ("peer", (group - 1,) + strip + (256,), BF16),
        ("lse", (NARROW, 8, mine), F32), ("total", (mine, dim), F32), ("total2", (mine, dim), F32),
        ("grad", (mine, dim), F32), ("mid", (mine, dim), F32), ("low", (mine, dim), BF16), ("att", (mine, dim), BF16),
        ("x0", (mine, dim), BF16), ("active", (mine, hidden), BF16), ("g_hid", (mine, hidden), BF16),
        ("g_red", (mine, rank), BF16), ("wq", (NARROW // 2, dim, 768), BF16), ("wp", (dim, dim), BF16),
        ("wu", (NARROW, dim, hidden // NARROW), BF16), ("wd", (hidden, dim), BF16),
    ]
    scratch += [("part%d" % j, strip + (256,), BF16) for j in range(group)]
    scratch += [(name, table.shape, table.dtype) for name, table in small]
    for kind, size in sizes.items():
        outputs.append(("land_" + kind, (layers, n_col, rank, size), BF16, far))
        outputs.append(("parts_" + kind, (layers, n_row, seqs, rank, size), BF16, far))
        scratch.append(("grads_" + kind, (NARROW, rank, size), BF16))
        scratch.append(("stage_" + kind, (n_col, rank, size), BF16))
        scratch.append(("sum_" + kind, (seqs, rank, size), BF16))
    scratch = [(name, pltpu.VMEM(shape, kind)) for name, shape, kind in scratch]
    scratch += [
        ("sem", pltpu.SemaphoreType.DMA((72 * layers + 16,))),
        ("out_sem", pltpu.SemaphoreType.DMA(((4 + group * NARROW) * layers + 4,))),
        ("in_sem", pltpu.SemaphoreType.DMA(((4 + group * NARROW) * layers + 4,))),
    ]
    names = [x[0] for x in inputs] + [x[0] for x in outputs] + [x[0] for x in scratch]
    made = pl.pallas_call(
        functools.partial(backward_body, layers, group, n_row, n_col, tuple(names)),
        out_shape=[shape_of(shape, kind) for _, shape, kind, _ in outputs],
        in_specs=[spec for _, _, spec in inputs],
        out_specs=[spec for _, _, _, spec in outputs],
        scratch_shapes=[shape for _, shape in scratch],
        compiler_params=pltpu.CompilerParams(
            collective_id=1, has_side_effects=True, vmem_limit_bytes=62 * 2**20
        ),
        name="backward",
    )(*[array for _, array, _ in inputs])
    return dict(zip([x[0] for x in outputs], made))


def place_body(sizes, weights, *refs):
    parts, outs = refs[: len(sizes)], refs[len(sizes) :]
    adapters = outs[0].shape[1]
    sequences = parts[0].shape[1]
    l = pl.program_id(0)
    n = 0
    for part, (kind, pieces) in zip(parts, sizes):
        at = 0
        for site, size in zip(SITES[kind], pieces):
            for a in range(adapters):
                value = 0.0
                for q in range(sequences):
                    value = value + part[0, q, :, at : at + size].astype(F32) * weights[a, site * sequences + q]
                outs[n][0, a] = value
            at += size
            n += 1


def place(parts, sizes, weights):
    layers, sequences, rank, _ = parts[0].shape
    adapters = weights.shape[0]
    widths = [size for _, pieces in sizes for size in pieces]
    return pl.pallas_call(
        functools.partial(place_body, sizes),
        grid=(layers,),
        out_shape=[shape_of((layers, adapters, rank, size), F32) for size in widths],
        in_specs=[pl.BlockSpec(memory_space=pltpu.SMEM)]
        + [pl.BlockSpec((1,) + part.shape[1:], lambda l: (l, 0, 0, 0)) for part in parts],
        out_specs=[pl.BlockSpec((1, adapters, rank, size), lambda l: (l, 0, 0, 0)) for size in widths],
        compiler_params=PARAMS,
        name="place",
    )(weights, *parts)


def to_rows_body(held, x, out):
    n = 0
    for s in range(x.shape[0] // (len(held) * len(held[0]))):
        for g in range(len(held)):
            for place in held[g]:
                start = (s * BLOCKS + place) * BLOCK
                out[start : start + BLOCK, :] = x[n].astype(F32)
                n += 1


def to_rows(held, x):
    blocks, _, width = x.shape
    return pl.pallas_call(
        functools.partial(to_rows_body, held),
        out_shape=shape_of((blocks * BLOCK, width), F32),
        compiler_params=PARAMS,
        name="to_rows",
    )(x)


def pick_body(count, ids, *refs):
    for ref, out in zip(refs[:count], refs[count:]):
        out[...] = ref[...]


def pick_tables(ids, tables):
    def chosen(site, shape):
        return pl.BlockSpec((shape[0], None) + shape[2:], lambda i, ids: (0, ids[site], 0, 0))

    return pl.pallas_call(
        functools.partial(pick_body, len(tables)),
        grid_spec=pltpu.PrefetchScalarGridSpec(
            num_scalar_prefetch=1,
            grid=(1,),
            in_specs=[chosen(site, table.shape) for site, table in tables],
            out_specs=[
                pl.BlockSpec(table.shape[:1] + table.shape[2:], lambda i, ids: (0, 0, 0)) for _, table in tables
            ],
        ),
        out_shape=[shape_of(table.shape[:1] + table.shape[2:], BF16) for _, table in tables],
        compiler_params=PARAMS,
        name="pick",
    )(ids, *[table for _, table in tables])


def shards(mesh_shape, *args):
    (
        tokens, cotangent, adapter_ids, qkv_weight, qkv_bias, proj_weight, proj_bias,
        up_weight, up_bias, down_weight, down_bias, first_gain, first_shift, second_gain,
        second_shift, qkv_lower, qkv_raise, proj_lower, proj_raise, up_lower, up_raise,
        down_lower, down_raise,
    ) = args
    n_row, n_col = mesh_shape
    layers, adapters, dim, rank = qkv_lower.shape
    rows, width = tokens.shape
    units = up_weight.shape[2]
    seqs = rows // LEN
    group = n_col // seqs
    held = positions(group)
    per = BLOCKS // group
    mine = per * BLOCK
    merge = 128 // width
    c = lax.axis_index("col")
    g = lax.rem(c, group)
    ids = lax.dynamic_index_in_dim(adapter_ids, c // group, 0, keepdims=False)

    def line(pieces):
        row = jnp.concatenate([piece.reshape(layers, -1).astype(F32) for piece in pieces], axis=1)
        return jnp.pad(row, ((0, 0), (0, 512 - row.shape[1])))

    vector = jnp.stack(
        [
            line([qkv_bias]), line([up_bias]), line([proj_bias, down_bias, first_gain, first_shift]),
            line([second_gain, second_shift]),
        ],
        axis=1,
    ).reshape(layers * 4, 512)

    def turned(table):
        return jnp.swapaxes(table, 2, 3)

    tables = pick_tables(ids, [
        (0, turned(qkv_lower)), (1, turned(proj_lower)), (1, proj_raise), (2, turned(up_lower)), (2, up_raise),
        (3, turned(down_lower)), (3, down_raise),
    ])
    raise_qkv = lax.dynamic_index_in_dim(qkv_raise, ids[0], 1, keepdims=False)
    raise_qkv = raise_qkv.reshape(layers, rank, 3, NARROW, 128).transpose(0, 3, 1, 2, 4)
    tables = [tables[0], raise_qkv.reshape(layers, NARROW, rank, 384)] + list(tables[1:])
    fused = FUSED and width == 128
    outs = gather_inputs(
        n_row, n_col, group, qkv_weight.reshape(layers, -1, 3 * width), proj_weight, up_weight,
        down_weight, tokens, cotangent, vector, tables if fused else None
    )
    g_one = g.reshape(1)

    def peer_values(x, step):
        pairs = [(q, q - q % group + (q + step) % group) for q in range(n_col)]
        return lax.ppermute(x, "col", pairs)

    def to_columns(x):
        if merge > 1:
            x = x.reshape(NARROW, mine, merge, width).transpose(0, 2, 1, 3).reshape(n_col, mine, width)
        x = lax.all_to_all(x, "col", split_axis=0, concat_axis=0, tiled=True)
        return to_rows(held, x.reshape(n_col * per, BLOCK, width))

    if not fused:
        x = outs["tokens"].astype(F32)
        kept = {name: [] for name in SAVED + ("reds",)}
        for l in range(layers):
            q, kv, red = qkv_kernel(l, x, outs["vec"], outs["qkv"], tables[0], tables[1])
            kvs = [kv] + [peer_values(kv, s) for s in range(1, group)]
            att, lse = attend_kernel(group, g_one, q, kvs)
            mid, x, active, slope, reds = mlp_kernel(
                l, l == layers - 1, x, att, outs["vec"], outs["proj"], outs["up"], outs["down"], tables[2:]
            )
            reds = jnp.concatenate([red[None], reds])
            peer = jnp.stack(kvs[1:]) if group > 1 else kv[None][:0]
            for name, value in zip(SAVED + ("reds",), (q, kv, peer, att, lse, mid, active, slope, x, reds)):
                kept[name].append(value)
        for name in SAVED:
            outs["saved_" + name] = jnp.stack(kept[name][: layers - 1] if name == "x" else kept[name])
        outs["reds"] = jnp.stack(kept["reds"])
        outs["result"] = x
    if fused:
        ids_rows = jnp.pad(adapter_ids.astype(F32), ((0, 8 - seqs), (0, 128 - adapter_ids.shape[1])))
        made = backward(n_row, n_col, group, outs, tables, ids_rows)
        every = made["all_ids"][:, :seqs, : adapter_ids.shape[1]].reshape(n_row * seqs, -1).T.reshape(-1)
        weights = (every[None, :] == jnp.arange(adapters, dtype=F32)[:, None]).astype(F32)
        wide = units
        sizes = (("qkv", (128, 384)), ("mlp", (128, 128, 128, wide, wide, 128)))
        parts = [made["parts_" + kind].reshape(layers, n_row * seqs, rank, -1) for kind, _ in sizes]
        sums = place(parts, sizes, weights)
        final = [made["columns"][0].astype(F32), made["columns"][1].astype(F32)]
        for number, p in enumerate(sums):
            if number == 1:
                p = p.reshape(layers, adapters, rank, 3, width)
            elif number % 2 == 0:
                p = p.transpose(0, 1, 3, 2)
            final.append(p)
        return tuple(final)

    result = to_columns(outs["result"])

    onehot = (adapter_ids.T[:, :, None] == jnp.arange(adapters)[None, None, :]).astype(BF16)

    def all_rows(x):
        pairs = [[(q, (q + s) % n_row) for q in range(n_row)] for s in range(1, n_row)]
        return [x] + [lax.ppermute(x, "row", pair) for pair in pairs]

    onehots = jnp.concatenate(all_rows(onehot), axis=1)

    def collect(parts, named):
        if merge > 1:
            pieces, at = [], 0
            for _, size in named:
                piece = parts[:, :, at : at + size]
                at += size
                if size == 384:
                    piece = piece.reshape(NARROW, rank, 3, merge, width).transpose(0, 3, 1, 2, 4)
                else:
                    piece = piece.reshape(NARROW, rank, merge, size // merge).transpose(0, 2, 1, 3)
                pieces.append(piece.reshape(n_col, rank, size // merge))
            parts = jnp.concatenate(pieces, axis=2)
        parts = lax.all_to_all(parts, "col", split_axis=0, concat_axis=0, tiled=True)
        parts = parts.reshape((seqs, group) + parts.shape[1:]).astype(F32).sum(axis=1).astype(BF16)
        parts = jnp.concatenate(all_rows(parts), axis=0)
        sums, at = [], 0
        for site, size in named:
            piece = parts[:, :, at : at + size // merge]
            at += size // merge
            sums.append(jnp.einsum("sa,srn->arn", onehots[site], piece, preferred_element_type=F32))
        return sums

    wide = outs["down"].shape[1] // NARROW
    grads, carried = [None] * layers, None
    for l in reversed(range(layers + 1)):
        lq, lm = (l if l < layers else None), (l - 1 if l > 0 else None)
        made = back_kernel(lq, lm, group, g_one, outs, tables, carried)
        if lm is not None:
            grads[lm] = collect(made["grads_mlp"], [(1, 128), (1, 128), (2, 128), (2, wide), (3, wide), (3, 128)])
            parts = [made["out_part%d" % s] for s in range(group)]
            parts = [parts[0]] + [peer_values(parts[s], group - s) for s in range(1, group)]
            carried = (made["out_g_mid"], made["out_gq"], parts)
        if lq is not None:
            grads[lq] = collect(made["grads_qkv"], [(0, 128), (0, 384)]) + grads[lq]
    grad = made["out"]
    input_grad = to_columns(grad)

    final = []
    for number in range(8):
        p = jnp.stack([grads[l][number] for l in range(layers)])
        if number == 1:
            p = p.reshape(layers, adapters, rank, 3, width)
        elif number % 2 == 0:
            p = p.transpose(0, 1, 3, 2)
        final.append(p)
    return (result, input_grad) + tuple(final)


def solution(mesh):
    mesh_shape = (mesh.shape["row"], mesh.shape["col"])
    return jax.shard_map(
        functools.partial(shards, mesh_shape),
        mesh=mesh,
        in_specs=(
            P("row", "col"), P("row", "col"), P("row", None),
            P(None, "row", None, "col"), P(None, None, "col"),
            P(None, "col", "row"), P(None, "col"),
            P(None, "row", "col"), P(None, "col"),
            P(None, "col", "row"), P(None, "col"),
            P(None, "col"), P(None, "col"), P(None, "col"), P(None, "col"),
            P(), P(), P(), P(), P(), P(), P(), P(),
        ),
        out_specs=(
            P("row", "col"), P("row", "col"),
            P(None, None, "col", None), P(None, None, None, None, "col"),
            P(None, None, "col", None), P(None, None, None, "col"),
            P(None, None, "col", None), P(None, None, None, "col"),
            P(None, None, "col", None), P(None, None, None, "col"),
        ),
        check_vma=False,
    )
```

```python
import functools
import math

import jax
import jax.numpy as jnp
from jax import lax
from jax.experimental import pallas as pl
from jax.experimental.pallas import tpu as pltpu
from jax.sharding import PartitionSpec as P

HD = 64
LEN = 1024
BLOCK = 256
BLOCKS = LEN // BLOCK
EPSILON = 1e-05
SCALE = HD**-0.5
ROOT = (2.0 / 3.141592653589793) ** 0.5
MESH = pl.DeviceIdType.MESH
F32 = jnp.float32
BF16 = jnp.bfloat16


ROW_FIRST = (("z", 0, 1), ("z", 1, 0))
ROW_SECOND = ((0, "z", 1), (1, "z", 0))
ORDERS = (
    {"qkv": (ROW_FIRST,), "proj": (ROW_SECOND,), "up": (ROW_FIRST,) * 2, "down": (ROW_SECOND, ROW_FIRST)},
    {"qkv": (ROW_SECOND,), "proj": (ROW_FIRST,), "up": (ROW_SECOND,) * 2, "down": (ROW_SECOND,) * 2},
)
CUTS = {kind: 2 * len(pairs) for kind, pairs in ORDERS[0].items()}
KINDS = ("qkv", "proj", "up", "down")
DEPTH = 4
FUSED = True
LINK = 90e3
DELAY, ROW_DELAY = 2.0, 4.0
FIRST = 12.0


def transfer_plan(order, n_row):
    masks, rows, steps = [0], False, []
    for d in order:
        if d == "z":
            steps += [(("z", hop), tuple(masks), rows) for hop in range(1, n_row)]
            rows = True
        else:
            steps.append((d, tuple(masks), rows))
            masks = masks + [m ^ d for m in masks]
    steps.append((None, tuple(masks), rows))
    return steps


def transfer_schedule(pieces, n_row, tasks):
    cost, parts = {}, {}
    for k, (name, order, size) in enumerate(pieces):
        parts.setdefault(name, set()).add(k)
        for p, (d, masks, rows) in enumerate(transfer_plan(order, n_row)[:-1]):
            axis = "z" if isinstance(d, tuple) else d
            cost[k, p] = (axis, 2 * len(masks) * (n_row if rows else 1) * size / LINK)
    ready = {d: [] for d, _ in cost.values()}
    free = {d: 0.0 if d == "z" else FIRST for d in ready}
    flight = {d: [] for d in ready}
    for k in range(len(pieces)):
        ready[cost[k, 0][0]].append((k, 0))
    tasks, left = list(tasks), {}
    for task in tasks:
        left[task[4]] = left.get(task[4], 0) + 1
    landed, staged, now, ops = {}, {}, 0.0, []

    def stage(name):
        kind, l = name
        if name in landed and name not in staged and landed[name] <= now and not left.get((kind, l - 1)):
            staged[name] = now + 3.0
            ops.append(("stage", kind, l))

    while tasks or any(ready.values()) or any(flight.values()):
        for d in ready:
            while ready[d] and len(flight[d]) < DEPTH:
                k, p = ready[d].pop(0)
                free[d] = max(now, free[d]) + cost[k, p][1]
                flight[d].append((free[d] + (ROW_DELAY if d == "z" else DELAY), k, p))
                ops.append(("start", k, p))
        if tasks:
            for name in list(landed):
                stage(name)
        events = [f for line in flight.values() for f in line]
        event = min(events) if events else None
        due = None
        if tasks:
            need = tasks[0][4]
            due = now if need is None else staged.get(need)
            if due is None and need in landed and not left.get((need[0], need[1] - 1)):
                due = landed[need]
        if due is not None and (event is None or max(due, now) < event[0]):
            now = max(due, now)
            need = tasks[0][4]
            if need is not None and need not in staged:
                continue
            name, l, part, micros, _ = tasks.pop(0)
            left[need] -= 1
            now += micros
            ops.append(("task", name, (l, part)))
            continue
        now, k, p = max(now, event[0]), event[1], event[2]
        d = cost[k, p][0]
        flight[d].remove(event)
        ops.append(("wait", k, p))
        if (k, p + 1) in cost:
            later = ready[cost[k, p + 1][0]]
            later.append((k, p + 1))
            later.sort()
        else:
            name = pieces[k][0]
            parts[name].discard(k)
            if not parts[name]:
                landed[name] = now + 4.0
    return ops


def place_of(group, g, b):
    if group == 2:
        return g + b * (BLOCKS - 1 - 2 * g)
    return g * (BLOCKS // group) + b


def positions(group):
    per = BLOCKS // group
    return tuple(tuple(place_of(group, g, b) for b in range(per)) for g in range(group))


NARROW = 8
CROSS = ((0,), (0,))
TURNED = ((1,), (1,))


def dot(a, b, dims=((1,), (0,))):
    return lax.dot_general(a, b, (dims, ((), ())), preferred_element_type=F32)


def columns(i, size=128):
    if isinstance(i, int):
        return pl.ds(i * size, size)
    return pl.ds(pl.multiple_of(i * size, size), size)


def norm_parts(x):
    center = x - jnp.mean(x, axis=1, keepdims=True)
    inverse = lax.rsqrt(jnp.mean(center * center, axis=1, keepdims=True) + EPSILON)
    return center * inverse, inverse


def norm_grad(grad, scaled, inverse, gain):
    w = grad * gain
    first = jnp.mean(w, axis=1, keepdims=True)
    second = jnp.mean(w * scaled, axis=1, keepdims=True)
    return inverse * (w - first - scaled * second)


def norm_low(x, gain, shift):
    return (norm_parts(x)[0] * gain + shift).astype(BF16)


def pair_state(held):
    group, per = len(held), len(held[0])
    state = {}
    for s in range(per):
        for j in range(group):
            for b in range(per):
                seen = {held[(g - j) % group][b] <= held[g][s] for g in range(group)}
                state[s, j, b] = 0 if len(seen) == 2 else (1 if True in seen else -1)
    return state


def pair_bias(held, g):
    group = len(held)
    bias = {}
    for (s, j, b), state in pair_state(held).items():
        if state == 0:
            keys = place_of(group, lax.rem(g - j + group, group), b)
            bias[s, j, b] = jnp.where(keys <= place_of(group, g, s), 0.0, -1e9).astype(F32)
    return bias


def head_mask(h):
    lane = lax.broadcasted_iota(jnp.int32, (1, 128), 1)
    return (lane // HD) == h


def turning_pair(held, g):
    if len(held) != 2:
        return None, [0.0] * len(held[0])
    at = 1 - g
    return at, [jnp.where(at == n, 1.0, 0.0).astype(F32) for n in range(len(held[0]))]


def both_heads(x):
    return jnp.concatenate([jnp.where(head_mask(h), x, 0).astype(BF16) for h in range(2)], axis=0)


def slots_of(held, j, b, fixed):
    state = pair_state(held)
    return [s for s in range(len(held[0])) if state[s, j, b] > 0 or (state[s, j, b] == 0 and not fixed)]


def attend_strip(held, bias, g, i, q, kvs, out, lse):
    group, per = len(held), len(held[0])
    at, here = turning_pair(held, g)
    wide = 2 * BLOCK
    blocks = [(j, b, slots_of(held, j, b, at is not None)) for j in range(group) for b in range(per)]
    queries = [both_heads(q[i, s * BLOCK : (s + 1) * BLOCK, :] * SCALE) for s in range(per)]
    scores = {s: [] for s in range(per)}
    for j, b, slots in blocks:
        if slots:
            keys = kvs[j][i, b * BLOCK : (b + 1) * BLOCK, :128]
            score = dot(keys, jnp.concatenate([queries[s] for s in slots], axis=0), TURNED)
            for n, s in enumerate(slots):
                part = score[:, n * wide : (n + 1) * wide]
                scores[s].append(((j, b), part + bias[s, j, b] if (s, j, b) in bias and at is None else part))
    turned = {(j, b): kvs[j][i, b * BLOCK : (b + 1) * BLOCK, 128:].T for j, b, slots in blocks if slots}

    def weigh(e, values):
        e = e.astype(BF16)
        return jnp.concatenate(
            [dot(values[h * HD : (h + 1) * HD], e[:, h * BLOCK : (h + 1) * BLOCK]) for h in range(2)], axis=1
        )

    extra = None
    if at is not None:
        moving = pl.ds(pl.multiple_of(at * BLOCK, BLOCK), BLOCK)
        score = dot(kvs[1][i, moving, :128], both_heads(q[i, moving, :] * SCALE), TURNED)
        top = jnp.max(score, axis=0, keepdims=True)
        e = jnp.exp(score - top)
        extra = (top, jnp.sum(e, axis=0, keepdims=True), weigh(e, kvs[1][i, moving, 128:].T))
    for s in range(per):
        tops = [jnp.max(x, axis=0, keepdims=True) for _, x in scores[s]]
        if extra:
            tops.append(extra[0] + (here[s] - 1.0) * 1e9)
        top = functools.reduce(jnp.maximum, tops)
        total, made = 0.0, 0.0
        for place, score in scores[s]:
            e = jnp.exp(score - top)
            total = total + jnp.sum(e, axis=0, keepdims=True)
            made = made + weigh(e, turned[place])
        if extra:
            weight = jnp.exp(tops[-1] - top) * here[s]
            total = total + weight * extra[1]
            made = made + weight * extra[2]
        made = made / total
        level = top + jnp.log(total)
        rows = pl.ds(s * BLOCK, BLOCK)
        for h in range(2):
            lse[i, h : h + 1, rows] = level[:, h * BLOCK : (h + 1) * BLOCK]
        both = jnp.concatenate([made[:, :BLOCK], made[:, BLOCK:]], axis=0)
        out[rows, columns(i)] = both.T.astype(BF16)


def attend_back_strip(held, bias, g, i, q, lse, out, grad, kvs, gq, gkvs):
    group, per = len(held), len(held[0])
    at, here = turning_pair(held, g)

    def slot(rows):
        up = grad[rows, columns(i)]
        product = (up.astype(F32) * out[rows, columns(i)].astype(F32)).T
        inner = [jnp.sum(product[h * HD : (h + 1) * HD], axis=0, keepdims=True) for h in range(2)]
        level = [lse[i, h : h + 1, rows] for h in range(2)]
        return [
            both_heads(q[i, rows, :] * SCALE), both_heads(up),
            jnp.concatenate(inner, axis=1), jnp.concatenate(level, axis=1),
        ]

    def block(parts, keys, values):
        query, given = [jnp.concatenate([part[n] for part in parts], axis=0) for n in (0, 1)]
        inner, level = [jnp.concatenate([part[n] for part in parts], axis=1) for n in (2, 3)]
        probs = jnp.exp(dot(keys, query, TURNED) - level)
        g_scores = (probs * (dot(values, given, TURNED) - inner)).astype(BF16)
        turned = keys.T
        made = []
        for n in range(len(parts)):
            pieces = []
            for h in range(2):
                first = (2 * n + h) * BLOCK
                pieces.append(dot(turned[h * HD : (h + 1) * HD], g_scores[:, first : first + BLOCK]))
            made.append(jnp.concatenate(pieces, axis=0))
        return made, dot(g_scores, query), dot(probs.astype(BF16), given)

    slots = [slot(pl.ds(s * BLOCK, BLOCK)) for s in range(per)]
    total = [0.0] * per
    moved = None
    if at is not None:
        moving = pl.ds(pl.multiple_of(at * BLOCK, BLOCK), BLOCK)
        moved = block([slot(moving)], kvs[1][i, moving, :128], kvs[1][i, moving, 128:])
        total = [here[s] * moved[0][0] for s in range(per)]
    for j in range(group):
        for b in range(per):
            rows = pl.ds(b * BLOCK, BLOCK)
            k, v = 0.0, 0.0
            wanted = slots_of(held, j, b, at is not None)
            if wanted:
                parts = []
                for s in wanted:
                    part = list(slots[s])
                    if at is None and (s, j, b) in bias:
                        part[3] = part[3] - bias[s, j, b]
                    parts.append(part)
                made, k, v = block(parts, kvs[j][i, rows, :128], kvs[j][i, rows, 128:])
                for n, s in enumerate(wanted):
                    total[s] = total[s] + made[n]
            if at is not None and j == 1:
                k, v = k + here[b] * moved[1], v + here[b] * moved[2]
            gkvs[j][i, rows, :128] = k.astype(BF16)
            gkvs[j][i, rows, 128:] = v.astype(BF16)
    for s in range(per):
        gq[i, pl.ds(s * BLOCK, BLOCK), :] = (total[s] * SCALE).T.astype(BF16)


def by_rows(count, body, size=128):
    each(count // size, lambda n: body(pl.ds(pl.multiple_of(n * size, size), size)))


def keep(value, red, red_out):
    red[...] = value.astype(BF16)
    red_out[...] = value.T.astype(BF16)


def each(count, body):
    def step(i, carry):
        body(i)
        return carry

    lax.fori_loop(0, count, step, 0)


def qkv_stage(x, gain, shift, w, bias, low, up, q, kv, red, red_out, normed):
    def norm(rows):
        normed[rows, :] = norm_low(x[rows, :], gain, shift)

    by_rows(x.shape[0], norm)
    keep(dot(normed[...], low[...], TURNED), red, red_out)

    def pair(j):
        made = dot(normed[...], w[j])
        for n in range(2):
            i = 2 * j + n
            mixed = made[:, n * 384 : (n + 1) * 384] + (bias[i] + dot(red[...], up[i]))
            q[i] = mixed[:, :128].astype(BF16)
            kv[i] = mixed[:, 128:].astype(BF16)

    each(NARROW // 2, pair)


def proj_stage(x, att, w, bias, low, up, gain, shift, low_up, mid, normed, red, red_out, red_up, red_up_out):
    keep(dot(att[...], low[...], TURNED), red, red_out)

    def part(rows):
        value = x[rows, :] + (dot(att[rows, :], w[...]) + bias + dot(red[rows, :], up[...]))
        mid[rows, :] = value
        normed[rows, :] = norm_low(value, gain, shift)

    by_rows(x.shape[0], part, 256)
    keep(dot(normed[...], low_up[...], TURNED), red_up, red_up_out)


def up_strip(i, normed, w, bias, red_up, up, active, slope):
    units = w.shape[2]
    cols = columns(i, units)
    value = dot(normed[...], w[i]) + (bias[i] + dot(red_up[...], up[:, cols]))
    made, made_slope = gelu_parts(value)
    active[:, cols] = made.astype(BF16)
    slope[:, cols] = made_slope.astype(BF16)


def down_stage(mid, active, w, bias, up, red, put):
    for n in range(mid.shape[1] // 256):
        cols = slice(n * 256, (n + 1) * 256)
        put(n, mid[:, cols] + (dot(active[...], w[:, cols]) + bias[:, cols] + dot(red[...], up[:, cols])))


def gelu_parts(x):
    square = x * x
    t = jnp.tanh(ROOT * (x + 0.044715 * (x * square)))
    half = 0.5 * (1.0 + t)
    slope = half + 0.5 * x * (1.0 - t * t) * (ROOT * (1.0 + 3 * 0.044715 * square))
    return x * half, slope


class Vectors:
    def __init__(self, ref, l):
        self.ref, self.l = ref, l

    def qkv(self, i):
        return self.ref[i, pl.ds(4 * self.l, 1), :384]

    def up(self, i):
        return self.ref[i, pl.ds(4 * self.l + 1, 1), :]

    def row(self, name):
        at = ("proj", "down", "gain1", "shift1", "gain2", "shift2").index(name)
        row, lane = 4 * self.l + 2 + at // 4, at % 4 * 128
        return jnp.concatenate([self.ref[i, row : row + 1, lane : lane + 128] for i in range(NARROW)], axis=1)


class Strips:
    def __init__(self, read):
        self.read = read

    def __getitem__(self, i):
        return self.read(i)


TABLES = ("low_qkv", "up_qkv", "low_proj", "up_proj", "low_up", "up_up", "low_down", "up_down")
SAVED = ("q", "kv", "peer", "att", "lse", "mid", "active", "slope", "x")


def task_list(layers):
    tasks = [("load", 0, 0, 3.0, None)]
    for l in range(layers):
        tasks.append(("qkv", l, 0, 7.0, ("qkv", l)))
        tasks += [("attend", l, n, 5.5, None) for n in range(2)]
        tasks.append(("proj", l, 0, 4.0, ("proj", l)))
        tasks += [("up", l, n, 6.0, ("up", l)) for n in range(2)]
        tasks.append(("down", l, 0, 6.0, ("down", l)))
    return tasks


class ForwardWork:
    def __init__(self, n_col, group, refs):
        self.__dict__.update(refs)
        self.group = group
        self.held = positions(group)
        self.r, self.c = lax.axis_index("row"), lax.axis_index("col")
        self.g = lax.rem(self.c, group)
        self.bias = pair_bias(self.held, self.g)
        self.layers = self.low_qkv.shape[0]

    def stage_copies(self, kind, l):
        full = self.full[kind]
        if kind == "qkv":
            pieces = []
            for i in range(NARROW):
                src = full.at[l, i]
                pieces.append((src, self.wq.at[i // 2, :, :, :, pl.ds(i % 2 * 384, 384)]))
            return pieces, self.wq
        if kind == "up":
            return [(full.at[l, i], self.wu.at[i]) for i in range(NARROW)], self.wu
        target = self.wp if kind == "proj" else self.wd
        return [(full.at[l, i], target.at[i]) for i in range(NARROW)], target

    def stage(self, kind, l):
        for src, dst in self.stage_copies(kind, l)[0]:
            pltpu.make_async_copy(src, dst, self.stage_sem.at[KINDS.index(kind)]).start()

    def staged(self, kind, l):
        target = self.stage_copies(kind, l)[1]
        pltpu.make_async_copy(target, target, self.stage_sem.at[KINDS.index(kind)]).wait()

    def save_copy(self, name, l):
        src = {
            "q": self.q, "kv": self.kv, "peer": self.peer.at[l], "att": self.att, "lse": self.lse,
            "mid": self.mid, "active": self.active, "slope": self.slope, "x": self.x,
        }[name]
        return pltpu.make_async_copy(src, self.saved[name].at[l], self.save_sem.at[l, SAVED.index(name)])

    def save(self, *names, l):
        for name in names:
            self.save_copy(name, l).start()

    def settled(self, *names, l):
        if l >= 0:
            for name in names:
                self.save_copy(name, l).wait()

    def exchange(self, l, s):
        to = self.c - self.g + lax.rem(self.g + s, self.group)
        return pltpu.make_async_remote_copy(
            src_ref=self.kv, dst_ref=self.peer.at[l, s - 1],
            send_sem=self.kv_send.at[l, s - 1], recv_sem=self.kv_recv.at[l, s - 1],
            device_id=(self.r, to), device_id_type=MESH,
        )

    def run(self, name, l, part):
        vec = Vectors(self.vec, l)
        if name == "load":
            self.arrive_tokens()
            self.x[...] = self.tokens_v[...].astype(F32)
        elif name == "qkv":
            self.staged("qkv", l)
            self.settled("q", "kv", l=l - 1)
            if l > 0:
                for s in range(1, self.group):
                    self.exchange(l - 1, s).wait_send()
            w = self.wq.reshape(NARROW // 2, -1, 768)
            qkv_stage(
                self.x, vec.row("gain1"), vec.row("shift1"), w, Strips(vec.qkv), self.low_qkv.at[l],
                self.up_qkv.at[l], self.q, self.kv, self.red, self.reds.at[l, 0], self.normed,
            )
            for s in range(1, self.group):
                self.exchange(l, s).start()
            self.save("q", "kv", l=l)
        elif name == "attend":
            if part == 0:
                for s in range(1, self.group):
                    self.exchange(l, s).wait_recv()
                self.save("peer", l=l)
                self.settled("att", "lse", l=l - 1)
            kvs = [self.kv] + [self.peer.at[l, s - 1] for s in range(1, self.group)]
            size = NARROW // 2
            each(size, lambda n: attend_strip(self.held, self.bias, self.g, part * size + n, self.q, kvs, self.att, self.lse))
            if part == 1:
                self.save("att", "lse", l=l)
        elif name == "proj":
            self.staged("proj", l)
            self.settled("mid", l=l - 1)
            dim = self.att.shape[1]
            proj_stage(
                self.x, self.att, self.wp.reshape(dim, dim), vec.row("proj"), self.low_proj.at[l],
                self.up_proj.at[l], vec.row("gain2"), vec.row("shift2"), self.low_up.at[l],
                self.mid, self.normed, self.red, self.reds.at[l, 1], self.red_up, self.reds.at[l, 2],
            )
            self.save("mid", l=l)
        elif name == "up":
            if part == 0:
                self.staged("up", l)
                self.settled("active", "slope", l=l - 1)
            w = self.wu.reshape(NARROW, self.x.shape[1], -1)
            size = NARROW // 2
            each(size, lambda n: up_strip(
                part * size + n, self.normed, w, Strips(vec.up), self.red_up, self.up_up.at[l],
                self.active, self.slope,
            ))
            if part == 1:
                self.save("active", "slope", l=l)
                keep(dot(self.active[...], self.low_down[l], TURNED), self.red, self.reds.at[l, 3])
        elif name == "down":
            self.staged("down", l)
            self.settled("x", l=l - 1)
            dim = self.x.shape[1]

            def put(n, value):
                if l < self.layers - 1:
                    self.x[:, columns(n, 256)] = value
                else:
                    for m in range(2):
                        self.result[2 * n + m] = value[:, m * 128 : (m + 1) * 128].astype(BF16)

            down_stage(
                self.mid, self.active, self.wd.reshape(-1, dim), vec.row("down"), self.up_down.at[l], self.red, put,
            )
            if l < self.layers - 1:
                self.save("x", l=l)

    def close(self):
        last = self.layers - 1
        self.settled(*[name for name in SAVED if name not in ("x", "peer")], l=last)
        for l in range(self.layers):
            self.settled("peer", l=l)
        for s in range(1, self.group):
            self.exchange(last, s).wait_send()
        if last > 0:
            pass


def gather_body(n_row, n_col, layers, group, names, *refs):
    refs = dict(zip(names, refs))
    shard = {kind: refs["shard_" + kind] for kind in KINDS}
    full = {kind: refs["full_" + kind] for kind in KINDS}
    tokens, cotangent, vector = refs["tokens"], refs["cotangent"], refs["vector"]
    own_tokens, own_cotangent, vectors = refs["own_tokens"], refs["own_cotangent"], refs["vectors"]
    local_sem, send_sem, recv_sem = refs["local_sem"], refs["send_sem"], refs["recv_sem"]
    near_sem, out_sem, in_sem = refs["near_sem"], refs["out_sem"], refs["in_sem"]
    r = lax.axis_index("row")
    c = lax.axis_index("col")
    link_bits = [b for b in (2**k for k in range(1, 8)) if b < n_col]
    depth = shard["up"].shape[1]

    def row_peer(s):
        return (lax.rem(r + s, n_row), c)

    def col_peer(bit):
        return (r, c ^ bit)

    peers = [row_peer(s) for s in range(1, n_row)]
    peers += [(r, lax.rem(c + d, n_col)) for d in range(1, n_col)]
    barrier = pltpu.get_barrier_semaphore()
    for peer in peers:
        pl.semaphore_signal(barrier, inc=1, device_id=peer, device_id_type=MESH)
    pl.semaphore_wait(barrier, len(peers))

    per, width = BLOCKS // group, tokens.shape[1]

    def own_place(ref, b, col):
        if len(ref.shape) == 2:
            start = pl.multiple_of(col * width, width)
            return ref.at[pl.ds(b * BLOCK, BLOCK), pl.ds(start, width)]
        return ref.at[col, pl.ds(b * BLOCK, BLOCK)]

    def from_place(ref, b, col):
        start = (col // group) * LEN + place_of(group, lax.rem(col, group), b) * BLOCK
        return ref.at[pl.ds(pl.multiple_of(start, BLOCK), BLOCK)]

    exchanged = ((tokens, own_tokens), (cotangent, own_cotangent))

    def near(n, b):
        src, dst = exchanged[n]
        return pltpu.make_async_copy(from_place(src, b, c), own_place(dst, b, c), near_sem.at[n * per + b])

    def near_vector():
        return pltpu.make_async_copy(vector, vectors.at[c], near_sem.at[2 * per])

    def far(src, dst, n, peer):
        return pltpu.make_async_remote_copy(
            src_ref=src, dst_ref=dst, send_sem=out_sem.at[n], recv_sem=in_sem.at[n],
            device_id=peer, device_id_type=MESH,
        )

    def start_exchange(n):
        src, dst = exchanged[n]
        for b in range(per):
            near(n, b).start()
        for d in range(1, n_col):
            to = lax.rem(c + d, n_col)
            for b in range(per):
                far(from_place(src, b, to), own_place(dst, b, c), n, (r, to)).start()

    def wait_exchange(n):
        _, dst = exchanged[n]
        for b in range(per):
            near(n, b).wait()
        if len(dst.shape) == 2:
            ref = dst.at[:, pl.ds(0, (n_col - 1) * width)]
        else:
            ref = dst.at[pl.ds(0, n_col - 1)]
        far(ref, ref, n, col_peer(1)).wait()

    def own(kind, l, h, dst):
        ref = shard[kind]
        size = ref.shape[-2] // CUTS[kind]
        if len(ref.shape) == 3:
            return [(ref.at[l, pl.ds(h * size, size)], dst)]
        return [
            (ref.at[l, n, pl.ds(h * size, size)], dst.at[:, pl.ds(n * ref.shape[3], ref.shape[3])])
            for n in range(ref.shape[1])
        ]

    def block(kind, l, h, row, col):
        if kind in ("qkv", "up"):
            return full[kind].at[l, col, row, h]
        start = pl.multiple_of(row * depth, depth)
        return full[kind].at[l, col, h, :, pl.ds(start, depth)]

    def strip(kind, l, h, col):
        if kind in ("qkv", "up"):
            return full[kind].at[l, col, :, h]
        return full[kind].at[l, col, h]

    def amount(kind, l, h, strips, rows):
        if kind in ("qkv", "up"):
            return full[kind].at[l, pl.ds(0, strips), pl.ds(0, rows), h]
        return full[kind].at[l, pl.ds(0, strips), h, :, pl.ds(0, rows * depth)]

    chunks = []
    for l in range(layers):
        for kind in KINDS:
            for h in range(CUTS[kind]):
                order = []
                for d in ORDERS[l % len(ORDERS)][kind][h // 2][h % 2]:
                    if d == "z":
                        order.append("z")
                    elif d < len(link_bits):
                        order.append(link_bits[d])
                order += link_bits[2:]
                chunks.append((kind, l, h, tuple(order)))
    phases = len(link_bits) + n_row - 1

    def remote(src, dst, k, p, peer, way=0):
        at = (k * (phases + 1) + p) * 2 + way
        return pltpu.make_async_remote_copy(
            src_ref=src, dst_ref=dst, send_sem=send_sem.at[at], recv_sem=recv_sem.at[at],
            device_id=peer, device_id_type=MESH,
        )

    def plan(k):
        return transfer_plan(chunks[k][3], n_row)

    def ways(hop):
        return (
            (r - hop + 1, (r - hop + 1 >= 0) & (r + 1 < n_row), r - hop >= 0, 1),
            (r + hop - 1, (r + hop - 1 < n_row) & (r >= 1), r + hop < n_row, n_row - 1),
        )

    def local_start(k):
        kind, l, h, _ = chunks[k]
        for src, dst in own(kind, l, h, block(kind, l, h, r, c)):
            pltpu.make_async_copy(src, dst, local_sem.at[k]).start()

    def local_wait(k):
        kind, l, h, _ = chunks[k]
        ref = block(kind, l, h, r, c)
        pltpu.make_async_copy(ref, ref, local_sem.at[k]).wait()

    def issue(k, p):
        kind, l, h, order = chunks[k]
        d, masks, rows = plan(k)[p]

        def send(m, row, first, peer, way):
            dst = block(kind, l, h, row, c ^ m)
            for src, to in own(kind, l, h, dst) if m == 0 and first else [(dst, dst)]:
                remote(src, to, k, p, peer, way).start()

        if isinstance(d, tuple):
            for way, (row, goes, _, step) in enumerate(ways(d[1])):

                @pl.when(goes)
                def _():
                    for m in masks:
                        send(m, row, d[1] == 1, row_peer(step), way)

            return
        for m in masks:
            if rows:
                ref = strip(kind, l, h, c ^ m)
                remote(ref, ref, k, p, col_peer(d)).start()
            else:
                send(m, r, True, col_peer(d), 0)

    def moved(k, p, send):
        kind, l, h, order = chunks[k]
        d, masks, rows = plan(k)[p]
        ref = amount(kind, l, h, len(masks), n_row if rows else 1)
        if not isinstance(d, tuple):
            copy = remote(ref, ref, k, p, col_peer(1))
            copy.wait_send() if send else copy.wait_recv()
            return
        for way, (_, goes, comes, step) in enumerate(ways(d[1])):

            @pl.when(goes if send else comes)
            def _():
                copy = remote(ref, ref, k, p, row_peer(step), way)
                copy.wait_send() if send else copy.wait_recv()

    def share(k, p):
        kind, l, h, order = chunks[k]
        (d, masks, _), (_, later, rows) = plan(k)[p : p + 2]
        if not rows:
            return
        fresh = masks if isinstance(d, tuple) else later[len(masks):]
        for m in fresh:
            ref = strip(kind, l, h, c ^ m)
            remote(ref, ref, k, phases, col_peer(1)).start()

    def shared(k):
        kind, l, h, _ = chunks[k]
        ref = amount(kind, l, h, n_col // 2, n_row)
        return remote(ref, ref, k, phases, col_peer(1))

    def finish(k, p):
        moved(k, p, False)
        if plan(k)[p][0] == ("z", n_row - 1):
            local_wait(k)
        share(k, p)

    count = len(chunks)
    near_vector().start()
    for d in range(1, n_col):
        far(vector, vectors.at[c], 2, (r, lax.rem(c + d, n_col))).start()
    start_exchange(0)
    for k in range(count):
        local_start(k)
    def vectors_arrive():
        near_vector().wait()
        rest = vectors.at[pl.ds(0, n_col - 1)]
        far(rest, rest, 2, col_peer(1)).wait()

    work = None
    if "x" in refs:
        refs.update(full=full, saved={name: refs["saved_" + name] for name in SAVED})

        def arrive_tokens():
            vectors_arrive()
            wait_exchange(0)
            load_sem = refs["load_sem"]
            loads = [(own_tokens, refs["tokens_v"]), (vectors, refs["vec"])]
            copies = [pltpu.make_async_copy(s, d, load_sem.at[n]) for n, (s, d) in enumerate(loads)]
            for copy in copies:
                copy.start()
            for copy in copies:
                copy.wait()

        refs.update(arrive_tokens=arrive_tokens)
        work = ForwardWork(n_col, group, refs)

    pieces = []
    for kind, l, h, order in chunks:
        size = 2 * math.prod(shard[kind].shape[1:]) // CUTS[kind]
        pieces.append(((kind, l), order, size))
    ops = transfer_schedule(pieces, n_row, task_list(layers) if work else [])
    quiet = max(n for n, (op, _, _) in enumerate(ops) if op == "wait")
    for n, (op, k, p) in enumerate(ops):
        if op == "start":
            issue(k, p)
        elif op == "wait":
            finish(k, p)
        elif op == "stage":
            for at, (kind, l, _, _) in enumerate(chunks):
                if (kind, l) == (k, p):
                    shared(at).wait_recv()
            work.stage(k, p)
        else:
            work.run(k, *p)
        if n == quiet:
            start_exchange(1)
    for k in range(count):
        for p in range(phases):
            moved(k, p, True)
        shared(k).wait_send()
        if not work:
            shared(k).wait_recv()
    if work:
        work.close()
    else:
        vectors_arrive()
        wait_exchange(0)
    wait_exchange(1)


def gather_inputs(n_row, n_col, group, qkv, proj, up, down, tokens, cotangent, vector, tables=None):
    layers, depth = up.shape[0], up.shape[1]
    width, units = proj.shape[1], down.shape[1]
    dim, hidden = depth * n_row, units * n_col
    mine = LEN // group
    cuts = [CUTS[kind] for kind in KINDS]
    own = (mine, dim) if width % 128 == 0 else (n_col, mine, width)
    hbm = pl.BlockSpec(memory_space=pltpu.HBM)
    vmem = pl.BlockSpec(memory_space=pltpu.VMEM)
    dma = pltpu.SemaphoreType.DMA
    count = layers * sum(cuts)
    phases = n_col.bit_length() + n_row - 2
    inputs = [("shard_" + kind, array, hbm) for kind, array in zip(KINDS, (qkv, proj, up, down))]
    inputs += [("tokens", tokens, hbm), ("cotangent", cotangent, hbm), ("vector", vector, hbm)]
    outputs = [
        ("full_qkv", (layers, n_col, n_row, cuts[0], depth // cuts[0], 3 * width), BF16, hbm),
        ("full_proj", (layers, n_col, cuts[1], width // cuts[1], dim), BF16, hbm),
        ("full_up", (layers, n_col, n_row, cuts[2], depth // cuts[2], units), BF16, hbm),
        ("full_down", (layers, n_col, cuts[3], units // cuts[3], dim), BF16, hbm),
        ("own_tokens", own, BF16, hbm),
        ("own_cotangent", own, BF16, hbm),
        ("vectors", (n_col,) + vector.shape, F32, hbm),
    ]
    scratch = [
        ("local_sem", dma((count,))),
        ("send_sem", dma((count * phases * 2,))),
        ("recv_sem", dma((count * phases * 2,))),
        ("near_sem", dma((2 * (BLOCKS // group) + 1,))),
        ("out_sem", dma((3,))),
        ("in_sem", dma((3,))),
    ]
    if tables is not None:
        rank = tables[0].shape[1]
        inputs += [(name, table, vmem) for name, table in zip(TABLES, tables)]
        strip = (NARROW, mine)
        kept = {
            "q": (strip + (128,), BF16), "kv": (strip + (256,), BF16), "att": ((mine, dim), BF16),
            "lse": ((NARROW, 8, mine), F32), "mid": ((mine, dim), F32), "active": ((mine, hidden), BF16),
            "slope": ((mine, hidden), BF16),
            "x": ((mine, dim), F32), "peer": ((group - 1,) + strip + (256,), BF16),
        }
        outputs += [("saved_" + name, (layers,) + kept[name][0], kept[name][1], hbm) for name in SAVED]
        outputs += [
            ("reds", (layers, 4, rank, mine), BF16, vmem),
            ("result", (NARROW, mine, 128), BF16, vmem),
        ]
        scratch += [
            (name, pltpu.VMEM(((layers,) if name == "peer" else ()) + kept[name][0], kept[name][1]))
            for name in SAVED
        ]
        scratch += [
            ("wq", pltpu.VMEM((NARROW // 2, n_row, cuts[0], depth // cuts[0], 768), BF16)),
            ("wp", pltpu.VMEM((NARROW, cuts[1], width // cuts[1], dim), BF16)),
            ("wu", pltpu.VMEM((NARROW, n_row, cuts[2], depth // cuts[2], units), BF16)),
            ("wd", pltpu.VMEM((NARROW, cuts[3], units // cuts[3], dim), BF16)),
            ("tokens_v", pltpu.VMEM((mine, dim), BF16)),
            ("normed", pltpu.VMEM((mine, dim), BF16)),
            ("red", pltpu.VMEM((mine, rank), BF16)),
            ("red_up", pltpu.VMEM((mine, rank), BF16)),
            ("vec", pltpu.VMEM((n_col,) + vector.shape, F32)),
            ("stage_sem", dma((4,))),
            ("save_sem", dma((layers, len(SAVED)))),
            ("kv_send", dma((layers, group - 1))),
            ("kv_recv", dma((layers, group - 1))),
            ("load_sem", dma((2,))),
        ]
    names = [x[0] for x in inputs] + [x[0] for x in outputs] + [x[0] for x in scratch]
    outs = pl.pallas_call(
        functools.partial(gather_body, n_row, n_col, layers, group, tuple(names)),
        out_shape=[jax.ShapeDtypeStruct(shape, kind) for _, shape, kind, _ in outputs],
        in_specs=[spec for _, _, spec in inputs],
        out_specs=[spec for _, _, _, spec in outputs],
        scratch_shapes=[shape for _, shape in scratch],
        compiler_params=pltpu.CompilerParams(
            collective_id=0, has_side_effects=True, vmem_limit_bytes=60 * 2**20
        ),
        name="gather_inputs",
    )(*[array for _, array, _ in inputs])
    outs = dict(zip([x[0] for x in outputs], outs))

    merge = 128 // width
    strips = n_col // merge
    qkv_full = outs["full_qkv"].reshape(layers, n_col, dim, 3 * width)
    up_full = outs["full_up"].reshape(layers, n_col, dim, units)
    rows, vec = [outs["own_tokens"], outs["own_cotangent"]], outs["vectors"]
    if merge > 1:
        qkv_full = qkv_full.reshape(layers, strips, merge, dim, 3, width).transpose(0, 1, 3, 4, 2, 5)
        up_full = up_full.reshape(layers, strips, merge, dim, units).transpose(0, 1, 3, 2, 4)
        rows = [x.transpose(1, 0, 2).reshape(mine, dim) for x in rows]
        vec = vec.reshape(strips, merge, layers, 4, 4 * 128)
        first = vec[:, :, :, 0, : 3 * width].reshape(strips, merge, layers, 3, width).transpose(0, 2, 3, 1, 4)
        first = jnp.pad(first.reshape(strips, layers, 384), ((0, 0), (0, 0), (0, 128)))
        second = vec[:, :, :, 1, :units].transpose(0, 2, 1, 3).reshape(strips, layers, 512)
        rest = vec[:, :, :, 2:, : 4 * width].reshape(strips, merge, layers, 2, 4, width)
        rest = rest.transpose(0, 2, 3, 4, 1, 5).reshape(strips, layers, 2, 512)
        vec = jnp.concatenate([first[:, :, None], second[:, :, None], rest], axis=2)
        vec = vec.reshape(strips, layers * 4, 512)
    outs.update(
        qkv=qkv_full.reshape(layers, strips, dim, 384),
        proj=outs["full_proj"].reshape(layers, dim, dim),
        up=up_full.reshape(layers, strips, dim, units * merge),
        down=outs["full_down"].reshape(layers, hidden, dim),
        tokens=rows[0], cotangent=rows[1], vec=vec,
    )
    return outs


PARAMS = pltpu.CompilerParams(vmem_limit_bytes=60 * 2**20)


def shape_of(shape, kind):
    return jax.ShapeDtypeStruct(shape, kind)


def kernel(body, name, inputs, outputs, scratch=()):
    spaces = (pl.BlockSpec(memory_space=pltpu.VMEM), pl.BlockSpec(memory_space=pltpu.HBM))
    return pl.pallas_call(
        body,
        out_shape=[shape_of(shape, kind) for shape, kind, _ in outputs],
        in_specs=[spaces[far] for _, far in inputs],
        out_specs=[spaces[far] for _, _, far in outputs],
        scratch_shapes=list(scratch),
        compiler_params=PARAMS,
        name=name,
    )(*[array for array, _ in inputs])


def own_group(group):
    return lax.rem(lax.axis_index("col"), group)


def qkv_body(l, x, vec, w, low, up, q, kv, red_out, red, normed, buf, sem):
    copies = []
    for i in range(NARROW):
        copies.append(pltpu.make_async_copy(w.at[l, i], buf.at[i // 2, :, columns(i % 2, 384)], sem.at[i]))
        copies[-1].start()
    for copy in copies:
        copy.wait()
    v = Vectors(vec, l)
    qkv_stage(x, v.row("gain1"), v.row("shift1"), buf, Strips(v.qkv), low.at[l], up.at[l], q, kv, red, red_out, normed)


def qkv_kernel(l, x, vec, w, low, up):
    tokens, dim = x.shape
    return kernel(
        functools.partial(qkv_body, l), "qkv",
        [(x, False), (vec, False), (w, True), (low, False), (up, False)],
        [((NARROW, tokens, 128), BF16, False), ((NARROW, tokens, 256), BF16, False), ((low.shape[1], tokens), BF16, False)],
        [pltpu.VMEM((tokens, low.shape[1]), BF16), pltpu.VMEM((tokens, dim), BF16), pltpu.VMEM((NARROW // 2, dim, 768), BF16), pltpu.SemaphoreType.DMA((NARROW,))],
    )


def attend_body(group, g_ref, q, *refs):
    held = positions(group)
    kvs, (out, lse) = refs[:group], refs[group:]
    bias = pair_bias(held, g_ref[0])
    each(NARROW, lambda i: attend_strip(held, bias, g_ref[0], i, q, kvs, out, lse))


def attend_kernel(group, g, q, kvs):
    tokens = q.shape[1]
    return pl.pallas_call(
        functools.partial(attend_body, group),
        out_shape=[shape_of((tokens, NARROW * 128), BF16), shape_of((NARROW, 8, tokens), F32)],
        in_specs=[pl.BlockSpec(memory_space=pltpu.SMEM)] + [pl.BlockSpec(memory_space=pltpu.VMEM)] * (group + 1),
        out_specs=[pl.BlockSpec(memory_space=pltpu.VMEM)] * 2,
        compiler_params=PARAMS,
        name="attend",
    )(g, q, *kvs)


def mlp_body(l, x, att, vec, wp, wu, wd, *refs):
    low_proj, up_proj, low_up, up_up, low_down, up_down = [ref.at[l] for ref in refs[:6]]
    mid, result, active, slope, reds, red, red_up, normed, bp, bu, bd, sem = refs[6:]
    copies = []
    for n, (src, dst) in enumerate(((wp.at[l], bp), (wu.at[l], bu), (wd.at[l], bd))):
        copies.append(pltpu.make_async_copy(src, dst, sem.at[n]))
        copies[-1].start()
    v = Vectors(vec, l)
    copies[0].wait()
    proj_stage(
        x, att, bp, v.row("proj"), low_proj, up_proj, v.row("gain2"), v.row("shift2"), low_up,
        mid, normed, red, reds.at[0], red_up, reds.at[1],
    )
    copies[1].wait()
    each(NARROW, lambda i: up_strip(i, normed, bu, Strips(v.up), red_up, up_up, active, slope))
    copies[2].wait()

    def put(n, value):
        if len(result.shape) == 2:
            result[:, columns(n, 256)] = value
        else:
            for m in range(2):
                result[2 * n + m] = value[:, m * 128 : (m + 1) * 128].astype(BF16)

    keep(dot(active[...], low_down[...], TURNED), red, reds.at[2])
    down_stage(mid, active, bd, v.row("down"), up_down, red, put)


def mlp_kernel(l, final, x, att, vec, wp, wu, wd, tables):
    tokens, dim = x.shape
    hidden = wd.shape[1]
    rank = tables[0].shape[1]
    result = ((NARROW, tokens, 128), BF16, False) if final else ((tokens, dim), F32, False)
    return kernel(
        functools.partial(mlp_body, l), "mlp",
        [(x, False), (att, False), (vec, False), (wp, True), (wu, True), (wd, True)] + [(t, False) for t in tables],
        [((tokens, dim), F32, False), result] + [((tokens, hidden), BF16, False)] * 2 + [((3, rank, tokens), BF16, False)],
        [
            pltpu.VMEM((tokens, rank), BF16), pltpu.VMEM((tokens, rank), BF16),
            pltpu.VMEM((tokens, dim), BF16), pltpu.VMEM(wp.shape[1:], BF16),
            pltpu.VMEM(wu.shape[1:], BF16), pltpu.VMEM(wd.shape[1:], BF16), pltpu.SemaphoreType.DMA((3,)),
        ],
    )


def mlp_back_stage(vec, grad, active, g_hid, mid, att, low, total, wp, wu, wd, reds, t, grads, g_mid, waits, strip_waits):
    low[...] = grad[...].astype(BF16)
    g_red = dot(low[...], t["up_down"], TURNED).astype(BF16)
    rank = g_red.shape[1]
    units = wu.shape[2]
    total[...] = jnp.zeros_like(total)

    def strip(i):
        cols = columns(i, units)
        strip_waits(i)
        g_active = dot(low[...], wd[cols, :], TURNED) + dot(g_red, t["low_down"][:, cols])
        g_hid[:, cols] = (g_active * g_hid[:, cols].astype(F32)).astype(BF16)
        total[...] += dot(g_hid[:, cols], wu[i], TURNED)

    each(NARROW, strip)

    def give(at, value):
        size = value.shape[1] // NARROW
        for i in range(NARROW):
            grads[i, :, at : at + size] = value[:, i * size : (i + 1) * size].astype(BF16)

    give(384 + 2 * units, dot(reds[3], low[...]))
    give(384 + units, dot(g_red, active[...], CROSS))
    give(384, dot(reds[2], g_hid[...]))
    g_hid[:, :rank] = dot(g_hid[...], t["up_up"][...], TURNED).astype(BF16)
    waits("mid")
    gain, shift = vec.row("gain2"), vec.row("shift2")
    dim = mid.shape[1]

    def norm(rows):
        scaled, inverse = norm_parts(mid[rows, :])
        active[rows, :dim] = (scaled * gain + shift).astype(BF16)
        g_normed = total[rows, :] + dot(g_hid[rows, :rank], t["low_up"])
        value = grad[rows, :] + norm_grad(g_normed, scaled, inverse, gain)
        g_mid[rows, :] = value
        low[rows, :] = value.astype(BF16)

    by_rows(mid.shape[0], norm)
    give(256, dot(g_hid[:, :rank], active[:, :dim], CROSS))
    give(128, dot(reds[1], low[...]))
    g_red_proj = dot(low[...], t["up_proj"], TURNED).astype(BF16)
    waits("att")
    waits("proj")
    give(0, dot(g_red_proj, att[...], CROSS))
    low[...] = (dot(low[...], wp[...], TURNED) + dot(g_red_proj, t["low_proj"])).astype(BF16)


def qkv_back_stage(vec, x, g_mid, gq, parts, total, g_red, normed, wq, red, low, up, grads, put, waits):
    waits("gq")
    waits("qkv")
    rank, tokens = red.shape
    small = jnp.zeros((tokens, rank), F32)
    for j in range(NARROW // 2):
        pieces = []
        for i in (2 * j, 2 * j + 1):
            waits(("part", i))
            g_kv = sum(part[i].astype(F32) for part in parts).astype(BF16)
            g_mixed = jnp.concatenate([gq[i], g_kv], axis=1)
            grads[i, :, 128:512] = dot(red[...], g_mixed).astype(BF16)
            small = small + dot(g_mixed, up[i], TURNED)
            pieces.append(g_mixed)
        made = dot(jnp.concatenate(pieces, axis=1), wq[j], TURNED)
        total[...] = made if j == 0 else total[...] + made
    g_low_rank = small.astype(BF16)
    g_red[...] = g_low_rank
    waits("x")
    waits("g_mid")
    gain, shift = vec.row("gain1"), vec.row("shift1")

    def norm(rows):
        scaled, inverse = norm_parts(x[rows, :].astype(F32))
        normed[rows, :] = (scaled * gain + shift).astype(BF16)
        g_normed = total[rows, :] + dot(g_red[rows, :], low[...])
        put(rows, g_mid[rows, :] + norm_grad(g_normed, scaled, inverse, gain))

    by_rows(tokens, norm)
    g_low = dot(g_low_rank, normed[...], CROSS).astype(BF16)
    for i in range(NARROW):
        grads[i, :, :128] = g_low[:, i * 128 : (i + 1) * 128]


def back_body(lq, lm, group, names, *refs):
    R = dict(zip(names, refs))
    held = positions(group)
    sem, started = R["sem"], {}

    def waits(name):
        for copy in started.pop(name, ()):
            copy.wait()

    count = [0]

    def begin(name, *copies):
        started[name] = []
        for src, dst in copies:
            copy = pltpu.make_async_copy(src, dst, sem.at[count[0]])
            count[0] += 1
            copy.start()
            started[name].append(copy)

    def strip_copies(l, i, base):
        cols = columns(i, R["wu"].shape[2])
        pairs = (
            (R["slopes"].at[l, :, cols], R["g_hid"].at[:, cols]), (R["actives"].at[l, :, cols], R["active"].at[:, cols]),
            (R["w_down"].at[l, cols], R["wd"].at[cols]), (R["w_up"].at[l, i], R["wu"].at[i]),
        )
        return [pltpu.make_async_copy(src, dst, sem.at[base + 4 * i + n]) for n, (src, dst) in enumerate(pairs)]

    strip_base = {}

    def load_strips(l):
        strip_base[l] = count[0]
        count[0] += 4 * NARROW
        for i in range(NARROW):
            for copy in strip_copies(l, i, strip_base[l]):
                copy.start()

    def strip_waits(l):
        def wait(i):
            for copy in strip_copies(l, i, strip_base[l]):
                copy.wait()

        return wait

    if lq is not None:
        begin("gq", (R["in_gq"], R["gq"]), *[(R["in_part%d" % j], R["part%d" % j]) for j in range(group)])
        begin("qkv", *[
            (R["w_qkv"].at[lq, i], R["wq"].at[i // 2, :, columns(i % 2, 384)]) for i in range(NARROW)
        ])
        begin("x", (R["in_x"], R["x"]))
        begin("g_mid", (R["in_g_mid"], R["total2"]))
    else:
        begin("cotangent", (R["cotangent"], R["low"]))
    if lm is not None:
        load_strips(lm)
        begin("proj", (R["w_proj"].at[lm], R["wp"]))
        begin("att", (R["atts"].at[lm], R["att"]))
        begin("kv", (R["kvs"].at[lm], R["kv"]), (R["peers"].at[lm], R["peer"]), (R["lses"].at[lm], R["lse"]))
    if lq is not None:
        vec = Vectors(R["vec"], lq)

        def put(rows, value):
            if lm is None:
                for i in range(NARROW):
                    R["out"][i, rows, :] = value[:, i * 128 : (i + 1) * 128].astype(BF16)
            else:
                R["grad"][rows, :] = value

        qkv_back_stage(
            vec, R["x"], R["total2"], R["gq"], [R["part%d" % j] for j in range(group)], R["total"],
            R["g_red"], R["low"], R["wq"],
            R["reds"].at[lq, 0], R["low_qkv"].at[lq], R["up_qkv"].at[lq], R["grads_qkv"], put, waits,
        )
    else:
        waits("cotangent")
        R["grad"][...] = R["low"][...].astype(F32)
    if lm is None:
        return
    begin("q", (R["qs"].at[lm], R["gq"]))
    begin("mid", (R["mids"].at[lm], R["x" if lq is not None and R["x"].dtype == F32 else "mid"]))
    mid = R["x" if lq is not None and R["x"].dtype == F32 else "mid"]
    t = {name: R[name].at[lm] for name in TABLES}
    vec = Vectors(R["vec"], lm)
    mlp_back_stage(
        vec, R["grad"], R["active"], R["g_hid"], mid, R["att"], R["low"], R["total"], R["wp"], R["wu"], R["wd"],
        R["reds"].at[lm], {k: (v if k in ("low_down", "up_up") else v[...]) for k, v in t.items() if "qkv" not in k},
        R["grads_mlp"], R["total2"], waits, strip_waits(lm),
    )
    out_mid = pltpu.make_async_copy(R["total2"], R["out_g_mid"], sem.at[count[0]])
    out_mid.start()
    waits("q")
    waits("kv")
    bias = pair_bias(held, R["g"][0])
    kvs = [R["kv"]] + [R["peer"].at[j] for j in range(group - 1)]
    gkvs = [R["part%d" % j] for j in range(group)]
    each(NARROW, lambda i: attend_back_strip(
        held, bias, R["g"][0], i, R["gq"], R["lse"], R["att"], R["low"], kvs, R["gq"], gkvs
    ))
    outs = [(R["gq"], R["out_gq"])] + [(R["part%d" % j], R["out_part%d" % j]) for j in range(group)]
    copies = [pltpu.make_async_copy(src, dst, sem.at[count[0] + 1 + n]) for n, (src, dst) in enumerate(outs)]
    for copy in copies:
        copy.start()
    for copy in copies:
        copy.wait()
    out_mid.wait()


def back_kernel(lq, lm, group, g, outs, tables, carried):
    layers, _, dim, _ = outs["qkv"].shape
    hidden = outs["down"].shape[1]
    tokens = outs["tokens"].shape[0]
    rank = tables[0].shape[1]
    strip = (NARROW, tokens)
    inputs = [("g", g, pl.BlockSpec(memory_space=pltpu.SMEM))]
    near, far = pl.BlockSpec(memory_space=pltpu.VMEM), pl.BlockSpec(memory_space=pltpu.HBM)
    inputs += [(name, table, near) for name, table in zip(TABLES, tables)]
    inputs += [("vec", outs["vec"], near), ("reds", outs["reds"], near)]
    outputs, scratch = [], []

    def vmem(name, shape, kind):
        scratch.append((name, pltpu.VMEM(shape, kind)))

    vmem("gq", strip + (128,), BF16)
    for j in range(group):
        vmem("part%d" % j, strip + (256,), BF16)
    vmem("total", (tokens, dim), F32)
    vmem("total2", (tokens, dim), F32)
    vmem("low", (tokens, dim), BF16)
    if lq is not None:
        g_mid, gq, parts = carried
        x = outs["tokens"] if lq == 0 else outs["saved_x"][lq - 1]
        inputs += [("in_gq", gq, far), ("in_g_mid", g_mid, far), ("in_x", x, far), ("w_qkv", outs["qkv"], far)]
        inputs += [("in_part%d" % j, part, far) for j, part in enumerate(parts)]
        vmem("wq", (NARROW // 2, dim, 768), BF16)
        vmem("g_red", (tokens, rank), BF16)
        vmem("x", (tokens, dim), x.dtype)
        outputs.append(("grads_qkv", (NARROW, rank, 512), BF16, near))
        if lm is None:
            outputs.append(("out", strip + (128,), BF16, near))
    if lm is not None:
        if lq is None:
            inputs.append(("cotangent", outs["cotangent"], far))
        for name in ("active", "slope", "mid", "att", "q", "kv", "peer", "lse"):
            inputs.append((name + "s", outs["saved_" + name], far))
        inputs += [("w_" + name, outs[name], far) for name in ("proj", "up", "down")]
        vmem("wp", (dim, dim), BF16)
        vmem("wu", (NARROW, dim, hidden // NARROW), BF16)
        vmem("wd", (hidden, dim), BF16)
        vmem("grad", (tokens, dim), F32)
        if lq is None or x.dtype != F32:
            vmem("mid", (tokens, dim), F32)
        vmem("att", (tokens, dim), BF16)
        vmem("active", (tokens, hidden), BF16)
        vmem("g_hid", (tokens, hidden), BF16)
        vmem("kv", strip + (256,), BF16)
        vmem("peer", (group - 1,) + strip + (256,), BF16)
        vmem("lse", (NARROW, 8, tokens), F32)
        outputs.append(("grads_mlp", (NARROW, rank, 512 + 2 * hidden // NARROW), BF16, near))
        outputs += [("out_g_mid", (tokens, dim), F32, far), ("out_gq", strip + (128,), BF16, far)]
        outputs += [("out_part%d" % j, strip + (256,), BF16, far) for j in range(group)]
    scratch.append(("sem", pltpu.SemaphoreType.DMA((96,))))
    names = [x[0] for x in inputs] + [x[0] for x in outputs] + [x[0] for x in scratch]
    made = pl.pallas_call(
        functools.partial(back_body, lq, lm, group, tuple(names)),
        out_shape=[shape_of(shape, kind) for _, shape, kind, _ in outputs],
        in_specs=[spec for _, _, spec in inputs],
        out_specs=[spec for _, _, _, spec in outputs],
        scratch_shapes=[shape for _, shape in scratch],
        compiler_params=PARAMS,
        name="back",
    )(*[array for _, array, _ in inputs])
    return dict(zip([x[0] for x in outputs], made))


SITES = {"mlp": (1, 1, 2, 2, 3, 3), "qkv": (0, 0)}


def backward_body(layers, group, n_row, n_col, names, *refs):
    R = dict(zip(names, refs))
    held = positions(group)
    per = BLOCKS // group
    r, c = lax.axis_index("row"), lax.axis_index("col")
    g = lax.rem(c, group)
    seqs = n_col // group
    tokens = per * BLOCK
    bias = pair_bias(held, g)

    def row_peer(s):
        return (lax.rem(r + s, n_row), c)

    def col_peer(d):
        return lax.rem(c + d, n_col)

    peers = [row_peer(s) for s in range(1, n_row)] + [(r, col_peer(d)) for d in range(1, n_col)]
    barrier = pltpu.get_barrier_semaphore()
    for peer in peers:
        pl.semaphore_signal(barrier, inc=1, device_id=peer, device_id_type=MESH)
    pl.semaphore_wait(barrier, len(peers))

    sem, started, count = R["sem"], {}, [0]

    def begin(name, *copies):
        started[name] = []
        for src, dst in copies:
            copy = pltpu.make_async_copy(src, dst, sem.at[count[0]])
            count[0] += 1
            copy.start()
            started[name].append(copy)

    def waits(name):
        for copy in started.pop(name, ()):
            copy.wait()

    def strip_copies(l, i, base):
        cols = columns(i, R["wu"].shape[2])
        pairs = (
            (R["slopes"].at[l, :, cols], R["g_hid"].at[:, cols]), (R["actives"].at[l, :, cols], R["active"].at[:, cols]),
            (R["w_down"].at[l, cols], R["wd"].at[cols]), (R["w_up"].at[l, i], R["wu"].at[i]),
        )
        return [pltpu.make_async_copy(src, dst, sem.at[base + 4 * i + n]) for n, (src, dst) in enumerate(pairs)]

    strip_base = {}

    def load_strips(l):
        strip_base[l] = count[0]
        count[0] += 4 * NARROW
        for i in range(NARROW):
            for copy in strip_copies(l, i, strip_base[l]):
                copy.start()

    def strip_waits(l):
        def wait(i):
            for copy in strip_copies(l, i, strip_base[l]):
                copy.wait()

        return wait

    far = [0]

    def remote(src, dst, n, peer):
        return pltpu.make_async_remote_copy(
            src_ref=src, dst_ref=dst, send_sem=R["out_sem"].at[n], recv_sem=R["in_sem"].at[n],
            device_id=peer, device_id_type=MESH,
        )

    def new_far():
        far[0] += 1
        return far[0] - 1

    def columns_start(n, src):
        to, at = R["columns"].at[n], new_far()
        start = (c // group) * LEN
        places = [pl.ds(pl.multiple_of(start + place_of(group, g, b) * BLOCK, BLOCK), BLOCK) for b in range(per)]
        begin("columns%d" % n, *[(src.at[c, pl.ds(b * BLOCK, BLOCK)], to.at[places[b]]) for b in range(per)])
        for d in range(1, n_col):
            for b in range(per):
                remote(src.at[col_peer(d), pl.ds(b * BLOCK, BLOCK)], to.at[places[b]], at, (r, col_peer(d))).start()
        return at

    def columns_end(n, at):
        waits("columns%d" % n)
        ref = R["columns"].at[n, pl.ds(0, (n_col - 1) * tokens)]
        remote(ref, ref, at, (r, col_peer(1))).wait()

    ends = {}

    def spread(kind, l):
        src, land, at = R["grads_" + kind], R["land_" + kind].at[l], new_far()
        begin("own_%s%d" % (kind, l), (src.at[c], land.at[c]))
        for d in range(1, n_col):
            remote(src.at[col_peer(d)], land.at[c], at, (r, col_peer(d))).start()
        ends["spread", kind, l] = at

    def spread_sent(kind, l):
        if l < layers:
            ref = R["land_" + kind].at[l, pl.ds(0, n_col - 1)]
            remote(ref, ref, ends["spread", kind, l], (r, col_peer(1))).wait_send()

    def add_load(kind, l):
        land = R["land_" + kind].at[l]
        ref = land.at[pl.ds(0, n_col - 1)]
        remote(ref, ref, ends["spread", kind, l], (r, col_peer(1))).wait_recv()
        waits("own_%s%d" % (kind, l))
        begin("stage_" + kind, (land, R["stage_" + kind]))

    def add(kind, l):
        stage, total = R["stage_" + kind], R["sum_" + kind]
        add_sent(kind, l + 1)
        waits("stage_" + kind)
        for q in range(seqs):
            value = sum(stage[q * group + n].astype(F32) for n in range(group))
            total[q] = value.astype(BF16)
        parts, at = R["parts_" + kind], new_far()
        begin("part_%s%d" % (kind, l), (total, parts.at[l, r]))
        for q in range(1, n_row):
            remote(total, parts.at[l, r], at, row_peer(q)).start()
        ends["add", kind, l] = at

    def added(kind, l):
        ref = R["parts_" + kind].at[l, pl.ds(0, n_row - 1)]
        return remote(ref, ref, ends["add", kind, l], row_peer(1))

    def add_sent(kind, l):
        if l < layers:
            waits("part_%s%d" % (kind, l))
            added(kind, l).wait_send()

    def part_copy(l, j, i, at):
        to = c - g + lax.rem(g - j + group, group)
        strip = pl.ds(i, 1)
        return remote(R["part%d" % j].at[strip], R["in_part"].at[l, j - 1, strip], at[j] + i, (r, to))

    def back_strip(l, i, at):
        kvs = [R["kv"]] + [R["peer"].at[j] for j in range(group - 1)]
        gkvs = [R["part%d" % j] for j in range(group)]
        attend_back_strip(held, bias, g, i, R["gq"], R["lse"], R["att"], R["low"], kvs, R["gq"], gkvs)
        for j in range(1, group):
            part_copy(l, j, i, at).start()

    def load_qkv(l):
        begin("qkv", *[
            (R["w_qkv"].at[l, i], R["wq"].at[i // 2, :, columns(i % 2, 384)]) for i in range(NARROW)
        ])

    def load_mlp(l):
        load_strips(l)
        begin("proj", (R["w_proj"].at[l], R["wp"]))

    def load_attention(l):
        begin("mid", (R["mids"].at[l], R["mid"]))
        begin("att", (R["atts"].at[l], R["att"]))
        begin("q", (R["qs"].at[l], R["gq"]))
        begin("kv", (R["kvs"].at[l], R["kv"]), (R["peers"].at[l], R["peer"]), (R["lses"].at[l], R["lse"]))

    last = layers - 1
    begin("cotangent", (R["cotangent"], R["low"]))
    begin("tables", *[(R["in_" + name], R[name]) for name in TABLES + ("vec", "reds")])
    load_mlp(last)
    load_attention(last)
    load_qkv(last)
    at_result = columns_start(0, R["result"])
    at_ids = new_far()
    begin("ids", (R["ids"], R["all_ids"].at[r]))
    for q in range(1, n_row):
        remote(R["ids"], R["all_ids"].at[r], at_ids, row_peer(q)).start()
    waits("cotangent")

    def widen(rows):
        R["grad"][rows, :] = R["low"][rows, :].astype(F32)

    by_rows(tokens, widen)
    waits("tables")
    for l in reversed(range(layers)):
        t = {name: R[name].at[l] for name in TABLES if "qkv" not in name}
        vec = Vectors(R["vec"], l)
        spread_sent("mlp", l + 1)
        mlp_back_stage(
            vec, R["grad"], R["active"], R["g_hid"], R["mid"], R["att"], R["low"], R["total"], R["wp"], R["wu"],
            R["wd"], R["reds"].at[l], {k: (v if k in ("low_down", "up_up") else v[...]) for k, v in t.items()},
            R["grads_mlp"], R["total2"], waits, strip_waits(l),
        )
        spread("mlp", l)
        if l > 0:
            load_mlp(l - 1)
        begin("x", (R["tokens"] if l == 0 else R["xs"].at[l - 1], R["x0"] if l == 0 else R["mid"]))
        waits("q")
        waits("kv")
        at = [far[0] + j * NARROW for j in range(group)]
        far[0] += group * NARROW
        half = NARROW // 2
        if l < last:
            add_load("qkv", l + 1)
        each(half, lambda i: back_strip(l, i, at))
        add_load("mlp", l)
        if l < last:
            add("qkv", l + 1)
        add("mlp", l)
        each(half, lambda i: back_strip(l, half + i, at))
        for i in range(NARROW):
            for j in range(1, group):
                part_copy(l, j, i, at).wait_recv()
            begin(("part", i), *[(R["in_part"].at[l, j, i], R["peer"].at[j, i]) for j in range(group - 1)])
        parts = [R["part0"]] + [R["peer"].at[j] for j in range(group - 1)]
        spread_sent("qkv", l + 1)

        def put(rows, value):
            if l > 0:
                R["grad"][rows, :] = value
            else:
                for i in range(NARROW):
                    R["part0"][i, rows, :128] = value[:, i * 128 : (i + 1) * 128].astype(BF16)

        qkv_back_stage(
            vec, R["x0"] if l == 0 else R["mid"], R["total2"], R["gq"], parts, R["total"], R["g_red"], R["low"],
            R["wq"], R["reds"].at[l, 0], R["low_qkv"].at[l], R["up_qkv"].at[l], R["grads_qkv"], put, waits,
        )
        spread("qkv", l)
        for i in range(NARROW):
            for j in range(1, group):
                part_copy(l, j, i, at).wait_send()
        if l > 0:
            load_qkv(l - 1)
            load_attention(l - 1)
    at_grad = columns_start(1, R["part0"].at[:, :, pl.ds(0, 128)])
    add_load("qkv", 0)
    add("qkv", 0)
    columns_end(0, at_result)
    columns_end(1, at_grad)
    waits("ids")
    rest = R["all_ids"].at[pl.ds(0, n_row - 1)]
    remote(rest, rest, at_ids, row_peer(1)).wait()
    for kind in ("mlp", "qkv"):
        spread_sent(kind, 0)
        add_sent(kind, 0)
        for l in range(layers):
            added(kind, l).wait_recv()


def backward(n_row, n_col, group, outs, tables, ids):
    layers, _, dim, _ = outs["qkv"].shape
    hidden = outs["down"].shape[1]
    mine = outs["tokens"].shape[0]
    rank = tables[0].shape[1]
    seqs = n_col // group
    strip = (NARROW, mine)
    near, far = pl.BlockSpec(memory_space=pltpu.VMEM), pl.BlockSpec(memory_space=pltpu.HBM)
    small = list(zip(TABLES, tables)) + [("vec", outs["vec"]), ("reds", outs["reds"])]
    inputs = [("in_" + name, table, far) for name, table in small] + [("ids", ids, far)]
    for name in ("active", "slope", "mid", "att", "q", "kv", "peer", "lse", "x"):
        inputs.append((name + "s", outs["saved_" + name], far))
    inputs += [("w_" + name, outs[name], far) for name in KINDS]
    inputs += [(name, outs[name], far) for name in ("tokens", "cotangent", "result")]
    sizes = {"mlp": 512 + 2 * hidden // NARROW, "qkv": 512}
    outputs = [
        ("columns", (2, n_col * mine, 128), BF16, far),
        ("all_ids", (n_row,) + ids.shape, F32, far),
        ("in_part", (layers, group - 1) + strip + (256,), BF16, far),
    ]
    scratch = [
        ("gq", strip + (128,), BF16), ("kv", strip + (256,), BF16), ("peer", (group - 1,) + strip + (256,), BF16),
        ("lse", (NARROW, 8, mine), F32), ("total", (mine, dim), F32), ("total2", (mine, dim), F32),
        ("grad", (mine, dim), F32), ("mid", (mine, dim), F32), ("low", (mine, dim), BF16), ("att", (mine, dim), BF16),
        ("x0", (mine, dim), BF16), ("active", (mine, hidden), BF16), ("g_hid", (mine, hidden), BF16),
        ("g_red", (mine, rank), BF16), ("wq", (NARROW // 2, dim, 768), BF16), ("wp", (dim, dim), BF16),
        ("wu", (NARROW, dim, hidden // NARROW), BF16), ("wd", (hidden, dim), BF16),
    ]
    scratch += [("part%d" % j, strip + (256,), BF16) for j in range(group)]
    scratch += [(name, table.shape, table.dtype) for name, table in small]
    for kind, size in sizes.items():
        outputs.append(("land_" + kind, (layers, n_col, rank, size), BF16, far))
        outputs.append(("parts_" + kind, (layers, n_row, seqs, rank, size), BF16, far))
        scratch.append(("grads_" + kind, (NARROW, rank, size), BF16))
        scratch.append(("stage_" + kind, (n_col, rank, size), BF16))
        scratch.append(("sum_" + kind, (seqs, rank, size), BF16))
    scratch = [(name, pltpu.VMEM(shape, kind)) for name, shape, kind in scratch]
    scratch += [
        ("sem", pltpu.SemaphoreType.DMA((72 * layers + 16,))),
        ("out_sem", pltpu.SemaphoreType.DMA(((4 + group * NARROW) * layers + 4,))),
        ("in_sem", pltpu.SemaphoreType.DMA(((4 + group * NARROW) * layers + 4,))),
    ]
    names = [x[0] for x in inputs] + [x[0] for x in outputs] + [x[0] for x in scratch]
    made = pl.pallas_call(
        functools.partial(backward_body, layers, group, n_row, n_col, tuple(names)),
        out_shape=[shape_of(shape, kind) for _, shape, kind, _ in outputs],
        in_specs=[spec for _, _, spec in inputs],
        out_specs=[spec for _, _, _, spec in outputs],
        scratch_shapes=[shape for _, shape in scratch],
        compiler_params=pltpu.CompilerParams(
            collective_id=1, has_side_effects=True, vmem_limit_bytes=62 * 2**20
        ),
        name="backward",
    )(*[array for _, array, _ in inputs])
    return dict(zip([x[0] for x in outputs], made))


def place_body(layers, names, *refs):
    R = dict(zip(names, refs))
    sem, ends = R["sem"], []

    def copy(src, dst, n):
        made = pltpu.make_async_copy(src, dst, sem.at[n])
        made.start()
        return made

    loads = [copy(R["columns"].at[n], R["low"].at[n], n) for n in range(2)]
    ins = {kind: copy(R["parts_" + kind], R["in_" + kind], 2 + n) for n, kind in enumerate(SITES)}
    for n in range(2):
        loads[n].wait()
        R["wide"][n] = R["low"][n].astype(F32)
        ends.append(copy(R["wide"].at[n], R["column_out%d" % n], 4 + n))
    rows, adapters, rank = R["ids"].shape[0], R["keep0"].shape[1], R["keep0"].shape[2]
    sequences = R["in_qkv"].shape[1]
    shape = (adapters * rank, sequences * rank)
    down, across = [lax.broadcasted_iota(jnp.int32, shape, axis) for axis in (0, 1)]
    weights = {}
    for site in range(4):
        chosen = jnp.zeros((1, shape[1]), F32)
        for q in range(sequences):
            value = R["ids"][q // (sequences // rows), q % (sequences // rows), site]
            chosen = jnp.where(across[:1] // rank == q, value, chosen)
        same = (chosen == (down // rank).astype(F32)) & (down % rank == across % rank)
        weights[site] = jnp.where(same, 1.0, 0.0).astype(BF16)
    number = 0
    for kind in ("qkv", "mlp"):
        ins[kind].wait()
        stage = R["in_" + kind]
        sequences, rank = stage.shape[1:3]
        at = 0
        for site, size in zip(SITES[kind], R["sizes"][kind]):
            out, keep = R["out%d" % number], R["keep%d" % number]
            for l in range(layers):
                part = stage[l, :, :, at : at + size]
                made = dot(weights[site], part.reshape(sequences * rank, size)).reshape(-1, rank, size)
                if number == 1:
                    for n in range(3):
                        keep[l, :, n] = made[:, :, n * 128 : (n + 1) * 128]
                else:
                    keep[l] = made
            ends.append(copy(keep, out, 6 + number))
            at += size
            number += 1
    for end in ends:
        end.wait()


def place(made, sizes, adapters):
    layers, rank = made["parts_qkv"].shape[0], made["parts_qkv"].shape[-2]
    hbm = pl.BlockSpec(memory_space=pltpu.HBM)
    columns = made["columns"]
    parts = {kind: made["parts_" + kind].reshape(layers, -1, rank, sum(sizes[kind])) for kind in SITES}
    widths = [size for kind in ("qkv", "mlp") for size in sizes[kind]]
    inputs = [("ids", made["all_ids"], pl.BlockSpec(memory_space=pltpu.SMEM)), ("columns", columns, hbm)]
    inputs += [("parts_" + kind, parts[kind], hbm) for kind in SITES]
    outputs = [("column_out%d" % n, columns.shape[1:], F32) for n in range(2)]
    shapes = [(layers, adapters, rank, size) for size in widths]
    shapes[1] = (layers, adapters, 3, rank, 128)
    outputs += [("out%d" % n, shape, F32) for n, shape in enumerate(shapes)]
    scratch = [("low", pltpu.VMEM(columns.shape, BF16)), ("wide", pltpu.VMEM(columns.shape, F32))]
    scratch += [("in_" + kind, pltpu.VMEM(parts[kind].shape, BF16)) for kind in SITES]
    scratch += [("keep%d" % n, pltpu.VMEM(shape, F32)) for n, shape in enumerate(shapes)]
    scratch.append(("sem", pltpu.SemaphoreType.DMA((6 + len(widths),))))
    names = [x[0] for x in inputs] + [x[0] for x in outputs] + [x[0] for x in scratch]

    def body(*refs):
        place_body(layers, names + ["sizes"], *refs, sizes)

    return pl.pallas_call(
        body,
        out_shape=[shape_of(shape, kind) for _, shape, kind in outputs],
        in_specs=[spec for _, _, spec in inputs],
        out_specs=[hbm] * len(outputs),
        scratch_shapes=[shape for _, shape in scratch],
        compiler_params=PARAMS,
        name="place",
    )(*[array for _, array, _ in inputs])


def to_rows_body(held, x, out):
    n = 0
    for s in range(x.shape[0] // (len(held) * len(held[0]))):
        for g in range(len(held)):
            for place in held[g]:
                start = (s * BLOCKS + place) * BLOCK
                out[start : start + BLOCK, :] = x[n].astype(F32)
                n += 1


def to_rows(held, x):
    blocks, _, width = x.shape
    return pl.pallas_call(
        functools.partial(to_rows_body, held),
        out_shape=shape_of((blocks * BLOCK, width), F32),
        compiler_params=PARAMS,
        name="to_rows",
    )(x)


def pick_body(width, units, ids, *refs):
    tables, raise_qkv, vectors, every = refs[:7], refs[7], refs[8:16], refs[16]
    qkv_b, up_b, proj_b, down_b, gain1, shift1, gain2, shift2 = vectors
    outs, raise_out, vector, ids_rows = refs[17:24], refs[24], refs[25], refs[26]
    for ref, out in zip(tables, outs):
        out[...] = ref[...]
    layers = raise_qkv.shape[0]
    vector[...] = jnp.zeros_like(vector)
    for l in range(layers):
        for n in range(3):
            row = raise_qkv[l, n]
            for i in range(NARROW):
                raise_out[l, i, :, n * 128 : (n + 1) * 128] = row[:, i * 128 : (i + 1) * 128]
            vector[4 * l : 4 * l + 1, n * width : (n + 1) * width] = qkv_b[n, l : l + 1, :].astype(F32)
        vector[4 * l + 1 : 4 * l + 2, :units] = up_b[l : l + 1, :].astype(F32)
        for n, ref in enumerate((proj_b, down_b, gain1, shift1, gain2, shift2)):
            row, lane = 4 * l + 2 + n // 4, n % 4 * width
            vector[row : row + 1, lane : lane + width] = ref[l : l + 1, :].astype(F32)
    ids_rows[...] = jnp.zeros_like(ids_rows)
    ids_rows[: every.shape[0], : every.shape[1]] = every[...].astype(F32)


def pick(group, adapter_ids, tables, raise_qkv, vectors):
    layers, _, _, rank, dim = raise_qkv.shape
    width, units = vectors[2].shape[1], vectors[1].shape[1]

    def chosen(site, shape):
        rest = (0,) * (len(shape) - 2)
        return pl.BlockSpec(
            (shape[0], None) + shape[2:], lambda i, ids: (0, ids[lax.axis_index("col") // group, site]) + rest
        )

    def whole(shape):
        return pl.BlockSpec(shape, lambda i, ids: (0,) * len(shape))

    shapes = [(table.shape[:1] + table.shape[2:], BF16) for _, table in tables]
    shapes += [((layers, NARROW, rank, 384), BF16), ((4 * layers, 512), F32), ((8, 128), F32)]
    return pl.pallas_call(
        functools.partial(pick_body, width, units),
        grid_spec=pltpu.PrefetchScalarGridSpec(
            num_scalar_prefetch=1,
            grid=(1,),
            in_specs=[chosen(site, table.shape) for site, table in tables]
            + [chosen(0, raise_qkv.shape)]
            + [whole(x.shape) for x in vectors]
            + [whole(adapter_ids.shape)],
            out_specs=[whole(shape) for shape, _ in shapes],
        ),
        out_shape=[shape_of(shape, kind) for shape, kind in shapes],
        compiler_params=PARAMS,
        name="pick",
    )(adapter_ids, *[table for _, table in tables], raise_qkv, *vectors, adapter_ids)


def shards(mesh_shape, *args):
    (
        tokens, cotangent, adapter_ids, qkv_weight, qkv_bias, proj_weight, proj_bias,
        up_weight, up_bias, down_weight, down_bias, first_gain, first_shift, second_gain,
        second_shift, qkv_lower, qkv_raise, proj_lower, proj_raise, up_lower, up_raise,
        down_lower, down_raise,
    ) = args
    n_row, n_col = mesh_shape
    layers, adapters, dim, rank = qkv_lower.shape
    rows, width = tokens.shape
    units = up_weight.shape[2]
    seqs = rows // LEN
    group = n_col // seqs
    held = positions(group)
    per = BLOCKS // group
    mine = per * BLOCK
    merge = 128 // width
    c = lax.axis_index("col")
    g = lax.rem(c, group)
    def turned(table):
        return jnp.swapaxes(table, 2, 3)

    *picked, vector, ids_rows = pick(
        group, adapter_ids,
        [
            (0, turned(qkv_lower)), (1, turned(proj_lower)), (1, proj_raise), (2, turned(up_lower)), (2, up_raise),
            (3, turned(down_lower)), (3, down_raise),
        ],
        qkv_raise.transpose(0, 1, 3, 2, 4),
        (qkv_bias.transpose(1, 0, 2), up_bias, proj_bias, down_bias, first_gain, first_shift, second_gain, second_shift),
    )
    tables = [picked[0], picked[7]] + list(picked[1:7])
    fused = FUSED and width == 128
    if width == 128:
        qkv_shard = qkv_weight.transpose(0, 2, 1, 3)
    else:
        qkv_shard = qkv_weight.reshape(layers, -1, 3 * width)
    outs = gather_inputs(
        n_row, n_col, group, qkv_shard, proj_weight, up_weight,
        down_weight, tokens, cotangent, vector, tables if fused else None
    )
    g_one = g.reshape(1)

    def peer_values(x, step):
        pairs = [(q, q - q % group + (q + step) % group) for q in range(n_col)]
        return lax.ppermute(x, "col", pairs)

    def to_columns(x):
        if merge > 1:
            x = x.reshape(NARROW, mine, merge, width).transpose(0, 2, 1, 3).reshape(n_col, mine, width)
        x = lax.all_to_all(x, "col", split_axis=0, concat_axis=0, tiled=True)
        return to_rows(held, x.reshape(n_col * per, BLOCK, width))

    if not fused:
        x = outs["tokens"].astype(F32)
        kept = {name: [] for name in SAVED + ("reds",)}
        for l in range(layers):
            q, kv, red = qkv_kernel(l, x, outs["vec"], outs["qkv"], tables[0], tables[1])
            kvs = [kv] + [peer_values(kv, s) for s in range(1, group)]
            att, lse = attend_kernel(group, g_one, q, kvs)
            mid, x, active, slope, reds = mlp_kernel(
                l, l == layers - 1, x, att, outs["vec"], outs["proj"], outs["up"], outs["down"], tables[2:]
            )
            reds = jnp.concatenate([red[None], reds])
            peer = jnp.stack(kvs[1:]) if group > 1 else kv[None][:0]
            for name, value in zip(SAVED + ("reds",), (q, kv, peer, att, lse, mid, active, slope, x, reds)):
                kept[name].append(value)
        for name in SAVED:
            outs["saved_" + name] = jnp.stack(kept[name][: layers - 1] if name == "x" else kept[name])
        outs["reds"] = jnp.stack(kept["reds"])
        outs["result"] = x
    if fused:
        made = backward(n_row, n_col, group, outs, tables, ids_rows)
        sizes = {"qkv": (128, 384), "mlp": (128, 128, 128, units, units, 128)}
        sums = place(made, sizes, adapters)
        final = list(sums[:2])
        for number, p in enumerate(sums[2:]):
            if number == 1:
                p = p.transpose(0, 1, 3, 2, 4)
            elif number % 2 == 0:
                p = p.transpose(0, 1, 3, 2)
            final.append(p)
        return tuple(final)

    result = to_columns(outs["result"])

    onehot = (adapter_ids.T[:, :, None] == jnp.arange(adapters)[None, None, :]).astype(BF16)

    def all_rows(x):
        pairs = [[(q, (q + s) % n_row) for q in range(n_row)] for s in range(1, n_row)]
        return [x] + [lax.ppermute(x, "row", pair) for pair in pairs]

    onehots = jnp.concatenate(all_rows(onehot), axis=1)

    def collect(parts, named):
        if merge > 1:
            pieces, at = [], 0
            for _, size in named:
                piece = parts[:, :, at : at + size]
                at += size
                if size == 384:
                    piece = piece.reshape(NARROW, rank, 3, merge, width).transpose(0, 3, 1, 2, 4)
                else:
                    piece = piece.reshape(NARROW, rank, merge, size // merge).transpose(0, 2, 1, 3)
                pieces.append(piece.reshape(n_col, rank, size // merge))
            parts = jnp.concatenate(pieces, axis=2)
        parts = lax.all_to_all(parts, "col", split_axis=0, concat_axis=0, tiled=True)
        parts = parts.reshape((seqs, group) + parts.shape[1:]).astype(F32).sum(axis=1).astype(BF16)
        parts = jnp.concatenate(all_rows(parts), axis=0)
        sums, at = [], 0
        for site, size in named:
            piece = parts[:, :, at : at + size // merge]
            at += size // merge
            sums.append(jnp.einsum("sa,srn->arn", onehots[site], piece, preferred_element_type=F32))
        return sums

    wide = outs["down"].shape[1] // NARROW
    grads, carried = [None] * layers, None
    for l in reversed(range(layers + 1)):
        lq, lm = (l if l < layers else None), (l - 1 if l > 0 else None)
        made = back_kernel(lq, lm, group, g_one, outs, tables, carried)
        if lm is not None:
            grads[lm] = collect(made["grads_mlp"], [(1, 128), (1, 128), (2, 128), (2, wide), (3, wide), (3, 128)])
            parts = [made["out_part%d" % s] for s in range(group)]
            parts = [parts[0]] + [peer_values(parts[s], group - s) for s in range(1, group)]
            carried = (made["out_g_mid"], made["out_gq"], parts)
        if lq is not None:
            grads[lq] = collect(made["grads_qkv"], [(0, 128), (0, 384)]) + grads[lq]
    grad = made["out"]
    input_grad = to_columns(grad)

    final = []
    for number in range(8):
        p = jnp.stack([grads[l][number] for l in range(layers)])
        if number == 1:
            p = p.reshape(layers, adapters, rank, 3, width)
        elif number % 2 == 0:
            p = p.transpose(0, 1, 3, 2)
        final.append(p)
    return (result, input_grad) + tuple(final)


def solution(mesh):
    mesh_shape = (mesh.shape["row"], mesh.shape["col"])
    return jax.shard_map(
        functools.partial(shards, mesh_shape),
        mesh=mesh,
        in_specs=(
            P("row", "col"), P("row", "col"), P("row", None),
            P(None, "row", None, "col"), P(None, None, "col"),
            P(None, "col", "row"), P(None, "col"),
            P(None, "row", "col"), P(None, "col"),
            P(None, "col", "row"), P(None, "col"),
            P(None, "col"), P(None, "col"), P(None, "col"), P(None, "col"),
            P(), P(), P(), P(), P(), P(), P(), P(),
        ),
        out_specs=(
            P("row", "col"), P("row", "col"),
            P(None, None, "col", None), P(None, None, None, None, "col"),
            P(None, None, "col", None), P(None, None, None, "col"),
            P(None, None, "col", None), P(None, None, None, "col"),
            P(None, None, "col", None), P(None, None, None, "col"),
        ),
        check_vma=False,
    )
```

```python
import functools
import math

import jax
import jax.numpy as jnp
from jax import lax
from jax.experimental import pallas as pl
from jax.experimental.pallas import tpu as pltpu
from jax.sharding import PartitionSpec as P

HD = 64
LEN = 1024
BLOCK = 256
BLOCKS = LEN // BLOCK
EPSILON = 1e-05
SCALE = HD**-0.5
ROOT = (2.0 / 3.141592653589793) ** 0.5
MESH = pl.DeviceIdType.MESH
F32 = jnp.float32
BF16 = jnp.bfloat16


ROW_FIRST = (("z", 0, 1), ("z", 1, 0))
ROW_SECOND = ((0, "z", 1), (1, "z", 0))
ORDERS = (
    {"qkv": (ROW_FIRST,), "proj": (ROW_SECOND,), "up": (ROW_FIRST,) * 2, "down": (ROW_SECOND, ROW_FIRST)},
    {"qkv": (ROW_SECOND,), "proj": (ROW_FIRST,), "up": (ROW_SECOND,) * 2, "down": (ROW_SECOND,) * 2},
)
CUTS = {kind: 2 * len(pairs) for kind, pairs in ORDERS[0].items()}
KINDS = ("qkv", "proj", "up", "down")
DEPTH = 4
FUSED = True
LINK = 90e3
DELAY, ROW_DELAY = 2.0, 4.0
FIRST = 12.0


def transfer_plan(order, n_row):
    masks, rows, steps = [0], False, []
    for d in order:
        if d == "z":
            steps += [(("z", hop), tuple(masks), rows) for hop in range(1, n_row)]
            rows = True
        else:
            steps.append((d, tuple(masks), rows))
            masks = masks + [m ^ d for m in masks]
    steps.append((None, tuple(masks), rows))
    return steps


def transfer_schedule(pieces, n_row, tasks):
    cost, parts = {}, {}
    for k, (name, order, size) in enumerate(pieces):
        parts.setdefault(name, set()).add(k)
        for p, (d, masks, rows) in enumerate(transfer_plan(order, n_row)[:-1]):
            axis = "z" if isinstance(d, tuple) else d
            cost[k, p] = (axis, 2 * len(masks) * (n_row if rows else 1) * size / LINK)
    ready = {d: [] for d, _ in cost.values()}
    free = {d: 0.0 if d == "z" else FIRST for d in ready}
    flight = {d: [] for d in ready}
    for k in range(len(pieces)):
        ready[cost[k, 0][0]].append((k, 0))
    tasks, left = list(tasks), {}
    for task in tasks:
        left[task[4]] = left.get(task[4], 0) + 1
    landed, staged, now, ops = {}, {}, 0.0, []

    def stage(name):
        kind, l = name
        if name in landed and name not in staged and landed[name] <= now and not left.get((kind, l - 1)):
            staged[name] = now + 3.0
            ops.append(("stage", kind, l))

    while tasks or any(ready.values()) or any(flight.values()):
        for d in ready:
            while ready[d] and len(flight[d]) < DEPTH:
                k, p = ready[d].pop(0)
                free[d] = max(now, free[d]) + cost[k, p][1]
                flight[d].append((free[d] + (ROW_DELAY if d == "z" else DELAY), k, p))
                ops.append(("start", k, p))
        if tasks:
            for name in list(landed):
                stage(name)
        events = [f for line in flight.values() for f in line]
        event = min(events) if events else None
        due = None
        if tasks:
            need = tasks[0][4]
            due = now if need is None else staged.get(need)
            if due is None and need in landed and not left.get((need[0], need[1] - 1)):
                due = landed[need]
        if due is not None and (event is None or max(due, now) < event[0]):
            now = max(due, now)
            need = tasks[0][4]
            if need is not None and need not in staged:
                continue
            name, l, part, micros, _ = tasks.pop(0)
            left[need] -= 1
            now += micros
            ops.append(("task", name, (l, part)))
            continue
        now, k, p = max(now, event[0]), event[1], event[2]
        d = cost[k, p][0]
        flight[d].remove(event)
        ops.append(("wait", k, p))
        if (k, p + 1) in cost:
            later = ready[cost[k, p + 1][0]]
            later.append((k, p + 1))
            later.sort()
        else:
            name = pieces[k][0]
            parts[name].discard(k)
            if not parts[name]:
                landed[name] = now + 4.0
    return ops


def place_of(group, g, b):
    if group == 2:
        return g + b * (BLOCKS - 1 - 2 * g)
    return g * (BLOCKS // group) + b


def positions(group):
    per = BLOCKS // group
    return tuple(tuple(place_of(group, g, b) for b in range(per)) for g in range(group))


NARROW = 8
CROSS = ((0,), (0,))
TURNED = ((1,), (1,))


def dot(a, b, dims=((1,), (0,))):
    return lax.dot_general(a, b, (dims, ((), ())), preferred_element_type=F32)


def columns(i, size=128):
    if isinstance(i, int):
        return pl.ds(i * size, size)
    return pl.ds(pl.multiple_of(i * size, size), size)


def norm_parts(x):
    center = x - jnp.mean(x, axis=1, keepdims=True)
    inverse = lax.rsqrt(jnp.mean(center * center, axis=1, keepdims=True) + EPSILON)
    return center * inverse, inverse


def norm_grad(grad, scaled, inverse, gain):
    w = grad * gain
    first = jnp.mean(w, axis=1, keepdims=True)
    second = jnp.mean(w * scaled, axis=1, keepdims=True)
    return inverse * (w - first - scaled * second)


def norm_low(x, gain, shift):
    return (norm_parts(x)[0] * gain + shift).astype(BF16)


def pair_state(held):
    group, per = len(held), len(held[0])
    state = {}
    for s in range(per):
        for j in range(group):
            for b in range(per):
                seen = {held[(g - j) % group][b] <= held[g][s] for g in range(group)}
                state[s, j, b] = 0 if len(seen) == 2 else (1 if True in seen else -1)
    return state


def pair_bias(held, g):
    group = len(held)
    bias = {}
    for (s, j, b), state in pair_state(held).items():
        if state == 0:
            keys = place_of(group, lax.rem(g - j + group, group), b)
            bias[s, j, b] = jnp.where(keys <= place_of(group, g, s), 0.0, -1e9).astype(F32)
    return bias


def head_mask(h):
    lane = lax.broadcasted_iota(jnp.int32, (1, 128), 1)
    return (lane // HD) == h


def turning_pair(held, g):
    if len(held) != 2:
        return None, [0.0] * len(held[0])
    at = 1 - g
    return at, [jnp.where(at == n, 1.0, 0.0).astype(F32) for n in range(len(held[0]))]


def both_heads(x):
    return jnp.concatenate([jnp.where(head_mask(h), x, 0).astype(BF16) for h in range(2)], axis=0)


def slots_of(held, j, b, fixed):
    state = pair_state(held)
    return [s for s in range(len(held[0])) if state[s, j, b] > 0 or (state[s, j, b] == 0 and not fixed)]


def attend_strip(held, bias, g, i, q, kvs, out, lse):
    group, per = len(held), len(held[0])
    at, here = turning_pair(held, g)
    wide = 2 * BLOCK
    blocks = [(j, b, slots_of(held, j, b, at is not None)) for j in range(group) for b in range(per)]
    queries = [both_heads(q[i, s * BLOCK : (s + 1) * BLOCK, :] * SCALE) for s in range(per)]
    scores = {s: [] for s in range(per)}
    for j, b, slots in blocks:
        if slots:
            keys = kvs[j][i, b * BLOCK : (b + 1) * BLOCK, :128]
            score = dot(keys, jnp.concatenate([queries[s] for s in slots], axis=0), TURNED)
            for n, s in enumerate(slots):
                part = score[:, n * wide : (n + 1) * wide]
                scores[s].append(((j, b), part + bias[s, j, b] if (s, j, b) in bias and at is None else part))
    turned = {(j, b): kvs[j][i, b * BLOCK : (b + 1) * BLOCK, 128:].T for j, b, slots in blocks if slots}

    def weigh(e, values):
        e = e.astype(BF16)
        return jnp.concatenate(
            [dot(values[h * HD : (h + 1) * HD], e[:, h * BLOCK : (h + 1) * BLOCK]) for h in range(2)], axis=1
        )

    extra = None
    if at is not None:
        moving = pl.ds(pl.multiple_of(at * BLOCK, BLOCK), BLOCK)
        score = dot(kvs[1][i, moving, :128], both_heads(q[i, moving, :] * SCALE), TURNED)
        top = jnp.max(score, axis=0, keepdims=True)
        e = jnp.exp(score - top)
        extra = (top, jnp.sum(e, axis=0, keepdims=True), weigh(e, kvs[1][i, moving, 128:].T))
    for s in range(per):
        tops = [jnp.max(x, axis=0, keepdims=True) for _, x in scores[s]]
        if extra:
            tops.append(extra[0] + (here[s] - 1.0) * 1e9)
        top = functools.reduce(jnp.maximum, tops)
        total, made = 0.0, 0.0
        for place, score in scores[s]:
            e = jnp.exp(score - top)
            total = total + jnp.sum(e, axis=0, keepdims=True)
            made = made + weigh(e, turned[place])
        if extra:
            weight = jnp.exp(tops[-1] - top) * here[s]
            total = total + weight * extra[1]
            made = made + weight * extra[2]
        made = made / total
        level = top + jnp.log(total)
        rows = pl.ds(s * BLOCK, BLOCK)
        for h in range(2):
            lse[i, h : h + 1, rows] = level[:, h * BLOCK : (h + 1) * BLOCK]
        both = jnp.concatenate([made[:, :BLOCK], made[:, BLOCK:]], axis=0)
        out[rows, columns(i)] = both.T.astype(BF16)


def attend_back_strip(held, bias, g, i, q, lse, out, grad, kvs, gq, gkvs):
    group, per = len(held), len(held[0])
    at, here = turning_pair(held, g)

    def slot(rows):
        up = grad[rows, columns(i)]
        product = (up.astype(F32) * out[rows, columns(i)].astype(F32)).T
        inner = [jnp.sum(product[h * HD : (h + 1) * HD], axis=0, keepdims=True) for h in range(2)]
        level = [lse[i, h : h + 1, rows] for h in range(2)]
        return [
            both_heads(q[i, rows, :] * SCALE), both_heads(up),
            jnp.concatenate(inner, axis=1), jnp.concatenate(level, axis=1),
        ]

    def block(parts, keys, values):
        query, given = [jnp.concatenate([part[n] for part in parts], axis=0) for n in (0, 1)]
        inner, level = [jnp.concatenate([part[n] for part in parts], axis=1) for n in (2, 3)]
        probs = jnp.exp(dot(keys, query, TURNED) - level)
        g_scores = (probs * (dot(values, given, TURNED) - inner)).astype(BF16)
        turned = keys.T
        made = []
        for n in range(len(parts)):
            pieces = []
            for h in range(2):
                first = (2 * n + h) * BLOCK
                pieces.append(dot(turned[h * HD : (h + 1) * HD], g_scores[:, first : first + BLOCK]))
            made.append(jnp.concatenate(pieces, axis=0))
        return made, dot(g_scores, query), dot(probs.astype(BF16), given)

    slots = [slot(pl.ds(s * BLOCK, BLOCK)) for s in range(per)]
    total = [0.0] * per
    moved = None
    if at is not None:
        moving = pl.ds(pl.multiple_of(at * BLOCK, BLOCK), BLOCK)
        moved = block([slot(moving)], kvs[1][i, moving, :128], kvs[1][i, moving, 128:])
        total = [here[s] * moved[0][0] for s in range(per)]
    for j in range(group):
        for b in range(per):
            rows = pl.ds(b * BLOCK, BLOCK)
            k, v = 0.0, 0.0
            wanted = slots_of(held, j, b, at is not None)
            if wanted:
                parts = []
                for s in wanted:
                    part = list(slots[s])
                    if at is None and (s, j, b) in bias:
                        part[3] = part[3] - bias[s, j, b]
                    parts.append(part)
                made, k, v = block(parts, kvs[j][i, rows, :128], kvs[j][i, rows, 128:])
                for n, s in enumerate(wanted):
                    total[s] = total[s] + made[n]
            if at is not None and j == 1:
                k, v = k + here[b] * moved[1], v + here[b] * moved[2]
            gkvs[j][i, rows, :128] = k.astype(BF16)
            gkvs[j][i, rows, 128:] = v.astype(BF16)
    for s in range(per):
        gq[i, pl.ds(s * BLOCK, BLOCK), :] = (total[s] * SCALE).T.astype(BF16)


def by_rows(count, body, size=128):
    each(count // size, lambda n: body(pl.ds(pl.multiple_of(n * size, size), size)))


def keep(value, red, red_out):
    red[...] = value.astype(BF16)
    red_out[...] = value.T.astype(BF16)


def each(count, body):
    def step(i, carry):
        body(i)
        return carry

    lax.fori_loop(0, count, step, 0)


def qkv_stage(x, gain, shift, w, bias, low, up, q, kv, red, red_out, normed):
    def norm(rows):
        normed[rows, :] = norm_low(x[rows, :], gain, shift)

    by_rows(x.shape[0], norm)
    keep(dot(normed[...], low[...], TURNED), red, red_out)

    def pair(j):
        made = dot(normed[...], w[j])
        for n in range(2):
            i = 2 * j + n
            mixed = made[:, n * 384 : (n + 1) * 384] + (bias[i] + dot(red[...], up[i]))
            q[i] = mixed[:, :128].astype(BF16)
            kv[i] = mixed[:, 128:].astype(BF16)

    each(NARROW // 2, pair)


def proj_stage(x, att, w, bias, low, up, gain, shift, low_up, mid, normed, red, red_out, red_up, red_up_out):
    keep(dot(att[...], low[...], TURNED), red, red_out)

    def part(rows):
        value = x[rows, :] + (dot(att[rows, :], w[...]) + bias + dot(red[rows, :], up[...]))
        mid[rows, :] = value
        normed[rows, :] = norm_low(value, gain, shift)

    by_rows(x.shape[0], part, 256)
    keep(dot(normed[...], low_up[...], TURNED), red_up, red_up_out)


def up_strip(i, normed, w, bias, red_up, up, active, slope):
    units = w.shape[2]
    cols = columns(i, units)
    value = dot(normed[...], w[i]) + (bias[i] + dot(red_up[...], up[:, cols]))
    made, made_slope = gelu_parts(value)
    active[:, cols] = made.astype(BF16)
    slope[:, cols] = made_slope.astype(BF16)


def down_stage(mid, active, w, bias, up, red, put):
    for n in range(mid.shape[1] // 256):
        cols = slice(n * 256, (n + 1) * 256)
        put(n, mid[:, cols] + (dot(active[...], w[:, cols]) + bias[:, cols] + dot(red[...], up[:, cols])))


def gelu_parts(x):
    square = x * x
    t = jnp.tanh(ROOT * (x + 0.044715 * (x * square)))
    half = 0.5 * (1.0 + t)
    slope = half + 0.5 * x * (1.0 - t * t) * (ROOT * (1.0 + 3 * 0.044715 * square))
    return x * half, slope


class Vectors:
    def __init__(self, ref, l):
        self.ref, self.l = ref, l

    def qkv(self, i):
        return self.ref[i, pl.ds(4 * self.l, 1), :384]

    def up(self, i):
        return self.ref[i, pl.ds(4 * self.l + 1, 1), :]

    def row(self, name):
        at = ("proj", "down", "gain1", "shift1", "gain2", "shift2").index(name)
        row, lane = 4 * self.l + 2 + at // 4, at % 4 * 128
        return jnp.concatenate([self.ref[i, row : row + 1, lane : lane + 128] for i in range(NARROW)], axis=1)


class Strips:
    def __init__(self, read):
        self.read = read

    def __getitem__(self, i):
        return self.read(i)


TABLES = ("low_qkv", "up_qkv", "low_proj", "up_proj", "low_up", "up_up", "low_down", "up_down")
SAVED = ("q", "kv", "peer", "att", "lse", "mid", "active", "slope", "x")


def task_list(layers):
    tasks = [("load", 0, 0, 3.0, None)]
    for l in range(layers):
        tasks.append(("qkv", l, 0, 7.0, ("qkv", l)))
        tasks += [("attend", l, n, 5.5, None) for n in range(2)]
        tasks.append(("proj", l, 0, 4.0, ("proj", l)))
        tasks += [("up", l, n, 6.0, ("up", l)) for n in range(2)]
        tasks.append(("down", l, 0, 5.0, ("down", l)))
    return tasks


class ForwardWork:
    def __init__(self, n_col, group, refs):
        self.__dict__.update(refs)
        self.group = group
        self.held = positions(group)
        self.r, self.c = lax.axis_index("row"), lax.axis_index("col")
        self.g = lax.rem(self.c, group)
        self.bias = pair_bias(self.held, self.g)
        self.layers = self.low_qkv.shape[0]

    def stage_copies(self, kind, l):
        full = self.full[kind]
        if kind == "qkv":
            pieces = []
            for i in range(NARROW):
                src = full.at[l, i]
                pieces.append((src, self.wq.at[i // 2, :, :, :, pl.ds(i % 2 * 384, 384)]))
            return pieces, self.wq
        if kind == "up":
            return [(full.at[l, i], self.wu.at[i]) for i in range(NARROW)], self.wu
        target = self.wp if kind == "proj" else self.wd
        return [(full.at[l, i], target.at[i]) for i in range(NARROW)], target

    def stage(self, kind, l):
        for src, dst in self.stage_copies(kind, l)[0]:
            pltpu.make_async_copy(src, dst, self.stage_sem.at[KINDS.index(kind)]).start()

    def staged(self, kind, l):
        target = self.stage_copies(kind, l)[1]
        pltpu.make_async_copy(target, target, self.stage_sem.at[KINDS.index(kind)]).wait()

    def save_copy(self, name, l):
        src = {
            "q": self.q, "kv": self.kv, "peer": self.peer.at[l], "att": self.att, "lse": self.lse,
            "mid": self.mid, "active": self.active, "slope": self.slope, "x": self.x,
        }[name]
        return pltpu.make_async_copy(src, self.saved[name].at[l], self.save_sem.at[l, SAVED.index(name)])

    def save(self, *names, l):
        for name in names:
            self.save_copy(name, l).start()

    def settled(self, *names, l):
        if l >= 0:
            for name in names:
                self.save_copy(name, l).wait()

    def result_copy(self, n):
        pair = pl.ds(2 * n, 2)
        return pltpu.make_async_copy(self.result.at[pair], self.out_result.at[pair], self.result_sem.at[n])

    def exchange(self, l, s):
        to = self.c - self.g + lax.rem(self.g + s, self.group)
        return pltpu.make_async_remote_copy(
            src_ref=self.kv, dst_ref=self.peer.at[l, s - 1],
            send_sem=self.kv_send.at[l, s - 1], recv_sem=self.kv_recv.at[l, s - 1],
            device_id=(self.r, to), device_id_type=MESH,
        )

    def run(self, name, l, part):
        vec = Vectors(self.vec, l)
        if name == "load":
            self.arrive_tokens()
            self.x[...] = self.tokens_v[...].astype(F32)
        elif name == "qkv":
            self.staged("qkv", l)
            self.settled("q", "kv", l=l - 1)
            if l > 0:
                for s in range(1, self.group):
                    self.exchange(l - 1, s).wait_send()
            w = self.wq.reshape(NARROW // 2, -1, 768)
            qkv_stage(
                self.x, vec.row("gain1"), vec.row("shift1"), w, Strips(vec.qkv), self.low_qkv.at[l],
                self.up_qkv.at[l], self.q, self.kv, self.red, self.reds.at[l, 0], self.normed,
            )
            for s in range(1, self.group):
                self.exchange(l, s).start()
            self.save("q", "kv", l=l)
        elif name == "attend":
            if part == 0:
                for s in range(1, self.group):
                    self.exchange(l, s).wait_recv()
                self.save("peer", l=l)
                self.settled("att", "lse", l=l - 1)
            kvs = [self.kv] + [self.peer.at[l, s - 1] for s in range(1, self.group)]
            size = NARROW // 2
            each(size, lambda n: attend_strip(self.held, self.bias, self.g, part * size + n, self.q, kvs, self.att, self.lse))
            if part == 1:
                self.save("att", "lse", l=l)
        elif name == "proj":
            self.staged("proj", l)
            self.settled("mid", l=l - 1)
            dim = self.att.shape[1]
            proj_stage(
                self.x, self.att, self.wp.reshape(dim, dim), vec.row("proj"), self.low_proj.at[l],
                self.up_proj.at[l], vec.row("gain2"), vec.row("shift2"), self.low_up.at[l],
                self.mid, self.normed, self.red, self.reds.at[l, 1], self.red_up, self.reds.at[l, 2],
            )
            self.save("mid", l=l)
        elif name == "up":
            if part == 0:
                self.staged("up", l)
                self.settled("active", "slope", l=l - 1)
            w = self.wu.reshape(NARROW, self.x.shape[1], -1)
            size = NARROW // 2
            each(size, lambda n: up_strip(
                part * size + n, self.normed, w, Strips(vec.up), self.red_up, self.up_up.at[l],
                self.active, self.slope,
            ))
            if part == 1:
                self.save("active", "slope", l=l)
                keep(dot(self.active[...], self.low_down[l], TURNED), self.red, self.reds.at[l, 3])
        elif name == "down":
            self.staged("down", l)
            self.settled("x", l=l - 1)
            dim = self.x.shape[1]

            def put(n, value):
                if l < self.layers - 1:
                    self.x[:, columns(n, 256)] = value
                else:
                    for m in range(2):
                        self.result[2 * n + m] = value[:, m * 128 : (m + 1) * 128].astype(BF16)
                    self.result_copy(n).start()

            down_stage(
                self.mid, self.active, self.wd.reshape(-1, dim), vec.row("down"), self.up_down.at[l], self.red, put,
            )
            if l < self.layers - 1:
                self.save("x", l=l)

    def close(self):
        last = self.layers - 1
        self.settled(*[name for name in SAVED if name not in ("x", "peer")], l=last)
        for l in range(self.layers):
            self.settled("peer", l=l)
        for s in range(1, self.group):
            self.exchange(last, s).wait_send()
        for n in range(NARROW // 2):
            self.result_copy(n).wait()


def gather_body(n_row, n_col, layers, group, names, *refs):
    refs = dict(zip(names, refs))
    shard = {kind: refs["shard_" + kind] for kind in KINDS}
    full = {kind: refs["full_" + kind] for kind in KINDS}
    tokens, cotangent, vector = refs["tokens"], refs["cotangent"], refs["vector"]
    own_tokens, own_cotangent, vectors = refs["own_tokens"], refs["own_cotangent"], refs["vectors"]
    local_sem, send_sem, recv_sem = refs["local_sem"], refs["send_sem"], refs["recv_sem"]
    near_sem, out_sem, in_sem = refs["near_sem"], refs["out_sem"], refs["in_sem"]
    r = lax.axis_index("row")
    c = lax.axis_index("col")
    link_bits = [b for b in (2**k for k in range(1, 8)) if b < n_col]
    depth = shard["up"].shape[1]

    def row_peer(s):
        return (lax.rem(r + s, n_row), c)

    def col_peer(bit):
        return (r, c ^ bit)

    peers = [row_peer(s) for s in range(1, n_row)]
    peers += [(r, lax.rem(c + d, n_col)) for d in range(1, n_col)]
    barrier = pltpu.get_barrier_semaphore()
    for peer in peers:
        pl.semaphore_signal(barrier, inc=1, device_id=peer, device_id_type=MESH)
    pl.semaphore_wait(barrier, len(peers))

    per, width = BLOCKS // group, tokens.shape[1]

    def own_place(ref, b, col):
        if len(ref.shape) == 2:
            start = pl.multiple_of(col * width, width)
            return ref.at[pl.ds(b * BLOCK, BLOCK), pl.ds(start, width)]
        return ref.at[col, pl.ds(b * BLOCK, BLOCK)]

    def from_place(ref, b, col):
        start = (col // group) * LEN + place_of(group, lax.rem(col, group), b) * BLOCK
        return ref.at[pl.ds(pl.multiple_of(start, BLOCK), BLOCK)]

    exchanged = ((tokens, own_tokens), (cotangent, own_cotangent))

    def near(n, b):
        src, dst = exchanged[n]
        return pltpu.make_async_copy(from_place(src, b, c), own_place(dst, b, c), near_sem.at[n * per + b])

    def near_vector():
        return pltpu.make_async_copy(vector, vectors.at[c], near_sem.at[2 * per])

    def far(src, dst, n, peer):
        return pltpu.make_async_remote_copy(
            src_ref=src, dst_ref=dst, send_sem=out_sem.at[n], recv_sem=in_sem.at[n],
            device_id=peer, device_id_type=MESH,
        )

    def start_exchange(n):
        src, dst = exchanged[n]
        for b in range(per):
            near(n, b).start()
        for d in range(1, n_col):
            to = lax.rem(c + d, n_col)
            for b in range(per):
                far(from_place(src, b, to), own_place(dst, b, c), n, (r, to)).start()

    def wait_exchange(n):
        _, dst = exchanged[n]
        for b in range(per):
            near(n, b).wait()
        if len(dst.shape) == 2:
            ref = dst.at[:, pl.ds(0, (n_col - 1) * width)]
        else:
            ref = dst.at[pl.ds(0, n_col - 1)]
        far(ref, ref, n, col_peer(1)).wait()

    def own(kind, l, h, dst):
        ref = shard[kind]
        size = ref.shape[-2] // CUTS[kind]
        if len(ref.shape) == 3:
            return [(ref.at[l, pl.ds(h * size, size)], dst)]
        return [
            (ref.at[l, n, pl.ds(h * size, size)], dst.at[:, pl.ds(n * ref.shape[3], ref.shape[3])])
            for n in range(ref.shape[1])
        ]

    def block(kind, l, h, row, col):
        if kind in ("qkv", "up"):
            return full[kind].at[l, col, row, h]
        start = pl.multiple_of(row * depth, depth)
        return full[kind].at[l, col, h, :, pl.ds(start, depth)]

    def strip(kind, l, h, col):
        if kind in ("qkv", "up"):
            return full[kind].at[l, col, :, h]
        return full[kind].at[l, col, h]

    def amount(kind, l, h, strips, rows):
        if kind in ("qkv", "up"):
            return full[kind].at[l, pl.ds(0, strips), pl.ds(0, rows), h]
        return full[kind].at[l, pl.ds(0, strips), h, :, pl.ds(0, rows * depth)]

    chunks = []
    for l in range(layers):
        for kind in KINDS:
            for h in range(CUTS[kind]):
                order = []
                for d in ORDERS[l % len(ORDERS)][kind][h // 2][h % 2]:
                    if d == "z":
                        order.append("z")
                    elif d < len(link_bits):
                        order.append(link_bits[d])
                order += link_bits[2:]
                chunks.append((kind, l, h, tuple(order)))
    phases = len(link_bits) + n_row - 1

    def remote(src, dst, k, p, peer, way=0):
        at = (k * (phases + 1) + p) * 2 + way
        return pltpu.make_async_remote_copy(
            src_ref=src, dst_ref=dst, send_sem=send_sem.at[at], recv_sem=recv_sem.at[at],
            device_id=peer, device_id_type=MESH,
        )

    def plan(k):
        return transfer_plan(chunks[k][3], n_row)

    def ways(hop):
        return (
            (r - hop + 1, (r - hop + 1 >= 0) & (r + 1 < n_row), r - hop >= 0, 1),
            (r + hop - 1, (r + hop - 1 < n_row) & (r >= 1), r + hop < n_row, n_row - 1),
        )

    def local_start(k):
        kind, l, h, _ = chunks[k]
        for src, dst in own(kind, l, h, block(kind, l, h, r, c)):
            pltpu.make_async_copy(src, dst, local_sem.at[k]).start()

    def local_wait(k):
        kind, l, h, _ = chunks[k]
        ref = block(kind, l, h, r, c)
        pltpu.make_async_copy(ref, ref, local_sem.at[k]).wait()

    def issue(k, p):
        kind, l, h, order = chunks[k]
        d, masks, rows = plan(k)[p]

        def send(m, row, first, peer, way):
            dst = block(kind, l, h, row, c ^ m)
            for src, to in own(kind, l, h, dst) if m == 0 and first else [(dst, dst)]:
                remote(src, to, k, p, peer, way).start()

        if isinstance(d, tuple):
            for way, (row, goes, _, step) in enumerate(ways(d[1])):

                @pl.when(goes)
                def _():
                    for m in masks:
                        send(m, row, d[1] == 1, row_peer(step), way)

            return
        for m in masks:
            if rows:
                ref = strip(kind, l, h, c ^ m)
                remote(ref, ref, k, p, col_peer(d)).start()
            else:
                send(m, r, True, col_peer(d), 0)

    def moved(k, p, send):
        kind, l, h, order = chunks[k]
        d, masks, rows = plan(k)[p]
        ref = amount(kind, l, h, len(masks), n_row if rows else 1)
        if not isinstance(d, tuple):
            copy = remote(ref, ref, k, p, col_peer(1))
            copy.wait_send() if send else copy.wait_recv()
            return
        for way, (_, goes, comes, step) in enumerate(ways(d[1])):

            @pl.when(goes if send else comes)
            def _():
                copy = remote(ref, ref, k, p, row_peer(step), way)
                copy.wait_send() if send else copy.wait_recv()

    def share(k, p):
        kind, l, h, order = chunks[k]
        (d, masks, _), (_, later, rows) = plan(k)[p : p + 2]
        if not rows:
            return
        fresh = masks if isinstance(d, tuple) else later[len(masks):]
        for m in fresh:
            ref = strip(kind, l, h, c ^ m)
            remote(ref, ref, k, phases, col_peer(1)).start()

    def shared(k):
        kind, l, h, _ = chunks[k]
        ref = amount(kind, l, h, n_col // 2, n_row)
        return remote(ref, ref, k, phases, col_peer(1))

    def finish(k, p):
        moved(k, p, False)
        if plan(k)[p][0] == ("z", n_row - 1):
            local_wait(k)
        share(k, p)

    count = len(chunks)
    near_vector().start()
    for d in range(1, n_col):
        far(vector, vectors.at[c], 2, (r, lax.rem(c + d, n_col))).start()
    start_exchange(0)
    for k in range(count):
        local_start(k)
    def vectors_arrive():
        near_vector().wait()
        rest = vectors.at[pl.ds(0, n_col - 1)]
        far(rest, rest, 2, col_peer(1)).wait()

    work = None
    if "x" in refs:
        refs.update(full=full, saved={name: refs["saved_" + name] for name in SAVED})

        loads = [(refs["in_" + name], refs[name]) for name in TABLES]
        loads += [(own_tokens, refs["tokens_v"]), (vectors, refs["vec"])]
        loads = [pltpu.make_async_copy(s, d, refs["load_sem"].at[n]) for n, (s, d) in enumerate(loads)]
        for copy in loads[: len(TABLES)]:
            copy.start()

        def arrive_tokens():
            vectors_arrive()
            wait_exchange(0)
            for copy in loads[len(TABLES) :]:
                copy.start()
            for copy in loads:
                copy.wait()

        refs.update(arrive_tokens=arrive_tokens)
        work = ForwardWork(n_col, group, refs)

    pieces = []
    for kind, l, h, order in chunks:
        size = 2 * math.prod(shard[kind].shape[1:]) // CUTS[kind]
        pieces.append(((kind, l), order, size))
    ops = transfer_schedule(pieces, n_row, task_list(layers) if work else [])
    quiet = max(n for n, (op, _, _) in enumerate(ops) if op == "wait")
    for n, (op, k, p) in enumerate(ops):
        if op == "start":
            issue(k, p)
        elif op == "wait":
            finish(k, p)
        elif op == "stage":
            for at, (kind, l, _, _) in enumerate(chunks):
                if (kind, l) == (k, p):
                    shared(at).wait_recv()
            work.stage(k, p)
        else:
            work.run(k, *p)
        if n == quiet:
            start_exchange(1)
    for k in range(count):
        for p in range(phases):
            moved(k, p, True)
        shared(k).wait_send()
        if not work:
            shared(k).wait_recv()
    if work:
        work.close()
    else:
        vectors_arrive()
        wait_exchange(0)
    wait_exchange(1)


def gather_inputs(n_row, n_col, group, qkv, proj, up, down, tokens, cotangent, vector, tables=None):
    layers, depth = up.shape[0], up.shape[1]
    width, units = proj.shape[1], down.shape[1]
    dim, hidden = depth * n_row, units * n_col
    mine = LEN // group
    cuts = [CUTS[kind] for kind in KINDS]
    own = (mine, dim) if width % 128 == 0 else (n_col, mine, width)
    hbm = pl.BlockSpec(memory_space=pltpu.HBM)
    vmem = pl.BlockSpec(memory_space=pltpu.VMEM)
    dma = pltpu.SemaphoreType.DMA
    count = layers * sum(cuts)
    phases = n_col.bit_length() + n_row - 2
    inputs = [("shard_" + kind, array, hbm) for kind, array in zip(KINDS, (qkv, proj, up, down))]
    inputs += [("tokens", tokens, hbm), ("cotangent", cotangent, hbm), ("vector", vector, hbm)]
    outputs = [
        ("full_qkv", (layers, n_col, n_row, cuts[0], depth // cuts[0], 3 * width), BF16, hbm),
        ("full_proj", (layers, n_col, cuts[1], width // cuts[1], dim), BF16, hbm),
        ("full_up", (layers, n_col, n_row, cuts[2], depth // cuts[2], units), BF16, hbm),
        ("full_down", (layers, n_col, cuts[3], units // cuts[3], dim), BF16, hbm),
        ("own_tokens", own, BF16, hbm),
        ("own_cotangent", own, BF16, hbm),
        ("vectors", (n_col,) + vector.shape, F32, hbm),
    ]
    scratch = [
        ("local_sem", dma((count,))),
        ("send_sem", dma((count * phases * 2,))),
        ("recv_sem", dma((count * phases * 2,))),
        ("near_sem", dma((2 * (BLOCKS // group) + 1,))),
        ("out_sem", dma((3,))),
        ("in_sem", dma((3,))),
    ]
    if tables is not None:
        rank = tables[0].shape[1]
        inputs += [("in_" + name, table, hbm) for name, table in zip(TABLES, tables)]
        strip = (NARROW, mine)
        kept = {
            "q": (strip + (128,), BF16), "kv": (strip + (256,), BF16), "att": ((mine, dim), BF16),
            "lse": ((NARROW, 8, mine), F32), "mid": ((mine, dim), F32), "active": ((mine, hidden), BF16),
            "slope": ((mine, hidden), BF16),
            "x": ((mine, dim), F32), "peer": ((group - 1,) + strip + (256,), BF16),
        }
        outputs += [("saved_" + name, (layers,) + kept[name][0], kept[name][1], hbm) for name in SAVED]
        outputs += [
            ("reds", (layers, 4, rank, mine), BF16, vmem),
            ("out_result", (NARROW, mine, 128), BF16, hbm),
        ]
        scratch += [
            (name, pltpu.VMEM(((layers,) if name == "peer" else ()) + kept[name][0], kept[name][1]))
            for name in SAVED
        ]
        scratch += [
            *[(name, pltpu.VMEM(table.shape, table.dtype)) for name, table in zip(TABLES, tables)],
            ("wq", pltpu.VMEM((NARROW // 2, n_row, cuts[0], depth // cuts[0], 768), BF16)),
            ("wp", pltpu.VMEM((NARROW, cuts[1], width // cuts[1], dim), BF16)),
            ("wu", pltpu.VMEM((NARROW, n_row, cuts[2], depth // cuts[2], units), BF16)),
            ("wd", pltpu.VMEM((NARROW, cuts[3], units // cuts[3], dim), BF16)),
            ("tokens_v", pltpu.VMEM((mine, dim), BF16)),
            ("normed", pltpu.VMEM((mine, dim), BF16)),
            ("red", pltpu.VMEM((mine, rank), BF16)),
            ("red_up", pltpu.VMEM((mine, rank), BF16)),
            ("vec", pltpu.VMEM((n_col,) + vector.shape, F32)),
            ("stage_sem", dma((4,))),
            ("save_sem", dma((layers, len(SAVED)))),
            ("kv_send", dma((layers, group - 1))),
            ("kv_recv", dma((layers, group - 1))),
            ("load_sem", dma((2 + len(TABLES),))),
            ("result", pltpu.VMEM((NARROW, mine, 128), BF16)),
            ("result_sem", dma((NARROW // 2,))),
        ]
    names = [x[0] for x in inputs] + [x[0] for x in outputs] + [x[0] for x in scratch]
    outs = pl.pallas_call(
        functools.partial(gather_body, n_row, n_col, layers, group, tuple(names)),
        out_shape=[jax.ShapeDtypeStruct(shape, kind) for _, shape, kind, _ in outputs],
        in_specs=[spec for _, _, spec in inputs],
        out_specs=[spec for _, _, _, spec in outputs],
        scratch_shapes=[shape for _, shape in scratch],
        compiler_params=pltpu.CompilerParams(
            collective_id=0, has_side_effects=True, vmem_limit_bytes=60 * 2**20
        ),
        name="gather_inputs",
    )(*[array for _, array, _ in inputs])
    outs = dict(zip([x[0] for x in outputs], outs))

    merge = 128 // width
    strips = n_col // merge
    qkv_full = outs["full_qkv"].reshape(layers, n_col, dim, 3 * width)
    up_full = outs["full_up"].reshape(layers, n_col, dim, units)
    rows, vec = [outs["own_tokens"], outs["own_cotangent"]], outs["vectors"]
    if merge > 1:
        qkv_full = qkv_full.reshape(layers, strips, merge, dim, 3, width).transpose(0, 1, 3, 4, 2, 5)
        up_full = up_full.reshape(layers, strips, merge, dim, units).transpose(0, 1, 3, 2, 4)
        rows = [x.transpose(1, 0, 2).reshape(mine, dim) for x in rows]
        vec = vec.reshape(strips, merge, layers, 4, 4 * 128)
        first = vec[:, :, :, 0, : 3 * width].reshape(strips, merge, layers, 3, width).transpose(0, 2, 3, 1, 4)
        first = jnp.pad(first.reshape(strips, layers, 384), ((0, 0), (0, 0), (0, 128)))
        second = vec[:, :, :, 1, :units].transpose(0, 2, 1, 3).reshape(strips, layers, 512)
        rest = vec[:, :, :, 2:, : 4 * width].reshape(strips, merge, layers, 2, 4, width)
        rest = rest.transpose(0, 2, 3, 4, 1, 5).reshape(strips, layers, 2, 512)
        vec = jnp.concatenate([first[:, :, None], second[:, :, None], rest], axis=2)
        vec = vec.reshape(strips, layers * 4, 512)
    outs.update(
        qkv=qkv_full.reshape(layers, strips, dim, 384),
        proj=outs["full_proj"].reshape(layers, dim, dim),
        up=up_full.reshape(layers, strips, dim, units * merge),
        down=outs["full_down"].reshape(layers, hidden, dim),
        tokens=rows[0], cotangent=rows[1], vec=vec, result=outs.get("out_result"),
    )
    return outs


PARAMS = pltpu.CompilerParams(vmem_limit_bytes=60 * 2**20)


def shape_of(shape, kind):
    return jax.ShapeDtypeStruct(shape, kind)


def kernel(body, name, inputs, outputs, scratch=()):
    spaces = (pl.BlockSpec(memory_space=pltpu.VMEM), pl.BlockSpec(memory_space=pltpu.HBM))
    return pl.pallas_call(
        body,
        out_shape=[shape_of(shape, kind) for shape, kind, _ in outputs],
        in_specs=[spaces[far] for _, far in inputs],
        out_specs=[spaces[far] for _, _, far in outputs],
        scratch_shapes=list(scratch),
        compiler_params=PARAMS,
        name=name,
    )(*[array for array, _ in inputs])


def own_group(group):
    return lax.rem(lax.axis_index("col"), group)


def qkv_body(l, x, vec, w, low, up, q, kv, red_out, red, normed, buf, sem):
    copies = []
    for i in range(NARROW):
        copies.append(pltpu.make_async_copy(w.at[l, i], buf.at[i // 2, :, columns(i % 2, 384)], sem.at[i]))
        copies[-1].start()
    for copy in copies:
        copy.wait()
    v = Vectors(vec, l)
    qkv_stage(x, v.row("gain1"), v.row("shift1"), buf, Strips(v.qkv), low.at[l], up.at[l], q, kv, red, red_out, normed)


def qkv_kernel(l, x, vec, w, low, up):
    tokens, dim = x.shape
    return kernel(
        functools.partial(qkv_body, l), "qkv",
        [(x, False), (vec, False), (w, True), (low, False), (up, False)],
        [((NARROW, tokens, 128), BF16, False), ((NARROW, tokens, 256), BF16, False), ((low.shape[1], tokens), BF16, False)],
        [pltpu.VMEM((tokens, low.shape[1]), BF16), pltpu.VMEM((tokens, dim), BF16), pltpu.VMEM((NARROW // 2, dim, 768), BF16), pltpu.SemaphoreType.DMA((NARROW,))],
    )


def attend_body(group, g_ref, q, *refs):
    held = positions(group)
    kvs, (out, lse) = refs[:group], refs[group:]
    bias = pair_bias(held, g_ref[0])
    each(NARROW, lambda i: attend_strip(held, bias, g_ref[0], i, q, kvs, out, lse))


def attend_kernel(group, g, q, kvs):
    tokens = q.shape[1]
    return pl.pallas_call(
        functools.partial(attend_body, group),
        out_shape=[shape_of((tokens, NARROW * 128), BF16), shape_of((NARROW, 8, tokens), F32)],
        in_specs=[pl.BlockSpec(memory_space=pltpu.SMEM)] + [pl.BlockSpec(memory_space=pltpu.VMEM)] * (group + 1),
        out_specs=[pl.BlockSpec(memory_space=pltpu.VMEM)] * 2,
        compiler_params=PARAMS,
        name="attend",
    )(g, q, *kvs)


def mlp_body(l, x, att, vec, wp, wu, wd, *refs):
    low_proj, up_proj, low_up, up_up, low_down, up_down = [ref.at[l] for ref in refs[:6]]
    mid, result, active, slope, reds, red, red_up, normed, bp, bu, bd, sem = refs[6:]
    copies = []
    for n, (src, dst) in enumerate(((wp.at[l], bp), (wu.at[l], bu), (wd.at[l], bd))):
        copies.append(pltpu.make_async_copy(src, dst, sem.at[n]))
        copies[-1].start()
    v = Vectors(vec, l)
    copies[0].wait()
    proj_stage(
        x, att, bp, v.row("proj"), low_proj, up_proj, v.row("gain2"), v.row("shift2"), low_up,
        mid, normed, red, reds.at[0], red_up, reds.at[1],
    )
    copies[1].wait()
    each(NARROW, lambda i: up_strip(i, normed, bu, Strips(v.up), red_up, up_up, active, slope))
    copies[2].wait()

    def put(n, value):
        if len(result.shape) == 2:
            result[:, columns(n, 256)] = value
        else:
            for m in range(2):
                result[2 * n + m] = value[:, m * 128 : (m + 1) * 128].astype(BF16)

    keep(dot(active[...], low_down[...], TURNED), red, reds.at[2])
    down_stage(mid, active, bd, v.row("down"), up_down, red, put)


def mlp_kernel(l, final, x, att, vec, wp, wu, wd, tables):
    tokens, dim = x.shape
    hidden = wd.shape[1]
    rank = tables[0].shape[1]
    result = ((NARROW, tokens, 128), BF16, False) if final else ((tokens, dim), F32, False)
    return kernel(
        functools.partial(mlp_body, l), "mlp",
        [(x, False), (att, False), (vec, False), (wp, True), (wu, True), (wd, True)] + [(t, False) for t in tables],
        [((tokens, dim), F32, False), result] + [((tokens, hidden), BF16, False)] * 2 + [((3, rank, tokens), BF16, False)],
        [
            pltpu.VMEM((tokens, rank), BF16), pltpu.VMEM((tokens, rank), BF16),
            pltpu.VMEM((tokens, dim), BF16), pltpu.VMEM(wp.shape[1:], BF16),
            pltpu.VMEM(wu.shape[1:], BF16), pltpu.VMEM(wd.shape[1:], BF16), pltpu.SemaphoreType.DMA((3,)),
        ],
    )


def mlp_back_stage(vec, grad, active, g_hid, mid, att, low, total, wp, wu, wd, reds, t, grads, g_mid, waits, strip_waits):
    low[...] = grad[...].astype(BF16)
    g_red = dot(low[...], t["up_down"], TURNED).astype(BF16)
    rank = g_red.shape[1]
    units = wu.shape[2]
    total[...] = jnp.zeros_like(total)

    def strip(i):
        cols = columns(i, units)
        strip_waits(i)
        g_active = dot(low[...], wd[cols, :], TURNED) + dot(g_red, t["low_down"][:, cols])
        g_hid[:, cols] = (g_active * g_hid[:, cols].astype(F32)).astype(BF16)
        total[...] += dot(g_hid[:, cols], wu[i], TURNED)

    each(NARROW, strip)

    def give(at, value):
        size = value.shape[1] // NARROW
        for i in range(NARROW):
            grads[i, :, at : at + size] = value[:, i * size : (i + 1) * size].astype(BF16)

    give(384 + 2 * units, dot(reds[3], low[...]))
    give(384 + units, dot(g_red, active[...], CROSS))
    give(384, dot(reds[2], g_hid[...]))
    g_hid[:, :rank] = dot(g_hid[...], t["up_up"][...], TURNED).astype(BF16)
    waits("mid")
    gain, shift = vec.row("gain2"), vec.row("shift2")
    dim = mid.shape[1]

    def norm(rows):
        scaled, inverse = norm_parts(mid[rows, :])
        active[rows, :dim] = (scaled * gain + shift).astype(BF16)
        g_normed = total[rows, :] + dot(g_hid[rows, :rank], t["low_up"])
        value = grad[rows, :] + norm_grad(g_normed, scaled, inverse, gain)
        g_mid[rows, :] = value
        low[rows, :] = value.astype(BF16)

    by_rows(mid.shape[0], norm)
    give(256, dot(g_hid[:, :rank], active[:, :dim], CROSS))
    give(128, dot(reds[1], low[...]))
    g_red_proj = dot(low[...], t["up_proj"], TURNED).astype(BF16)
    waits("att")
    waits("proj")
    give(0, dot(g_red_proj, att[...], CROSS))
    low[...] = (dot(low[...], wp[...], TURNED) + dot(g_red_proj, t["low_proj"])).astype(BF16)


def qkv_back_stage(vec, x, g_mid, gq, parts, total, g_red, normed, wq, red, low, up, grads, put, waits, done=None):
    waits("gq")
    waits("qkv")
    rank, tokens = red.shape
    small = jnp.zeros((tokens, rank), F32)

    def mixed(i, rows):
        return jnp.concatenate([gq[i, rows, :], parts[0][i, rows, :]], axis=1)

    def product(j, rows):
        made = dot(jnp.concatenate([mixed(2 * j, rows), mixed(2 * j + 1, rows)], axis=1), wq[j], TURNED)
        total[rows, :] = made if j == 0 else total[rows, :] + made

    every = pl.ds(0, tokens)
    for j in range(NARROW // 2):
        for i in (2 * j, 2 * j + 1):
            waits(("part", i))
            parts[0][i] = sum(part[i].astype(F32) for part in parts).astype(BF16)
            g_mixed = mixed(i, every)
            grads[i, :, 128:512] = dot(red[...], g_mixed).astype(BF16)
            small = small + dot(g_mixed, up[i], TURNED)
        if not done:
            product(j, every)
    g_low_rank = small.astype(BF16)
    g_red[...] = g_low_rank
    waits("x")
    waits("g_mid")
    gain, shift = vec.row("gain1"), vec.row("shift1")

    def norm(rows):
        scaled, inverse = norm_parts(x[rows, :].astype(F32))
        normed[rows, :] = (scaled * gain + shift).astype(BF16)
        g_normed = total[rows, :] + dot(g_red[rows, :], low[...])
        put(rows, g_mid[rows, :] + norm_grad(g_normed, scaled, inverse, gain))

    def lower():
        g_low = dot(g_low_rank, normed[...], CROSS).astype(BF16)
        for i in range(NARROW):
            grads[i, :, :128] = g_low[:, i * 128 : (i + 1) * 128]

    if not done:
        by_rows(tokens, norm)
        lower()
        return

    def first_norm(rows):
        normed[rows, :] = norm_low(x[rows, :].astype(F32), gain, shift)

    by_rows(tokens, first_norm)
    lower()
    done(-1)
    for b in range(tokens // BLOCK):
        for j in range(NARROW // 2):
            product(j, pl.ds(b * BLOCK, BLOCK))
        for n in range(2):
            norm(pl.ds(b * BLOCK + n * BLOCK // 2, BLOCK // 2))
        done(b)


def back_body(lq, lm, group, names, *refs):
    R = dict(zip(names, refs))
    held = positions(group)
    sem, started = R["sem"], {}

    def waits(name):
        for copy in started.pop(name, ()):
            copy.wait()

    count = [0]

    def begin(name, *copies):
        started[name] = []
        for src, dst in copies:
            copy = pltpu.make_async_copy(src, dst, sem.at[count[0]])
            count[0] += 1
            copy.start()
            started[name].append(copy)

    def strip_copies(l, i, base):
        cols = columns(i, R["wu"].shape[2])
        pairs = (
            (R["slopes"].at[l, :, cols], R["g_hid"].at[:, cols]), (R["actives"].at[l, :, cols], R["active"].at[:, cols]),
            (R["w_down"].at[l, cols], R["wd"].at[cols]), (R["w_up"].at[l, i], R["wu"].at[i]),
        )
        return [pltpu.make_async_copy(src, dst, sem.at[base + 4 * i + n]) for n, (src, dst) in enumerate(pairs)]

    strip_base = {}

    def load_strips(l):
        strip_base[l] = count[0]
        count[0] += 4 * NARROW
        for i in range(NARROW):
            for copy in strip_copies(l, i, strip_base[l]):
                copy.start()

    def strip_waits(l):
        def wait(i):
            for copy in strip_copies(l, i, strip_base[l]):
                copy.wait()

        return wait

    if lq is not None:
        begin("gq", (R["in_gq"], R["gq"]), *[(R["in_part%d" % j], R["part%d" % j]) for j in range(group)])
        begin("qkv", *[
            (R["w_qkv"].at[lq, i], R["wq"].at[i // 2, :, columns(i % 2, 384)]) for i in range(NARROW)
        ])
        begin("x", (R["in_x"], R["x"]))
        begin("g_mid", (R["in_g_mid"], R["total2"]))
    else:
        begin("cotangent", (R["cotangent"], R["low"]))
    if lm is not None:
        load_strips(lm)
        begin("proj", (R["w_proj"].at[lm], R["wp"]))
        begin("att", (R["atts"].at[lm], R["att"]))
        begin("kv", (R["kvs"].at[lm], R["kv"]), (R["peers"].at[lm], R["peer"]), (R["lses"].at[lm], R["lse"]))
    if lq is not None:
        vec = Vectors(R["vec"], lq)

        def put(rows, value):
            if lm is None:
                for i in range(NARROW):
                    R["out"][i, rows, :] = value[:, i * 128 : (i + 1) * 128].astype(BF16)
            else:
                R["grad"][rows, :] = value

        qkv_back_stage(
            vec, R["x"], R["total2"], R["gq"], [R["part%d" % j] for j in range(group)], R["total"],
            R["g_red"], R["low"], R["wq"],
            R["reds"].at[lq, 0], R["low_qkv"].at[lq], R["up_qkv"].at[lq], R["grads_qkv"], put, waits,
        )
    else:
        waits("cotangent")
        R["grad"][...] = R["low"][...].astype(F32)
    if lm is None:
        return
    begin("q", (R["qs"].at[lm], R["gq"]))
    begin("mid", (R["mids"].at[lm], R["x" if lq is not None and R["x"].dtype == F32 else "mid"]))
    mid = R["x" if lq is not None and R["x"].dtype == F32 else "mid"]
    t = {name: R[name].at[lm] for name in TABLES}
    vec = Vectors(R["vec"], lm)
    mlp_back_stage(
        vec, R["grad"], R["active"], R["g_hid"], mid, R["att"], R["low"], R["total"], R["wp"], R["wu"], R["wd"],
        R["reds"].at[lm], {k: (v if k in ("low_down", "up_up") else v[...]) for k, v in t.items() if "qkv" not in k},
        R["grads_mlp"], R["total2"], waits, strip_waits(lm),
    )
    out_mid = pltpu.make_async_copy(R["total2"], R["out_g_mid"], sem.at[count[0]])
    out_mid.start()
    waits("q")
    waits("kv")
    bias = pair_bias(held, R["g"][0])
    kvs = [R["kv"]] + [R["peer"].at[j] for j in range(group - 1)]
    gkvs = [R["part%d" % j] for j in range(group)]
    each(NARROW, lambda i: attend_back_strip(
        held, bias, R["g"][0], i, R["gq"], R["lse"], R["att"], R["low"], kvs, R["gq"], gkvs
    ))
    outs = [(R["gq"], R["out_gq"])] + [(R["part%d" % j], R["out_part%d" % j]) for j in range(group)]
    copies = [pltpu.make_async_copy(src, dst, sem.at[count[0] + 1 + n]) for n, (src, dst) in enumerate(outs)]
    for copy in copies:
        copy.start()
    for copy in copies:
        copy.wait()
    out_mid.wait()


def back_kernel(lq, lm, group, g, outs, tables, carried):
    layers, _, dim, _ = outs["qkv"].shape
    hidden = outs["down"].shape[1]
    tokens = outs["tokens"].shape[0]
    rank = tables[0].shape[1]
    strip = (NARROW, tokens)
    inputs = [("g", g, pl.BlockSpec(memory_space=pltpu.SMEM))]
    near, far = pl.BlockSpec(memory_space=pltpu.VMEM), pl.BlockSpec(memory_space=pltpu.HBM)
    inputs += [(name, table, near) for name, table in zip(TABLES, tables)]
    inputs += [("vec", outs["vec"], near), ("reds", outs["reds"], near)]
    outputs, scratch = [], []

    def vmem(name, shape, kind):
        scratch.append((name, pltpu.VMEM(shape, kind)))

    vmem("gq", strip + (128,), BF16)
    for j in range(group):
        vmem("part%d" % j, strip + (256,), BF16)
    vmem("total", (tokens, dim), F32)
    vmem("total2", (tokens, dim), F32)
    vmem("low", (tokens, dim), BF16)
    if lq is not None:
        g_mid, gq, parts = carried
        x = outs["tokens"] if lq == 0 else outs["saved_x"][lq - 1]
        inputs += [("in_gq", gq, far), ("in_g_mid", g_mid, far), ("in_x", x, far), ("w_qkv", outs["qkv"], far)]
        inputs += [("in_part%d" % j, part, far) for j, part in enumerate(parts)]
        vmem("wq", (NARROW // 2, dim, 768), BF16)
        vmem("g_red", (tokens, rank), BF16)
        vmem("x", (tokens, dim), x.dtype)
        outputs.append(("grads_qkv", (NARROW, rank, 512), BF16, near))
        if lm is None:
            outputs.append(("out", strip + (128,), BF16, near))
    if lm is not None:
        if lq is None:
            inputs.append(("cotangent", outs["cotangent"], far))
        for name in ("active", "slope", "mid", "att", "q", "kv", "peer", "lse"):
            inputs.append((name + "s", outs["saved_" + name], far))
        inputs += [("w_" + name, outs[name], far) for name in ("proj", "up", "down")]
        vmem("wp", (dim, dim), BF16)
        vmem("wu", (NARROW, dim, hidden // NARROW), BF16)
        vmem("wd", (hidden, dim), BF16)
        vmem("grad", (tokens, dim), F32)
        if lq is None or x.dtype != F32:
            vmem("mid", (tokens, dim), F32)
        vmem("att", (tokens, dim), BF16)
        vmem("active", (tokens, hidden), BF16)
        vmem("g_hid", (tokens, hidden), BF16)
        vmem("kv", strip + (256,), BF16)
        vmem("peer", (group - 1,) + strip + (256,), BF16)
        vmem("lse", (NARROW, 8, tokens), F32)
        outputs.append(("grads_mlp", (NARROW, rank, 512 + 2 * hidden // NARROW), BF16, near))
        outputs += [("out_g_mid", (tokens, dim), F32, far), ("out_gq", strip + (128,), BF16, far)]
        outputs += [("out_part%d" % j, strip + (256,), BF16, far) for j in range(group)]
    scratch.append(("sem", pltpu.SemaphoreType.DMA((96,))))
    names = [x[0] for x in inputs] + [x[0] for x in outputs] + [x[0] for x in scratch]
    made = pl.pallas_call(
        functools.partial(back_body, lq, lm, group, tuple(names)),
        out_shape=[shape_of(shape, kind) for _, shape, kind, _ in outputs],
        in_specs=[spec for _, _, spec in inputs],
        out_specs=[spec for _, _, _, spec in outputs],
        scratch_shapes=[shape for _, shape in scratch],
        compiler_params=PARAMS,
        name="back",
    )(*[array for _, array, _ in inputs])
    return dict(zip([x[0] for x in outputs], made))


SITES = {"mlp": (1, 1, 2, 2, 3, 3), "qkv": (0, 0)}


def backward_body(layers, group, n_row, n_col, names, *refs):
    R = dict(zip(names, refs))
    held = positions(group)
    per = BLOCKS // group
    r, c = lax.axis_index("row"), lax.axis_index("col")
    g = lax.rem(c, group)
    seqs = n_col // group
    tokens = per * BLOCK
    bias = pair_bias(held, g)

    def row_peer(s):
        return (lax.rem(r + s, n_row), c)

    def col_peer(d):
        return lax.rem(c + d, n_col)

    peers = [row_peer(s) for s in range(1, n_row)] + [(r, col_peer(d)) for d in range(1, n_col)]
    barrier = pltpu.get_barrier_semaphore()
    for peer in peers:
        pl.semaphore_signal(barrier, inc=1, device_id=peer, device_id_type=MESH)
    pl.semaphore_wait(barrier, len(peers))

    sem, started, count = R["sem"], {}, [0]

    def begin(name, *copies):
        started[name] = []
        for src, dst in copies:
            copy = pltpu.make_async_copy(src, dst, sem.at[count[0]])
            count[0] += 1
            copy.start()
            started[name].append(copy)

    def waits(name):
        for copy in started.pop(name, ()):
            copy.wait()

    def strip_copies(l, i, base):
        cols = columns(i, R["wu"].shape[2])
        pairs = (
            (R["slopes"].at[l, :, cols], R["g_hid"].at[:, cols]), (R["actives"].at[l, :, cols], R["active"].at[:, cols]),
            (R["w_down"].at[l, cols], R["wd"].at[cols]), (R["w_up"].at[l, i], R["wu"].at[i]),
        )
        return [pltpu.make_async_copy(src, dst, sem.at[base + 4 * i + n]) for n, (src, dst) in enumerate(pairs)]

    strip_base = {}

    def load_strips(l):
        strip_base[l] = count[0]
        count[0] += 4 * NARROW
        for i in range(NARROW):
            for copy in strip_copies(l, i, strip_base[l]):
                copy.start()

    def strip_waits(l):
        def wait(i):
            for copy in strip_copies(l, i, strip_base[l]):
                copy.wait()

        return wait

    far = [0]

    def remote(src, dst, n, peer):
        return pltpu.make_async_remote_copy(
            src_ref=src, dst_ref=dst, send_sem=R["out_sem"].at[n], recv_sem=R["in_sem"].at[n],
            device_id=peer, device_id_type=MESH,
        )

    def new_far():
        far[0] += 1
        return far[0] - 1

    def columns_start(n, src, b, at):
        start = (c // group) * LEN + place_of(group, g, b) * BLOCK
        to, rows = R["columns"].at[n, pl.ds(pl.multiple_of(start, BLOCK), BLOCK)], pl.ds(b * BLOCK, BLOCK)
        begin("columns%d" % (n * per + b), (src.at[c, rows], to))
        for d in range(1, n_col):
            remote(src.at[col_peer(d), rows], to, at, (r, col_peer(d))).start()

    def columns_end(n, at):
        for b in range(per):
            waits("columns%d" % (n * per + b))
        ref = R["columns"].at[n, pl.ds(0, (n_col - 1) * tokens)]
        remote(ref, ref, at, (r, col_peer(1))).wait()

    ends = {}

    def spread(kind, l):
        src, land, at = R["grads_" + kind], R["land_" + kind].at[l], new_far()
        begin("own_%s%d" % (kind, l), (src.at[c], land.at[c]))
        for d in range(1, n_col):
            remote(src.at[col_peer(d)], land.at[c], at, (r, col_peer(d))).start()
        ends["spread", kind, l] = at

    def spread_sent(kind, l):
        if l < layers:
            ref = R["land_" + kind].at[l, pl.ds(0, n_col - 1)]
            remote(ref, ref, ends["spread", kind, l], (r, col_peer(1))).wait_send()

    def add_load(kind, l):
        land = R["land_" + kind].at[l]
        ref = land.at[pl.ds(0, n_col - 1)]
        remote(ref, ref, ends["spread", kind, l], (r, col_peer(1))).wait_recv()
        waits("own_%s%d" % (kind, l))
        begin("stage_" + kind, (land, R["stage_" + kind]))

    def add(kind, l):
        stage, total = R["stage_" + kind], R["sum_" + kind]
        add_sent(kind, l + 1)
        waits("stage_" + kind)
        for q in range(seqs):
            value = sum(stage[q * group + n].astype(F32) for n in range(group))
            total[q] = value.astype(BF16)
        parts, at = R["parts_" + kind], new_far()
        begin("part_%s%d" % (kind, l), (total, parts.at[l, r]))
        for q in range(1, n_row):
            remote(total, parts.at[l, r], at, row_peer(q)).start()
        ends["add", kind, l] = at

    def added(kind, l):
        ref = R["parts_" + kind].at[l, pl.ds(0, n_row - 1)]
        return remote(ref, ref, ends["add", kind, l], row_peer(1))

    def add_sent(kind, l):
        if l < layers:
            waits("part_%s%d" % (kind, l))
            added(kind, l).wait_send()

    def part_copy(l, j, i, at):
        to = c - g + lax.rem(g - j + group, group)
        strip = pl.ds(i, 1)
        return remote(R["part%d" % j].at[strip], R["in_part"].at[l, j - 1, strip], at[j] + i, (r, to))

    def back_strip(l, i, at):
        kvs = [R["kv"]] + [R["peer"].at[j] for j in range(group - 1)]
        gkvs = [R["part%d" % j] for j in range(group)]
        attend_back_strip(held, bias, g, i, R["gq"], R["lse"], R["att"], R["low"], kvs, R["gq"], gkvs)
        for j in range(1, group):
            part_copy(l, j, i, at).start()

    def load_qkv(l):
        begin("qkv", *[
            (R["w_qkv"].at[l, i], R["wq"].at[i // 2, :, columns(i % 2, 384)]) for i in range(NARROW)
        ])

    def load_mlp(l):
        load_strips(l)
        begin("proj", (R["w_proj"].at[l], R["wp"]))

    def load_attention(l):
        begin("mid", (R["mids"].at[l], R["mid"]))
        begin("att", (R["atts"].at[l], R["att"]))
        begin("q", (R["qs"].at[l], R["gq"]))
        begin("kv", (R["kvs"].at[l], R["kv"]), (R["peers"].at[l], R["peer"]), (R["lses"].at[l], R["lse"]))

    def block_done(b):
        if b < 0:
            spread("qkv", 0)
            return
        if b == per - 1:
            add("qkv", 0)
        columns_start(1, R["part0"].at[:, :, pl.ds(0, 128)], b, at_grad)
        if b == max(per - 2, 0):
            add_load("qkv", 0)

    last = layers - 1
    begin("cotangent", (R["cotangent"], R["low"]))
    begin("tables", *[(R["in_" + name], R[name]) for name in TABLES + ("vec", "reds")])
    load_mlp(last)
    load_attention(last)
    load_qkv(last)
    at_result, at_grad = new_far(), new_far()
    for b in range(per):
        columns_start(0, R["result"], b, at_result)
    at_ids = new_far()
    begin("ids", (R["ids"], R["all_ids"].at[r]))
    for q in range(1, n_row):
        remote(R["ids"], R["all_ids"].at[r], at_ids, row_peer(q)).start()
    waits("cotangent")

    def widen(rows):
        R["grad"][rows, :] = R["low"][rows, :].astype(F32)

    by_rows(tokens, widen)
    waits("tables")
    for l in reversed(range(layers)):
        t = {name: R[name].at[l] for name in TABLES if "qkv" not in name}
        vec = Vectors(R["vec"], l)
        spread_sent("mlp", l + 1)
        mlp_back_stage(
            vec, R["grad"], R["active"], R["g_hid"], R["mid"], R["att"], R["low"], R["total"], R["wp"], R["wu"],
            R["wd"], R["reds"].at[l], {k: (v if k in ("low_down", "up_up") else v[...]) for k, v in t.items()},
            R["grads_mlp"], R["total2"], waits, strip_waits(l),
        )
        spread("mlp", l)
        if l > 0:
            load_mlp(l - 1)
        begin("x", (R["tokens"] if l == 0 else R["xs"].at[l - 1], R["x0"] if l == 0 else R["mid"]))
        waits("q")
        waits("kv")
        at = [far[0] + j * NARROW for j in range(group)]
        far[0] += group * NARROW
        half = NARROW // 2
        if l < last:
            add_load("qkv", l + 1)
        each(half, lambda i: back_strip(l, i, at))
        add_load("mlp", l)
        if l < last:
            add("qkv", l + 1)
        add("mlp", l)
        each(half, lambda i: back_strip(l, half + i, at))
        for i in range(NARROW):
            for j in range(1, group):
                part_copy(l, j, i, at).wait_recv()
            begin(("part", i), *[(R["in_part"].at[l, j, i], R["peer"].at[j, i]) for j in range(group - 1)])
        parts = [R["part0"]] + [R["peer"].at[j] for j in range(group - 1)]
        spread_sent("qkv", l + 1)

        def put(rows, value):
            if l > 0:
                R["grad"][rows, :] = value
            else:
                for i in range(NARROW):
                    R["part0"][i, rows, :128] = value[:, i * 128 : (i + 1) * 128].astype(BF16)

        qkv_back_stage(
            vec, R["x0"] if l == 0 else R["mid"], R["total2"], R["gq"], parts, R["total"], R["g_red"], R["low"],
            R["wq"], R["reds"].at[l, 0], R["low_qkv"].at[l], R["up_qkv"].at[l], R["grads_qkv"], put, waits,
            None if l > 0 else block_done,
        )
        if l > 0:
            spread("qkv", l)
        for i in range(NARROW):
            for j in range(1, group):
                part_copy(l, j, i, at).wait_send()
        if l > 0:
            load_qkv(l - 1)
            load_attention(l - 1)
    columns_end(0, at_result)
    columns_end(1, at_grad)
    waits("ids")
    rest = R["all_ids"].at[pl.ds(0, n_row - 1)]
    remote(rest, rest, at_ids, row_peer(1)).wait()
    for kind in ("mlp", "qkv"):
        spread_sent(kind, 0)
        add_sent(kind, 0)
        for l in range(layers):
            added(kind, l).wait_recv()


def backward(n_row, n_col, group, outs, tables, ids):
    layers, _, dim, _ = outs["qkv"].shape
    hidden = outs["down"].shape[1]
    mine = outs["tokens"].shape[0]
    rank = tables[0].shape[1]
    seqs = n_col // group
    strip = (NARROW, mine)
    near, far = pl.BlockSpec(memory_space=pltpu.VMEM), pl.BlockSpec(memory_space=pltpu.HBM)
    small = list(zip(TABLES, tables)) + [("vec", outs["vec"]), ("reds", outs["reds"])]
    inputs = [("in_" + name, table, far) for name, table in small] + [("ids", ids, far)]
    for name in ("active", "slope", "mid", "att", "q", "kv", "peer", "lse", "x"):
        inputs.append((name + "s", outs["saved_" + name], far))
    inputs += [("w_" + name, outs[name], far) for name in KINDS]
    inputs += [(name, outs[name], far) for name in ("tokens", "cotangent", "result")]
    sizes = {"mlp": 512 + 2 * hidden // NARROW, "qkv": 512}
    outputs = [
        ("columns", (2, n_col * mine, 128), BF16, far),
        ("all_ids", (n_row,) + ids.shape, F32, far),
        ("in_part", (layers, group - 1) + strip + (256,), BF16, far),
    ]
    scratch = [
        ("gq", strip + (128,), BF16), ("kv", strip + (256,), BF16), ("peer", (group - 1,) + strip + (256,), BF16),
        ("lse", (NARROW, 8, mine), F32), ("total", (mine, dim), F32), ("total2", (mine, dim), F32),
        ("grad", (mine, dim), F32), ("mid", (mine, dim), F32), ("low", (mine, dim), BF16), ("att", (mine, dim), BF16),
        ("x0", (mine, dim), BF16), ("active", (mine, hidden), BF16), ("g_hid", (mine, hidden), BF16),
        ("g_red", (mine, rank), BF16), ("wq", (NARROW // 2, dim, 768), BF16), ("wp", (dim, dim), BF16),
        ("wu", (NARROW, dim, hidden // NARROW), BF16), ("wd", (hidden, dim), BF16),
    ]
    scratch += [("part%d" % j, strip + (256,), BF16) for j in range(group)]
    scratch += [(name, table.shape, table.dtype) for name, table in small]
    for kind, size in sizes.items():
        outputs.append(("land_" + kind, (layers, n_col, rank, size), BF16, far))
        outputs.append(("parts_" + kind, (layers, n_row, seqs, rank, size), BF16, far))
        scratch.append(("grads_" + kind, (NARROW, rank, size), BF16))
        scratch.append(("stage_" + kind, (n_col, rank, size), BF16))
        scratch.append(("sum_" + kind, (seqs, rank, size), BF16))
    scratch = [(name, pltpu.VMEM(shape, kind)) for name, shape, kind in scratch]
    scratch += [
        ("sem", pltpu.SemaphoreType.DMA((72 * layers + 16,))),
        ("out_sem", pltpu.SemaphoreType.DMA(((4 + group * NARROW) * layers + 4,))),
        ("in_sem", pltpu.SemaphoreType.DMA(((4 + group * NARROW) * layers + 4,))),
    ]
    names = [x[0] for x in inputs] + [x[0] for x in outputs] + [x[0] for x in scratch]
    made = pl.pallas_call(
        functools.partial(backward_body, layers, group, n_row, n_col, tuple(names)),
        out_shape=[shape_of(shape, kind) for _, shape, kind, _ in outputs],
        in_specs=[spec for _, _, spec in inputs],
        out_specs=[spec for _, _, _, spec in outputs],
        scratch_shapes=[shape for _, shape in scratch],
        compiler_params=pltpu.CompilerParams(
            collective_id=1, has_side_effects=True, vmem_limit_bytes=62 * 2**20
        ),
        name="backward",
    )(*[array for _, array, _ in inputs])
    return dict(zip([x[0] for x in outputs], made))


def place_body(layers, names, *refs):
    R = dict(zip(names, refs))
    sem, ends = R["sem"], []

    def copy(src, dst, n):
        made = pltpu.make_async_copy(src, dst, sem.at[n])
        made.start()
        return made

    loads = [copy(R["columns"].at[n], R["low"].at[n], n) for n in range(2)]
    ins = {kind: copy(R["parts_" + kind], R["in_" + kind], 2 + n) for n, kind in enumerate(SITES)}
    for n in range(2):
        loads[n].wait()
        R["wide"][n] = R["low"][n].astype(F32)
        ends.append(copy(R["wide"].at[n], R["column_out%d" % n], 4 + n))
    rows, adapters, rank = R["ids"].shape[0], R["keep0"].shape[1], R["keep0"].shape[2]
    sequences = R["in_qkv"].shape[1]
    shape = (adapters * rank, sequences * rank)
    down, across = [lax.broadcasted_iota(jnp.int32, shape, axis) for axis in (0, 1)]
    weights = {}
    for site in range(4):
        chosen = jnp.zeros((1, shape[1]), F32)
        for q in range(sequences):
            value = R["ids"][q // (sequences // rows), q % (sequences // rows), site]
            chosen = jnp.where(across[:1] // rank == q, value, chosen)
        same = (chosen == (down // rank).astype(F32)) & (down % rank == across % rank)
        weights[site] = jnp.where(same, 1.0, 0.0).astype(BF16)
    number = 0
    for kind in ("qkv", "mlp"):
        ins[kind].wait()
        stage = R["in_" + kind]
        sequences, rank = stage.shape[1:3]
        at = 0
        for site, size in zip(SITES[kind], R["sizes"][kind]):
            out, keep = R["out%d" % number], R["keep%d" % number]
            for l in range(layers):
                part = stage[l, :, :, at : at + size]
                made = dot(weights[site], part.reshape(sequences * rank, size)).reshape(-1, rank, size)
                if number == 1:
                    for n in range(3):
                        keep[l, :, n] = made[:, :, n * 128 : (n + 1) * 128]
                else:
                    keep[l] = made
            ends.append(copy(keep, out, 6 + number))
            at += size
            number += 1
    for end in ends:
        end.wait()


def place(made, sizes, adapters):
    layers, rank = made["parts_qkv"].shape[0], made["parts_qkv"].shape[-2]
    hbm = pl.BlockSpec(memory_space=pltpu.HBM)
    columns = made["columns"]
    parts = {kind: made["parts_" + kind].reshape(layers, -1, rank, sum(sizes[kind])) for kind in SITES}
    widths = [size for kind in ("qkv", "mlp") for size in sizes[kind]]
    inputs = [("ids", made["all_ids"], pl.BlockSpec(memory_space=pltpu.SMEM)), ("columns", columns, hbm)]
    inputs += [("parts_" + kind, parts[kind], hbm) for kind in SITES]
    outputs = [("column_out%d" % n, columns.shape[1:], F32) for n in range(2)]
    shapes = [(layers, adapters, rank, size) for size in widths]
    shapes[1] = (layers, adapters, 3, rank, 128)
    outputs += [("out%d" % n, shape, F32) for n, shape in enumerate(shapes)]
    scratch = [("low", pltpu.VMEM(columns.shape, BF16)), ("wide", pltpu.VMEM(columns.shape, F32))]
    scratch += [("in_" + kind, pltpu.VMEM(parts[kind].shape, BF16)) for kind in SITES]
    scratch += [("keep%d" % n, pltpu.VMEM(shape, F32)) for n, shape in enumerate(shapes)]
    scratch.append(("sem", pltpu.SemaphoreType.DMA((6 + len(widths),))))
    names = [x[0] for x in inputs] + [x[0] for x in outputs] + [x[0] for x in scratch]

    def body(*refs):
        place_body(layers, names + ["sizes"], *refs, sizes)

    return pl.pallas_call(
        body,
        out_shape=[shape_of(shape, kind) for _, shape, kind in outputs],
        in_specs=[spec for _, _, spec in inputs],
        out_specs=[hbm] * len(outputs),
        scratch_shapes=[shape for _, shape in scratch],
        compiler_params=PARAMS,
        name="place",
    )(*[array for _, array, _ in inputs])


def to_rows_body(held, x, out):
    n = 0
    for s in range(x.shape[0] // (len(held) * len(held[0]))):
        for g in range(len(held)):
            for place in held[g]:
                start = (s * BLOCKS + place) * BLOCK
                out[start : start + BLOCK, :] = x[n].astype(F32)
                n += 1


def to_rows(held, x):
    blocks, _, width = x.shape
    return pl.pallas_call(
        functools.partial(to_rows_body, held),
        out_shape=shape_of((blocks * BLOCK, width), F32),
        compiler_params=PARAMS,
        name="to_rows",
    )(x)


def pick_body(width, units, ids, *refs):
    tables, raise_qkv, vectors, every = refs[:7], refs[7], refs[8:16], refs[16]
    qkv_b, up_b, proj_b, down_b, gain1, shift1, gain2, shift2 = vectors
    outs, raise_out, vector, ids_rows = refs[17:24], refs[24], refs[25], refs[26]
    for ref, out in zip(tables, outs):
        out[...] = ref[...]
    layers = raise_qkv.shape[0]
    vector[...] = jnp.zeros_like(vector)
    for l in range(layers):
        for n in range(3):
            row = raise_qkv[l, n]
            for i in range(NARROW):
                raise_out[l, i, :, n * 128 : (n + 1) * 128] = row[:, i * 128 : (i + 1) * 128]
            vector[4 * l : 4 * l + 1, n * width : (n + 1) * width] = qkv_b[n, l : l + 1, :].astype(F32)
        vector[4 * l + 1 : 4 * l + 2, :units] = up_b[l : l + 1, :].astype(F32)
        for n, ref in enumerate((proj_b, down_b, gain1, shift1, gain2, shift2)):
            row, lane = 4 * l + 2 + n // 4, n % 4 * width
            vector[row : row + 1, lane : lane + width] = ref[l : l + 1, :].astype(F32)
    ids_rows[...] = jnp.zeros_like(ids_rows)
    ids_rows[: every.shape[0], : every.shape[1]] = every[...].astype(F32)


def pick(group, adapter_ids, tables, raise_qkv, vectors):
    layers, _, _, rank, dim = raise_qkv.shape
    width, units = vectors[2].shape[1], vectors[1].shape[1]

    def chosen(site, shape):
        rest = (0,) * (len(shape) - 2)
        return pl.BlockSpec(
            (shape[0], None) + shape[2:], lambda i, ids: (0, ids[lax.axis_index("col") // group, site]) + rest
        )

    def whole(shape):
        return pl.BlockSpec(shape, lambda i, ids: (0,) * len(shape))

    shapes = [(table.shape[:1] + table.shape[2:], BF16) for _, table in tables]
    shapes += [((layers, NARROW, rank, 384), BF16), ((4 * layers, 512), F32), ((8, 128), F32)]
    return pl.pallas_call(
        functools.partial(pick_body, width, units),
        grid_spec=pltpu.PrefetchScalarGridSpec(
            num_scalar_prefetch=1,
            grid=(1,),
            in_specs=[chosen(site, table.shape) for site, table in tables]
            + [chosen(0, raise_qkv.shape)]
            + [whole(x.shape) for x in vectors]
            + [whole(adapter_ids.shape)],
            out_specs=[whole(shape) for shape, _ in shapes],
        ),
        out_shape=[shape_of(shape, kind) for shape, kind in shapes],
        compiler_params=PARAMS,
        name="pick",
    )(adapter_ids, *[table for _, table in tables], raise_qkv, *vectors, adapter_ids)


def shards(mesh_shape, *args):
    (
        tokens, cotangent, adapter_ids, qkv_weight, qkv_bias, proj_weight, proj_bias,
        up_weight, up_bias, down_weight, down_bias, first_gain, first_shift, second_gain,
        second_shift, qkv_lower, qkv_raise, proj_lower, proj_raise, up_lower, up_raise,
        down_lower, down_raise,
    ) = args
    n_row, n_col = mesh_shape
    layers, adapters, dim, rank = qkv_lower.shape
    rows, width = tokens.shape
    units = up_weight.shape[2]
    seqs = rows // LEN
    group = n_col // seqs
    held = positions(group)
    per = BLOCKS // group
    mine = per * BLOCK
    merge = 128 // width
    c = lax.axis_index("col")
    g = lax.rem(c, group)
    def turned(table):
        return jnp.swapaxes(table, 2, 3)

    *picked, vector, ids_rows = pick(
        group, adapter_ids,
        [
            (0, turned(qkv_lower)), (1, turned(proj_lower)), (1, proj_raise), (2, turned(up_lower)), (2, up_raise),
            (3, turned(down_lower)), (3, down_raise),
        ],
        qkv_raise.transpose(0, 1, 3, 2, 4),
        (qkv_bias.transpose(1, 0, 2), up_bias, proj_bias, down_bias, first_gain, first_shift, second_gain, second_shift),
    )
    tables = [picked[0], picked[7]] + list(picked[1:7])
    fused = FUSED and width == 128
    if width == 128:
        qkv_shard = qkv_weight.transpose(0, 2, 1, 3)
    else:
        qkv_shard = qkv_weight.reshape(layers, -1, 3 * width)
    outs = gather_inputs(
        n_row, n_col, group, qkv_shard, proj_weight, up_weight,
        down_weight, tokens, cotangent, vector, tables if fused else None
    )
    g_one = g.reshape(1)

    def peer_values(x, step):
        pairs = [(q, q - q % group + (q + step) % group) for q in range(n_col)]
        return lax.ppermute(x, "col", pairs)

    def to_columns(x):
        if merge > 1:
            x = x.reshape(NARROW, mine, merge, width).transpose(0, 2, 1, 3).reshape(n_col, mine, width)
        x = lax.all_to_all(x, "col", split_axis=0, concat_axis=0, tiled=True)
        return to_rows(held, x.reshape(n_col * per, BLOCK, width))

    if not fused:
        x = outs["tokens"].astype(F32)
        kept = {name: [] for name in SAVED + ("reds",)}
        for l in range(layers):
            q, kv, red = qkv_kernel(l, x, outs["vec"], outs["qkv"], tables[0], tables[1])
            kvs = [kv] + [peer_values(kv, s) for s in range(1, group)]
            att, lse = attend_kernel(group, g_one, q, kvs)
            mid, x, active, slope, reds = mlp_kernel(
                l, l == layers - 1, x, att, outs["vec"], outs["proj"], outs["up"], outs["down"], tables[2:]
            )
            reds = jnp.concatenate([red[None], reds])
            peer = jnp.stack(kvs[1:]) if group > 1 else kv[None][:0]
            for name, value in zip(SAVED + ("reds",), (q, kv, peer, att, lse, mid, active, slope, x, reds)):
                kept[name].append(value)
        for name in SAVED:
            outs["saved_" + name] = jnp.stack(kept[name][: layers - 1] if name == "x" else kept[name])
        outs["reds"] = jnp.stack(kept["reds"])
        outs["result"] = x
    if fused:
        made = backward(n_row, n_col, group, outs, tables, ids_rows)
        sizes = {"qkv": (128, 384), "mlp": (128, 128, 128, units, units, 128)}
        sums = place(made, sizes, adapters)
        final = list(sums[:2])
        for number, p in enumerate(sums[2:]):
            if number == 1:
                p = p.transpose(0, 1, 3, 2, 4)
            elif number % 2 == 0:
                p = p.transpose(0, 1, 3, 2)
            final.append(p)
        return tuple(final)

    result = to_columns(outs["result"])

    onehot = (adapter_ids.T[:, :, None] == jnp.arange(adapters)[None, None, :]).astype(BF16)

    def all_rows(x):
        pairs = [[(q, (q + s) % n_row) for q in range(n_row)] for s in range(1, n_row)]
        return [x] + [lax.ppermute(x, "row", pair) for pair in pairs]

    onehots = jnp.concatenate(all_rows(onehot), axis=1)

    def collect(parts, named):
        if merge > 1:
            pieces, at = [], 0
            for _, size in named:
                piece = parts[:, :, at : at + size]
                at += size
                if size == 384:
                    piece = piece.reshape(NARROW, rank, 3, merge, width).transpose(0, 3, 1, 2, 4)
                else:
                    piece = piece.reshape(NARROW, rank, merge, size // merge).transpose(0, 2, 1, 3)
                pieces.append(piece.reshape(n_col, rank, size // merge))
            parts = jnp.concatenate(pieces, axis=2)
        parts = lax.all_to_all(parts, "col", split_axis=0, concat_axis=0, tiled=True)
        parts = parts.reshape((seqs, group) + parts.shape[1:]).astype(F32).sum(axis=1).astype(BF16)
        parts = jnp.concatenate(all_rows(parts), axis=0)
        sums, at = [], 0
        for site, size in named:
            piece = parts[:, :, at : at + size // merge]
            at += size // merge
            sums.append(jnp.einsum("sa,srn->arn", onehots[site], piece, preferred_element_type=F32))
        return sums

    wide = outs["down"].shape[1] // NARROW
    grads, carried = [None] * layers, None
    for l in reversed(range(layers + 1)):
        lq, lm = (l if l < layers else None), (l - 1 if l > 0 else None)
        made = back_kernel(lq, lm, group, g_one, outs, tables, carried)
        if lm is not None:
            grads[lm] = collect(made["grads_mlp"], [(1, 128), (1, 128), (2, 128), (2, wide), (3, wide), (3, 128)])
            parts = [made["out_part%d" % s] for s in range(group)]
            parts = [parts[0]] + [peer_values(parts[s], group - s) for s in range(1, group)]
            carried = (made["out_g_mid"], made["out_gq"], parts)
        if lq is not None:
            grads[lq] = collect(made["grads_qkv"], [(0, 128), (0, 384)]) + grads[lq]
    grad = made["out"]
    input_grad = to_columns(grad)

    final = []
    for number in range(8):
        p = jnp.stack([grads[l][number] for l in range(layers)])
        if number == 1:
            p = p.reshape(layers, adapters, rank, 3, width)
        elif number % 2 == 0:
            p = p.transpose(0, 1, 3, 2)
        final.append(p)
    return (result, input_grad) + tuple(final)


def solution(mesh):
    mesh_shape = (mesh.shape["row"], mesh.shape["col"])
    return jax.shard_map(
        functools.partial(shards, mesh_shape),
        mesh=mesh,
        in_specs=(
            P("row", "col"), P("row", "col"), P("row", None),
            P(None, "row", None, "col"), P(None, None, "col"),
            P(None, "col", "row"), P(None, "col"),
            P(None, "row", "col"), P(None, "col"),
            P(None, "col", "row"), P(None, "col"),
            P(None, "col"), P(None, "col"), P(None, "col"), P(None, "col"),
            P(), P(), P(), P(), P(), P(), P(), P(),
        ),
        out_specs=(
            P("row", "col"), P("row", "col"),
            P(None, None, "col", None), P(None, None, None, None, "col"),
            P(None, None, "col", None), P(None, None, None, "col"),
            P(None, None, "col", None), P(None, None, None, "col"),
            P(None, None, "col", None), P(None, None, None, "col"),
        ),
        check_vma=False,
    )
```

```python
import functools
import math

import jax
import jax.numpy as jnp
from jax import lax
from jax.experimental import pallas as pl
from jax.experimental.pallas import tpu as pltpu
from jax.sharding import PartitionSpec as P

HD = 64
LEN = 1024
BLOCK = 256
BLOCKS = LEN // BLOCK
EPSILON = 1e-05
SCALE = HD**-0.5
ROOT = (2.0 / 3.141592653589793) ** 0.5
MESH = pl.DeviceIdType.MESH
F32 = jnp.float32
BF16 = jnp.bfloat16


ROW_FIRST = (("z", 0, 1), ("z", 1, 0))
ROW_SECOND = ((0, "z", 1), (1, "z", 0))
ORDERS = (
    {"qkv": (ROW_FIRST,), "proj": (ROW_SECOND,), "up": (ROW_FIRST,) * 2, "down": (ROW_FIRST, ROW_SECOND)},
    {"qkv": (ROW_SECOND,), "proj": (ROW_FIRST,), "up": (ROW_SECOND,) * 2, "down": (ROW_SECOND,) * 2},
)
CUTS = {kind: 2 * len(pairs) for kind, pairs in ORDERS[0].items()}
KINDS = ("qkv", "proj", "up", "down")
DEPTH = 4
FUSED = True
LINK = 90e3
DELAY, ROW_DELAY = 2.0, 4.0
FIRST = 12.0


def transfer_plan(order, n_row):
    masks, rows, steps = [0], False, []
    for d in order:
        if d == "z":
            steps += [(("z", hop), tuple(masks), rows) for hop in range(1, n_row)]
            rows = True
        else:
            steps.append((d, tuple(masks), rows))
            masks = masks + [m ^ d for m in masks]
    steps.append((None, tuple(masks), rows))
    return steps


def transfer_schedule(pieces, n_row, tasks):
    cost, parts = {}, {}
    for k, (name, order, size) in enumerate(pieces):
        parts.setdefault(name, set()).add(k)
        for p, (d, masks, rows) in enumerate(transfer_plan(order, n_row)[:-1]):
            axis = "z" if isinstance(d, tuple) else d
            cost[k, p] = (axis, 2 * len(masks) * (n_row if rows else 1) * size / LINK)
    ready = {d: [] for d, _ in cost.values()}
    free = {d: 0.0 if d == "z" else FIRST for d in ready}
    flight = {d: [] for d in ready}
    for k in range(len(pieces)):
        ready[cost[k, 0][0]].append((k, 0))
    tasks, left = list(tasks), {}
    for task in tasks:
        left[task[4]] = left.get(task[4], 0) + 1
    landed, staged, now, ops = {}, {}, 0.0, []

    def stage(name):
        kind, l = name
        if name in landed and name not in staged and landed[name] <= now and not left.get((kind, l - 1)):
            staged[name] = now + 3.0
            ops.append(("stage", kind, l))

    while tasks or any(ready.values()) or any(flight.values()):
        for d in ready:
            while ready[d] and len(flight[d]) < DEPTH:
                k, p = ready[d].pop(0)
                free[d] = max(now, free[d]) + cost[k, p][1]
                flight[d].append((free[d] + (ROW_DELAY if d == "z" else DELAY), k, p))
                ops.append(("start", k, p))
        if tasks:
            for name in list(landed):
                stage(name)
        events = [f for line in flight.values() for f in line]
        event = min(events) if events else None
        due = None
        if tasks:
            need = tasks[0][4]
            due = now if need is None else staged.get(need)
            if due is None and need in landed and not left.get((need[0], need[1] - 1)):
                due = landed[need]
        if due is not None and (event is None or max(due, now) < event[0]):
            now = max(due, now)
            need = tasks[0][4]
            if need is not None and need not in staged:
                continue
            name, l, part, micros, _ = tasks.pop(0)
            left[need] -= 1
            now += micros
            ops.append(("task", name, (l, part)))
            continue
        now, k, p = max(now, event[0]), event[1], event[2]
        d = cost[k, p][0]
        flight[d].remove(event)
        ops.append(("wait", k, p))
        if (k, p + 1) in cost:
            later = ready[cost[k, p + 1][0]]
            later.append((k, p + 1))
            later.sort()
        else:
            name = pieces[k][0]
            parts[name].discard(k)
            if not parts[name]:
                landed[name] = now + 4.0
    return ops


def place_of(group, g, b):
    if group == 2:
        return g + b * (BLOCKS - 1 - 2 * g)
    return g * (BLOCKS // group) + b


def positions(group):
    per = BLOCKS // group
    return tuple(tuple(place_of(group, g, b) for b in range(per)) for g in range(group))


NARROW = 8
CROSS = ((0,), (0,))
TURNED = ((1,), (1,))


def dot(a, b, dims=((1,), (0,))):
    return lax.dot_general(a, b, (dims, ((), ())), preferred_element_type=F32)


def columns(i, size=128):
    if isinstance(i, int):
        return pl.ds(i * size, size)
    return pl.ds(pl.multiple_of(i * size, size), size)


def norm_parts(x):
    center = x - jnp.mean(x, axis=1, keepdims=True)
    inverse = lax.rsqrt(jnp.mean(center * center, axis=1, keepdims=True) + EPSILON)
    return center * inverse, inverse


def norm_grad(grad, scaled, inverse, gain):
    w = grad * gain
    first = jnp.mean(w, axis=1, keepdims=True)
    second = jnp.mean(w * scaled, axis=1, keepdims=True)
    return inverse * (w - first - scaled * second)


def norm_low(x, gain, shift):
    return (norm_parts(x)[0] * gain + shift).astype(BF16)


def pair_state(held):
    group, per = len(held), len(held[0])
    state = {}
    for s in range(per):
        for j in range(group):
            for b in range(per):
                seen = {held[(g - j) % group][b] <= held[g][s] for g in range(group)}
                state[s, j, b] = 0 if len(seen) == 2 else (1 if True in seen else -1)
    return state


def pair_bias(held, g):
    group = len(held)
    bias = {}
    for (s, j, b), state in pair_state(held).items():
        if state == 0:
            keys = place_of(group, lax.rem(g - j + group, group), b)
            bias[s, j, b] = jnp.where(keys <= place_of(group, g, s), 0.0, -1e9).astype(F32)
    return bias


def head_mask(h):
    lane = lax.broadcasted_iota(jnp.int32, (1, 128), 1)
    return (lane // HD) == h


def turning_pair(held, g):
    if len(held) != 2:
        return None, [0.0] * len(held[0])
    at = 1 - g
    return at, [jnp.where(at == n, 1.0, 0.0).astype(F32) for n in range(len(held[0]))]


def both_heads(x):
    return jnp.concatenate([jnp.where(head_mask(h), x, 0).astype(BF16) for h in range(2)], axis=0)


def slots_of(held, j, b, fixed):
    state = pair_state(held)
    return [s for s in range(len(held[0])) if state[s, j, b] > 0 or (state[s, j, b] == 0 and not fixed)]


def attend_strip(held, bias, g, i, q, kvs, out, lse):
    group, per = len(held), len(held[0])
    at, here = turning_pair(held, g)
    wide = 2 * BLOCK
    blocks = [(j, b, slots_of(held, j, b, at is not None)) for j in range(group) for b in range(per)]
    queries = [both_heads(q[i, s * BLOCK : (s + 1) * BLOCK, :] * SCALE) for s in range(per)]
    scores = {s: [] for s in range(per)}
    for j, b, slots in blocks:
        if slots:
            keys = kvs[j][i, b * BLOCK : (b + 1) * BLOCK, :128]
            score = dot(keys, jnp.concatenate([queries[s] for s in slots], axis=0), TURNED)
            for n, s in enumerate(slots):
                part = score[:, n * wide : (n + 1) * wide]
                scores[s].append(((j, b), part + bias[s, j, b] if (s, j, b) in bias and at is None else part))
    turned = {(j, b): kvs[j][i, b * BLOCK : (b + 1) * BLOCK, 128:].T for j, b, slots in blocks if slots}

    def weigh(e, values):
        e = e.astype(BF16)
        return jnp.concatenate(
            [dot(values[h * HD : (h + 1) * HD], e[:, h * BLOCK : (h + 1) * BLOCK]) for h in range(2)], axis=1
        )

    extra = None
    if at is not None:
        moving = pl.ds(pl.multiple_of(at * BLOCK, BLOCK), BLOCK)
        score = dot(kvs[1][i, moving, :128], both_heads(q[i, moving, :] * SCALE), TURNED)
        top = jnp.max(score, axis=0, keepdims=True)
        e = jnp.exp(score - top)
        extra = (top, jnp.sum(e, axis=0, keepdims=True), weigh(e, kvs[1][i, moving, 128:].T))
    for s in range(per):
        tops = [jnp.max(x, axis=0, keepdims=True) for _, x in scores[s]]
        if extra:
            tops.append(extra[0] + (here[s] - 1.0) * 1e9)
        top = functools.reduce(jnp.maximum, tops)
        total, made = 0.0, 0.0
        for place, score in scores[s]:
            e = jnp.exp(score - top)
            total = total + jnp.sum(e, axis=0, keepdims=True)
            made = made + weigh(e, turned[place])
        if extra:
            weight = jnp.exp(tops[-1] - top) * here[s]
            total = total + weight * extra[1]
            made = made + weight * extra[2]
        made = made / total
        level = top + jnp.log(total)
        rows = pl.ds(s * BLOCK, BLOCK)
        for h in range(2):
            lse[i, h : h + 1, rows] = level[:, h * BLOCK : (h + 1) * BLOCK]
        both = jnp.concatenate([made[:, :BLOCK], made[:, BLOCK:]], axis=0)
        out[rows, columns(i)] = both.T.astype(BF16)


def attend_back_strip(held, bias, g, i, q, lse, out, grad, kvs, gq, gkvs):
    group, per = len(held), len(held[0])
    at, here = turning_pair(held, g)

    def slot(rows):
        up = grad[rows, columns(i)]
        product = (up.astype(F32) * out[rows, columns(i)].astype(F32)).T
        inner = [jnp.sum(product[h * HD : (h + 1) * HD], axis=0, keepdims=True) for h in range(2)]
        level = [lse[i, h : h + 1, rows] for h in range(2)]
        return [
            both_heads(q[i, rows, :] * SCALE), both_heads(up),
            jnp.concatenate(inner, axis=1), jnp.concatenate(level, axis=1),
        ]

    def block(parts, keys, values):
        query, given = [jnp.concatenate([part[n] for part in parts], axis=0) for n in (0, 1)]
        inner, level = [jnp.concatenate([part[n] for part in parts], axis=1) for n in (2, 3)]
        probs = jnp.exp(dot(keys, query, TURNED) - level)
        g_scores = (probs * (dot(values, given, TURNED) - inner)).astype(BF16)
        turned = keys.T
        made = []
        for n in range(len(parts)):
            pieces = []
            for h in range(2):
                first = (2 * n + h) * BLOCK
                pieces.append(dot(turned[h * HD : (h + 1) * HD], g_scores[:, first : first + BLOCK]))
            made.append(jnp.concatenate(pieces, axis=0))
        return made, dot(g_scores, query), dot(probs.astype(BF16), given)

    slots = [slot(pl.ds(s * BLOCK, BLOCK)) for s in range(per)]
    total = [0.0] * per
    moved = None
    if at is not None:
        moving = pl.ds(pl.multiple_of(at * BLOCK, BLOCK), BLOCK)
        moved = block([slot(moving)], kvs[1][i, moving, :128], kvs[1][i, moving, 128:])
        total = [here[s] * moved[0][0] for s in range(per)]
    for j in range(group):
        for b in range(per):
            rows = pl.ds(b * BLOCK, BLOCK)
            k, v = 0.0, 0.0
            wanted = slots_of(held, j, b, at is not None)
            if wanted:
                parts = []
                for s in wanted:
                    part = list(slots[s])
                    if at is None and (s, j, b) in bias:
                        part[3] = part[3] - bias[s, j, b]
                    parts.append(part)
                made, k, v = block(parts, kvs[j][i, rows, :128], kvs[j][i, rows, 128:])
                for n, s in enumerate(wanted):
                    total[s] = total[s] + made[n]
            if at is not None and j == 1:
                k, v = k + here[b] * moved[1], v + here[b] * moved[2]
            gkvs[j][i, rows, :128] = k.astype(BF16)
            gkvs[j][i, rows, 128:] = v.astype(BF16)
    for s in range(per):
        gq[i, pl.ds(s * BLOCK, BLOCK), :] = (total[s] * SCALE).T.astype(BF16)


def by_rows(count, body, size=128):
    each(count // size, lambda n: body(pl.ds(pl.multiple_of(n * size, size), size)))


def keep(value, red, red_out):
    red[...] = value.astype(BF16)
    red_out[...] = value.T.astype(BF16)


def each(count, body):
    def step(i, carry):
        body(i)
        return carry

    lax.fori_loop(0, count, step, 0)


def qkv_stage(x, gain, shift, w, bias, low, up, q, kv, red, red_out, normed):
    def norm(rows):
        normed[rows, :] = norm_low(x[rows, :], gain, shift)

    by_rows(x.shape[0], norm)
    keep(dot(normed[...], low[...], TURNED), red, red_out)

    def pair(j):
        made = dot(normed[...], w[j])
        for n in range(2):
            i = 2 * j + n
            mixed = made[:, n * 384 : (n + 1) * 384] + (bias[i] + dot(red[...], up[i]))
            q[i] = mixed[:, :128].astype(BF16)
            kv[i] = mixed[:, 128:].astype(BF16)

    each(NARROW // 2, pair)


def proj_stage(x, att, w, bias, low, up, gain, shift, low_up, mid, normed, red, red_out, red_up, red_up_out):
    keep(dot(att[...], low[...], TURNED), red, red_out)

    def part(rows):
        value = x[rows, :] + (dot(att[rows, :], w[...]) + bias + dot(red[rows, :], up[...]))
        mid[rows, :] = value
        normed[rows, :] = norm_low(value, gain, shift)

    by_rows(x.shape[0], part, 256)
    keep(dot(normed[...], low_up[...], TURNED), red_up, red_up_out)


def up_strip(i, normed, w, bias, red_up, up, active, slope):
    units = w.shape[2]
    cols = columns(i, units)
    value = dot(normed[...], w[i]) + (bias[i] + dot(red_up[...], up[:, cols]))
    made, made_slope = gelu_parts(value)
    active[:, cols] = made.astype(BF16)
    slope[:, cols] = made_slope.astype(BF16)


def down_stage(mid, active, w, bias, up, red, put):
    for n in range(mid.shape[1] // 256):
        cols = slice(n * 256, (n + 1) * 256)
        put(n, mid[:, cols] + (dot(active[...], w[:, cols]) + bias[:, cols] + dot(red[...], up[:, cols])))


def gelu_parts(x):
    square = x * x
    t = jnp.tanh(ROOT * (x + 0.044715 * (x * square)))
    half = 0.5 * (1.0 + t)
    slope = half + 0.5 * x * (1.0 - t * t) * (ROOT * (1.0 + 3 * 0.044715 * square))
    return x * half, slope


class Vectors:
    def __init__(self, ref, l):
        self.ref, self.l = ref, l

    def qkv(self, i):
        return self.ref[i, pl.ds(4 * self.l, 1), :384]

    def up(self, i):
        return self.ref[i, pl.ds(4 * self.l + 1, 1), :]

    def row(self, name):
        at = ("proj", "down", "gain1", "shift1", "gain2", "shift2").index(name)
        row, lane = 4 * self.l + 2 + at // 4, at % 4 * 128
        return jnp.concatenate([self.ref[i, row : row + 1, lane : lane + 128] for i in range(NARROW)], axis=1)


class Strips:
    def __init__(self, read):
        self.read = read

    def __getitem__(self, i):
        return self.read(i)


TABLES = ("low_qkv", "up_qkv", "low_proj", "up_proj", "low_up", "up_up", "low_down", "up_down")
SAVED = ("q", "kv", "peer", "att", "lse", "mid", "active", "slope", "x")


def task_list(layers):
    tasks = [("load", 0, 0, 3.0, None)]
    for l in range(layers):
        tasks.append(("qkv", l, 0, 7.0, ("qkv", l)))
        tasks += [("attend", l, n, 5.5, None) for n in range(2)]
        tasks.append(("proj", l, 0, 4.0, ("proj", l)))
        tasks += [("up", l, n, 6.0, ("up", l)) for n in range(2)]
        tasks.append(("down", l, 0, 5.0, ("down", l)))
    return tasks


class ForwardWork:
    def __init__(self, n_col, group, refs):
        self.__dict__.update(refs)
        self.group = group
        self.held = positions(group)
        self.r, self.c = lax.axis_index("row"), lax.axis_index("col")
        self.g = lax.rem(self.c, group)
        self.bias = pair_bias(self.held, self.g)
        self.layers = self.low_qkv.shape[0]

    def stage_copies(self, kind, l):
        full = self.full[kind]
        if kind == "qkv":
            pieces = []
            for i in range(NARROW):
                src = full.at[l, i]
                pieces.append((src, self.wq.at[i // 2, :, :, :, pl.ds(i % 2 * 384, 384)]))
            return pieces, self.wq
        if kind == "up":
            return [(full.at[l, i], self.wu.at[i]) for i in range(NARROW)], self.wu
        target = self.wp if kind == "proj" else self.wd
        return [(full.at[l, i], target.at[i]) for i in range(NARROW)], target

    def stage(self, kind, l):
        for src, dst in self.stage_copies(kind, l)[0]:
            pltpu.make_async_copy(src, dst, self.stage_sem.at[KINDS.index(kind)]).start()

    def staged(self, kind, l):
        target = self.stage_copies(kind, l)[1]
        pltpu.make_async_copy(target, target, self.stage_sem.at[KINDS.index(kind)]).wait()

    def save_copy(self, name, l):
        src = {
            "q": self.q, "kv": self.kv, "peer": self.peer.at[l], "att": self.att, "lse": self.lse,
            "mid": self.mid, "active": self.active, "slope": self.slope, "x": self.x,
        }[name]
        return pltpu.make_async_copy(src, self.saved[name].at[l], self.save_sem.at[l, SAVED.index(name)])

    def save(self, *names, l):
        for name in names:
            self.save_copy(name, l).start()

    def settled(self, *names, l):
        if l >= 0:
            for name in names:
                self.save_copy(name, l).wait()

    def result_copy(self, n):
        pair = pl.ds(2 * n, 2)
        return pltpu.make_async_copy(self.result.at[pair], self.out_result.at[pair], self.result_sem.at[n])

    def exchange(self, l, s):
        to = self.c - self.g + lax.rem(self.g + s, self.group)
        return pltpu.make_async_remote_copy(
            src_ref=self.kv, dst_ref=self.peer.at[l, s - 1],
            send_sem=self.kv_send.at[l, s - 1], recv_sem=self.kv_recv.at[l, s - 1],
            device_id=(self.r, to), device_id_type=MESH,
        )

    def run(self, name, l, part):
        vec = Vectors(self.vec, l)
        if name == "load":
            self.arrive_tokens()
            self.x[...] = self.tokens_v[...].astype(F32)
        elif name == "qkv":
            self.staged("qkv", l)
            self.settled("q", "kv", l=l - 1)
            if l > 0:
                for s in range(1, self.group):
                    self.exchange(l - 1, s).wait_send()
            w = self.wq.reshape(NARROW // 2, -1, 768)
            qkv_stage(
                self.x, vec.row("gain1"), vec.row("shift1"), w, Strips(vec.qkv), self.low_qkv.at[l],
                self.up_qkv.at[l], self.q, self.kv, self.red, self.reds.at[l, 0], self.normed,
            )
            for s in range(1, self.group):
                self.exchange(l, s).start()
            self.save("q", "kv", l=l)
        elif name == "attend":
            if part == 0:
                for s in range(1, self.group):
                    self.exchange(l, s).wait_recv()
                self.save("peer", l=l)
                self.settled("att", "lse", l=l - 1)
            kvs = [self.kv] + [self.peer.at[l, s - 1] for s in range(1, self.group)]
            size = NARROW // 2
            each(size, lambda n: attend_strip(self.held, self.bias, self.g, part * size + n, self.q, kvs, self.att, self.lse))
            if part == 1:
                self.save("att", "lse", l=l)
        elif name == "proj":
            self.staged("proj", l)
            self.settled("mid", l=l - 1)
            dim = self.att.shape[1]
            proj_stage(
                self.x, self.att, self.wp.reshape(dim, dim), vec.row("proj"), self.low_proj.at[l],
                self.up_proj.at[l], vec.row("gain2"), vec.row("shift2"), self.low_up.at[l],
                self.mid, self.normed, self.red, self.reds.at[l, 1], self.red_up, self.reds.at[l, 2],
            )
            self.save("mid", l=l)
        elif name == "up":
            if part == 0:
                self.staged("up", l)
                self.settled("active", "slope", l=l - 1)
            w = self.wu.reshape(NARROW, self.x.shape[1], -1)
            size = NARROW // 2
            each(size, lambda n: up_strip(
                part * size + n, self.normed, w, Strips(vec.up), self.red_up, self.up_up.at[l],
                self.active, self.slope,
            ))
            if part == 1:
                self.save("active", "slope", l=l)
                keep(dot(self.active[...], self.low_down[l], TURNED), self.red, self.reds.at[l, 3])
        elif name == "down":
            self.staged("down", l)
            self.settled("x", l=l - 1)
            dim = self.x.shape[1]

            def put(n, value):
                if l < self.layers - 1:
                    self.x[:, columns(n, 256)] = value
                else:
                    for m in range(2):
                        self.result[2 * n + m] = value[:, m * 128 : (m + 1) * 128].astype(BF16)
                    self.result_copy(n).start()

            down_stage(
                self.mid, self.active, self.wd.reshape(-1, dim), vec.row("down"), self.up_down.at[l], self.red, put,
            )
            if l < self.layers - 1:
                self.save("x", l=l)

    def close(self):
        last = self.layers - 1
        self.settled(*[name for name in SAVED if name not in ("x", "peer")], l=last)
        for l in range(self.layers):
            self.settled("peer", l=l)
        for s in range(1, self.group):
            self.exchange(last, s).wait_send()
        for n in range(NARROW // 2):
            self.result_copy(n).wait()


def gather_body(n_row, n_col, layers, group, names, *refs):
    refs = dict(zip(names, refs))
    shard = {kind: refs["shard_" + kind] for kind in KINDS}
    full = {kind: refs["full_" + kind] for kind in KINDS}
    tokens, cotangent, vector = refs["tokens"], refs["cotangent"], refs["vector"]
    own_tokens, own_cotangent, vectors = refs["own_tokens"], refs["own_cotangent"], refs["vectors"]
    local_sem, send_sem, recv_sem = refs["local_sem"], refs["send_sem"], refs["recv_sem"]
    near_sem, out_sem, in_sem = refs["near_sem"], refs["out_sem"], refs["in_sem"]
    r = lax.axis_index("row")
    c = lax.axis_index("col")
    link_bits = [b for b in (2**k for k in range(1, 8)) if b < n_col]
    depth = shard["up"].shape[1]

    def row_peer(s):
        return (lax.rem(r + s, n_row), c)

    def col_peer(bit):
        return (r, c ^ bit)

    peers = [row_peer(s) for s in range(1, n_row)]
    peers += [(r, lax.rem(c + d, n_col)) for d in range(1, n_col)]
    barrier = pltpu.get_barrier_semaphore()
    for peer in peers:
        pl.semaphore_signal(barrier, inc=1, device_id=peer, device_id_type=MESH)
    pl.semaphore_wait(barrier, len(peers))

    per, width = BLOCKS // group, tokens.shape[1]

    def own_place(ref, b, col):
        if len(ref.shape) == 2:
            start = pl.multiple_of(col * width, width)
            return ref.at[pl.ds(b * BLOCK, BLOCK), pl.ds(start, width)]
        return ref.at[col, pl.ds(b * BLOCK, BLOCK)]

    def from_place(ref, b, col):
        start = (col // group) * LEN + place_of(group, lax.rem(col, group), b) * BLOCK
        return ref.at[pl.ds(pl.multiple_of(start, BLOCK), BLOCK)]

    exchanged = ((tokens, own_tokens), (cotangent, own_cotangent))

    def near(n, b):
        src, dst = exchanged[n]
        return pltpu.make_async_copy(from_place(src, b, c), own_place(dst, b, c), near_sem.at[n * per + b])

    def near_vector():
        return pltpu.make_async_copy(vector, vectors.at[c], near_sem.at[2 * per])

    def far(src, dst, n, peer):
        return pltpu.make_async_remote_copy(
            src_ref=src, dst_ref=dst, send_sem=out_sem.at[n], recv_sem=in_sem.at[n],
            device_id=peer, device_id_type=MESH,
        )

    def start_exchange(n):
        src, dst = exchanged[n]
        for b in range(per):
            near(n, b).start()
        for d in range(1, n_col):
            to = lax.rem(c + d, n_col)
            for b in range(per):
                far(from_place(src, b, to), own_place(dst, b, c), n, (r, to)).start()

    def wait_exchange(n):
        _, dst = exchanged[n]
        for b in range(per):
            near(n, b).wait()
        if len(dst.shape) == 2:
            ref = dst.at[:, pl.ds(0, (n_col - 1) * width)]
        else:
            ref = dst.at[pl.ds(0, n_col - 1)]
        far(ref, ref, n, col_peer(1)).wait()

    def own(kind, l, h, dst):
        ref = shard[kind]
        size = ref.shape[-2] // CUTS[kind]
        if len(ref.shape) == 3:
            return [(ref.at[l, pl.ds(h * size, size)], dst)]
        return [
            (ref.at[l, n, pl.ds(h * size, size)], dst.at[:, pl.ds(n * ref.shape[3], ref.shape[3])])
            for n in range(ref.shape[1])
        ]

    def block(kind, l, h, row, col):
        if kind in ("qkv", "up"):
            return full[kind].at[l, col, row, h]
        start = pl.multiple_of(row * depth, depth)
        return full[kind].at[l, col, h, :, pl.ds(start, depth)]

    def strip(kind, l, h, col):
        if kind in ("qkv", "up"):
            return full[kind].at[l, col, :, h]
        return full[kind].at[l, col, h]

    def amount(kind, l, h, strips, rows):
        if kind in ("qkv", "up"):
            return full[kind].at[l, pl.ds(0, strips), pl.ds(0, rows), h]
        return full[kind].at[l, pl.ds(0, strips), h, :, pl.ds(0, rows * depth)]

    chunks = []
    for l in range(layers):
        for kind in KINDS:
            for h in range(CUTS[kind]):
                order = []
                for d in ORDERS[l % len(ORDERS)][kind][h // 2][h % 2]:
                    if d == "z":
                        order.append("z")
                    elif d < len(link_bits):
                        order.append(link_bits[d])
                order += link_bits[2:]
                chunks.append((kind, l, h, tuple(order)))
    phases = len(link_bits) + n_row - 1

    def remote(src, dst, k, p, peer, way=0):
        at = (k * (phases + 1) + p) * 2 + way
        return pltpu.make_async_remote_copy(
            src_ref=src, dst_ref=dst, send_sem=send_sem.at[at], recv_sem=recv_sem.at[at],
            device_id=peer, device_id_type=MESH,
        )

    def plan(k):
        return transfer_plan(chunks[k][3], n_row)

    def ways(hop):
        return (
            (r - hop + 1, (r - hop + 1 >= 0) & (r + 1 < n_row), r - hop >= 0, 1),
            (r + hop - 1, (r + hop - 1 < n_row) & (r >= 1), r + hop < n_row, n_row - 1),
        )

    def local_start(k):
        kind, l, h, _ = chunks[k]
        for src, dst in own(kind, l, h, block(kind, l, h, r, c)):
            pltpu.make_async_copy(src, dst, local_sem.at[k]).start()

    def local_wait(k):
        kind, l, h, _ = chunks[k]
        ref = block(kind, l, h, r, c)
        pltpu.make_async_copy(ref, ref, local_sem.at[k]).wait()

    def issue(k, p):
        kind, l, h, order = chunks[k]
        d, masks, rows = plan(k)[p]

        def send(m, row, first, peer, way):
            dst = block(kind, l, h, row, c ^ m)
            for src, to in own(kind, l, h, dst) if m == 0 and first else [(dst, dst)]:
                remote(src, to, k, p, peer, way).start()

        if isinstance(d, tuple):
            for way, (row, goes, _, step) in enumerate(ways(d[1])):

                @pl.when(goes)
                def _():
                    for m in masks:
                        send(m, row, d[1] == 1, row_peer(step), way)

            return
        for m in masks:
            if rows:
                ref = strip(kind, l, h, c ^ m)
                remote(ref, ref, k, p, col_peer(d)).start()
            else:
                send(m, r, True, col_peer(d), 0)

    def moved(k, p, send):
        kind, l, h, order = chunks[k]
        d, masks, rows = plan(k)[p]
        ref = amount(kind, l, h, len(masks), n_row if rows else 1)
        if not isinstance(d, tuple):
            copy = remote(ref, ref, k, p, col_peer(1))
            copy.wait_send() if send else copy.wait_recv()
            return
        for way, (_, goes, comes, step) in enumerate(ways(d[1])):

            @pl.when(goes if send else comes)
            def _():
                copy = remote(ref, ref, k, p, row_peer(step), way)
                copy.wait_send() if send else copy.wait_recv()

    def share(k, p):
        kind, l, h, order = chunks[k]
        (d, masks, _), (_, later, rows) = plan(k)[p : p + 2]
        if not rows:
            return
        fresh = masks if isinstance(d, tuple) else later[len(masks):]
        for m in fresh:
            ref = strip(kind, l, h, c ^ m)
            remote(ref, ref, k, phases, col_peer(1)).start()

    def shared(k):
        kind, l, h, _ = chunks[k]
        ref = amount(kind, l, h, n_col // 2, n_row)
        return remote(ref, ref, k, phases, col_peer(1))

    def finish(k, p):
        moved(k, p, False)
        if plan(k)[p][0] == ("z", n_row - 1):
            local_wait(k)
        share(k, p)

    count = len(chunks)
    near_vector().start()
    for d in range(1, n_col):
        far(vector, vectors.at[c], 2, (r, lax.rem(c + d, n_col))).start()
    start_exchange(0)
    for k in range(count):
        local_start(k)
    def vectors_arrive():
        near_vector().wait()
        rest = vectors.at[pl.ds(0, n_col - 1)]
        far(rest, rest, 2, col_peer(1)).wait()

    work = None
    if "x" in refs:
        refs.update(full=full, saved={name: refs["saved_" + name] for name in SAVED})

        loads = [(refs["in_" + name], refs[name]) for name in TABLES]
        loads += [(own_tokens, refs["tokens_v"]), (vectors, refs["vec"])]
        loads = [pltpu.make_async_copy(s, d, refs["load_sem"].at[n]) for n, (s, d) in enumerate(loads)]
        for copy in loads[: len(TABLES)]:
            copy.start()

        def arrive_tokens():
            vectors_arrive()
            wait_exchange(0)
            for copy in loads[len(TABLES) :]:
                copy.start()
            for copy in loads:
                copy.wait()

        refs.update(arrive_tokens=arrive_tokens)
        work = ForwardWork(n_col, group, refs)

    pieces = []
    for kind, l, h, order in chunks:
        size = 2 * math.prod(shard[kind].shape[1:]) // CUTS[kind]
        pieces.append(((kind, l), order, size))
    ops = transfer_schedule(pieces, n_row, task_list(layers) if work else [])
    quiet = max(n for n, (op, _, _) in enumerate(ops) if op == "wait")
    for n, (op, k, p) in enumerate(ops):
        if op == "start":
            issue(k, p)
        elif op == "wait":
            finish(k, p)
        elif op == "stage":
            for at, (kind, l, _, _) in enumerate(chunks):
                if (kind, l) == (k, p):
                    shared(at).wait_recv()
            work.stage(k, p)
        else:
            work.run(k, *p)
        if n == quiet:
            start_exchange(1)
    for k in range(count):
        for p in range(phases):
            moved(k, p, True)
        shared(k).wait_send()
        if not work:
            shared(k).wait_recv()
    if work:
        work.close()
    else:
        vectors_arrive()
        wait_exchange(0)
    wait_exchange(1)


def gather_inputs(n_row, n_col, group, qkv, proj, up, down, tokens, cotangent, vector, tables=None):
    layers, depth = up.shape[0], up.shape[1]
    width, units = proj.shape[1], down.shape[1]
    dim, hidden = depth * n_row, units * n_col
    mine = LEN // group
    cuts = [CUTS[kind] for kind in KINDS]
    own = (mine, dim) if width % 128 == 0 else (n_col, mine, width)
    hbm = pl.BlockSpec(memory_space=pltpu.HBM)
    vmem = pl.BlockSpec(memory_space=pltpu.VMEM)
    dma = pltpu.SemaphoreType.DMA
    count = layers * sum(cuts)
    phases = n_col.bit_length() + n_row - 2
    inputs = [("shard_" + kind, array, hbm) for kind, array in zip(KINDS, (qkv, proj, up, down))]
    inputs += [("tokens", tokens, hbm), ("cotangent", cotangent, hbm), ("vector", vector, hbm)]
    outputs = [
        ("full_qkv", (layers, n_col, n_row, cuts[0], depth // cuts[0], 3 * width), BF16, hbm),
        ("full_proj", (layers, n_col, cuts[1], width // cuts[1], dim), BF16, hbm),
        ("full_up", (layers, n_col, n_row, cuts[2], depth // cuts[2], units), BF16, hbm),
        ("full_down", (layers, n_col, cuts[3], units // cuts[3], dim), BF16, hbm),
        ("own_tokens", own, BF16, hbm),
        ("own_cotangent", own, BF16, hbm),
        ("vectors", (n_col,) + vector.shape, F32, hbm),
    ]
    scratch = [
        ("local_sem", dma((count,))),
        ("send_sem", dma((count * phases * 2,))),
        ("recv_sem", dma((count * phases * 2,))),
        ("near_sem", dma((2 * (BLOCKS // group) + 1,))),
        ("out_sem", dma((3,))),
        ("in_sem", dma((3,))),
    ]
    if tables is not None:
        rank = tables[0].shape[1]
        inputs += [("in_" + name, table, hbm) for name, table in zip(TABLES, tables)]
        strip = (NARROW, mine)
        kept = {
            "q": (strip + (128,), BF16), "kv": (strip + (256,), BF16), "att": ((mine, dim), BF16),
            "lse": ((NARROW, 8, mine), F32), "mid": ((mine, dim), F32), "active": ((mine, hidden), BF16),
            "slope": ((mine, hidden), BF16),
            "x": ((mine, dim), F32), "peer": ((group - 1,) + strip + (256,), BF16),
        }
        outputs += [("saved_" + name, (layers,) + kept[name][0], kept[name][1], hbm) for name in SAVED]
        outputs += [
            ("reds", (layers, 4, rank, mine), BF16, vmem),
            ("out_result", (NARROW, mine, 128), BF16, hbm),
        ]
        scratch += [
            (name, pltpu.VMEM(((layers,) if name == "peer" else ()) + kept[name][0], kept[name][1]))
            for name in SAVED
        ]
        scratch += [
            *[(name, pltpu.VMEM(table.shape, table.dtype)) for name, table in zip(TABLES, tables)],
            ("wq", pltpu.VMEM((NARROW // 2, n_row, cuts[0], depth // cuts[0], 768), BF16)),
            ("wp", pltpu.VMEM((NARROW, cuts[1], width // cuts[1], dim), BF16)),
            ("wu", pltpu.VMEM((NARROW, n_row, cuts[2], depth // cuts[2], units), BF16)),
            ("wd", pltpu.VMEM((NARROW, cuts[3], units // cuts[3], dim), BF16)),
            ("tokens_v", pltpu.VMEM((mine, dim), BF16)),
            ("normed", pltpu.VMEM((mine, dim), BF16)),
            ("red", pltpu.VMEM((mine, rank), BF16)),
            ("red_up", pltpu.VMEM((mine, rank), BF16)),
            ("vec", pltpu.VMEM((n_col,) + vector.shape, F32)),
            ("stage_sem", dma((4,))),
            ("save_sem", dma((layers, len(SAVED)))),
            ("kv_send", dma((layers, group - 1))),
            ("kv_recv", dma((layers, group - 1))),
            ("load_sem", dma((2 + len(TABLES),))),
            ("result", pltpu.VMEM((NARROW, mine, 128), BF16)),
            ("result_sem", dma((NARROW // 2,))),
        ]
    names = [x[0] for x in inputs] + [x[0] for x in outputs] + [x[0] for x in scratch]
    outs = pl.pallas_call(
        functools.partial(gather_body, n_row, n_col, layers, group, tuple(names)),
        out_shape=[jax.ShapeDtypeStruct(shape, kind) for _, shape, kind, _ in outputs],
        in_specs=[spec for _, _, spec in inputs],
        out_specs=[spec for _, _, _, spec in outputs],
        scratch_shapes=[shape for _, shape in scratch],
        compiler_params=pltpu.CompilerParams(
            collective_id=0, has_side_effects=True, vmem_limit_bytes=60 * 2**20
        ),
        name="gather_inputs",
    )(*[array for _, array, _ in inputs])
    outs = dict(zip([x[0] for x in outputs], outs))

    merge = 128 // width
    strips = n_col // merge
    qkv_full = outs["full_qkv"].reshape(layers, n_col, dim, 3 * width)
    up_full = outs["full_up"].reshape(layers, n_col, dim, units)
    rows, vec = [outs["own_tokens"], outs["own_cotangent"]], outs["vectors"]
    if merge > 1:
        qkv_full = qkv_full.reshape(layers, strips, merge, dim, 3, width).transpose(0, 1, 3, 4, 2, 5)
        up_full = up_full.reshape(layers, strips, merge, dim, units).transpose(0, 1, 3, 2, 4)
        rows = [x.transpose(1, 0, 2).reshape(mine, dim) for x in rows]
        vec = vec.reshape(strips, merge, layers, 4, 4 * 128)
        first = vec[:, :, :, 0, : 3 * width].reshape(strips, merge, layers, 3, width).transpose(0, 2, 3, 1, 4)
        first = jnp.pad(first.reshape(strips, layers, 384), ((0, 0), (0, 0), (0, 128)))
        second = vec[:, :, :, 1, :units].transpose(0, 2, 1, 3).reshape(strips, layers, 512)
        rest = vec[:, :, :, 2:, : 4 * width].reshape(strips, merge, layers, 2, 4, width)
        rest = rest.transpose(0, 2, 3, 4, 1, 5).reshape(strips, layers, 2, 512)
        vec = jnp.concatenate([first[:, :, None], second[:, :, None], rest], axis=2)
        vec = vec.reshape(strips, layers * 4, 512)
    outs.update(
        qkv=qkv_full.reshape(layers, strips, dim, 384),
        proj=outs["full_proj"].reshape(layers, dim, dim),
        up=up_full.reshape(layers, strips, dim, units * merge),
        down=outs["full_down"].reshape(layers, hidden, dim),
        tokens=rows[0], cotangent=rows[1], vec=vec, result=outs.get("out_result"),
    )
    return outs


PARAMS = pltpu.CompilerParams(vmem_limit_bytes=60 * 2**20)


def shape_of(shape, kind):
    return jax.ShapeDtypeStruct(shape, kind)


def kernel(body, name, inputs, outputs, scratch=()):
    spaces = (pl.BlockSpec(memory_space=pltpu.VMEM), pl.BlockSpec(memory_space=pltpu.HBM))
    return pl.pallas_call(
        body,
        out_shape=[shape_of(shape, kind) for shape, kind, _ in outputs],
        in_specs=[spaces[far] for _, far in inputs],
        out_specs=[spaces[far] for _, _, far in outputs],
        scratch_shapes=list(scratch),
        compiler_params=PARAMS,
        name=name,
    )(*[array for array, _ in inputs])


def own_group(group):
    return lax.rem(lax.axis_index("col"), group)


def qkv_body(l, x, vec, w, low, up, q, kv, red_out, red, normed, buf, sem):
    copies = []
    for i in range(NARROW):
        copies.append(pltpu.make_async_copy(w.at[l, i], buf.at[i // 2, :, columns(i % 2, 384)], sem.at[i]))
        copies[-1].start()
    for copy in copies:
        copy.wait()
    v = Vectors(vec, l)
    qkv_stage(x, v.row("gain1"), v.row("shift1"), buf, Strips(v.qkv), low.at[l], up.at[l], q, kv, red, red_out, normed)


def qkv_kernel(l, x, vec, w, low, up):
    tokens, dim = x.shape
    return kernel(
        functools.partial(qkv_body, l), "qkv",
        [(x, False), (vec, False), (w, True), (low, False), (up, False)],
        [((NARROW, tokens, 128), BF16, False), ((NARROW, tokens, 256), BF16, False), ((low.shape[1], tokens), BF16, False)],
        [pltpu.VMEM((tokens, low.shape[1]), BF16), pltpu.VMEM((tokens, dim), BF16), pltpu.VMEM((NARROW // 2, dim, 768), BF16), pltpu.SemaphoreType.DMA((NARROW,))],
    )


def attend_body(group, g_ref, q, *refs):
    held = positions(group)
    kvs, (out, lse) = refs[:group], refs[group:]
    bias = pair_bias(held, g_ref[0])
    each(NARROW, lambda i: attend_strip(held, bias, g_ref[0], i, q, kvs, out, lse))


def attend_kernel(group, g, q, kvs):
    tokens = q.shape[1]
    return pl.pallas_call(
        functools.partial(attend_body, group),
        out_shape=[shape_of((tokens, NARROW * 128), BF16), shape_of((NARROW, 8, tokens), F32)],
        in_specs=[pl.BlockSpec(memory_space=pltpu.SMEM)] + [pl.BlockSpec(memory_space=pltpu.VMEM)] * (group + 1),
        out_specs=[pl.BlockSpec(memory_space=pltpu.VMEM)] * 2,
        compiler_params=PARAMS,
        name="attend",
    )(g, q, *kvs)


def mlp_body(l, x, att, vec, wp, wu, wd, *refs):
    low_proj, up_proj, low_up, up_up, low_down, up_down = [ref.at[l] for ref in refs[:6]]
    mid, result, active, slope, reds, red, red_up, normed, bp, bu, bd, sem = refs[6:]
    copies = []
    for n, (src, dst) in enumerate(((wp.at[l], bp), (wu.at[l], bu), (wd.at[l], bd))):
        copies.append(pltpu.make_async_copy(src, dst, sem.at[n]))
        copies[-1].start()
    v = Vectors(vec, l)
    copies[0].wait()
    proj_stage(
        x, att, bp, v.row("proj"), low_proj, up_proj, v.row("gain2"), v.row("shift2"), low_up,
        mid, normed, red, reds.at[0], red_up, reds.at[1],
    )
    copies[1].wait()
    each(NARROW, lambda i: up_strip(i, normed, bu, Strips(v.up), red_up, up_up, active, slope))
    copies[2].wait()

    def put(n, value):
        if len(result.shape) == 2:
            result[:, columns(n, 256)] = value
        else:
            for m in range(2):
                result[2 * n + m] = value[:, m * 128 : (m + 1) * 128].astype(BF16)

    keep(dot(active[...], low_down[...], TURNED), red, reds.at[2])
    down_stage(mid, active, bd, v.row("down"), up_down, red, put)


def mlp_kernel(l, final, x, att, vec, wp, wu, wd, tables):
    tokens, dim = x.shape
    hidden = wd.shape[1]
    rank = tables[0].shape[1]
    result = ((NARROW, tokens, 128), BF16, False) if final else ((tokens, dim), F32, False)
    return kernel(
        functools.partial(mlp_body, l), "mlp",
        [(x, False), (att, False), (vec, False), (wp, True), (wu, True), (wd, True)] + [(t, False) for t in tables],
        [((tokens, dim), F32, False), result] + [((tokens, hidden), BF16, False)] * 2 + [((3, rank, tokens), BF16, False)],
        [
            pltpu.VMEM((tokens, rank), BF16), pltpu.VMEM((tokens, rank), BF16),
            pltpu.VMEM((tokens, dim), BF16), pltpu.VMEM(wp.shape[1:], BF16),
            pltpu.VMEM(wu.shape[1:], BF16), pltpu.VMEM(wd.shape[1:], BF16), pltpu.SemaphoreType.DMA((3,)),
        ],
    )


def mlp_back_stage(vec, grad, active, g_hid, mid, att, low, total, wp, wu, wd, reds, t, grads, g_mid, waits, strip_waits):
    low[...] = grad[...].astype(BF16)
    g_red = dot(low[...], t["up_down"], TURNED).astype(BF16)
    rank = g_red.shape[1]
    units = wu.shape[2]
    total[...] = jnp.zeros_like(total)

    def strip(i):
        cols = columns(i, units)
        strip_waits(i)
        g_active = dot(low[...], wd[cols, :], TURNED) + dot(g_red, t["low_down"][:, cols])
        g_hid[:, cols] = (g_active * g_hid[:, cols].astype(F32)).astype(BF16)
        total[...] += dot(g_hid[:, cols], wu[i], TURNED)

    each(NARROW, strip)

    def give(at, value):
        size = value.shape[1] // NARROW
        for i in range(NARROW):
            grads[i, :, at : at + size] = value[:, i * size : (i + 1) * size].astype(BF16)

    give(384 + 2 * units, dot(reds[3], low[...]))
    give(384 + units, dot(g_red, active[...], CROSS))
    give(384, dot(reds[2], g_hid[...]))
    g_hid[:, :rank] = dot(g_hid[...], t["up_up"][...], TURNED).astype(BF16)
    waits("mid")
    gain, shift = vec.row("gain2"), vec.row("shift2")
    dim = mid.shape[1]

    def norm(rows):
        scaled, inverse = norm_parts(mid[rows, :])
        active[rows, :dim] = (scaled * gain + shift).astype(BF16)
        g_normed = total[rows, :] + dot(g_hid[rows, :rank], t["low_up"])
        value = grad[rows, :] + norm_grad(g_normed, scaled, inverse, gain)
        g_mid[rows, :] = value
        low[rows, :] = value.astype(BF16)

    by_rows(mid.shape[0], norm)
    give(256, dot(g_hid[:, :rank], active[:, :dim], CROSS))
    give(128, dot(reds[1], low[...]))
    g_red_proj = dot(low[...], t["up_proj"], TURNED).astype(BF16)
    waits("att")
    waits("proj")
    give(0, dot(g_red_proj, att[...], CROSS))
    low[...] = (dot(low[...], wp[...], TURNED) + dot(g_red_proj, t["low_proj"])).astype(BF16)


def qkv_back_stage(vec, x, g_mid, gq, parts, total, g_red, normed, wq, red, low, up, grads, put, waits, done=None):
    waits("gq")
    waits("qkv")
    rank, tokens = red.shape
    small = jnp.zeros((tokens, rank), F32)

    def mixed(i, rows):
        return jnp.concatenate([gq[i, rows, :], parts[0][i, rows, :]], axis=1)

    def product(j, rows):
        made = dot(jnp.concatenate([mixed(2 * j, rows), mixed(2 * j + 1, rows)], axis=1), wq[j], TURNED)
        total[rows, :] = made if j == 0 else total[rows, :] + made

    every = pl.ds(0, tokens)
    for j in range(NARROW // 2):
        for i in (2 * j, 2 * j + 1):
            waits(("part", i))
            parts[0][i] = sum(part[i].astype(F32) for part in parts).astype(BF16)
            g_mixed = mixed(i, every)
            grads[i, :, 128:512] = dot(red[...], g_mixed).astype(BF16)
            small = small + dot(g_mixed, up[i], TURNED)
        if not done:
            product(j, every)
    g_low_rank = small.astype(BF16)
    g_red[...] = g_low_rank
    waits("x")
    waits("g_mid")
    gain, shift = vec.row("gain1"), vec.row("shift1")

    def norm(rows):
        scaled, inverse = norm_parts(x[rows, :].astype(F32))
        normed[rows, :] = (scaled * gain + shift).astype(BF16)
        g_normed = total[rows, :] + dot(g_red[rows, :], low[...])
        put(rows, g_mid[rows, :] + norm_grad(g_normed, scaled, inverse, gain))

    def lower():
        g_low = dot(g_low_rank, normed[...], CROSS).astype(BF16)
        for i in range(NARROW):
            grads[i, :, :128] = g_low[:, i * 128 : (i + 1) * 128]

    if not done:
        by_rows(tokens, norm)
        lower()
        return

    def first_norm(rows):
        normed[rows, :] = norm_low(x[rows, :].astype(F32), gain, shift)

    by_rows(tokens, first_norm)
    lower()
    done(-1)
    for b in range(tokens // BLOCK):
        for j in range(NARROW // 2):
            product(j, pl.ds(b * BLOCK, BLOCK))
        for n in range(2):
            norm(pl.ds(b * BLOCK + n * BLOCK // 2, BLOCK // 2))
        done(b)


def back_body(lq, lm, group, names, *refs):
    R = dict(zip(names, refs))
    held = positions(group)
    sem, started = R["sem"], {}

    def waits(name):
        for copy in started.pop(name, ()):
            copy.wait()

    count = [0]

    def begin(name, *copies):
        started[name] = []
        for src, dst in copies:
            copy = pltpu.make_async_copy(src, dst, sem.at[count[0]])
            count[0] += 1
            copy.start()
            started[name].append(copy)

    def strip_copies(l, i, base):
        cols = columns(i, R["wu"].shape[2])
        pairs = (
            (R["slopes"].at[l, :, cols], R["g_hid"].at[:, cols]), (R["actives"].at[l, :, cols], R["active"].at[:, cols]),
            (R["w_down"].at[l, cols], R["wd"].at[cols]), (R["w_up"].at[l, i], R["wu"].at[i]),
        )
        return [pltpu.make_async_copy(src, dst, sem.at[base + 4 * i + n]) for n, (src, dst) in enumerate(pairs)]

    strip_base = {}

    def load_strips(l):
        strip_base[l] = count[0]
        count[0] += 4 * NARROW
        for i in range(NARROW):
            for copy in strip_copies(l, i, strip_base[l]):
                copy.start()

    def strip_waits(l):
        def wait(i):
            for copy in strip_copies(l, i, strip_base[l]):
                copy.wait()

        return wait

    if lq is not None:
        begin("gq", (R["in_gq"], R["gq"]), *[(R["in_part%d" % j], R["part%d" % j]) for j in range(group)])
        begin("qkv", *[
            (R["w_qkv"].at[lq, i], R["wq"].at[i // 2, :, columns(i % 2, 384)]) for i in range(NARROW)
        ])
        begin("x", (R["in_x"], R["x"]))
        begin("g_mid", (R["in_g_mid"], R["total2"]))
    else:
        begin("cotangent", (R["cotangent"], R["low"]))
    if lm is not None:
        load_strips(lm)
        begin("proj", (R["w_proj"].at[lm], R["wp"]))
        begin("att", (R["atts"].at[lm], R["att"]))
        begin("kv", (R["kvs"].at[lm], R["kv"]), (R["peers"].at[lm], R["peer"]), (R["lses"].at[lm], R["lse"]))
    if lq is not None:
        vec = Vectors(R["vec"], lq)

        def put(rows, value):
            if lm is None:
                for i in range(NARROW):
                    R["out"][i, rows, :] = value[:, i * 128 : (i + 1) * 128].astype(BF16)
            else:
                R["grad"][rows, :] = value

        qkv_back_stage(
            vec, R["x"], R["total2"], R["gq"], [R["part%d" % j] for j in range(group)], R["total"],
            R["g_red"], R["low"], R["wq"],
            R["reds"].at[lq, 0], R["low_qkv"].at[lq], R["up_qkv"].at[lq], R["grads_qkv"], put, waits,
        )
    else:
        waits("cotangent")
        R["grad"][...] = R["low"][...].astype(F32)
    if lm is None:
        return
    begin("q", (R["qs"].at[lm], R["gq"]))
    begin("mid", (R["mids"].at[lm], R["x" if lq is not None and R["x"].dtype == F32 else "mid"]))
    mid = R["x" if lq is not None and R["x"].dtype == F32 else "mid"]
    t = {name: R[name].at[lm] for name in TABLES}
    vec = Vectors(R["vec"], lm)
    mlp_back_stage(
        vec, R["grad"], R["active"], R["g_hid"], mid, R["att"], R["low"], R["total"], R["wp"], R["wu"], R["wd"],
        R["reds"].at[lm], {k: (v if k in ("low_down", "up_up") else v[...]) for k, v in t.items() if "qkv" not in k},
        R["grads_mlp"], R["total2"], waits, strip_waits(lm),
    )
    out_mid = pltpu.make_async_copy(R["total2"], R["out_g_mid"], sem.at[count[0]])
    out_mid.start()
    waits("q")
    waits("kv")
    bias = pair_bias(held, R["g"][0])
    kvs = [R["kv"]] + [R["peer"].at[j] for j in range(group - 1)]
    gkvs = [R["part%d" % j] for j in range(group)]
    each(NARROW, lambda i: attend_back_strip(
        held, bias, R["g"][0], i, R["gq"], R["lse"], R["att"], R["low"], kvs, R["gq"], gkvs
    ))
    outs = [(R["gq"], R["out_gq"])] + [(R["part%d" % j], R["out_part%d" % j]) for j in range(group)]
    copies = [pltpu.make_async_copy(src, dst, sem.at[count[0] + 1 + n]) for n, (src, dst) in enumerate(outs)]
    for copy in copies:
        copy.start()
    for copy in copies:
        copy.wait()
    out_mid.wait()


def back_kernel(lq, lm, group, g, outs, tables, carried):
    layers, _, dim, _ = outs["qkv"].shape
    hidden = outs["down"].shape[1]
    tokens = outs["tokens"].shape[0]
    rank = tables[0].shape[1]
    strip = (NARROW, tokens)
    inputs = [("g", g, pl.BlockSpec(memory_space=pltpu.SMEM))]
    near, far = pl.BlockSpec(memory_space=pltpu.VMEM), pl.BlockSpec(memory_space=pltpu.HBM)
    inputs += [(name, table, near) for name, table in zip(TABLES, tables)]
    inputs += [("vec", outs["vec"], near), ("reds", outs["reds"], near)]
    outputs, scratch = [], []

    def vmem(name, shape, kind):
        scratch.append((name, pltpu.VMEM(shape, kind)))

    vmem("gq", strip + (128,), BF16)
    for j in range(group):
        vmem("part%d" % j, strip + (256,), BF16)
    vmem("total", (tokens, dim), F32)
    vmem("total2", (tokens, dim), F32)
    vmem("low", (tokens, dim), BF16)
    if lq is not None:
        g_mid, gq, parts = carried
        x = outs["tokens"] if lq == 0 else outs["saved_x"][lq - 1]
        inputs += [("in_gq", gq, far), ("in_g_mid", g_mid, far), ("in_x", x, far), ("w_qkv", outs["qkv"], far)]
        inputs += [("in_part%d" % j, part, far) for j, part in enumerate(parts)]
        vmem("wq", (NARROW // 2, dim, 768), BF16)
        vmem("g_red", (tokens, rank), BF16)
        vmem("x", (tokens, dim), x.dtype)
        outputs.append(("grads_qkv", (NARROW, rank, 512), BF16, near))
        if lm is None:
            outputs.append(("out", strip + (128,), BF16, near))
    if lm is not None:
        if lq is None:
            inputs.append(("cotangent", outs["cotangent"], far))
        for name in ("active", "slope", "mid", "att", "q", "kv", "peer", "lse"):
            inputs.append((name + "s", outs["saved_" + name], far))
        inputs += [("w_" + name, outs[name], far) for name in ("proj", "up", "down")]
        vmem("wp", (dim, dim), BF16)
        vmem("wu", (NARROW, dim, hidden // NARROW), BF16)
        vmem("wd", (hidden, dim), BF16)
        vmem("grad", (tokens, dim), F32)
        if lq is None or x.dtype != F32:
            vmem("mid", (tokens, dim), F32)
        vmem("att", (tokens, dim), BF16)
        vmem("active", (tokens, hidden), BF16)
        vmem("g_hid", (tokens, hidden), BF16)
        vmem("kv", strip + (256,), BF16)
        vmem("peer", (group - 1,) + strip + (256,), BF16)
        vmem("lse", (NARROW, 8, tokens), F32)
        outputs.append(("grads_mlp", (NARROW, rank, 512 + 2 * hidden // NARROW), BF16, near))
        outputs += [("out_g_mid", (tokens, dim), F32, far), ("out_gq", strip + (128,), BF16, far)]
        outputs += [("out_part%d" % j, strip + (256,), BF16, far) for j in range(group)]
    scratch.append(("sem", pltpu.SemaphoreType.DMA((96,))))
    names = [x[0] for x in inputs] + [x[0] for x in outputs] + [x[0] for x in scratch]
    made = pl.pallas_call(
        functools.partial(back_body, lq, lm, group, tuple(names)),
        out_shape=[shape_of(shape, kind) for _, shape, kind, _ in outputs],
        in_specs=[spec for _, _, spec in inputs],
        out_specs=[spec for _, _, _, spec in outputs],
        scratch_shapes=[shape for _, shape in scratch],
        compiler_params=PARAMS,
        name="back",
    )(*[array for _, array, _ in inputs])
    return dict(zip([x[0] for x in outputs], made))


SITES = {"mlp": (1, 1, 2, 2, 3, 3), "qkv": (0, 0)}


def backward_body(layers, group, n_row, n_col, names, *refs):
    R = dict(zip(names, refs))
    held = positions(group)
    per = BLOCKS // group
    r, c = lax.axis_index("row"), lax.axis_index("col")
    g = lax.rem(c, group)
    seqs = n_col // group
    tokens = per * BLOCK
    bias = pair_bias(held, g)

    def row_peer(s):
        return (lax.rem(r + s, n_row), c)

    def col_peer(d):
        return lax.rem(c + d, n_col)

    peers = [row_peer(s) for s in range(1, n_row)] + [(r, col_peer(d)) for d in range(1, n_col)]
    barrier = pltpu.get_barrier_semaphore()
    for peer in peers:
        pl.semaphore_signal(barrier, inc=1, device_id=peer, device_id_type=MESH)
    pl.semaphore_wait(barrier, len(peers))

    sem, started, count = R["sem"], {}, [0]

    def begin(name, *copies):
        started[name] = []
        for src, dst in copies:
            copy = pltpu.make_async_copy(src, dst, sem.at[count[0]])
            count[0] += 1
            copy.start()
            started[name].append(copy)

    def waits(name):
        for copy in started.pop(name, ()):
            copy.wait()

    def strip_copies(l, i, base):
        cols = columns(i, R["wu"].shape[2])
        pairs = (
            (R["slopes"].at[l, :, cols], R["g_hid"].at[:, cols]), (R["actives"].at[l, :, cols], R["active"].at[:, cols]),
            (R["w_down"].at[l, cols], R["wd"].at[cols]), (R["w_up"].at[l, i], R["wu"].at[i]),
        )
        return [pltpu.make_async_copy(src, dst, sem.at[base + 4 * i + n]) for n, (src, dst) in enumerate(pairs)]

    strip_base = {}

    def load_strips(l):
        strip_base[l] = count[0]
        count[0] += 4 * NARROW
        for i in range(NARROW):
            for copy in strip_copies(l, i, strip_base[l]):
                copy.start()

    def strip_waits(l):
        def wait(i):
            for copy in strip_copies(l, i, strip_base[l]):
                copy.wait()

        return wait

    far = [0]

    def remote(src, dst, n, peer):
        return pltpu.make_async_remote_copy(
            src_ref=src, dst_ref=dst, send_sem=R["out_sem"].at[n], recv_sem=R["in_sem"].at[n],
            device_id=peer, device_id_type=MESH,
        )

    def new_far():
        far[0] += 1
        return far[0] - 1

    def columns_start(n, src, b, at):
        start = (c // group) * LEN + place_of(group, g, b) * BLOCK
        to, rows = R["columns"].at[n, pl.ds(pl.multiple_of(start, BLOCK), BLOCK)], pl.ds(b * BLOCK, BLOCK)
        begin("columns%d" % (n * per + b), (src.at[c, rows], to))
        for d in range(1, n_col):
            remote(src.at[col_peer(d), rows], to, at, (r, col_peer(d))).start()

    def columns_end(n, at):
        for b in range(per):
            waits("columns%d" % (n * per + b))
        ref = R["columns"].at[n, pl.ds(0, (n_col - 1) * tokens)]
        remote(ref, ref, at, (r, col_peer(1))).wait()

    ends = {}

    def spread(kind, l):
        src, land, at = R["grads_" + kind], R["land_" + kind].at[l], new_far()
        begin("own_%s%d" % (kind, l), (src.at[c], land.at[c]))
        for d in range(1, n_col):
            remote(src.at[col_peer(d)], land.at[c], at, (r, col_peer(d))).start()
        ends["spread", kind, l] = at

    def spread_sent(kind, l):
        if l < layers:
            ref = R["land_" + kind].at[l, pl.ds(0, n_col - 1)]
            remote(ref, ref, ends["spread", kind, l], (r, col_peer(1))).wait_send()

    def add_load(kind, l):
        land = R["land_" + kind].at[l]
        ref = land.at[pl.ds(0, n_col - 1)]
        remote(ref, ref, ends["spread", kind, l], (r, col_peer(1))).wait_recv()
        waits("own_%s%d" % (kind, l))
        begin("stage_" + kind, (land, R["stage_" + kind]))

    def add(kind, l):
        stage, total = R["stage_" + kind], R["sum_" + kind]
        add_sent(kind, l + 1)
        waits("stage_" + kind)
        for q in range(seqs):
            value = sum(stage[q * group + n].astype(F32) for n in range(group))
            total[q] = value.astype(BF16)
        parts, at = R["parts_" + kind], new_far()
        begin("part_%s%d" % (kind, l), (total, parts.at[l, r]))
        for q in range(1, n_row):
            remote(total, parts.at[l, r], at, row_peer(q)).start()
        ends["add", kind, l] = at

    def added(kind, l):
        ref = R["parts_" + kind].at[l, pl.ds(0, n_row - 1)]
        return remote(ref, ref, ends["add", kind, l], row_peer(1))

    def add_sent(kind, l):
        if l < layers:
            waits("part_%s%d" % (kind, l))
            added(kind, l).wait_send()

    def part_copy(l, j, i, at):
        to = c - g + lax.rem(g - j + group, group)
        strip = pl.ds(i, 1)
        return remote(R["part%d" % j].at[strip], R["in_part"].at[l, j - 1, strip], at[j] + i, (r, to))

    def back_strip(l, i, at):
        kvs = [R["kv"]] + [R["peer"].at[j] for j in range(group - 1)]
        gkvs = [R["part%d" % j] for j in range(group)]
        attend_back_strip(held, bias, g, i, R["gq"], R["lse"], R["att"], R["low"], kvs, R["gq"], gkvs)
        for j in range(1, group):
            part_copy(l, j, i, at).start()

    def load_qkv(l):
        begin("qkv", *[
            (R["w_qkv"].at[l, i], R["wq"].at[i // 2, :, columns(i % 2, 384)]) for i in range(NARROW)
        ])

    def load_mlp(l):
        load_strips(l)
        begin("proj", (R["w_proj"].at[l], R["wp"]))

    def load_attention(l):
        begin("mid", (R["mids"].at[l], R["mid"]))
        begin("att", (R["atts"].at[l], R["att"]))
        begin("q", (R["qs"].at[l], R["gq"]))
        begin("kv", (R["kvs"].at[l], R["kv"]), (R["peers"].at[l], R["peer"]), (R["lses"].at[l], R["lse"]))

    def block_done(b):
        if b < 0:
            spread("qkv", 0)
            return
        if b == per - 1:
            add("qkv", 0)
        columns_start(1, R["part0"].at[:, :, pl.ds(0, 128)], b, at_grad)
        if b == max(per - 2, 0):
            add_load("qkv", 0)

    last = layers - 1
    begin("cotangent", (R["cotangent"], R["low"]))
    begin("tables", *[(R["in_" + name], R[name]) for name in TABLES + ("vec", "reds")])
    load_mlp(last)
    load_attention(last)
    load_qkv(last)
    at_result, at_grad = new_far(), new_far()
    for b in range(per):
        columns_start(0, R["result"], b, at_result)
    at_ids = new_far()
    begin("ids", (R["ids"], R["all_ids"].at[r]))
    for q in range(1, n_row):
        remote(R["ids"], R["all_ids"].at[r], at_ids, row_peer(q)).start()
    waits("cotangent")

    def widen(rows):
        R["grad"][rows, :] = R["low"][rows, :].astype(F32)

    by_rows(tokens, widen)
    waits("tables")
    for l in reversed(range(layers)):
        t = {name: R[name].at[l] for name in TABLES if "qkv" not in name}
        vec = Vectors(R["vec"], l)
        spread_sent("mlp", l + 1)
        mlp_back_stage(
            vec, R["grad"], R["active"], R["g_hid"], R["mid"], R["att"], R["low"], R["total"], R["wp"], R["wu"],
            R["wd"], R["reds"].at[l], {k: (v if k in ("low_down", "up_up") else v[...]) for k, v in t.items()},
            R["grads_mlp"], R["total2"], waits, strip_waits(l),
        )
        spread("mlp", l)
        if l > 0:
            load_mlp(l - 1)
        begin("x", (R["tokens"] if l == 0 else R["xs"].at[l - 1], R["x0"] if l == 0 else R["mid"]))
        waits("q")
        waits("kv")
        at = [far[0] + j * NARROW for j in range(group)]
        far[0] += group * NARROW
        half = NARROW // 2
        if l < last:
            add_load("qkv", l + 1)
        each(half, lambda i: back_strip(l, i, at))
        add_load("mlp", l)
        if l < last:
            add("qkv", l + 1)
        add("mlp", l)
        each(half, lambda i: back_strip(l, half + i, at))

        def fetch_parts(first, end):
            for i in range(first, end):
                for j in range(1, group):
                    part_copy(l, j, i, at).wait_recv()
                begin(("part", i), *[(R["in_part"].at[l, j, i], R["peer"].at[j, i]) for j in range(group - 1)])

        def part_waits(name):
            if name == ("part", 2):
                fetch_parts(NARROW - 3, NARROW)
            waits(name)

        fetch_parts(0, NARROW - 3)
        parts = [R["part0"]] + [R["peer"].at[j] for j in range(group - 1)]
        spread_sent("qkv", l + 1)

        def put(rows, value):
            if l > 0:
                R["grad"][rows, :] = value
            else:
                for i in range(NARROW):
                    R["part0"][i, rows, :128] = value[:, i * 128 : (i + 1) * 128].astype(BF16)

        qkv_back_stage(
            vec, R["x0"] if l == 0 else R["mid"], R["total2"], R["gq"], parts, R["total"], R["g_red"], R["low"],
            R["wq"], R["reds"].at[l, 0], R["low_qkv"].at[l], R["up_qkv"].at[l], R["grads_qkv"], put, part_waits,
            None if l > 0 else block_done,
        )
        if l > 0:
            spread("qkv", l)
        for i in range(NARROW):
            for j in range(1, group):
                part_copy(l, j, i, at).wait_send()
        if l > 0:
            load_qkv(l - 1)
            load_attention(l - 1)
    columns_end(0, at_result)
    columns_end(1, at_grad)
    waits("ids")
    rest = R["all_ids"].at[pl.ds(0, n_row - 1)]
    remote(rest, rest, at_ids, row_peer(1)).wait()
    for kind in ("mlp", "qkv"):
        spread_sent(kind, 0)
        add_sent(kind, 0)
        for l in range(layers):
            added(kind, l).wait_recv()


def backward(n_row, n_col, group, outs, tables, ids):
    layers, _, dim, _ = outs["qkv"].shape
    hidden = outs["down"].shape[1]
    mine = outs["tokens"].shape[0]
    rank = tables[0].shape[1]
    seqs = n_col // group
    strip = (NARROW, mine)
    near, far = pl.BlockSpec(memory_space=pltpu.VMEM), pl.BlockSpec(memory_space=pltpu.HBM)
    small = list(zip(TABLES, tables)) + [("vec", outs["vec"]), ("reds", outs["reds"])]
    inputs = [("in_" + name, table, far) for name, table in small] + [("ids", ids, far)]
    for name in ("active", "slope", "mid", "att", "q", "kv", "peer", "lse", "x"):
        inputs.append((name + "s", outs["saved_" + name], far))
    inputs += [("w_" + name, outs[name], far) for name in KINDS]
    inputs += [(name, outs[name], far) for name in ("tokens", "cotangent", "result")]
    sizes = {"mlp": 512 + 2 * hidden // NARROW, "qkv": 512}
    outputs = [
        ("columns", (2, n_col * mine, 128), BF16, far),
        ("all_ids", (n_row,) + ids.shape, F32, far),
        ("in_part", (layers, group - 1) + strip + (256,), BF16, far),
    ]
    scratch = [
        ("gq", strip + (128,), BF16), ("kv", strip + (256,), BF16), ("peer", (group - 1,) + strip + (256,), BF16),
        ("lse", (NARROW, 8, mine), F32), ("total", (mine, dim), F32), ("total2", (mine, dim), F32),
        ("grad", (mine, dim), F32), ("mid", (mine, dim), F32), ("low", (mine, dim), BF16), ("att", (mine, dim), BF16),
        ("x0", (mine, dim), BF16), ("active", (mine, hidden), BF16), ("g_hid", (mine, hidden), BF16),
        ("g_red", (mine, rank), BF16), ("wq", (NARROW // 2, dim, 768), BF16), ("wp", (dim, dim), BF16),
        ("wu", (NARROW, dim, hidden // NARROW), BF16), ("wd", (hidden, dim), BF16),
    ]
    scratch += [("part%d" % j, strip + (256,), BF16) for j in range(group)]
    scratch += [(name, table.shape, table.dtype) for name, table in small]
    for kind, size in sizes.items():
        outputs.append(("land_" + kind, (layers, n_col, rank, size), BF16, far))
        outputs.append(("parts_" + kind, (layers, n_row, seqs, rank, size), BF16, far))
        scratch.append(("grads_" + kind, (NARROW, rank, size), BF16))
        scratch.append(("stage_" + kind, (n_col, rank, size), BF16))
        scratch.append(("sum_" + kind, (seqs, rank, size), BF16))
    scratch = [(name, pltpu.VMEM(shape, kind)) for name, shape, kind in scratch]
    scratch += [
        ("sem", pltpu.SemaphoreType.DMA((72 * layers + 16,))),
        ("out_sem", pltpu.SemaphoreType.DMA(((4 + group * NARROW) * layers + 4,))),
        ("in_sem", pltpu.SemaphoreType.DMA(((4 + group * NARROW) * layers + 4,))),
    ]
    names = [x[0] for x in inputs] + [x[0] for x in outputs] + [x[0] for x in scratch]
    made = pl.pallas_call(
        functools.partial(backward_body, layers, group, n_row, n_col, tuple(names)),
        out_shape=[shape_of(shape, kind) for _, shape, kind, _ in outputs],
        in_specs=[spec for _, _, spec in inputs],
        out_specs=[spec for _, _, _, spec in outputs],
        scratch_shapes=[shape for _, shape in scratch],
        compiler_params=pltpu.CompilerParams(
            collective_id=1, has_side_effects=True, vmem_limit_bytes=62 * 2**20
        ),
        name="backward",
    )(*[array for _, array, _ in inputs])
    return dict(zip([x[0] for x in outputs], made))


def place_body(layers, names, *refs):
    R = dict(zip(names, refs))
    sem, ends = R["sem"], []

    def copy(src, dst, n):
        made = pltpu.make_async_copy(src, dst, sem.at[n])
        made.start()
        return made

    loads = [copy(R["columns"].at[n], R["low"].at[n], n) for n in range(2)]
    ins = {kind: copy(R["parts_" + kind], R["in_" + kind], 2 + n) for n, kind in enumerate(SITES)}
    for n in range(2):
        loads[n].wait()
        R["wide"][n] = R["low"][n].astype(F32)
        ends.append(copy(R["wide"].at[n], R["column_out%d" % n], 4 + n))
    rows, adapters, rank = R["ids"].shape[0], R["keep0"].shape[1], R["keep0"].shape[2]
    sequences = R["in_qkv"].shape[1]
    shape = (adapters * rank, sequences * rank)
    down, across = [lax.broadcasted_iota(jnp.int32, shape, axis) for axis in (0, 1)]
    weights = {}
    for site in range(4):
        chosen = jnp.zeros((1, shape[1]), F32)
        for q in range(sequences):
            value = R["ids"][q // (sequences // rows), q % (sequences // rows), site]
            chosen = jnp.where(across[:1] // rank == q, value, chosen)
        same = (chosen == (down // rank).astype(F32)) & (down % rank == across % rank)
        weights[site] = jnp.where(same, 1.0, 0.0).astype(BF16)
    number = 0
    for kind in ("qkv", "mlp"):
        ins[kind].wait()
        stage = R["in_" + kind]
        sequences, rank = stage.shape[1:3]
        at = 0
        for site, size in zip(SITES[kind], R["sizes"][kind]):
            out, keep = R["out%d" % number], R["keep%d" % number]
            for l in range(layers):
                part = stage[l, :, :, at : at + size]
                made = dot(weights[site], part.reshape(sequences * rank, size)).reshape(-1, rank, size)
                if number == 1:
                    for n in range(3):
                        keep[l, :, n] = made[:, :, n * 128 : (n + 1) * 128]
                else:
                    keep[l] = made
            ends.append(copy(keep, out, 6 + number))
            at += size
            number += 1
    for end in ends:
        end.wait()


def place(made, sizes, adapters):
    layers, rank = made["parts_qkv"].shape[0], made["parts_qkv"].shape[-2]
    hbm = pl.BlockSpec(memory_space=pltpu.HBM)
    columns = made["columns"]
    parts = {kind: made["parts_" + kind].reshape(layers, -1, rank, sum(sizes[kind])) for kind in SITES}
    widths = [size for kind in ("qkv", "mlp") for size in sizes[kind]]
    inputs = [("ids", made["all_ids"], pl.BlockSpec(memory_space=pltpu.SMEM)), ("columns", columns, hbm)]
    inputs += [("parts_" + kind, parts[kind], hbm) for kind in SITES]
    outputs = [("column_out%d" % n, columns.shape[1:], F32) for n in range(2)]
    shapes = [(layers, adapters, rank, size) for size in widths]
    shapes[1] = (layers, adapters, 3, rank, 128)
    outputs += [("out%d" % n, shape, F32) for n, shape in enumerate(shapes)]
    scratch = [("low", pltpu.VMEM(columns.shape, BF16)), ("wide", pltpu.VMEM(columns.shape, F32))]
    scratch += [("in_" + kind, pltpu.VMEM(parts[kind].shape, BF16)) for kind in SITES]
    scratch += [("keep%d" % n, pltpu.VMEM(shape, F32)) for n, shape in enumerate(shapes)]
    scratch.append(("sem", pltpu.SemaphoreType.DMA((6 + len(widths),))))
    names = [x[0] for x in inputs] + [x[0] for x in outputs] + [x[0] for x in scratch]

    def body(*refs):
        place_body(layers, names + ["sizes"], *refs, sizes)

    return pl.pallas_call(
        body,
        out_shape=[shape_of(shape, kind) for _, shape, kind in outputs],
        in_specs=[spec for _, _, spec in inputs],
        out_specs=[hbm] * len(outputs),
        scratch_shapes=[shape for _, shape in scratch],
        compiler_params=PARAMS,
        name="place",
    )(*[array for _, array, _ in inputs])


def to_rows_body(held, x, out):
    n = 0
    for s in range(x.shape[0] // (len(held) * len(held[0]))):
        for g in range(len(held)):
            for place in held[g]:
                start = (s * BLOCKS + place) * BLOCK
                out[start : start + BLOCK, :] = x[n].astype(F32)
                n += 1


def to_rows(held, x):
    blocks, _, width = x.shape
    return pl.pallas_call(
        functools.partial(to_rows_body, held),
        out_shape=shape_of((blocks * BLOCK, width), F32),
        compiler_params=PARAMS,
        name="to_rows",
    )(x)


def pick_body(width, units, ids, *refs):
    tables, raise_qkv, vectors, every = refs[:7], refs[7], refs[8:16], refs[16]
    qkv_b, up_b, proj_b, down_b, gain1, shift1, gain2, shift2 = vectors
    outs, raise_out, vector, ids_rows = refs[17:24], refs[24], refs[25], refs[26]
    for ref, out in zip(tables, outs):
        out[...] = ref[...]
    layers = raise_qkv.shape[0]
    vector[...] = jnp.zeros_like(vector)
    for l in range(layers):
        for n in range(3):
            row = raise_qkv[l, n]
            for i in range(NARROW):
                raise_out[l, i, :, n * 128 : (n + 1) * 128] = row[:, i * 128 : (i + 1) * 128]
            vector[4 * l : 4 * l + 1, n * width : (n + 1) * width] = qkv_b[n, l : l + 1, :].astype(F32)
        vector[4 * l + 1 : 4 * l + 2, :units] = up_b[l : l + 1, :].astype(F32)
        for n, ref in enumerate((proj_b, down_b, gain1, shift1, gain2, shift2)):
            row, lane = 4 * l + 2 + n // 4, n % 4 * width
            vector[row : row + 1, lane : lane + width] = ref[l : l + 1, :].astype(F32)
    ids_rows[...] = jnp.zeros_like(ids_rows)
    ids_rows[: every.shape[0], : every.shape[1]] = every[...].astype(F32)


def pick(group, adapter_ids, tables, raise_qkv, vectors):
    layers, _, _, rank, dim = raise_qkv.shape
    width, units = vectors[2].shape[1], vectors[1].shape[1]

    def chosen(site, shape):
        rest = (0,) * (len(shape) - 2)
        return pl.BlockSpec(
            (shape[0], None) + shape[2:], lambda i, ids: (0, ids[lax.axis_index("col") // group, site]) + rest
        )

    def whole(shape):
        return pl.BlockSpec(shape, lambda i, ids: (0,) * len(shape))

    shapes = [(table.shape[:1] + table.shape[2:], BF16) for _, table in tables]
    shapes += [((layers, NARROW, rank, 384), BF16), ((4 * layers, 512), F32), ((8, 128), F32)]
    return pl.pallas_call(
        functools.partial(pick_body, width, units),
        grid_spec=pltpu.PrefetchScalarGridSpec(
            num_scalar_prefetch=1,
            grid=(1,),
            in_specs=[chosen(site, table.shape) for site, table in tables]
            + [chosen(0, raise_qkv.shape)]
            + [whole(x.shape) for x in vectors]
            + [whole(adapter_ids.shape)],
            out_specs=[whole(shape) for shape, _ in shapes],
        ),
        out_shape=[shape_of(shape, kind) for shape, kind in shapes],
        compiler_params=PARAMS,
        name="pick",
    )(adapter_ids, *[table for _, table in tables], raise_qkv, *vectors, adapter_ids)


def shards(mesh_shape, *args):
    (
        tokens, cotangent, adapter_ids, qkv_weight, qkv_bias, proj_weight, proj_bias,
        up_weight, up_bias, down_weight, down_bias, first_gain, first_shift, second_gain,
        second_shift, qkv_lower, qkv_raise, proj_lower, proj_raise, up_lower, up_raise,
        down_lower, down_raise,
    ) = args
    n_row, n_col = mesh_shape
    layers, adapters, dim, rank = qkv_lower.shape
    rows, width = tokens.shape
    units = up_weight.shape[2]
    seqs = rows // LEN
    group = n_col // seqs
    held = positions(group)
    per = BLOCKS // group
    mine = per * BLOCK
    merge = 128 // width
    c = lax.axis_index("col")
    g = lax.rem(c, group)
    def turned(table):
        return jnp.swapaxes(table, 2, 3)

    *picked, vector, ids_rows = pick(
        group, adapter_ids,
        [
            (0, turned(qkv_lower)), (1, turned(proj_lower)), (1, proj_raise), (2, turned(up_lower)), (2, up_raise),
            (3, turned(down_lower)), (3, down_raise),
        ],
        qkv_raise.transpose(0, 1, 3, 2, 4),
        (qkv_bias.transpose(1, 0, 2), up_bias, proj_bias, down_bias, first_gain, first_shift, second_gain, second_shift),
    )
    tables = [picked[0], picked[7]] + list(picked[1:7])
    fused = FUSED and width == 128
    if width == 128:
        qkv_shard = qkv_weight.transpose(0, 2, 1, 3)
    else:
        qkv_shard = qkv_weight.reshape(layers, -1, 3 * width)
    outs = gather_inputs(
        n_row, n_col, group, qkv_shard, proj_weight, up_weight,
        down_weight, tokens, cotangent, vector, tables if fused else None
    )
    g_one = g.reshape(1)

    def peer_values(x, step):
        pairs = [(q, q - q % group + (q + step) % group) for q in range(n_col)]
        return lax.ppermute(x, "col", pairs)

    def to_columns(x):
        if merge > 1:
            x = x.reshape(NARROW, mine, merge, width).transpose(0, 2, 1, 3).reshape(n_col, mine, width)
        x = lax.all_to_all(x, "col", split_axis=0, concat_axis=0, tiled=True)
        return to_rows(held, x.reshape(n_col * per, BLOCK, width))

    if not fused:
        x = outs["tokens"].astype(F32)
        kept = {name: [] for name in SAVED + ("reds",)}
        for l in range(layers):
            q, kv, red = qkv_kernel(l, x, outs["vec"], outs["qkv"], tables[0], tables[1])
            kvs = [kv] + [peer_values(kv, s) for s in range(1, group)]
            att, lse = attend_kernel(group, g_one, q, kvs)
            mid, x, active, slope, reds = mlp_kernel(
                l, l == layers - 1, x, att, outs["vec"], outs["proj"], outs["up"], outs["down"], tables[2:]
            )
            reds = jnp.concatenate([red[None], reds])
            peer = jnp.stack(kvs[1:]) if group > 1 else kv[None][:0]
            for name, value in zip(SAVED + ("reds",), (q, kv, peer, att, lse, mid, active, slope, x, reds)):
                kept[name].append(value)
        for name in SAVED:
            outs["saved_" + name] = jnp.stack(kept[name][: layers - 1] if name == "x" else kept[name])
        outs["reds"] = jnp.stack(kept["reds"])
        outs["result"] = x
    if fused:
        made = backward(n_row, n_col, group, outs, tables, ids_rows)
        sizes = {"qkv": (128, 384), "mlp": (128, 128, 128, units, units, 128)}
        sums = place(made, sizes, adapters)
        final = list(sums[:2])
        for number, p in enumerate(sums[2:]):
            if number == 1:
                p = p.transpose(0, 1, 3, 2, 4)
            elif number % 2 == 0:
                p = p.transpose(0, 1, 3, 2)
            final.append(p)
        return tuple(final)

    result = to_columns(outs["result"])

    onehot = (adapter_ids.T[:, :, None] == jnp.arange(adapters)[None, None, :]).astype(BF16)

    def all_rows(x):
        pairs = [[(q, (q + s) % n_row) for q in range(n_row)] for s in range(1, n_row)]
        return [x] + [lax.ppermute(x, "row", pair) for pair in pairs]

    onehots = jnp.concatenate(all_rows(onehot), axis=1)

    def collect(parts, named):
        if merge > 1:
            pieces, at = [], 0
            for _, size in named:
                piece = parts[:, :, at : at + size]
                at += size
                if size == 384:
                    piece = piece.reshape(NARROW, rank, 3, merge, width).transpose(0, 3, 1, 2, 4)
                else:
                    piece = piece.reshape(NARROW, rank, merge, size // merge).transpose(0, 2, 1, 3)
                pieces.append(piece.reshape(n_col, rank, size // merge))
            parts = jnp.concatenate(pieces, axis=2)
        parts = lax.all_to_all(parts, "col", split_axis=0, concat_axis=0, tiled=True)
        parts = parts.reshape((seqs, group) + parts.shape[1:]).astype(F32).sum(axis=1).astype(BF16)
        parts = jnp.concatenate(all_rows(parts), axis=0)
        sums, at = [], 0
        for site, size in named:
            piece = parts[:, :, at : at + size // merge]
            at += size // merge
            sums.append(jnp.einsum("sa,srn->arn", onehots[site], piece, preferred_element_type=F32))
        return sums

    wide = outs["down"].shape[1] // NARROW
    grads, carried = [None] * layers, None
    for l in reversed(range(layers + 1)):
        lq, lm = (l if l < layers else None), (l - 1 if l > 0 else None)
        made = back_kernel(lq, lm, group, g_one, outs, tables, carried)
        if lm is not None:
            grads[lm] = collect(made["grads_mlp"], [(1, 128), (1, 128), (2, 128), (2, wide), (3, wide), (3, 128)])
            parts = [made["out_part%d" % s] for s in range(group)]
            parts = [parts[0]] + [peer_values(parts[s], group - s) for s in range(1, group)]
            carried = (made["out_g_mid"], made["out_gq"], parts)
        if lq is not None:
            grads[lq] = collect(made["grads_qkv"], [(0, 128), (0, 384)]) + grads[lq]
    grad = made["out"]
    input_grad = to_columns(grad)

    final = []
    for number in range(8):
        p = jnp.stack([grads[l][number] for l in range(layers)])
        if number == 1:
            p = p.reshape(layers, adapters, rank, 3, width)
        elif number % 2 == 0:
            p = p.transpose(0, 1, 3, 2)
        final.append(p)
    return (result, input_grad) + tuple(final)


def solution(mesh):
    mesh_shape = (mesh.shape["row"], mesh.shape["col"])
    return jax.shard_map(
        functools.partial(shards, mesh_shape),
        mesh=mesh,
        in_specs=(
            P("row", "col"), P("row", "col"), P("row", None),
            P(None, "row", None, "col"), P(None, None, "col"),
            P(None, "col", "row"), P(None, "col"),
            P(None, "row", "col"), P(None, "col"),
            P(None, "col", "row"), P(None, "col"),
            P(None, "col"), P(None, "col"), P(None, "col"), P(None, "col"),
            P(), P(), P(), P(), P(), P(), P(), P(),
        ),
        out_specs=(
            P("row", "col"), P("row", "col"),
            P(None, None, "col", None), P(None, None, None, None, "col"),
            P(None, None, "col", None), P(None, None, None, "col"),
            P(None, None, "col", None), P(None, None, None, "col"),
            P(None, None, "col", None), P(None, None, None, "col"),
        ),
        check_vma=False,
    )
```
